32 devices in a mesh: groups: 2 (over y), blk: 4 (over z), rep: 4 (over x, core).
Axes of the slice: x: 2, y: 2, z: 4, core: 2. Of those that a mesh axis runs over, the one named last changes fastest.
Arguments:
- embeddings: float32 [8192, 128], P(('groups', 'blk')), parts along dimension 0, may hold values from -6 to 6
- degrees: int32 [8192], P(('groups', 'blk')), parts along dimension 0, may hold values from 1 to 12800, as said below
- tile_values: bfloat16 [8, 4, 1, 24, 128, 128], P(('groups', 'blk'), 'rep'), parts along dimension 0
- tile_rows: int32 [8, 4, 1, 24], P(('groups', 'blk'), 'rep'), parts along dimension 0, may hold values from 0 to 7
- tile_columns: int32 [8, 4, 1, 24], P(('groups', 'blk'), 'rep'), parts along dimension 0, may hold values from 0 to 7
- slot_counts: int32 [8, 4, 1], P(('groups', 'blk'), 'rep'), parts along dimension 0, may hold values from 6 to 24, as said below
Outputs:
- combined: float32 [8192, 128], P(('groups', 'blk', 'rep')), parts along dimension 0
The draws below stay inside these ranges and needn't reach their ends.
There are 2 independent parts, one for each index of `groups`. The reference program is written for one: setup_inputs(seed, part) draws one part's arguments, and reference() takes and returns one part's arrays. A program takes and returns all parts, laid end to end along the dimension named above; each array names one. Nothing has to cross between parts.
Inputs may be any that keep to these rules, and one draw needn't show every extreme that they name: `degrees`: each node's degree is at least the number of nonzero entries in its row of A. `slot_counts`: some arc position of some device has all 24 slots live in every draw.
All inputs are finite; a program needn't handle non-finite values.
Results may differ from the reference program's by a relative error of at most 0.0003.
Values sent between devices are 32-bit elements; how exact they have to be, the bound alone decides.
No kernel may reach another device: no remote copies, remote signals or barrier semaphores. Data moves between devices by JAX's collectives and lax.ppermute only.
A program may use at most 64 MiB of HBM per device.

```python
import math
import jax
import jax.numpy as jnp
from jax import lax

WIDTH = 128
TILE = 128
RB_DEV = 8
CAP = 24
LAYERS = 2
CYCLE = 4
TEAMS = 4
ARC = 1
NODES = 4096


def shard_keys(key, shard_index):
    own_key = jax.random.fold_in(key, 202)
    shard_key = jax.random.fold_in(own_key, shard_index)
    return jax.random.split(shard_key)


def shard_mask(key, shard_index):
    mask_key, value_key = shard_keys(key, shard_index)
    slot_shape = (TEAMS, ARC, CAP, TILE, TILE)
    return jax.random.randint(mask_key, slot_shape, 0, 4) == 0


def rows_helper(key):
    own_key = jax.random.fold_in(key, 303)
    first_key, second_key = jax.random.split(own_key)
    slot_shape = (CYCLE, TEAMS, ARC, CAP)
    first_rows = jax.random.randint(first_key, slot_shape, 0, RB_DEV)
    second_rows = jax.random.randint(second_key, slot_shape, 0, RB_DEV)
    return jnp.minimum(first_rows, second_rows).astype(jnp.int32)


def counts_helper(key):
    own_key = jax.random.fold_in(key, 404)
    halve_key, chosen_key = jax.random.split(own_key)
    count_shape = (CYCLE, TEAMS, ARC)
    halvings = jax.random.randint(halve_key, count_shape, 0, 3)
    full_value = jnp.full(count_shape, CAP, jnp.int32)
    counts = jnp.maximum(jnp.right_shift(full_value, halvings), 1)
    flat_counts = counts.reshape(-1)
    chosen_slot = jax.random.randint(chosen_key, (), 0, CYCLE * TEAMS * ARC)
    flat_counts = jnp.where(jnp.arange(CYCLE * TEAMS * ARC) == chosen_slot, CAP, flat_counts)
    return flat_counts.reshape(count_shape).astype(jnp.int32)


def draw_degrees(key, part):
    own_key = jax.random.fold_in(key, 101)
    power_key, extra_key, top_key = jax.random.split(own_key, 3)
    exponents = jax.random.randint(power_key, (NODES,), 0, 9)
    base_value = jnp.left_shift(jnp.ones((NODES,), jnp.int32), exponents)
    extra_value = jax.random.randint(extra_key, (NODES,), 0, base_value)
    outside = base_value + extra_value
    all_rows = rows_helper(key)
    all_counts = counts_helper(key)
    slot_numbers = jnp.arange(CAP, dtype=jnp.int32)
    block_numbers = jnp.arange(RB_DEV, dtype=jnp.int32)

    def one_shard(shard_index):
        kept = shard_mask(key, shard_index).astype(jnp.int32)
        live = (slot_numbers < all_counts[shard_index][..., None]).astype(jnp.int32)
        row_nonzeros = jnp.sum(kept, axis=-1) * live[..., None]
        onehot = (all_rows[shard_index][..., None] == block_numbers).astype(jnp.int32)
        return jnp.einsum('rkjc,rkja->ca', onehot, row_nonzeros)
    inside = lax.map(one_shard, jnp.arange(CYCLE, dtype=jnp.int32)).reshape(NODES)
    total = (inside + outside).astype(jnp.int32)
    top_node = jax.random.randint(top_key, (), 0, NODES)
    top_value = CYCLE * CAP * TILE + 512
    return jnp.where(jnp.arange(NODES, dtype=jnp.int32) == top_node, top_value, total).astype(jnp.int32)


def draw_tile_values(key, part):
    slot_shape = (TEAMS, ARC, CAP, TILE, TILE)

    def one_shard(shard_index):
        mask_key, value_key = shard_keys(key, shard_index)
        kept_mask = shard_mask(key, shard_index)
        weights = jnp.exp(jax.random.uniform(value_key, slot_shape, jnp.float32, math.log(0.5), math.log(5.0)))
        return jnp.where(kept_mask, weights, 0.0).astype(jnp.bfloat16)
    return lax.map(one_shard, jnp.arange(CYCLE, dtype=jnp.int32))


def draw_tile_rows(key, part):
    return rows_helper(key)


def draw_slot_counts(key, part):
    return counts_helper(key)


def plant(values, stream_key, smallest, largest):
    place = [jax.random.randint(jax.random.fold_in(stream_key, axis), (), 0, length) for axis, length in enumerate(values.shape)]
    widest = values.shape.index(max(values.shape))
    next_to = place[:widest] + [(place[widest] + 1) % values.shape[widest]] + place[widest + 1:]
    return values.at[tuple(place)].set(smallest).at[tuple(next_to)].set(largest)


def level_of(rng, shape, pieces, low, largest):
    factor_of = 1.0
    for dim, shards_of in pieces:
        draws = jax.random.uniform(jax.random.fold_in(jax.random.fold_in(rng, 6), dim), (shards_of,), jnp.float32, low / len(pieces), largest / len(pieces))
        factor_of = factor_of * jnp.repeat(jnp.exp(draws), shape[dim] // shards_of).reshape((-1,) + (1,) * (len(shape) - 1 - dim))
    return factor_of


def scatter_about(key, shape, scale, reach, pieces=(), held_as=jnp.bfloat16):
    entries = jax.random.normal(key, shape, jnp.float32) * scale
    if len(pieces) > 0:
        entries = level_of(key, shape, pieces, -0.22, 0.18) * entries
    return jnp.clip(entries, min=-reach, max=reach).astype(held_as)


def setup_inputs(seed: int = 0, part: int = 0) -> dict:
    arg_keys = jax.random.split(jax.random.key(seed), 7)
    part_splits = jax.random.split(jax.random.fold_in(arg_keys[6], part), 7)
    embeddings = scatter_about(part_splits[0], (NODES, WIDTH), 1.0, 6.0, ((0, 4),), jnp.float32)
    degrees = draw_degrees(jax.random.fold_in(jax.random.fold_in(arg_keys[6], part), 71), part)
    tile_values = draw_tile_values(jax.random.fold_in(jax.random.fold_in(arg_keys[6], part), 71), part)
    tile_rows = draw_tile_rows(jax.random.fold_in(jax.random.fold_in(arg_keys[6], part), 71), part)
    tile_columns = plant(jax.random.randint(part_splits[4], (CYCLE, TEAMS, ARC, CAP), 0, RB_DEV), jax.random.fold_in(part_splits[4], 1), 0, RB_DEV - 1).astype(jnp.int32)
    slot_counts = draw_slot_counts(jax.random.fold_in(jax.random.fold_in(arg_keys[6], part), 71), part)
    return {"embeddings": embeddings, "degrees": degrees, "tile_values": tile_values, "tile_rows": tile_rows, "tile_columns": tile_columns, "slot_counts": slot_counts}


def propagate(current, norm_scale, tile_values, tile_rows, tile_columns, slot_counts):
    scaled = (current * norm_scale[:, None]).reshape(CYCLE, RB_DEV, TILE, WIDTH)
    team_offsets = jnp.arange(TEAMS, dtype=jnp.int32)[:, None] * ARC
    arc_offsets = jnp.arange(ARC, dtype=jnp.int32)[None, :]
    slot_numbers = jnp.arange(CAP, dtype=jnp.int32)
    block_numbers = jnp.arange(RB_DEV, dtype=jnp.int32)

    def shard_rows(shard_index):
        sources = jnp.mod(shard_index - team_offsets - arc_offsets, CYCLE).astype(jnp.int32)
        columns = tile_columns[shard_index]
        blocks = scaled[sources[:, :, None], columns]
        products = jnp.einsum('rkjab,rkjbw->rkjaw', tile_values[shard_index].astype(jnp.float32), blocks, precision=lax.Precision.HIGHEST)
        live_slots = slot_numbers < slot_counts[shard_index][..., None]
        placement = ((tile_rows[shard_index][..., None] == block_numbers) & live_slots[..., None]).astype(jnp.float32)
        return jnp.einsum('rkjc,rkjaw->caw', placement, products, precision=lax.Precision.HIGHEST)
    summed = lax.map(shard_rows, jnp.arange(CYCLE, dtype=jnp.int32))
    return summed.reshape(NODES, WIDTH) * norm_scale[:, None]

def reference(embeddings, degrees, tile_values, tile_rows, tile_columns, slot_counts):
    norm_scale = lax.rsqrt(degrees.astype(jnp.float32))
    current = embeddings
    combined = embeddings
    for layer_index in range(LAYERS):
        current = propagate(current, norm_scale, tile_values, tile_rows, tile_columns, slot_counts)
        combined = combined + current
    return combined / (LAYERS + 1.0)
```

```python
import functools

import jax
import jax.numpy as jnp
from jax import lax
from jax.experimental import pallas as pl
from jax.experimental.pallas import tpu as pltpu
from jax.sharding import PartitionSpec as P

LAYERS = 2
VMEM_LIMIT = 16 * 1024 * 1024


def arc_kernel(
    counts_ref, rows_ref, columns_ref, tiles_ref, *refs, team_count, has_partial
):
    pieces = refs[:team_count]
    refs = refs[team_count:]
    partials = refs[:team_count] if has_partial else None
    refs = refs[team_count:] if has_partial else refs
    outs = refs[:team_count]
    split_ref, products_ref, sums_ref = refs[team_count:]
    team_index = lax.axis_index("rep")
    share_rows, width = pieces[0].shape
    slot_total, tile_size, _ = tiles_ref.shape
    panel_rows = share_rows * team_count
    for k in range(team_count):
        owner = lax.rem(team_index + team_count - k, team_count)
        start = pl.multiple_of(owner * share_rows, share_rows)
        value = pieces[k][...]
        high = value.astype(jnp.bfloat16)
        low = (value - high.astype(jnp.float32)).astype(jnp.bfloat16)
        split_ref[pl.ds(start, share_rows), :width] = high
        split_ref[pl.ds(start, share_rows), width:] = low
    for j in range(slot_total):
        source = pl.multiple_of(columns_ref[j] * tile_size, tile_size)
        product = jnp.dot(
            tiles_ref[j],
            split_ref[pl.ds(source, tile_size), :],
            preferred_element_type=jnp.float32,
        )
        products_ref[j] = product[:, :width] + product[:, width:]
    for k in range(team_count):
        at = pl.ds(k * share_rows, share_rows)
        sums_ref[at, :] = partials[k][...] if has_partial else jnp.zeros((share_rows, width), jnp.float32)

    @pl.loop(0, counts_ref[0])
    def _(j):
        start = rows_ref[j] * tile_size - team_index * share_rows
        start = jnp.where(start < 0, start + panel_rows, start)
        at = pl.ds(pl.multiple_of(start, tile_size), tile_size)
        sums_ref[at, :] += products_ref[j]

    for k in range(team_count):
        outs[k][...] = sums_ref[k * share_rows : (k + 1) * share_rows, :]


def arc_step(slots, pieces, partials):
    tile_values, tile_rows, tile_columns, slot_count = slots
    team_count = len(pieces)
    share_rows, width = pieces[0].shape
    slot_total, tile_size, _ = tile_values.shape
    panel_rows = share_rows * team_count
    smem = pl.BlockSpec(memory_space=pltpu.SMEM)
    vmem = pl.BlockSpec(memory_space=pltpu.VMEM)
    share = jax.ShapeDtypeStruct((share_rows, width), jnp.float32)
    operands = [slot_count, tile_rows, tile_columns, tile_values, *pieces, *(partials or ())]
    return pl.pallas_call(
        functools.partial(arc_kernel, team_count=team_count, has_partial=partials is not None),
        out_shape=[share] * team_count,
        in_specs=[smem] * 3 + [vmem] * (len(operands) - 3),
        out_specs=[vmem] * team_count,
        scratch_shapes=[
            pltpu.VMEM((panel_rows, 2 * width), jnp.bfloat16),
            pltpu.VMEM((slot_total, tile_size, width), jnp.float32),
            pltpu.VMEM((panel_rows, width), jnp.float32),
        ],
        compiler_params=pltpu.CompilerParams(vmem_limit_bytes=VMEM_LIMIT),
    )(*operands)


def gather_panel(share, arc_length):
    cycle, team_count = lax.axis_size("blk"), lax.axis_size("rep")
    pieces = []
    for k in range(team_count):
        pairs = []
        for shard in range(cycle):
            for team in range(team_count):
                to_team = (team + k) % team_count
                to_shard = (shard + to_team * arc_length) % cycle
                pairs.append((shard * team_count + team, to_shard * team_count + to_team))
        pieces.append(lax.ppermute(share, ("blk", "rep"), pairs))
    return pieces


def scatter_sum(parts):
    team_count = lax.axis_size("rep")
    total = parts[0]
    for k in range(1, team_count):
        pairs = [(team, (team + k) % team_count) for team in range(team_count)]
        total = total + lax.ppermute(parts[k], "rep", pairs)
    return total


def next_shard(piece):
    cycle = lax.axis_size("blk")
    return lax.ppermute(piece, "blk", [(i, (i + 1) % cycle) for i in range(cycle)])


def per_device(embeddings, degrees, tile_values, tile_rows, tile_columns, slot_counts):
    arc_length = tile_values.shape[2]
    team_index = lax.axis_index("rep")
    team_count = lax.axis_size("rep")
    share_rows = embeddings.shape[0] // team_count
    own = team_index * share_rows
    norm_scale = lax.rsqrt(lax.dynamic_slice_in_dim(degrees, own, share_rows).astype(jnp.float32))
    norm_scale = norm_scale[:, None]
    current = lax.dynamic_slice_in_dim(embeddings, own, share_rows)
    combined = current
    for _ in range(LAYERS):
        pieces = gather_panel(current * norm_scale, arc_length)
        partials = None
        for arc_slot in range(arc_length):
            slots = (
                tile_values[0, 0, arc_slot],
                tile_rows[0, 0, arc_slot],
                tile_columns[0, 0, arc_slot],
                slot_counts[0, 0, arc_slot : arc_slot + 1],
            )
            partials = arc_step(slots, pieces, partials)
            if arc_slot + 1 < arc_length:
                pieces = [next_shard(piece) for piece in pieces]
        current = scatter_sum(partials) * norm_scale
        combined = combined + current
    return combined / (LAYERS + 1.0)


def solution(mesh):
    in_specs = (
        P(("groups", "blk"), None),
        P(("groups", "blk")),
        P(("groups", "blk"), "rep", None, None, None, None),
        P(("groups", "blk"), "rep", None, None),
        P(("groups", "blk"), "rep", None, None),
        P(("groups", "blk"), "rep", None),
    )
    out_specs = P(("groups", "blk", "rep"), None)
    return jax.shard_map(
        per_device, mesh=mesh, in_specs=in_specs, out_specs=out_specs, check_vma=False
    )
```

```python
import functools

import jax
import jax.numpy as jnp
from jax import lax
from jax.experimental import pallas as pl
from jax.experimental.pallas import tpu as pltpu
from jax.sharding import PartitionSpec as P

LAYERS = 2
VMEM_LIMIT = 16 * 1024 * 1024
SMEM = pl.BlockSpec(memory_space=pltpu.SMEM)
VMEM = pl.BlockSpec(memory_space=pltpu.VMEM)
ANY = pl.BlockSpec(memory_space=pl.ANY)


def pair_teams(team_index, column, team_count):
    columns = team_count // 2
    return 2 * lax.rem(team_index // 2 + column, columns) + lax.rem(team_index, 2)


def write_norm(degrees_ref, norm_ref):
    block_count, tile_size = degrees_ref.shape
    width = norm_ref.shape[1]
    turned = jnp.transpose(lax.rsqrt(degrees_ref[...].astype(jnp.float32)))
    for block in range(block_count):
        norm_ref[block * tile_size : (block + 1) * tile_size, :] = jnp.broadcast_to(
            turned[:, block : block + 1], (tile_size, width)
        )


def norm_kernel(degrees_ref, norm_ref):
    write_norm(degrees_ref, norm_ref)


def norm_panel(degrees, width):
    block_count, tile_size = degrees.shape
    return pl.pallas_call(
        norm_kernel,
        out_shape=jax.ShapeDtypeStruct((block_count * tile_size, width), jnp.float32),
        in_specs=[VMEM],
        out_specs=VMEM,
        compiler_params=pltpu.CompilerParams(vmem_limit_bytes=VMEM_LIMIT),
    )(degrees)


def prepare_kernel(
    degrees_ref, embeddings_ref, tiles_ref, *refs, team_count
):
    columns = team_count // 2
    held_tiles_ref, share_ref = refs[:2]
    norm_refs = refs[2 : 2 + columns]
    panel_ref, sems = refs[2 + columns :]
    share_rows = share_ref.shape[0]
    team_index = lax.axis_index("rep")
    start = pl.multiple_of(team_index * share_rows, share_rows)
    tiles_copy = pltpu.make_async_copy(tiles_ref, held_tiles_ref, sems.at[0])
    share_copy = pltpu.make_async_copy(
        embeddings_ref.at[pl.ds(start, share_rows), :], share_ref, sems.at[1]
    )
    tiles_copy.start()
    share_copy.start()
    write_norm(degrees_ref, panel_ref)
    for column in range(columns):
        team = pair_teams(team_index, column, team_count)
        at = pl.ds(pl.multiple_of(team * share_rows, share_rows), share_rows)
        norm_refs[column][...] = panel_ref[at, :]
    share_copy.wait()
    tiles_copy.wait()


def prepare(degrees, embeddings, tile_values):
    team_count = lax.axis_size("rep")
    panel_rows, width = embeddings.shape
    share = jax.ShapeDtypeStruct((panel_rows // team_count, width), jnp.float32)
    held = jax.ShapeDtypeStruct(tile_values.shape, tile_values.dtype)
    columns = team_count // 2
    tiles, own, *norms = pl.pallas_call(
        functools.partial(prepare_kernel, team_count=team_count),
        out_shape=[held, share] + [share] * columns,
        in_specs=[VMEM, ANY, ANY],
        out_specs=[VMEM] * (2 + columns),
        scratch_shapes=[
            pltpu.VMEM((panel_rows, width), jnp.float32),
            pltpu.SemaphoreType.DMA((2,)),
        ],
        compiler_params=pltpu.CompilerParams(vmem_limit_bytes=VMEM_LIMIT),
        cost_estimate=pl.CostEstimate(flops=panel_rows * width, bytes_accessed=4 * panel_rows * width, transcendentals=0),
    )(degrees, embeddings, tile_values)
    return tiles, own, norms


def arc_kernel(info_ref, tiles_ref, *refs, team_count, piece_count, scaled, has_partial):
    norm_ref = refs[0] if scaled else None
    refs = refs[1:] if scaled else refs
    pieces, refs = refs[:piece_count], refs[piece_count:]
    partials, refs = (refs[:2], refs[2:]) if has_partial else (None, refs)
    outs, (split_ref, products_ref, sums_ref) = refs[:2], refs[2:]
    team_index = lax.axis_index("rep")
    columns = team_count // 2
    slot_total, tile_size, _ = tiles_ref.shape
    panel_rows, width = sums_ref.shape
    share_rows = panel_rows // team_count

    def split(value, at):
        high = value.astype(jnp.bfloat16)
        split_ref[at, :width] = high
        split_ref[at, width:] = (value - high.astype(jnp.float32)).astype(jnp.bfloat16)

    if piece_count == 1:
        value = pieces[0][...]
        split(value * norm_ref[...] if scaled else value, pl.ds(0, panel_rows))
    else:
        for k in range(piece_count):
            team = team_index if k % 2 == 0 else team_count - 1 - team_index
            team = pair_teams(team, k // 2, team_count)
            split(pieces[k][...], pl.ds(pl.multiple_of(team * share_rows, share_rows), share_rows))
    for j in range(slot_total):
        source = pl.multiple_of(info_ref[1 + slot_total + j] * tile_size, tile_size)
        product = jnp.dot(
            tiles_ref[j],
            split_ref[pl.ds(source, tile_size), :],
            preferred_element_type=jnp.float32,
        )
        products_ref[j] = product[:, :width] + product[:, width:]
    sums_ref[...] = jnp.zeros_like(sums_ref)

    @pl.loop(0, info_ref[0])
    def _(j):
        at = pl.ds(pl.multiple_of(info_ref[1 + j] * tile_size, tile_size), tile_size)
        sums_ref[at, :] += products_ref[j]

    for half in range(2):
        for column in range(columns):
            team = pair_teams(team_index, column, team_count)
            team = team if half == 0 else team + 1 - 2 * lax.rem(team, 2)
            at = pl.ds(pl.multiple_of(team * share_rows, share_rows), share_rows)
            to = slice(column * share_rows, (column + 1) * share_rows)
            value = sums_ref[at, :]
            outs[half][to, :] = value + partials[half][to, :] if has_partial else value


def arc_step(info, tiles, norm, pieces, partials):
    team_count = lax.axis_size("rep")
    panel_rows = sum(piece.shape[0] for piece in pieces)
    width = pieces[0].shape[1]
    slot_total, tile_size, _ = tiles.shape
    half = jax.ShapeDtypeStruct((panel_rows // 2, width), jnp.float32)
    operands = [info, tiles, *(() if norm is None else (norm,)), *pieces, *(partials or ())]
    return pl.pallas_call(
        functools.partial(
            arc_kernel,
            team_count=team_count,
            piece_count=len(pieces),
            scaled=norm is not None,
            has_partial=partials is not None,
        ),
        out_shape=[half] * 2,
        in_specs=[SMEM] + [VMEM] * (len(operands) - 1),
        out_specs=[VMEM] * 2,
        scratch_shapes=[
            pltpu.VMEM((panel_rows, 2 * width), jnp.bfloat16),
            pltpu.VMEM((slot_total, tile_size, width), jnp.float32),
            pltpu.VMEM((panel_rows, width), jnp.float32),
        ],
        compiler_params=pltpu.CompilerParams(vmem_limit_bytes=VMEM_LIMIT),
    )(*operands)


def to_arc_start(value, source_team, arc_length):
    cycle, team_count = lax.axis_size("blk"), lax.axis_size("rep")
    pairs = []
    for shard in range(cycle):
        for team in range(team_count):
            to_shard = (shard + team * arc_length) % cycle
            pairs.append((shard * team_count + source_team(team), to_shard * team_count + team))
    return lax.ppermute(value, ("blk", "rep"), pairs)


def next_shard(value):
    cycle = lax.axis_size("blk")
    return lax.ppermute(value, "blk", [(i, (i + 1) % cycle) for i in range(cycle)])


def from_mate(value):
    team_count = lax.axis_size("rep")
    return lax.ppermute(value, "rep", [(team, team ^ 1) for team in range(team_count)])


def from_column(value, distance):
    team_count = lax.axis_size("rep")
    pairs = [((team + 2 * distance) % team_count, team) for team in range(team_count)]
    return lax.ppermute(value, "rep", pairs)


def column_sum(shares, column):
    columns = len(shares)
    total = shares[column]
    for distance in range(1, columns):
        total = total + from_column(shares[(column - distance) % columns], distance)
    return total


def per_device(embeddings, degrees, tile_values, tile_rows, tile_columns, slot_counts):
    arc_length, slot_total, tile_size, _ = tile_values.shape[2:]
    panel_rows, width = embeddings.shape
    team_count = lax.axis_size("rep")
    columns = team_count // 2
    share_rows = panel_rows // team_count
    spread = (1, 2, 0, 3) if team_count == 4 else tuple(range(team_count))
    degrees = degrees.reshape(panel_rows // tile_size, tile_size)

    panel = to_arc_start(embeddings, lambda team: spread[team], arc_length)
    source_degrees = to_arc_start(degrees, lambda team: spread[team], arc_length)
    tiles, own, norms = prepare(degrees, embeddings, tile_values[0, 0])
    info = jnp.concatenate([slot_counts[0, 0][:, None], tile_rows[0, 0], tile_columns[0, 0]], axis=1)
    source_norm = norm_panel(source_degrees, width)

    pieces, combined = [panel], own
    for layer in range(LAYERS):
        partials = None
        for arc_slot in range(arc_length):
            partials = arc_step(info[arc_slot], tiles[arc_slot], source_norm, pieces, partials)
            if arc_slot + 1 < arc_length:
                pieces = [next_shard(piece) for piece in pieces]
                if source_norm is not None:
                    source_degrees = next_shard(source_degrees)
                    source_norm = norm_panel(source_degrees, width)
        source_norm = None
        summed = partials[0] + from_mate(partials[1])
        shares = [summed[i * share_rows : (i + 1) * share_rows] for i in range(columns)]
        last = layer + 1 == LAYERS
        pieces = []
        for column in range(1 if last else columns):
            current = column_sum(shares, column) * norms[column]
            if column == 0:
                combined = combined + current
            if not last:
                scaled = current * norms[column]
                pieces.append(to_arc_start(scaled, lambda team: team, arc_length))
                pieces.append(to_arc_start(scaled, lambda team: team_count - 1 - team, arc_length))
    return combined / (LAYERS + 1.0)


def solution(mesh):
    in_specs = (
        P(("groups", "blk"), None),
        P(("groups", "blk")),
        P(("groups", "blk"), "rep", None, None, None, None),
        P(("groups", "blk"), "rep", None, None),
        P(("groups", "blk"), "rep", None, None),
        P(("groups", "blk"), "rep", None),
    )
    out_specs = P(("groups", "blk", "rep"), None)
    return jax.shard_map(
        per_device, mesh=mesh, in_specs=in_specs, out_specs=out_specs, check_vma=False
    )
```

```python
import functools

import jax
import jax.numpy as jnp
from jax import lax
from jax.experimental import pallas as pl
from jax.experimental.pallas import tpu as pltpu
from jax.sharding import PartitionSpec as P

LAYERS = 2
PARTS = 2
VMEM_LIMIT = 16 * 1024 * 1024
SMEM = pl.BlockSpec(memory_space=pltpu.SMEM)
VMEM = pl.BlockSpec(memory_space=pltpu.VMEM)
HBM = pl.BlockSpec(memory_space=pltpu.HBM)
ANY = pl.BlockSpec(memory_space=pl.ANY)


def pair_teams(team_index, column, team_count):
    columns = team_count // 2
    return 2 * lax.rem(team_index // 2 + column, columns) + lax.rem(team_index, 2)


def lower_lanes(shape):
    return lax.broadcasted_iota(jnp.int32, shape, 1) < shape[1] // 2


def swap_lanes(value):
    return pltpu.roll(value, value.shape[1] // 2, 1)


def lane_join(lower, upper):
    return jnp.where(lower_lanes(lower.shape), lower, upper)


def write_norm(degrees_ref, norm_ref):
    block_count, tile_size = degrees_ref.shape
    width = norm_ref.shape[1]
    turned = jnp.transpose(lax.rsqrt(degrees_ref[...].astype(jnp.float32)))
    for block in range(block_count):
        norm_ref[block * tile_size : (block + 1) * tile_size, :] = jnp.broadcast_to(
            turned[:, block : block + 1], (tile_size, width)
        )


def pack_kernel(degrees_hbm, embeddings_hbm, first_ref, second_ref, degrees_ref, norm_ref, held_ref, sems, *, team_count):
    share_rows = held_ref.shape[0] // team_count
    half = share_rows // 2
    copies = [pltpu.make_async_copy(degrees_hbm, degrees_ref, sems.at[team_count])]
    for team in range(team_count):
        at = pl.ds(team * share_rows, share_rows)
        copies.append(pltpu.make_async_copy(embeddings_hbm.at[at, :], held_ref.at[at, :], sems.at[team]))
    for copy in copies:
        copy.start()
    copies[0].wait()
    write_norm(degrees_ref, norm_ref)
    for team in range(team_count):
        copies[1 + team].wait()
        at = pl.ds(team * share_rows, half)
        upper_at = pl.ds(team * share_rows + half, half)
        top = held_ref[at, :] * norm_ref[at, :]
        bottom = held_ref[upper_at, :] * norm_ref[upper_at, :]
        to = pl.ds(team * half, half)
        first_ref[to, :] = lane_join(top, swap_lanes(bottom))
        second_ref[to, :] = lane_join(swap_lanes(top), bottom)


def pack_panel(degrees, embeddings):
    team_count = lax.axis_size("rep")
    panel_rows, width = embeddings.shape
    packed = jax.ShapeDtypeStruct((panel_rows // PARTS, width), jnp.float32)
    return pl.pallas_call(
        functools.partial(pack_kernel, team_count=team_count),
        out_shape=[packed] * PARTS,
        in_specs=[HBM, HBM],
        out_specs=[VMEM] * PARTS,
        scratch_shapes=[
            pltpu.VMEM(degrees.shape, degrees.dtype),
            pltpu.VMEM((panel_rows, width), jnp.float32),
            pltpu.VMEM((panel_rows, width), jnp.float32),
            pltpu.SemaphoreType.DMA((team_count + 1,)),
        ],
        compiler_params=pltpu.CompilerParams(vmem_limit_bytes=VMEM_LIMIT),
    )(degrees, embeddings)


def prepare_kernel(
    degrees_hbm, embeddings_hbm, tiles_hbm, held_tiles_ref, own_ref, norms_ref, degrees_ref, panel_ref, sems, *, team_count
):
    share_rows = own_ref.shape[0]
    half = share_rows // 2
    team_index = lax.axis_index("rep")
    start = pl.multiple_of(team_index * share_rows, share_rows)
    degrees_copy = pltpu.make_async_copy(degrees_hbm, degrees_ref, sems.at[0])
    tiles_copy = pltpu.make_async_copy(tiles_hbm, held_tiles_ref, sems.at[1])
    own_copy = pltpu.make_async_copy(embeddings_hbm.at[pl.ds(start, share_rows), :], own_ref, sems.at[2])
    degrees_copy.start()
    tiles_copy.start()
    own_copy.start()
    degrees_copy.wait()
    write_norm(degrees_ref, panel_ref)
    for column in range(team_count // 2):
        first_row = pair_teams(team_index, column, team_count) * share_rows
        top = panel_ref[pl.ds(pl.multiple_of(first_row, half), half), :]
        bottom = panel_ref[pl.ds(pl.multiple_of(first_row + half, half), half), :]
        norms_ref[pl.ds(column * half, half), :] = lane_join(top, bottom)
    own_copy.wait()
    tiles_copy.wait()


def prepare(degrees, embeddings, tile_values):
    team_count = lax.axis_size("rep")
    panel_rows, width = embeddings.shape
    return pl.pallas_call(
        functools.partial(prepare_kernel, team_count=team_count),
        out_shape=[
            jax.ShapeDtypeStruct(tile_values.shape, tile_values.dtype),
            jax.ShapeDtypeStruct((panel_rows // team_count, width), jnp.float32),
            jax.ShapeDtypeStruct((panel_rows // 4, width), jnp.float32),
        ],
        in_specs=[HBM, HBM, HBM],
        out_specs=[VMEM] * 3,
        scratch_shapes=[
            pltpu.VMEM(degrees.shape, degrees.dtype),
            pltpu.VMEM((panel_rows, width), jnp.float32),
            pltpu.SemaphoreType.DMA((3,)),
        ],
        compiler_params=pltpu.CompilerParams(vmem_limit_bytes=VMEM_LIMIT),
        cost_estimate=pl.CostEstimate(
            flops=panel_rows * width, bytes_accessed=4 * panel_rows * width, transcendentals=0
        ),
    )(degrees, embeddings, tile_values)


def arc_kernel(info_ref, tiles_ref, *refs, team_count, piece_count, has_partial, after_count):
    pieces, refs = refs[:piece_count], refs[piece_count:]
    partials, refs = (refs[:2], refs[2:]) if has_partial else (None, refs)
    outs, (split_ref, products_ref, sums_ref) = refs[after_count : after_count + 2], refs[after_count + 2 :]
    team_index = lax.axis_index("rep")
    columns = team_count // 2
    slot_total, tile_size, _ = tiles_ref.shape
    panel_rows, width = sums_ref.shape
    half = panel_rows // team_count // 2

    def split(value, team):
        high = value.astype(jnp.bfloat16).astype(jnp.float32)
        low = value - high
        top = lane_join(high, swap_lanes(low)).astype(jnp.bfloat16)
        bottom = lane_join(swap_lanes(high), low).astype(jnp.bfloat16)
        split_ref[pl.ds(pl.multiple_of(team * 2 * half, half), half), :] = top
        split_ref[pl.ds(pl.multiple_of(team * 2 * half + half, half), half), :] = bottom

    if piece_count == 1:
        for team in range(team_count):
            split(pieces[0][team * half : (team + 1) * half, :], team)
    else:
        for k in range(piece_count):
            source = team_index if k == 0 else team_count - 1 - team_index
            for column in range(columns):
                value = pieces[k][column * half : (column + 1) * half, :]
                split(value, pair_teams(source, column, team_count))
    for j in range(slot_total):
        source = pl.multiple_of(info_ref[1 + slot_total + j] * tile_size, tile_size)
        products_ref[j] = jnp.dot(
            tiles_ref[j],
            split_ref[pl.ds(source, tile_size), :],
            preferred_element_type=jnp.float32,
        )
    sums_ref[...] = jnp.zeros_like(sums_ref)

    @pl.loop(0, info_ref[0])
    def _(j):
        at = pl.ds(pl.multiple_of(info_ref[1 + j] * tile_size, tile_size), tile_size)
        sums_ref[at, :] += products_ref[j]

    for parity in range(2):
        for column in range(columns):
            team = pair_teams(team_index, column, team_count)
            team = team if parity == 0 else team + 1 - 2 * lax.rem(team, 2)
            top = sums_ref[pl.ds(pl.multiple_of(team * 2 * half, half), half), :]
            bottom = sums_ref[pl.ds(pl.multiple_of(team * 2 * half + half, half), half), :]
            value = lane_join(top + swap_lanes(top), bottom + swap_lanes(bottom))
            to = slice(column * half, (column + 1) * half)
            outs[parity][to, :] = value + partials[parity][to, :] if has_partial else value


def arc_step(info, tiles, pieces, partials, after):
    team_count = lax.axis_size("rep")
    packed_rows = sum(piece.shape[0] for piece in pieces)
    width = pieces[0].shape[1]
    slot_total, tile_size, _ = tiles.shape
    parity = jax.ShapeDtypeStruct((packed_rows // 2, width), jnp.float32)
    operands = [info, tiles, *pieces, *(partials or ()), *after]
    return pl.pallas_call(
        functools.partial(
            arc_kernel,
            team_count=team_count,
            piece_count=len(pieces),
            has_partial=partials is not None,
            after_count=len(after),
        ),
        out_shape=[parity] * 2,
        in_specs=[SMEM] + [VMEM] * (len(operands) - 1 - len(after)) + [ANY] * len(after),
        out_specs=[VMEM] * 2,
        scratch_shapes=[
            pltpu.VMEM((2 * packed_rows, width), jnp.bfloat16),
            pltpu.VMEM((slot_total, tile_size, width), jnp.float32),
            pltpu.VMEM((2 * packed_rows, width), jnp.float32),
        ],
        compiler_params=pltpu.CompilerParams(vmem_limit_bytes=VMEM_LIMIT),
        cost_estimate=pl.CostEstimate(
            flops=2 * slot_total * tile_size * tile_size * width, bytes_accessed=8 * packed_rows * width, transcendentals=0
        ),
    )(*operands)


def column_sum_kernel(shares_ref, norms_ref, *refs):
    others, (current_ref, source_ref) = refs[:-2], refs[-2:]
    half = current_ref.shape[0]
    columns = shares_ref.shape[0] // half
    for column in range(columns):
        at = pl.ds(column * half, half)
        total = shares_ref[at, :]
        for distance, other_ref in enumerate(others, 1):
            total = total + other_ref[pl.ds((column - distance) % columns * half, half), :]
        current = total * norms_ref[at, :]
        if column == 0:
            current_ref[...] = current
        source_ref[at, :] = current * norms_ref[at, :]


def column_sum(shares, norms, others, half):
    return pl.pallas_call(
        column_sum_kernel,
        out_shape=[
            jax.ShapeDtypeStruct((half, shares.shape[1]), jnp.float32),
            jax.ShapeDtypeStruct(shares.shape, jnp.float32),
        ],
        in_specs=[VMEM] * (2 + len(others)),
        out_specs=[VMEM] * 2,
        compiler_params=pltpu.CompilerParams(vmem_limit_bytes=VMEM_LIMIT),
    )(shares, norms, *others)


def finish_kernel(own_ref, norms_ref, *refs, layer_count):
    out_ref = refs[-1]
    half = out_ref.shape[0] // 2
    terms = len(refs[:-1]) // PARTS
    parts = []
    for part in range(PARTS):
        current_ref, shares_ref, *others = refs[part * terms : (part + 1) * terms]
        total = shares_ref[:half, :]
        for other_ref in others:
            total = total + other_ref[...]
        parts.append(current_ref[...] + total * norms_ref[:half, :])
    top = lane_join(parts[0], swap_lanes(parts[1]))
    bottom = lane_join(swap_lanes(parts[0]), parts[1])
    out_ref[:half, :] = (own_ref[:half, :] + top) / layer_count
    out_ref[half:, :] = (own_ref[half:, :] + bottom) / layer_count


def finish(own, norms, parts):
    operands = [operand for part in parts for operand in part]
    return pl.pallas_call(
        functools.partial(finish_kernel, layer_count=LAYERS + 1.0),
        out_shape=jax.ShapeDtypeStruct(own.shape, jnp.float32),
        in_specs=[VMEM] * (2 + len(operands)),
        out_specs=VMEM,
        compiler_params=pltpu.CompilerParams(vmem_limit_bytes=VMEM_LIMIT),
    )(own, norms, *operands)


def hold_kernel(value_ref, after_ref, out_ref):
    del value_ref, after_ref, out_ref


def hold(value, after):
    return pl.pallas_call(
        hold_kernel,
        out_shape=jax.ShapeDtypeStruct(value.shape, value.dtype),
        in_specs=[ANY, ANY],
        out_specs=ANY,
        input_output_aliases={0: 0},
        compiler_params=pltpu.CompilerParams(vmem_limit_bytes=VMEM_LIMIT),
    )(value, after)


def to_arc_start(value, source_team, arc_length):
    cycle, team_count = lax.axis_size("blk"), lax.axis_size("rep")
    pairs = []
    for shard in range(cycle):
        for team in range(team_count):
            to_shard = (shard + team * arc_length) % cycle
            pairs.append((shard * team_count + source_team(team), to_shard * team_count + team))
    return lax.ppermute(value, ("blk", "rep"), pairs)


def next_shard(value):
    cycle = lax.axis_size("blk")
    return lax.ppermute(value, "blk", [(i, (i + 1) % cycle) for i in range(cycle)])


def from_mate(value):
    team_count = lax.axis_size("rep")
    return lax.ppermute(value, "rep", [(team, team ^ 1) for team in range(team_count)])


def from_column(value, distance):
    team_count = lax.axis_size("rep")
    pairs = [((team + 2 * distance) % team_count, team) for team in range(team_count)]
    return lax.ppermute(value, "rep", pairs)


def per_device(embeddings, degrees, tile_values, tile_rows, tile_columns, slot_counts):
    arc_length, slot_total, tile_size, _ = tile_values.shape[2:]
    panel_rows, width = embeddings.shape
    team_count = lax.axis_size("rep")
    columns = team_count // 2
    half = panel_rows // team_count // 2
    spread = (1, 2, 0, 3) if team_count == 4 else tuple(range(team_count))
    degrees = degrees.reshape(panel_rows // tile_size, tile_size)
    info = jnp.concatenate([slot_counts[0, 0][:, None], tile_rows[0, 0], tile_columns[0, 0]], axis=1)

    def arc(pieces, after):
        partials = None
        for arc_slot in range(arc_length):
            partials = arc_step(info[arc_slot], tiles[arc_slot], pieces, partials, after if arc_slot == 0 else ())
            if arc_slot + 1 < arc_length:
                pieces = [next_shard(piece) for piece in pieces]
        return partials

    packed = pack_panel(degrees, embeddings)
    pieces = [to_arc_start(packed[0], lambda team: spread[team], arc_length)]
    pieces.append(to_arc_start(hold(packed[1], pieces[0]), lambda team: spread[team], arc_length))
    pieces = [[piece] for piece in pieces]
    tiles, own, norms = prepare(degrees, embeddings, tile_values[0, 0])
    layers = [[] for _ in range(PARTS)]
    after = ()
    for layer in range(LAYERS):
        last = layer + 1 == LAYERS
        for part in range(PARTS):
            keep, give = arc(pieces[part], after)
            shares = keep + from_mate(give)
            after = (shares,)
            if last:
                others = [
                    from_column(lax.slice_in_dim(shares, at * half, (at + 1) * half), columns - at)
                    for at in range(1, columns)
                ]
                layers[part] += [shares, *others]
                continue
            others = [from_column(shares, distance) for distance in range(1, columns)]
            current, source = column_sum(shares, norms, others, half)
            layers[part].append(current)
            pieces[part] = [
                to_arc_start(source, lambda team: team, arc_length),
                to_arc_start(source, lambda team: team_count - 1 - team, arc_length),
            ]
    return finish(own, norms, layers)


def solution(mesh):
    in_specs = (
        P(("groups", "blk"), None),
        P(("groups", "blk")),
        P(("groups", "blk"), "rep", None, None, None, None),
        P(("groups", "blk"), "rep", None, None),
        P(("groups", "blk"), "rep", None, None),
        P(("groups", "blk"), "rep", None),
    )
    out_specs = P(("groups", "blk", "rep"), None)
    return jax.shard_map(
        per_device, mesh=mesh, in_specs=in_specs, out_specs=out_specs, check_vma=False
    )
```

```python
import functools

import jax
import jax.numpy as jnp
from jax import lax
from jax.experimental import pallas as pl
from jax.experimental.pallas import tpu as pltpu
from jax.sharding import PartitionSpec as P

LAYERS = 2
VMEM_LIMIT = 16 * 1024 * 1024
VMEM = pl.BlockSpec(memory_space=pltpu.VMEM)
ANY = pl.BlockSpec(memory_space=pl.ANY)


def pair_teams(team_index, column, team_count):
    columns = team_count // 2
    return 2 * lax.rem(team_index // 2 + column, columns) + lax.rem(team_index, 2)


def norm_columns(degrees):
    return jnp.transpose(lax.rsqrt(degrees.astype(jnp.float32)))


def prepare_kernel(degrees_ref, embeddings_ref, tiles_ref, held_tiles_ref, own_ref, norm_ref, panel_ref, sems):
    share_rows, width = own_ref.shape
    block_count, tile_size = degrees_ref.shape
    team_index = lax.axis_index("rep")
    at = pl.ds(pl.multiple_of(team_index * share_rows, share_rows), share_rows)
    tiles_copy = pltpu.make_async_copy(tiles_ref, held_tiles_ref, sems.at[0])
    own_copy = pltpu.make_async_copy(embeddings_ref.at[at, :], own_ref, sems.at[1])
    tiles_copy.start()
    own_copy.start()
    norms = norm_columns(degrees_ref[...])
    for block in range(block_count):
        panel_ref[block * tile_size : (block + 1) * tile_size, :] = jnp.broadcast_to(
            norms[:, block : block + 1], (tile_size, width)
        )
    norm_ref[...] = panel_ref[at, :]
    own_copy.wait()
    tiles_copy.wait()


def prepare(degrees, embeddings, tile_values):
    panel_rows, width = embeddings.shape
    share = jax.ShapeDtypeStruct((panel_rows // lax.axis_size("rep"), width), jnp.float32)
    return pl.pallas_call(
        prepare_kernel,
        out_shape=[jax.ShapeDtypeStruct(tile_values.shape, tile_values.dtype), share, share],
        in_specs=[VMEM, ANY, ANY],
        out_specs=[VMEM] * 3,
        scratch_shapes=[pltpu.VMEM((panel_rows, width), jnp.float32), pltpu.SemaphoreType.DMA((2,))],
        compiler_params=pltpu.CompilerParams(vmem_limit_bytes=VMEM_LIMIT),
        cost_estimate=pl.CostEstimate(
            flops=panel_rows * width, bytes_accessed=4 * panel_rows * width, transcendentals=0
        ),
    )(degrees, embeddings, tile_values)


def arc_kernel(info_ref, tiles_ref, *refs, team_count, piece_count, scaled, partial_count):
    columns = team_count // 2
    degrees_ref = refs[0] if scaled else None
    refs = refs[1:] if scaled else refs
    pieces, refs = refs[:piece_count], refs[piece_count:]
    partials, refs = refs[:partial_count], refs[partial_count:]
    outs, (table_ref, split_ref, sums_ref, sem) = refs[: columns + 1], refs[columns + 1 :]
    team_index = lax.axis_index("rep")
    slot_total, tile_size, _ = tiles_ref.shape
    panel_rows, width = split_ref.shape[0], split_ref.shape[1] // 2
    share_rows = panel_rows // team_count
    block_count = panel_rows // tile_size
    table_copy = pltpu.make_async_copy(info_ref, table_ref, sem)
    table_copy.start()

    def split(value, at):
        high = value.astype(jnp.bfloat16)
        split_ref[at, :width] = high
        split_ref[at, width:] = (value - high.astype(jnp.float32)).astype(jnp.bfloat16)

    if piece_count == 1:
        norms = norm_columns(degrees_ref[...]) if scaled else None
        for block in range(block_count):
            at = pl.ds(block * tile_size, tile_size)
            value = pieces[0][at, :]
            split(value * norms[:, block : block + 1] if scaled else value, at)
    else:
        for k in range(piece_count):
            owner = lax.rem(team_index + team_count - k, team_count)
            split(pieces[k][...], pl.ds(pl.multiple_of(owner * share_rows, share_rows), share_rows))
    sums_ref[...] = jnp.zeros_like(sums_ref)
    table_copy.wait()
    live_count = table_ref[0]
    for j in range(slot_total):
        source = pl.multiple_of(table_ref[1 + slot_total + j] * tile_size, tile_size)
        product = jnp.dot(
            tiles_ref[j],
            split_ref[pl.ds(source, tile_size), :],
            preferred_element_type=jnp.float32,
        )
        row = jnp.where(j < live_count, table_ref[1 + j], block_count)
        at = pl.ds(pl.multiple_of(row * tile_size, tile_size), tile_size)
        sums_ref[at, :] += product[:, :width] + product[:, width:]

    for parity in range(2):
        for column in range(columns):
            team = pair_teams(team_index, column, team_count)
            team = team if parity == 0 else team + 1 - 2 * lax.rem(team, 2)
            value = sums_ref[pl.ds(pl.multiple_of(team * share_rows, share_rows), share_rows), :]
            to = pl.ds(0 if parity == 0 else column * share_rows, share_rows)
            target = column if parity == 0 else columns
            outs[target][to, :] = value + partials[target][to, :] if partials else value


def arc_step(info, tiles, degrees, pieces, partials):
    team_count = lax.axis_size("rep")
    columns = team_count // 2
    panel_rows = sum(piece.shape[0] for piece in pieces)
    width = pieces[0].shape[1]
    slot_total, tile_size, _ = tiles.shape
    share = jax.ShapeDtypeStruct((panel_rows // team_count, width), jnp.float32)
    other = jax.ShapeDtypeStruct((panel_rows // 2, width), jnp.float32)
    operands = [info, tiles, *(() if degrees is None else (degrees,)), *pieces, *partials]
    return pl.pallas_call(
        functools.partial(
            arc_kernel,
            team_count=team_count,
            piece_count=len(pieces),
            scaled=degrees is not None,
            partial_count=len(partials),
        ),
        out_shape=[share] * columns + [other],
        in_specs=[ANY] + [VMEM] * (len(operands) - 1),
        out_specs=[VMEM] * (columns + 1),
        scratch_shapes=[
            pltpu.SMEM(info.shape, info.dtype),
            pltpu.VMEM((panel_rows, 2 * width), jnp.bfloat16),
            pltpu.VMEM((panel_rows + tile_size, width), jnp.float32),
            pltpu.SemaphoreType.DMA,
        ],
        compiler_params=pltpu.CompilerParams(vmem_limit_bytes=VMEM_LIMIT),
        cost_estimate=pl.CostEstimate(
            flops=4 * slot_total * tile_size * tile_size * width, bytes_accessed=8 * panel_rows * width, transcendentals=0
        ),
    )(*operands)


def fetch(value, source_team, arc_length):
    cycle, team_count = lax.axis_size("blk"), lax.axis_size("rep")
    pairs = []
    for shard in range(cycle):
        for team in range(team_count):
            to_shard = (shard + team * arc_length) % cycle
            pairs.append((shard * team_count + source_team(team), to_shard * team_count + team))
    return lax.ppermute(value, ("blk", "rep"), pairs)


def next_shard(value):
    cycle = lax.axis_size("blk")
    return lax.ppermute(value, "blk", [(i, (i + 1) % cycle) for i in range(cycle)])


def from_mate(value):
    team_count = lax.axis_size("rep")
    return lax.ppermute(value, "rep", [(team, team ^ 1) for team in range(team_count)])


def from_column(value, distance):
    team_count = lax.axis_size("rep")
    pairs = [((team + 2 * distance) % team_count, team) for team in range(team_count)]
    return lax.ppermute(value, "rep", pairs)


def team_sum(sums):
    *own, other = sums
    columns = len(own)
    share_rows = own[0].shape[0]
    received = from_mate(other)
    shares = [
        own[column] + received[column * share_rows : (column + 1) * share_rows] for column in range(columns)
    ]
    total = shares[0]
    for distance in range(1, columns):
        total = total + from_column(shares[columns - distance], distance)
    return total


def per_device(embeddings, degrees, tile_values, tile_rows, tile_columns, slot_counts):
    arc_length, _, tile_size, _ = tile_values.shape[2:]
    panel_rows = embeddings.shape[0]
    team_count = lax.axis_size("rep")
    spread = (1, 2, 0, 3) if team_count == 4 else tuple(range(team_count))
    degrees = degrees.reshape(panel_rows // tile_size, tile_size)

    pieces = [fetch(embeddings, lambda team: spread[team], arc_length)]
    source_degrees = fetch(degrees, lambda team: spread[team], arc_length)
    tiles, own, norm_scale = prepare(degrees, embeddings, tile_values[0, 0])
    info = jnp.concatenate([slot_counts[0, 0][:, None], tile_rows[0, 0], tile_columns[0, 0]], axis=1)

    combined = own
    for layer in range(LAYERS):
        sums = ()
        for arc_slot in range(arc_length):
            sums = arc_step(info[arc_slot], tiles[arc_slot], source_degrees, pieces, sums)
            if arc_slot + 1 < arc_length:
                pieces = [next_shard(piece) for piece in pieces]
                if source_degrees is not None:
                    source_degrees = next_shard(source_degrees)
        source_degrees = None
        current = team_sum(sums) * norm_scale
        combined = combined + current
        if layer + 1 < LAYERS:
            source = current * norm_scale
            pieces = [
                fetch(source, lambda team, k=k: (team + team_count - k) % team_count, arc_length)
                for k in range(team_count)
            ]
    return combined / (LAYERS + 1.0)


def solution(mesh):
    in_specs = (
        P(("groups", "blk"), None),
        P(("groups", "blk")),
        P(("groups", "blk"), "rep", None, None, None, None),
        P(("groups", "blk"), "rep", None, None),
        P(("groups", "blk"), "rep", None, None),
        P(("groups", "blk"), "rep", None),
    )
    out_specs = P(("groups", "blk", "rep"), None)
    return jax.shard_map(
        per_device, mesh=mesh, in_specs=in_specs, out_specs=out_specs, check_vma=False
    )
```

```python
import functools

import jax
import jax.numpy as jnp
from jax import lax
from jax.experimental import pallas as pl
from jax.experimental.pallas import tpu as pltpu
from jax.sharding import PartitionSpec as P

LAYERS = 2
VMEM_LIMIT = 16 * 1024 * 1024
VMEM = pl.BlockSpec(memory_space=pltpu.VMEM)
ANY = pl.BlockSpec(memory_space=pl.ANY)


def pair_teams(team_index, column, team_count):
    columns = team_count // 2
    return 2 * lax.rem(team_index // 2 + column, columns) + lax.rem(team_index, 2)


def source_team(team, turn, team_count):
    if team_count == 4:
        return (2 * (team % 2) + team // 2) ^ turn
    return (team + turn) % team_count


def norm_columns(degrees):
    return jnp.transpose(lax.rsqrt(degrees.astype(jnp.float32)))


def prepare_kernel(degrees_ref, embeddings_ref, tiles_ref, held_tiles_ref, own_ref, norm_ref, panel_ref, sems):
    share_rows, width = own_ref.shape
    block_count, tile_size = degrees_ref.shape
    team_index = lax.axis_index("rep")
    at = pl.ds(pl.multiple_of(team_index * share_rows, share_rows), share_rows)
    tiles_copy = pltpu.make_async_copy(tiles_ref, held_tiles_ref, sems.at[0])
    own_copy = pltpu.make_async_copy(embeddings_ref.at[at, :], own_ref, sems.at[1])
    tiles_copy.start()
    own_copy.start()
    norms = norm_columns(degrees_ref[...])
    for block in range(block_count):
        panel_ref[block * tile_size : (block + 1) * tile_size, :] = jnp.broadcast_to(
            norms[:, block : block + 1], (tile_size, width)
        )
    norm_ref[...] = panel_ref[at, :]
    own_copy.wait()
    tiles_copy.wait()


def prepare(degrees, embeddings, tile_values):
    panel_rows, width = embeddings.shape
    share = jax.ShapeDtypeStruct((panel_rows // lax.axis_size("rep"), width), jnp.float32)
    return pl.pallas_call(
        prepare_kernel,
        out_shape=[jax.ShapeDtypeStruct(tile_values.shape, tile_values.dtype), share, share],
        in_specs=[VMEM, ANY, ANY],
        out_specs=[VMEM] * 3,
        scratch_shapes=[pltpu.VMEM((panel_rows, width), jnp.float32), pltpu.SemaphoreType.DMA((2,))],
        compiler_params=pltpu.CompilerParams(vmem_limit_bytes=VMEM_LIMIT),
        cost_estimate=pl.CostEstimate(
            flops=panel_rows * width, bytes_accessed=4 * panel_rows * width, transcendentals=0
        ),
    )(degrees, embeddings, tile_values)


def arc_kernel(info_ref, tiles_ref, *refs, team_count, piece_count, scaled, partial_count):
    columns = team_count // 2
    degrees_ref = refs[0] if scaled else None
    refs = refs[1:] if scaled else refs
    pieces, refs = refs[:piece_count], refs[piece_count:]
    partials, refs = refs[:partial_count], refs[partial_count:]
    outs, (table_ref, split_ref, sums_ref, sem) = refs[: columns + 1], refs[columns + 1 :]
    team_index = lax.axis_index("rep")
    slot_total, tile_size, _ = tiles_ref.shape
    panel_rows, width = split_ref.shape[0], split_ref.shape[1] // 2
    share_rows = panel_rows // team_count
    block_count = panel_rows // tile_size
    table_copy = pltpu.make_async_copy(info_ref, table_ref, sem)
    table_copy.start()

    def split(value, at):
        high = value.astype(jnp.bfloat16)
        split_ref[at, :width] = high
        split_ref[at, width:] = (value - high.astype(jnp.float32)).astype(jnp.bfloat16)

    if piece_count == 1:
        norms = norm_columns(degrees_ref[...]) if scaled else None
        for block in range(block_count):
            at = pl.ds(block * tile_size, tile_size)
            value = pieces[0][at, :]
            split(value * norms[:, block : block + 1] if scaled else value, at)
    else:
        for k in range(piece_count):
            owner = source_team(team_index, k, team_count)
            split(pieces[k][...], pl.ds(pl.multiple_of(owner * share_rows, share_rows), share_rows))
    sums_ref[...] = jnp.zeros_like(sums_ref)
    table_copy.wait()
    live_count = table_ref[0]
    for j in range(slot_total):
        source = pl.multiple_of(table_ref[1 + slot_total + j] * tile_size, tile_size)
        product = jnp.dot(
            tiles_ref[j],
            split_ref[pl.ds(source, tile_size), :],
            preferred_element_type=jnp.float32,
        )
        row = jnp.where(j < live_count, table_ref[1 + j], block_count)
        at = pl.ds(pl.multiple_of(row * tile_size, tile_size), tile_size)
        sums_ref[at, :] += product[:, :width] + product[:, width:]

    for parity in range(2):
        for column in range(columns):
            team = pair_teams(team_index, column, team_count)
            team = team if parity == 0 else team + 1 - 2 * lax.rem(team, 2)
            value = sums_ref[pl.ds(pl.multiple_of(team * share_rows, share_rows), share_rows), :]
            to = pl.ds(0 if parity == 0 else column * share_rows, share_rows)
            target = column if parity == 0 else columns
            outs[target][to, :] = value + partials[target][to, :] if partials else value


def arc_step(info, tiles, degrees, pieces, partials):
    team_count = lax.axis_size("rep")
    columns = team_count // 2
    panel_rows = sum(piece.shape[0] for piece in pieces)
    width = pieces[0].shape[1]
    slot_total, tile_size, _ = tiles.shape
    share = jax.ShapeDtypeStruct((panel_rows // team_count, width), jnp.float32)
    other = jax.ShapeDtypeStruct((panel_rows // 2, width), jnp.float32)
    operands = [info, tiles, *(() if degrees is None else (degrees,)), *pieces, *partials]
    return pl.pallas_call(
        functools.partial(
            arc_kernel,
            team_count=team_count,
            piece_count=len(pieces),
            scaled=degrees is not None,
            partial_count=len(partials),
        ),
        out_shape=[share] * columns + [other],
        in_specs=[ANY] + [VMEM] * (len(operands) - 1),
        out_specs=[VMEM] * (columns + 1),
        scratch_shapes=[
            pltpu.SMEM(info.shape, info.dtype),
            pltpu.VMEM((panel_rows, 2 * width), jnp.bfloat16),
            pltpu.VMEM((panel_rows + tile_size, width), jnp.float32),
            pltpu.SemaphoreType.DMA,
        ],
        compiler_params=pltpu.CompilerParams(vmem_limit_bytes=VMEM_LIMIT),
        cost_estimate=pl.CostEstimate(
            flops=4 * slot_total * tile_size * tile_size * width, bytes_accessed=8 * panel_rows * width, transcendentals=0
        ),
    )(*operands)


def fetch(value, source_team, arc_length):
    cycle, team_count = lax.axis_size("blk"), lax.axis_size("rep")
    pairs = []
    for shard in range(cycle):
        for team in range(team_count):
            to_shard = (shard + team * arc_length) % cycle
            pairs.append((shard * team_count + source_team(team), to_shard * team_count + team))
    return lax.ppermute(value, ("blk", "rep"), pairs)


def next_shard(value):
    cycle = lax.axis_size("blk")
    return lax.ppermute(value, "blk", [(i, (i + 1) % cycle) for i in range(cycle)])


def from_mate(value):
    team_count = lax.axis_size("rep")
    return lax.ppermute(value, "rep", [(team, team ^ 1) for team in range(team_count)])


def from_column(value, distance):
    team_count = lax.axis_size("rep")
    pairs = [((team + 2 * distance) % team_count, team) for team in range(team_count)]
    return lax.ppermute(value, "rep", pairs)


def team_sum(sums):
    *own, other = sums
    columns = len(own)
    share_rows = own[0].shape[0]
    received = from_mate(other)
    shares = [
        own[column] + received[column * share_rows : (column + 1) * share_rows] for column in range(columns)
    ]
    total = shares[0]
    for distance in range(1, columns):
        total = total + from_column(shares[columns - distance], distance)
    return total


def per_device(embeddings, degrees, tile_values, tile_rows, tile_columns, slot_counts):
    arc_length, _, tile_size, _ = tile_values.shape[2:]
    panel_rows = embeddings.shape[0]
    team_count = lax.axis_size("rep")
    spread = (1, 2, 0, 3) if team_count == 4 else tuple(range(team_count))
    degrees = degrees.reshape(panel_rows // tile_size, tile_size)

    pieces = [fetch(embeddings, lambda team: spread[team], arc_length)]
    source_degrees = fetch(degrees, lambda team: spread[team], arc_length)
    tiles, own, norm_scale = prepare(degrees, embeddings, tile_values[0, 0])
    info = jnp.concatenate([slot_counts[0, 0][:, None], tile_rows[0, 0], tile_columns[0, 0]], axis=1)

    combined = own
    for layer in range(LAYERS):
        sums = ()
        for arc_slot in range(arc_length):
            sums = arc_step(info[arc_slot], tiles[arc_slot], source_degrees, pieces, sums)
            if arc_slot + 1 < arc_length:
                pieces = [next_shard(piece) for piece in pieces]
                if source_degrees is not None:
                    source_degrees = next_shard(source_degrees)
        source_degrees = None
        current = team_sum(sums) * norm_scale
        combined = combined + current
        if layer + 1 < LAYERS:
            source = current * norm_scale
            pieces = [
                fetch(source, lambda team, k=k: source_team(team, k, team_count), arc_length)
                for k in range(team_count)
            ]
    return combined / (LAYERS + 1.0)


def solution(mesh):
    in_specs = (
        P(("groups", "blk"), None),
        P(("groups", "blk")),
        P(("groups", "blk"), "rep", None, None, None, None),
        P(("groups", "blk"), "rep", None, None),
        P(("groups", "blk"), "rep", None, None),
        P(("groups", "blk"), "rep", None),
    )
    out_specs = P(("groups", "blk", "rep"), None)
    return jax.shard_map(
        per_device, mesh=mesh, in_specs=in_specs, out_specs=out_specs, check_vma=False
    )
```

```python
import functools

import jax
import jax.numpy as jnp
from jax import lax
from jax.experimental import pallas as pl
from jax.experimental.pallas import tpu as pltpu
from jax.sharding import PartitionSpec as P

LAYERS = 2
VMEM_LIMIT = 16 * 1024 * 1024
VMEM = pl.BlockSpec(memory_space=pltpu.VMEM)
ANY = pl.BlockSpec(memory_space=pl.ANY)


def lower_lanes(shape):
    return lax.broadcasted_iota(jnp.int32, shape, 1) < shape[1] // 2


def swap_lanes(value):
    return pltpu.roll(value, value.shape[1] // 2, 1)


def lane_join(lower, upper):
    return jnp.where(lower_lanes(lower.shape), lower, upper)


def pack_kernel(degrees_hbm, embeddings_hbm, packed_ref, norms_ref, degrees_ref, held_ref, panel_ref, sems, *, team_count):
    share_rows = held_ref.shape[0] // team_count
    half = share_rows // 2
    parity = lax.axis_index("rep") % 2
    degrees_copy = pltpu.make_async_copy(degrees_hbm, degrees_ref, sems.at[team_count])
    degrees_copy.start()
    copies = []
    for team in range(team_count):
        at = pl.ds(team * share_rows, share_rows)
        copies.append(pltpu.make_async_copy(embeddings_hbm.at[at, :], held_ref.at[at, :], sems.at[team]))
        copies[-1].start()
    degrees_copy.wait()
    block_count, tile_size = degrees_ref.shape
    width = panel_ref.shape[1]
    norms = jnp.transpose(lax.rsqrt(degrees_ref[...].astype(jnp.float32)))
    for block in range(block_count):
        panel_ref[block * tile_size : (block + 1) * tile_size, :] = jnp.broadcast_to(
            norms[:, block : block + 1], (tile_size, width)
        )
    for team in range(team_count):
        copies[team].wait()
        top_at = pl.ds(team * share_rows, half)
        bottom_at = pl.ds(team * share_rows + half, half)
        at = pl.ds(team * half, half)
        norm = lane_join(panel_ref[top_at, :], panel_ref[bottom_at, :])
        norms_ref[at, :] = norm
        top, bottom = held_ref[top_at, :], held_ref[bottom_at, :]
        first = lane_join(top, swap_lanes(bottom))
        second = lane_join(swap_lanes(top), bottom)
        packed_ref[at, :] = jnp.where(parity == 0, first, second) * norm


def pack_panel(degrees, embeddings):
    team_count = lax.axis_size("rep")
    panel_rows, width = embeddings.shape
    packed = jax.ShapeDtypeStruct((panel_rows // 2, width), jnp.float32)
    return pl.pallas_call(
        functools.partial(pack_kernel, team_count=team_count),
        out_shape=[packed] * 2,
        in_specs=[ANY, ANY],
        out_specs=[VMEM] * 2,
        scratch_shapes=[
            pltpu.VMEM(degrees.shape, degrees.dtype),
            pltpu.VMEM((panel_rows, width), jnp.float32),
            pltpu.VMEM((panel_rows, width), jnp.float32),
            pltpu.SemaphoreType.DMA((team_count + 1,)),
        ],
    )(degrees, embeddings)


def widen_kernel(embeddings_ref, tiles_ref, after_ref, held_tiles_ref, wide_tiles_ref, own_ref, sems):
    del after_ref
    share_rows = own_ref.shape[0]
    start = pl.multiple_of(lax.axis_index("rep") * share_rows, share_rows)
    tiles_copy = pltpu.make_async_copy(tiles_ref, held_tiles_ref, sems.at[0])
    own_copy = pltpu.make_async_copy(embeddings_ref.at[pl.ds(start, share_rows), :], own_ref, sems.at[1])
    tiles_copy.start()
    own_copy.start()
    tiles_copy.wait()

    @pl.loop(0, held_tiles_ref.shape[0])
    def _(j):
        wide_tiles_ref[j] = held_tiles_ref[j].astype(jnp.float32)

    own_copy.wait()


def widen_tiles(embeddings, tiles, after):
    panel_rows, width = embeddings.shape
    return pl.pallas_call(
        widen_kernel,
        out_shape=[
            jax.ShapeDtypeStruct(tiles.shape, tiles.dtype),
            jax.ShapeDtypeStruct(tiles.shape, jnp.float32),
            jax.ShapeDtypeStruct((panel_rows // lax.axis_size("rep"), width), jnp.float32),
        ],
        in_specs=[ANY] * 3,
        out_specs=[VMEM] * 3,
        scratch_shapes=[pltpu.SemaphoreType.DMA((2,))],
        compiler_params=pltpu.CompilerParams(vmem_limit_bytes=VMEM_LIMIT),
        cost_estimate=pl.CostEstimate(flops=tiles.size, bytes_accessed=8 * tiles.size, transcendentals=0),
    )(embeddings, tiles, after)


def narrow_kernel(wide_tiles_ref, tiles_ref):
    @pl.loop(0, tiles_ref.shape[0])
    def _(j):
        tiles_ref[j] = wide_tiles_ref[j].astype(tiles_ref.dtype)


def narrow_tiles(wide_tiles, dtype):
    return pl.pallas_call(
        narrow_kernel,
        out_shape=jax.ShapeDtypeStruct(wide_tiles.shape, dtype),
        in_specs=[VMEM],
        out_specs=VMEM,
        compiler_params=pltpu.CompilerParams(vmem_limit_bytes=VMEM_LIMIT),
        cost_estimate=pl.CostEstimate(flops=wide_tiles.size, bytes_accessed=6 * wide_tiles.size, transcendentals=0),
    )(wide_tiles)


def hold_kernel(value_ref, after_ref, out_ref):
    del value_ref, after_ref, out_ref


def hold(value, after):
    return pl.pallas_call(
        hold_kernel,
        out_shape=jax.ShapeDtypeStruct(value.shape, value.dtype),
        in_specs=[ANY, ANY],
        out_specs=ANY,
        input_output_aliases={0: 0},
        compiler_params=pltpu.CompilerParams(vmem_limit_bytes=VMEM_LIMIT),
    )(value, after)


def arc_kernel(*refs, team_count, piece_count, slot_at, partial_count, out_count):
    tables, refs = refs[:2], refs[2:]
    tiles, refs = refs[:2], refs[2:]
    pieces, refs = refs[:piece_count], refs[piece_count:]
    partials, refs = refs[:partial_count], refs[partial_count:]
    outs, (table_ref, split_ref, sums_ref, sems) = refs[:out_count], refs[out_count:]
    columns = team_count // 2
    team_index = lax.axis_index("rep")
    column, parity = team_index // 2, team_index % 2
    slot_total, tile_size, _ = tiles[0].shape
    panel_rows = split_ref.shape[0] // 2
    block_count = panel_rows // tile_size
    half = panel_rows // team_count // 2
    copies = [pltpu.make_async_copy(tables[n].at[slot_at], table_ref.at[n], sems.at[n]) for n in range(2)]
    for copy in copies:
        copy.start()

    def split(panel_ref, start):
        for team in range(team_count):
            value = panel_ref[team * half : (team + 1) * half, :]
            high = value.astype(jnp.bfloat16).astype(jnp.float32)
            low = value - high
            at = start + team * 2 * half
            split_ref[pl.ds(pl.multiple_of(at, half), half), :] = lane_join(high, swap_lanes(low)).astype(jnp.bfloat16)
            split_ref[pl.ds(pl.multiple_of(at + half, half), half), :] = lane_join(swap_lanes(high), low).astype(
                jnp.bfloat16
            )

    @pl.when(column == 0)
    def _():
        split(pieces[0], 0)

    turns = [pieces[n : n + 2] for n in range(1, piece_count, 2)]
    for plane, (first, second) in enumerate(turns):
        here = parity == plane if len(turns) > 1 else parity >= 0

        @pl.when(here if columns == 2 else here & (column > 0))
        def _(first=first):
            split(first, jnp.where(column == 0, panel_rows, 0))

        @pl.when(here & (column > 0) if columns == 2 else here)
        def _(second=second):
            split(second, panel_rows)

    sums_ref[...] = jnp.zeros_like(sums_ref)
    for copy in copies:
        copy.wait()
    for n in range(2):
        start = jnp.where(parity == n, 0, panel_rows)
        for j in range(slot_total):
            source = pl.multiple_of(start + table_ref[n, 1 + slot_total + j] * tile_size, tile_size)
            row = jnp.where(j < table_ref[n, 0], table_ref[n, 1 + j], block_count)
            at = pl.ds(pl.multiple_of(row * tile_size, tile_size), tile_size)
            sums_ref[at, :] += jnp.dot(
                tiles[n][j], split_ref[pl.ds(source, tile_size), :], preferred_element_type=jnp.float32
            )

    for team in range(team_count):
        out_at = team // 2 if out_count > 1 else 0
        to = pl.ds((team % 2 if out_count > 1 else team) * half, half)
        from_team = 2 * ((column + team // 2) % columns) + team % 2 if out_count > 1 else team
        start = from_team * 2 * half
        top = sums_ref[pl.ds(pl.multiple_of(start, half), half), :]
        bottom = sums_ref[pl.ds(pl.multiple_of(start + half, half), half), :]
        value = lane_join(top + swap_lanes(top), bottom + swap_lanes(bottom))
        outs[out_at][to, :] = value + partials[out_at][to, :] if partials else value


def arc_step(tables, tiles, pieces, slot_at, partials, out_count):
    team_count = lax.axis_size("rep")
    packed_rows, width = pieces[0].shape
    slot_total, tile_size, _ = tiles[0].shape
    out = jax.ShapeDtypeStruct((packed_rows // out_count, width), jnp.float32)
    operands = [*tables, *tiles, *pieces, *partials]
    return pl.pallas_call(
        functools.partial(
            arc_kernel,
            team_count=team_count,
            piece_count=len(pieces),
            slot_at=slot_at,
            partial_count=len(partials),
            out_count=out_count,
        ),
        out_shape=[out] * out_count,
        in_specs=[ANY] * 2 + [VMEM] * (len(operands) - 2),
        out_specs=[VMEM] * out_count,
        scratch_shapes=[
            pltpu.SMEM((2, tables[0].shape[1]), jnp.int32),
            pltpu.VMEM((4 * packed_rows, width), jnp.bfloat16),
            pltpu.VMEM((2 * packed_rows + tile_size, width), jnp.float32),
            pltpu.SemaphoreType.DMA((2,)),
        ],
        compiler_params=pltpu.CompilerParams(vmem_limit_bytes=VMEM_LIMIT),
        cost_estimate=pl.CostEstimate(
            flops=4 * slot_total * tile_size * tile_size * width, bytes_accessed=16 * packed_rows * width, transcendentals=0
        ),
    )(*operands)


def finish_kernel(own_ref, mine_ref, received_ref, out_ref, *, layer_count):
    half = mine_ref.shape[0]
    mine, received = mine_ref[...], received_ref[...]
    parity = lax.axis_index("rep") % 2
    first = jnp.where(parity == 0, mine, received)
    second = jnp.where(parity == 0, received, mine)
    out_ref[:half, :] = (own_ref[:half, :] + lane_join(first, swap_lanes(second))) / layer_count
    out_ref[half:, :] = (own_ref[half:, :] + lane_join(swap_lanes(first), second)) / layer_count


def finish(own, mine, received):
    return pl.pallas_call(
        functools.partial(finish_kernel, layer_count=LAYERS + 1.0),
        out_shape=jax.ShapeDtypeStruct(own.shape, jnp.float32),
        in_specs=[VMEM] * 3,
        out_specs=VMEM,
        compiler_params=pltpu.CompilerParams(vmem_limit_bytes=VMEM_LIMIT),
    )(own, mine, received)


def fetch_panels(packed, planes, arc_length):
    cycle, team_count = lax.axis_size("blk"), lax.axis_size("rep")
    columns = team_count // 2
    if columns == 2:
        turns = [[(1, 0, 0), (0, 1, 1)], [(1, 1, 1)]]
    else:
        turns = [[(at, 0, at) for at in range(1, columns)], [(at, 1, at) for at in range(columns)]]
    received = []
    for turn in turns:
        pairs = []
        for shard in range(cycle):
            for to_column, core, from_at in turn:
                to_shard = (shard + (2 * to_column + core) * arc_length) % cycle
                for plane in planes:
                    source = shard * team_count + 2 * from_at + plane
                    pairs.append((source, to_shard * team_count + 2 * to_column + plane))
        received.append(lax.ppermute(packed, ("blk", "rep"), pairs))
    return received


def next_shard(value):
    cycle = lax.axis_size("blk")
    return lax.ppermute(value, "blk", [(i, (i + 1) % cycle) for i in range(cycle)])


def from_mate(value):
    team_count = lax.axis_size("rep")
    return lax.ppermute(value, "rep", [(team, team ^ 1) for team in range(team_count)])


def from_column(value, distance):
    team_count = lax.axis_size("rep")
    pairs = [((team + 2 * distance) % team_count, team) for team in range(team_count)]
    return lax.ppermute(value, "rep", pairs)


def per_device(embeddings, degrees, tile_values, tile_rows, tile_columns, slot_counts):
    arc_length, slot_total, tile_size, _ = tile_values.shape[2:]
    panel_rows, width = embeddings.shape
    team_count = lax.axis_size("rep")
    columns = team_count // 2
    half = panel_rows // team_count // 2
    column, parity = lax.axis_index("rep") // 2, lax.axis_index("rep") % 2

    packed, norms = pack_panel(degrees.reshape(panel_rows // tile_size, tile_size), embeddings)
    fetched = fetch_panels(packed, (0,), arc_length)
    table = jnp.concatenate([slot_counts[0, 0][:, None], tile_rows[0, 0], tile_columns[0, 0]], axis=1)
    tables = (table, from_mate(table))
    tile_values = tile_values.reshape(arc_length * slot_total, tile_size, tile_size)
    tiles, wide_tiles, own = widen_tiles(embeddings, tile_values, packed)
    wide_tiles = from_mate(wide_tiles)
    fetched += fetch_panels(hold(packed, wide_tiles), (1,), arc_length)
    tiles = (tiles, narrow_tiles(wide_tiles, tiles.dtype))

    def arc(pieces, out_count):
        sums = ()
        for at in range(arc_length):
            here = [t[at * slot_total : (at + 1) * slot_total] for t in tiles] if arc_length > 1 else tiles
            sums = arc_step(tables, here, pieces, at, sums, out_count)
            if at + 1 < arc_length:
                pieces = [next_shard(piece) for piece in pieces]
        return sums

    pieces = [packed, *fetched]
    norm = lax.dynamic_slice_in_dim(norms, column * 2 * half, 2 * half)
    layers_sum = 0.0
    for layer in range(LAYERS - 1):
        (total,) = arc(pieces, 1)
        for distance, other in [(d, from_column(total, d)) for d in range(1, columns)]:
            total = total + other
        current = total * norms
        layers_sum = layers_sum + lax.dynamic_slice_in_dim(current, column * 2 * half, 2 * half)
        source = current * norms
        pieces = [source, *fetch_panels(source, (0, 1), arc_length)]
    total, *others = arc(pieces, columns)
    for distance in range(1, columns):
        total = total + from_column(others[columns - distance - 1], distance)
    layers_sum = layers_sum + total * norm
    mine = lax.dynamic_slice_in_dim(layers_sum, parity * half, half)
    theirs = lax.dynamic_slice_in_dim(layers_sum, (1 - parity) * half, half)
    return finish(own, mine, from_mate(theirs))


def solution(mesh):
    in_specs = (
        P(("groups", "blk"), None),
        P(("groups", "blk")),
        P(("groups", "blk"), "rep", None, None, None, None),
        P(("groups", "blk"), "rep", None, None),
        P(("groups", "blk"), "rep", None, None),
        P(("groups", "blk"), "rep", None),
    )
    out_specs = P(("groups", "blk", "rep"), None)
    return jax.shard_map(
        per_device, mesh=mesh, in_specs=in_specs, out_specs=out_specs, check_vma=False
    )
```

```python
import functools

import jax
import jax.numpy as jnp
from jax import lax
from jax.experimental import pallas as pl
from jax.experimental.pallas import tpu as pltpu
from jax.sharding import PartitionSpec as P

LAYERS = 2
VMEM_LIMIT = 16 * 1024 * 1024
VMEM = pl.BlockSpec(memory_space=pltpu.VMEM)
ANY = pl.BlockSpec(memory_space=pl.ANY)


def lower_lanes(shape):
    return lax.broadcasted_iota(jnp.int32, shape, 1) < shape[1] // 2


def swap_lanes(value):
    return pltpu.roll(value, value.shape[1] // 2, 1)


def lane_join(lower, upper):
    return jnp.where(lower_lanes(lower.shape), lower, upper)


def pack_kernel(
    degrees_ref,
    embeddings_ref,
    tiles_ref,
    packed_ref,
    norms_ref,
    own_ref,
    held_tiles_ref,
    wide_tiles_ref,
    panel_ref,
    *,
    team_count,
):
    share_rows = own_ref.shape[0]
    half = share_rows // 2
    team_index = lax.axis_index("rep")
    block_count, tile_size = degrees_ref.shape
    width = panel_ref.shape[1]
    norms = jnp.transpose(lax.rsqrt(degrees_ref[...].astype(jnp.float32)))
    for block in range(block_count):
        panel_ref[block * tile_size : (block + 1) * tile_size, :] = jnp.broadcast_to(
            norms[:, block : block + 1], (tile_size, width)
        )
    for team in range(team_count):
        top_at = pl.ds(team * share_rows, half)
        bottom_at = pl.ds(team * share_rows + half, half)
        at = pl.ds(team * half, half)
        norm = lane_join(panel_ref[top_at, :], panel_ref[bottom_at, :])
        norms_ref[at, :] = norm
        top, bottom = embeddings_ref[top_at, :], embeddings_ref[bottom_at, :]
        first = lane_join(top, swap_lanes(bottom))
        second = lane_join(swap_lanes(top), bottom)
        packed_ref[at, :] = jnp.where(team_index % 2 == 0, first, second) * norm
    own_ref[...] = embeddings_ref[pl.ds(pl.multiple_of(team_index * share_rows, share_rows), share_rows), :]

    @pl.loop(0, tiles_ref.shape[0], unroll=2)
    def _(j):
        tile = tiles_ref[j]
        held_tiles_ref[j] = tile
        wide_tiles_ref[j] = tile.astype(jnp.float32)


def pack(degrees, embeddings, tiles):
    team_count = lax.axis_size("rep")
    panel_rows, width = embeddings.shape
    packed = jax.ShapeDtypeStruct((panel_rows // 2, width), jnp.float32)
    return pl.pallas_call(
        functools.partial(pack_kernel, team_count=team_count),
        out_shape=[
            packed,
            packed,
            jax.ShapeDtypeStruct((panel_rows // team_count, width), jnp.float32),
            jax.ShapeDtypeStruct(tiles.shape, tiles.dtype),
            jax.ShapeDtypeStruct(tiles.shape, jnp.float32),
        ],
        in_specs=[VMEM] * 3,
        out_specs=[VMEM] * 5,
        scratch_shapes=[pltpu.VMEM((panel_rows, width), jnp.float32)],
        compiler_params=pltpu.CompilerParams(vmem_limit_bytes=VMEM_LIMIT),
    )(degrees, embeddings, tiles)


def narrow_kernel(wide_tiles_ref, tiles_ref):
    @pl.loop(0, tiles_ref.shape[0])
    def _(j):
        tiles_ref[j] = wide_tiles_ref[j].astype(tiles_ref.dtype)


def narrow_tiles(wide_tiles, dtype):
    return pl.pallas_call(
        narrow_kernel,
        out_shape=jax.ShapeDtypeStruct(wide_tiles.shape, dtype),
        in_specs=[VMEM],
        out_specs=VMEM,
        compiler_params=pltpu.CompilerParams(vmem_limit_bytes=VMEM_LIMIT),
        cost_estimate=pl.CostEstimate(flops=wide_tiles.size, bytes_accessed=6 * wide_tiles.size, transcendentals=0),
    )(wide_tiles)


def hold_kernel(value_ref, after_ref, out_ref):
    del value_ref, after_ref, out_ref


def hold(value, after):
    return pl.pallas_call(
        hold_kernel,
        out_shape=jax.ShapeDtypeStruct(value.shape, value.dtype),
        in_specs=[ANY, ANY],
        out_specs=ANY,
        input_output_aliases={0: 0},
        compiler_params=pltpu.CompilerParams(vmem_limit_bytes=VMEM_LIMIT),
    )(value, after)


def arc_kernel(*refs, team_count, piece_count, slot_at, partial_count, out_count):
    tables, refs = refs[:2], refs[2:]
    tiles, refs = refs[:2], refs[2:]
    pieces, refs = refs[:piece_count], refs[piece_count:]
    partials, refs = refs[:partial_count], refs[partial_count:]
    outs, (table_ref, split_ref, sums_ref, sems) = refs[:out_count], refs[out_count:]
    columns = team_count // 2
    team_index = lax.axis_index("rep")
    column, parity = team_index // 2, team_index % 2
    slot_total, tile_size, _ = tiles[0].shape
    panel_rows = split_ref.shape[0] // 2
    block_count = panel_rows // tile_size
    half = panel_rows // team_count // 2
    copies = [pltpu.make_async_copy(tables[n].at[slot_at], table_ref.at[n], sems.at[n]) for n in range(2)]
    for copy in copies:
        copy.start()

    def split(panel_ref, start):
        for team in range(team_count):
            value = panel_ref[team * half : (team + 1) * half, :]
            high = value.astype(jnp.bfloat16).astype(jnp.float32)
            low = value - high
            at = start + team * 2 * half
            split_ref[pl.ds(pl.multiple_of(at, half), half), :] = lane_join(high, swap_lanes(low)).astype(jnp.bfloat16)
            split_ref[pl.ds(pl.multiple_of(at + half, half), half), :] = lane_join(swap_lanes(high), low).astype(
                jnp.bfloat16
            )

    @pl.when(column == 0)
    def _():
        split(pieces[0], 0)

    turns = [pieces[n : n + 2] for n in range(1, piece_count, 2)]
    for plane, (first, second) in enumerate(turns):
        here = parity == plane if len(turns) > 1 else parity >= 0

        @pl.when(here if columns == 2 else here & (column > 0))
        def _(first=first):
            split(first, jnp.where(column == 0, panel_rows, 0))

        @pl.when(here & (column > 0) if columns == 2 else here)
        def _(second=second):
            split(second, panel_rows)

    sums_ref[...] = jnp.zeros_like(sums_ref)
    for copy in copies:
        copy.wait()
    for n in range(2):
        start = jnp.where(parity == n, 0, panel_rows)
        for j in range(slot_total):
            source = pl.multiple_of(start + table_ref[n, 1 + slot_total + j] * tile_size, tile_size)
            row = jnp.where(j < table_ref[n, 0], table_ref[n, 1 + j], block_count)
            at = pl.ds(pl.multiple_of(row * tile_size, tile_size), tile_size)
            sums_ref[at, :] += jnp.dot(
                tiles[n][j], split_ref[pl.ds(source, tile_size), :], preferred_element_type=jnp.float32
            )

    for team in range(team_count):
        out_at = team // 2 if out_count > 1 else 0
        to = pl.ds((team % 2 if out_count > 1 else team) * half, half)
        from_team = 2 * ((column + team // 2) % columns) + team % 2 if out_count > 1 else team
        start = from_team * 2 * half
        top = sums_ref[pl.ds(pl.multiple_of(start, half), half), :]
        bottom = sums_ref[pl.ds(pl.multiple_of(start + half, half), half), :]
        value = lane_join(top + swap_lanes(top), bottom + swap_lanes(bottom))
        outs[out_at][to, :] = value + partials[out_at][to, :] if partials else value


def arc_step(tables, tiles, pieces, slot_at, partials, out_count):
    team_count = lax.axis_size("rep")
    packed_rows, width = pieces[0].shape
    slot_total, tile_size, _ = tiles[0].shape
    out = jax.ShapeDtypeStruct((packed_rows // out_count, width), jnp.float32)
    operands = [*tables, *tiles, *pieces, *partials]
    return pl.pallas_call(
        functools.partial(
            arc_kernel,
            team_count=team_count,
            piece_count=len(pieces),
            slot_at=slot_at,
            partial_count=len(partials),
            out_count=out_count,
        ),
        out_shape=[out] * out_count,
        in_specs=[ANY] * 2 + [VMEM] * (len(operands) - 2),
        out_specs=[VMEM] * out_count,
        scratch_shapes=[
            pltpu.SMEM((2, tables[0].shape[1]), jnp.int32),
            pltpu.VMEM((4 * packed_rows, width), jnp.bfloat16),
            pltpu.VMEM((2 * packed_rows + tile_size, width), jnp.float32),
            pltpu.SemaphoreType.DMA((2,)),
        ],
        compiler_params=pltpu.CompilerParams(vmem_limit_bytes=VMEM_LIMIT),
        cost_estimate=pl.CostEstimate(
            flops=4 * slot_total * tile_size * tile_size * width, bytes_accessed=16 * packed_rows * width, transcendentals=0
        ),
    )(*operands)


def finish_kernel(own_ref, mine_ref, received_ref, out_ref, *, layer_count):
    half = mine_ref.shape[0]
    mine, received = mine_ref[...], received_ref[...]
    parity = lax.axis_index("rep") % 2
    first = jnp.where(parity == 0, mine, received)
    second = jnp.where(parity == 0, received, mine)
    out_ref[:half, :] = (own_ref[:half, :] + lane_join(first, swap_lanes(second))) / layer_count
    out_ref[half:, :] = (own_ref[half:, :] + lane_join(swap_lanes(first), second)) / layer_count


def finish(own, mine, received):
    return pl.pallas_call(
        functools.partial(finish_kernel, layer_count=LAYERS + 1.0),
        out_shape=jax.ShapeDtypeStruct(own.shape, jnp.float32),
        in_specs=[VMEM] * 3,
        out_specs=VMEM,
        compiler_params=pltpu.CompilerParams(vmem_limit_bytes=VMEM_LIMIT),
    )(own, mine, received)


def fetch_panels(packed, planes, arc_length):
    cycle, team_count = lax.axis_size("blk"), lax.axis_size("rep")
    columns = team_count // 2
    if columns == 2:
        turns = [[(1, 0, 0), (0, 1, 1)], [(1, 1, 1)]]
    else:
        turns = [[(at, 0, at) for at in range(1, columns)], [(at, 1, at) for at in range(columns)]]
    received = []
    for turn in turns:
        pairs = []
        for shard in range(cycle):
            for to_column, core, from_at in turn:
                to_shard = (shard + (2 * to_column + core) * arc_length) % cycle
                for plane in planes:
                    source = shard * team_count + 2 * from_at + plane
                    pairs.append((source, to_shard * team_count + 2 * to_column + plane))
        received.append(lax.ppermute(packed, ("blk", "rep"), pairs))
    return received


def next_shard(value):
    cycle = lax.axis_size("blk")
    return lax.ppermute(value, "blk", [(i, (i + 1) % cycle) for i in range(cycle)])


def from_mate(value):
    team_count = lax.axis_size("rep")
    return lax.ppermute(value, "rep", [(team, team ^ 1) for team in range(team_count)])


def from_column(value, distance):
    team_count = lax.axis_size("rep")
    pairs = [((team + 2 * distance) % team_count, team) for team in range(team_count)]
    return lax.ppermute(value, "rep", pairs)


def per_device(embeddings, degrees, tile_values, tile_rows, tile_columns, slot_counts):
    arc_length, slot_total, tile_size, _ = tile_values.shape[2:]
    panel_rows, width = embeddings.shape
    team_count = lax.axis_size("rep")
    columns = team_count // 2
    half = panel_rows // team_count // 2
    column, parity = lax.axis_index("rep") // 2, lax.axis_index("rep") % 2

    tile_values = tile_values.reshape(arc_length * slot_total, tile_size, tile_size)
    degrees = degrees.reshape(panel_rows // tile_size, tile_size)
    packed, norms, own, tiles, wide_tiles = pack(degrees, embeddings, tile_values)
    fetched = fetch_panels(packed, (0,), arc_length)
    table = jnp.concatenate([slot_counts[0, 0][:, None], tile_rows[0, 0], tile_columns[0, 0]], axis=1)
    tables = (table, from_mate(table))
    wide_tiles = from_mate(wide_tiles)
    fetched += fetch_panels(hold(packed, wide_tiles), (1,), arc_length)
    tiles = (tiles, narrow_tiles(wide_tiles, tiles.dtype))

    def arc(pieces, out_count):
        sums = ()
        for at in range(arc_length):
            here = [t[at * slot_total : (at + 1) * slot_total] for t in tiles] if arc_length > 1 else tiles
            sums = arc_step(tables, here, pieces, at, sums, out_count)
            if at + 1 < arc_length:
                pieces = [next_shard(piece) for piece in pieces]
        return sums

    pieces = [packed, *fetched]
    norm = lax.dynamic_slice_in_dim(norms, column * 2 * half, 2 * half)
    layers_sum = 0.0
    for layer in range(LAYERS - 1):
        (total,) = arc(pieces, 1)
        for distance, other in [(d, from_column(total, d)) for d in range(1, columns)]:
            total = total + other
        current = total * norms
        layers_sum = layers_sum + lax.dynamic_slice_in_dim(current, column * 2 * half, 2 * half)
        source = current * norms
        pieces = [source, *fetch_panels(source, (0, 1), arc_length)]
    total, *others = arc(pieces, columns)
    for distance in range(1, columns):
        total = total + from_column(others[columns - distance - 1], distance)
    layers_sum = layers_sum + total * norm
    mine = lax.dynamic_slice_in_dim(layers_sum, parity * half, half)
    theirs = lax.dynamic_slice_in_dim(layers_sum, (1 - parity) * half, half)
    return finish(own, mine, from_mate(theirs))


def solution(mesh):
    in_specs = (
        P(("groups", "blk"), None),
        P(("groups", "blk")),
        P(("groups", "blk"), "rep", None, None, None, None),
        P(("groups", "blk"), "rep", None, None),
        P(("groups", "blk"), "rep", None, None),
        P(("groups", "blk"), "rep", None),
    )
    out_specs = P(("groups", "blk", "rep"), None)
    return jax.shard_map(
        per_device, mesh=mesh, in_specs=in_specs, out_specs=out_specs, check_vma=False
    )
```

```python
import functools

import jax
import jax.numpy as jnp
from jax import lax
from jax.experimental import pallas as pl
from jax.experimental.pallas import tpu as pltpu
from jax.sharding import PartitionSpec as P

LAYERS = 2
VMEM_LIMIT = 16 * 1024 * 1024
VMEM = pl.BlockSpec(memory_space=pltpu.VMEM)
ANY = pl.BlockSpec(memory_space=pl.ANY)


def pair_teams(team_index, column, team_count):
    columns = team_count // 2
    return 2 * lax.rem(team_index // 2 + column, columns) + lax.rem(team_index, 2)


def source_team(team, turn, team_count):
    if team_count == 4:
        return (2 * (team % 2) + team // 2) ^ (2 * turn)
    return (team + 2 * turn) % team_count


def norm_columns(degrees):
    return jnp.transpose(lax.rsqrt(degrees.astype(jnp.float32)))


def prepare_kernel(degrees_ref, embeddings_ref, tiles_ref, held_tiles_ref, own_ref, norm_ref, panel_ref, sems):
    share_rows, width = own_ref.shape
    block_count, tile_size = degrees_ref.shape
    team_index = lax.axis_index("rep")
    at = pl.ds(pl.multiple_of(team_index * share_rows, share_rows), share_rows)
    tiles_copy = pltpu.make_async_copy(tiles_ref, held_tiles_ref, sems.at[0])
    own_copy = pltpu.make_async_copy(embeddings_ref.at[at, :], own_ref, sems.at[1])
    tiles_copy.start()
    own_copy.start()
    norms = norm_columns(degrees_ref[...])
    for block in range(block_count):
        panel_ref[block * tile_size : (block + 1) * tile_size, :] = jnp.broadcast_to(
            norms[:, block : block + 1], (tile_size, width)
        )
    norm_ref[...] = panel_ref[at, :]
    own_copy.wait()
    tiles_copy.wait()


def prepare(degrees, embeddings, tile_values):
    panel_rows, width = embeddings.shape
    share = jax.ShapeDtypeStruct((panel_rows // lax.axis_size("rep"), width), jnp.float32)
    return pl.pallas_call(
        prepare_kernel,
        out_shape=[jax.ShapeDtypeStruct(tile_values.shape, tile_values.dtype), share, share],
        in_specs=[VMEM, ANY, ANY],
        out_specs=[VMEM] * 3,
        scratch_shapes=[pltpu.VMEM((panel_rows, width), jnp.float32), pltpu.SemaphoreType.DMA((2,))],
        compiler_params=pltpu.CompilerParams(vmem_limit_bytes=VMEM_LIMIT),
        cost_estimate=pl.CostEstimate(
            flops=panel_rows * width, bytes_accessed=4 * panel_rows * width, transcendentals=0
        ),
    )(degrees, embeddings, tile_values)


def arc_kernel(info_ref, tiles_ref, *refs, team_count, piece_count, scaled, partial_count):
    columns = team_count // 2
    degrees_ref = refs[0] if scaled else None
    refs = refs[1:] if scaled else refs
    pieces, refs = refs[:piece_count], refs[piece_count:]
    partials, refs = refs[:partial_count], refs[partial_count:]
    outs, (table_ref, split_ref, sums_ref, sem) = refs[: columns + 1], refs[columns + 1 :]
    team_index = lax.axis_index("rep")
    slot_total, tile_size, _ = tiles_ref.shape
    panel_rows, width = split_ref.shape[0], split_ref.shape[1] // 2
    share_rows = panel_rows // team_count
    block_count = panel_rows // tile_size
    table_copy = pltpu.make_async_copy(info_ref, table_ref, sem)
    table_copy.start()

    def split(value, at):
        high = value.astype(jnp.bfloat16)
        split_ref[at, :width] = high
        split_ref[at, width:] = (value - high.astype(jnp.float32)).astype(jnp.bfloat16)

    if piece_count == 1:
        norms = norm_columns(degrees_ref[...]) if scaled else None
        for block in range(block_count):
            at = pl.ds(block * tile_size, tile_size)
            value = pieces[0][at, :]
            split(value * norms[:, block : block + 1] if scaled else value, at)
    else:
        for k in range(piece_count):
            source = source_team(team_index, k, team_count)
            for at, owner in enumerate((source, source ^ 1)):
                value = pieces[k][at * share_rows : (at + 1) * share_rows, :]
                split(value, pl.ds(pl.multiple_of(owner * share_rows, share_rows), share_rows))
    sums_ref[...] = jnp.zeros_like(sums_ref)
    table_copy.wait()
    live_count = table_ref[0]
    for j in range(slot_total):
        source = pl.multiple_of(table_ref[1 + slot_total + j] * tile_size, tile_size)
        product = jnp.dot(
            tiles_ref[j],
            split_ref[pl.ds(source, tile_size), :],
            preferred_element_type=jnp.float32,
        )
        row = jnp.where(j < live_count, table_ref[1 + j], block_count)
        at = pl.ds(pl.multiple_of(row * tile_size, tile_size), tile_size)
        sums_ref[at, :] += product[:, :width] + product[:, width:]

    for parity in range(2):
        for column in range(columns):
            team = pair_teams(team_index, column, team_count)
            team = team if parity == 0 else team + 1 - 2 * lax.rem(team, 2)
            value = sums_ref[pl.ds(pl.multiple_of(team * share_rows, share_rows), share_rows), :]
            to = pl.ds(0 if parity == 0 else column * share_rows, share_rows)
            target = column if parity == 0 else columns
            outs[target][to, :] = value + partials[target][to, :] if partials else value


def arc_step(info, tiles, degrees, pieces, partials):
    team_count = lax.axis_size("rep")
    columns = team_count // 2
    panel_rows = sum(piece.shape[0] for piece in pieces)
    width = pieces[0].shape[1]
    slot_total, tile_size, _ = tiles.shape
    share = jax.ShapeDtypeStruct((panel_rows // team_count, width), jnp.float32)
    other = jax.ShapeDtypeStruct((panel_rows // 2, width), jnp.float32)
    operands = [info, tiles, *(() if degrees is None else (degrees,)), *pieces, *partials]
    return pl.pallas_call(
        functools.partial(
            arc_kernel,
            team_count=team_count,
            piece_count=len(pieces),
            scaled=degrees is not None,
            partial_count=len(partials),
        ),
        out_shape=[share] * columns + [other],
        in_specs=[ANY] + [VMEM] * (len(operands) - 1),
        out_specs=[VMEM] * (columns + 1),
        scratch_shapes=[
            pltpu.SMEM(info.shape, info.dtype),
            pltpu.VMEM((panel_rows, 2 * width), jnp.bfloat16),
            pltpu.VMEM((panel_rows + tile_size, width), jnp.float32),
            pltpu.SemaphoreType.DMA,
        ],
        compiler_params=pltpu.CompilerParams(vmem_limit_bytes=VMEM_LIMIT),
        cost_estimate=pl.CostEstimate(
            flops=4 * slot_total * tile_size * tile_size * width, bytes_accessed=8 * panel_rows * width, transcendentals=0
        ),
    )(*operands)


def fetch(value, source_team, arc_length):
    cycle, team_count = lax.axis_size("blk"), lax.axis_size("rep")
    pairs = []
    for shard in range(cycle):
        for team in range(team_count):
            to_shard = (shard + team * arc_length) % cycle
            pairs.append((shard * team_count + source_team(team), to_shard * team_count + team))
    return lax.ppermute(value, ("blk", "rep"), pairs)


def next_shard(value):
    cycle = lax.axis_size("blk")
    return lax.ppermute(value, "blk", [(i, (i + 1) % cycle) for i in range(cycle)])


def from_mate(value):
    team_count = lax.axis_size("rep")
    return lax.ppermute(value, "rep", [(team, team ^ 1) for team in range(team_count)])


def from_column(value, distance):
    team_count = lax.axis_size("rep")
    pairs = [((team + 2 * distance) % team_count, team) for team in range(team_count)]
    return lax.ppermute(value, "rep", pairs)


def team_sum(sums):
    *own, other = sums
    columns = len(own)
    share_rows = own[0].shape[0]
    received = from_mate(other)
    shares = [
        own[column] + received[column * share_rows : (column + 1) * share_rows] for column in range(columns)
    ]
    total = shares[0]
    for distance in range(1, columns):
        total = total + from_column(shares[columns - distance], distance)
    return total


def per_device(embeddings, degrees, tile_values, tile_rows, tile_columns, slot_counts):
    arc_length, _, tile_size, _ = tile_values.shape[2:]
    panel_rows = embeddings.shape[0]
    team_count = lax.axis_size("rep")
    spread = (1, 2, 0, 3) if team_count == 4 else tuple(range(team_count))
    degrees = degrees.reshape(panel_rows // tile_size, tile_size)

    pieces = [fetch(embeddings, lambda team: spread[team], arc_length)]
    source_degrees = fetch(degrees, lambda team: spread[team], arc_length)
    tiles, own, norm_scale = prepare(degrees, embeddings, tile_values[0, 0])
    info = jnp.concatenate([slot_counts[0, 0][:, None], tile_rows[0, 0], tile_columns[0, 0]], axis=1)

    combined = own
    for layer in range(LAYERS):
        sums = ()
        for arc_slot in range(arc_length):
            sums = arc_step(info[arc_slot], tiles[arc_slot], source_degrees, pieces, sums)
            if arc_slot + 1 < arc_length:
                pieces = [next_shard(piece) for piece in pieces]
                if source_degrees is not None:
                    source_degrees = next_shard(source_degrees)
        source_degrees = None
        current = team_sum(sums) * norm_scale
        combined = combined + current
        if layer + 1 < LAYERS:
            source = current * norm_scale
            source = jnp.concatenate([source, from_mate(source)])
            pieces = [
                fetch(source, lambda team, k=k: source_team(team, k, team_count), arc_length)
                for k in range(team_count // 2)
            ]
    return combined / (LAYERS + 1.0)


def solution(mesh):
    in_specs = (
        P(("groups", "blk"), None),
        P(("groups", "blk")),
        P(("groups", "blk"), "rep", None, None, None, None),
        P(("groups", "blk"), "rep", None, None),
        P(("groups", "blk"), "rep", None, None),
        P(("groups", "blk"), "rep", None),
    )
    out_specs = P(("groups", "blk", "rep"), None)
    return jax.shard_map(
        per_device, mesh=mesh, in_specs=in_specs, out_specs=out_specs, check_vma=False
    )
```

```python
import functools

import jax
import jax.numpy as jnp
from jax import lax
from jax.experimental import pallas as pl
from jax.experimental.pallas import tpu as pltpu
from jax.sharding import PartitionSpec as P

LAYERS = 2
PARTS = 2
VMEM_LIMIT = 16 * 1024 * 1024
VMEM = pl.BlockSpec(memory_space=pltpu.VMEM)
ANY = pl.BlockSpec(memory_space=pl.ANY)


def pair_teams(team_index, column, team_count):
    columns = team_count // 2
    return 2 * lax.rem(team_index // 2 + column, columns) + lax.rem(team_index, 2)


def source_team(team, turn, team_count):
    if team_count == 4:
        return (2 * (team % 2) + team // 2) ^ (2 * turn)
    return (team + 2 * turn) % team_count


def lower_lanes(shape):
    return lax.broadcasted_iota(jnp.int32, shape, 1) < shape[1] // 2


def swap_lanes(value):
    return pltpu.roll(value, value.shape[1] // 2, 1)


def lane_join(lower, upper):
    return jnp.where(lower_lanes(lower.shape), lower, upper)


def norm_columns(degrees):
    return jnp.transpose(lax.rsqrt(degrees.astype(jnp.float32)))


def prepare_kernel(degrees_ref, embeddings_ref, tiles_ref, held_tiles_ref, own_ref, norm_ref, panel_ref, sems):
    share_rows, width = own_ref.shape
    half = share_rows // 2
    block_count, tile_size = degrees_ref.shape
    start = pl.multiple_of(lax.axis_index("rep") * share_rows, share_rows)
    tiles_copy = pltpu.make_async_copy(tiles_ref, held_tiles_ref, sems.at[0])
    own_copy = pltpu.make_async_copy(embeddings_ref.at[pl.ds(start, share_rows), :], own_ref, sems.at[1])
    tiles_copy.start()
    own_copy.start()
    norms = norm_columns(degrees_ref[...])
    for block in range(block_count):
        panel_ref[block * tile_size : (block + 1) * tile_size, :] = jnp.broadcast_to(
            norms[:, block : block + 1], (tile_size, width)
        )
    top = panel_ref[pl.ds(start, half), :]
    bottom = panel_ref[pl.ds(pl.multiple_of(start + half, half), half), :]
    norm_ref[...] = lane_join(top, bottom)
    own_copy.wait()
    tiles_copy.wait()


def prepare(degrees, embeddings, tile_values):
    panel_rows, width = embeddings.shape
    share_rows = panel_rows // lax.axis_size("rep")
    return pl.pallas_call(
        prepare_kernel,
        out_shape=[
            jax.ShapeDtypeStruct(tile_values.shape, tile_values.dtype),
            jax.ShapeDtypeStruct((share_rows, width), jnp.float32),
            jax.ShapeDtypeStruct((share_rows // 2, width), jnp.float32),
        ],
        in_specs=[VMEM, ANY, ANY],
        out_specs=[VMEM] * 3,
        scratch_shapes=[pltpu.VMEM((panel_rows, width), jnp.float32), pltpu.SemaphoreType.DMA((2,))],
        compiler_params=pltpu.CompilerParams(vmem_limit_bytes=VMEM_LIMIT),
        cost_estimate=pl.CostEstimate(
            flops=panel_rows * width, bytes_accessed=4 * panel_rows * width, transcendentals=0
        ),
    )(degrees, embeddings, tile_values)


def multiply_slots(table_ref, tiles_ref, split_ref, sums_ref, fold):
    slot_total, tile_size, _ = tiles_ref.shape
    width = sums_ref.shape[1]
    block_count = sums_ref.shape[0] // tile_size - 1
    for j in range(slot_total):
        source = pl.multiple_of(table_ref[1 + slot_total + j] * tile_size, tile_size)
        product = jnp.dot(
            tiles_ref[j],
            split_ref[pl.ds(source, tile_size), :],
            preferred_element_type=jnp.float32,
        )
        row = jnp.where(j < table_ref[0], table_ref[1 + j], block_count)
        at = pl.ds(pl.multiple_of(row * tile_size, tile_size), tile_size)
        sums_ref[at, :] += product[:, :width] + product[:, width:] if fold else product


def write_shares(sums_ref, outs, partials, join):
    team_count = lax.axis_size("rep")
    team_index = lax.axis_index("rep")
    half = outs[0].shape[0] // (team_count // 2)
    for parity in range(2):
        for column in range(team_count // 2):
            team = pair_teams(team_index, column, team_count)
            team = team if parity == 0 else team ^ 1
            top = sums_ref[pl.ds(pl.multiple_of(team * 2 * half, half), half), :]
            bottom = sums_ref[pl.ds(pl.multiple_of(team * 2 * half + half, half), half), :]
            to = pl.ds(column * half, half)
            for part, value in enumerate(join(top, bottom)):
                at = 2 * part + parity
                outs[at][to, :] = value + partials[at][to, :] if partials else value


def panel_kernel(info_ref, tiles_ref, degrees_ref, panel_ref, *refs, partial_count):
    partials, refs = refs[:partial_count], refs[partial_count:]
    *outs, table_ref, split_ref, sums_ref, sem = refs
    panel_rows, width = panel_ref.shape
    block_count, tile_size = degrees_ref.shape
    table_copy = pltpu.make_async_copy(info_ref, table_ref, sem)
    table_copy.start()
    norms = norm_columns(degrees_ref[...])
    for block in range(block_count):
        at = pl.ds(block * tile_size, tile_size)
        value = panel_ref[at, :] * norms[:, block : block + 1]
        high = value.astype(jnp.bfloat16)
        split_ref[at, :width] = high
        split_ref[at, width:] = (value - high.astype(jnp.float32)).astype(jnp.bfloat16)
    sums_ref[...] = jnp.zeros_like(sums_ref)
    table_copy.wait()
    multiply_slots(table_ref, tiles_ref, split_ref, sums_ref, True)
    write_shares(
        sums_ref,
        outs,
        partials,
        lambda top, bottom: (lane_join(top, swap_lanes(bottom)), lane_join(swap_lanes(top), bottom)),
    )


def part_kernel(info_ref, tiles_ref, *refs, team_count, partial_count):
    columns = team_count // 2
    pieces, refs = refs[:columns], refs[columns:]
    partials, refs = refs[:partial_count], refs[partial_count:]
    *outs, table_ref, split_ref, sums_ref, sem = refs
    half = pieces[0].shape[0] // 2
    team_index = lax.axis_index("rep")
    table_copy = pltpu.make_async_copy(info_ref, table_ref, sem)
    table_copy.start()
    for k in range(columns):
        source = source_team(team_index, k, team_count)
        for at, owner in enumerate((source, source ^ 1)):
            value = pieces[k][at * half : (at + 1) * half, :]
            high = value.astype(jnp.bfloat16).astype(jnp.float32)
            low = value - high
            top = lane_join(high, swap_lanes(low)).astype(jnp.bfloat16)
            bottom = lane_join(swap_lanes(high), low).astype(jnp.bfloat16)
            split_ref[pl.ds(pl.multiple_of(owner * 2 * half, half), half), :] = top
            split_ref[pl.ds(pl.multiple_of(owner * 2 * half + half, half), half), :] = bottom
    sums_ref[...] = jnp.zeros_like(sums_ref)
    table_copy.wait()
    multiply_slots(table_ref, tiles_ref, split_ref, sums_ref, False)
    write_shares(
        sums_ref,
        outs,
        partials,
        lambda top, bottom: (lane_join(top + swap_lanes(top), bottom + swap_lanes(bottom)),),
    )


def arc_call(kernel, info, tiles, operands, partials, parts, split_width):
    team_count = lax.axis_size("rep")
    slot_total, tile_size, _ = tiles.shape
    width = operands[-1].shape[1]
    panel_rows = sum(operand.shape[0] for operand in operands if operand.dtype == jnp.float32) * (3 - parts)
    parity = jax.ShapeDtypeStruct((panel_rows // 4, width), jnp.float32)
    return pl.pallas_call(
        kernel,
        out_shape=[parity] * (2 * parts),
        in_specs=[ANY] + [VMEM] * (1 + len(operands) + len(partials)),
        out_specs=[VMEM] * (2 * parts),
        scratch_shapes=[
            pltpu.SMEM(info.shape, info.dtype),
            pltpu.VMEM((panel_rows, split_width), jnp.bfloat16),
            pltpu.VMEM((panel_rows + tile_size, width), jnp.float32),
            pltpu.SemaphoreType.DMA,
        ],
        compiler_params=pltpu.CompilerParams(vmem_limit_bytes=VMEM_LIMIT),
        cost_estimate=pl.CostEstimate(
            flops=2 * slot_total * tile_size * tile_size * split_width,
            bytes_accessed=8 * panel_rows * width,
            transcendentals=0,
        ),
    )(info, tiles, *operands, *partials)


def panel_step(info, tiles, degrees, panel, partials):
    kernel = functools.partial(panel_kernel, partial_count=len(partials))
    return arc_call(kernel, info, tiles, [degrees, panel], partials, PARTS, 2 * panel.shape[1])


def part_step(info, tiles, pieces, partials):
    kernel = functools.partial(part_kernel, team_count=lax.axis_size("rep"), partial_count=len(partials))
    return arc_call(kernel, info, tiles, pieces, partials, 1, pieces[0].shape[1])


def layer_kernel(norm_ref, shares_ref, *refs):
    others, (current_ref, source_ref) = refs[:-2], refs[-2:]
    total = shares_ref[: norm_ref.shape[0], :]
    for other_ref in others:
        total = total + other_ref[...]
    current = total * norm_ref[...]
    current_ref[...] = current
    source_ref[...] = current * norm_ref[...]


def layer_share(norm, shares, others):
    share = jax.ShapeDtypeStruct(norm.shape, jnp.float32)
    return pl.pallas_call(
        layer_kernel,
        out_shape=[share] * 2,
        in_specs=[VMEM] * (2 + len(others)),
        out_specs=[VMEM] * 2,
        compiler_params=pltpu.CompilerParams(vmem_limit_bytes=VMEM_LIMIT),
    )(norm, shares, *others)


def finish_kernel(own_ref, norm_ref, *refs, layer_count):
    out_ref = refs[-1]
    half = out_ref.shape[0] // 2
    terms = len(refs[:-1]) // PARTS
    parts = []
    for part in range(PARTS):
        current_ref, shares_ref, *others = refs[part * terms : (part + 1) * terms]
        total = shares_ref[:half, :]
        for other_ref in others:
            total = total + other_ref[...]
        parts.append(current_ref[...] + total * norm_ref[...])
    top = lane_join(parts[0], swap_lanes(parts[1]))
    bottom = lane_join(swap_lanes(parts[0]), parts[1])
    out_ref[:half, :] = (own_ref[:half, :] + top) / layer_count
    out_ref[half:, :] = (own_ref[half:, :] + bottom) / layer_count


def finish(own, norm, parts):
    operands = [operand for part in parts for operand in part]
    return pl.pallas_call(
        functools.partial(finish_kernel, layer_count=LAYERS + 1.0),
        out_shape=jax.ShapeDtypeStruct(own.shape, jnp.float32),
        in_specs=[VMEM] * (2 + len(operands)),
        out_specs=VMEM,
        compiler_params=pltpu.CompilerParams(vmem_limit_bytes=VMEM_LIMIT),
    )(own, norm, *operands)


def fetch(value, source_team, arc_length):
    cycle, team_count = lax.axis_size("blk"), lax.axis_size("rep")
    pairs = []
    for shard in range(cycle):
        for team in range(team_count):
            to_shard = (shard + team * arc_length) % cycle
            pairs.append((shard * team_count + source_team(team), to_shard * team_count + team))
    return lax.ppermute(value, ("blk", "rep"), pairs)


def next_shard(value):
    cycle = lax.axis_size("blk")
    return lax.ppermute(value, "blk", [(i, (i + 1) % cycle) for i in range(cycle)])


def from_mate(value):
    team_count = lax.axis_size("rep")
    return lax.ppermute(value, "rep", [(team, team ^ 1) for team in range(team_count)])


def from_column(value, distance):
    team_count = lax.axis_size("rep")
    pairs = [((team + 2 * distance) % team_count, team) for team in range(team_count)]
    return lax.ppermute(value, "rep", pairs)


def share_terms(keep, give):
    columns = lax.axis_size("rep") // 2
    sums = keep + from_mate(give)
    half = sums.shape[0] // columns
    others = [
        from_column(lax.slice_in_dim(sums, at * half, (at + 1) * half), columns - at) for at in range(1, columns)
    ]
    return sums, others


def per_device(embeddings, degrees, tile_values, tile_rows, tile_columns, slot_counts):
    arc_length, _, tile_size, _ = tile_values.shape[2:]
    panel_rows = embeddings.shape[0]
    team_count = lax.axis_size("rep")
    columns = team_count // 2
    half = panel_rows // team_count // 2
    spread = (1, 2, 0, 3) if team_count == 4 else tuple(range(team_count))
    degrees = degrees.reshape(panel_rows // tile_size, tile_size)

    panel = fetch(embeddings, lambda team: spread[team], arc_length)
    source_degrees = fetch(degrees, lambda team: spread[team], arc_length)
    tiles, own, norm = prepare(degrees, embeddings, tile_values[0, 0])
    info = jnp.concatenate([slot_counts[0, 0][:, None], tile_rows[0, 0], tile_columns[0, 0]], axis=1)

    sums = ()
    for at in range(arc_length):
        sums = panel_step(info[at], tiles[at], source_degrees, panel, sums)
        if at + 1 < arc_length:
            panel, source_degrees = next_shard(panel), next_shard(source_degrees)
    parts = [sums[2 * part : 2 * part + 2] for part in range(PARTS)]
    layers = [0.0] * PARTS
    for _ in range(LAYERS - 1):
        terms = [share_terms(*part) for part in parts]
        fetched = []
        for part in range(PARTS):
            current, source = layer_share(norm, *terms[part])
            layers[part] = layers[part] + current
            source = jnp.concatenate([source, from_mate(source)])
            fetched.append(
                [
                    fetch(source, lambda team, k=k: source_team(team, k, team_count), arc_length)
                    for k in range(columns)
                ]
            )
        terms = []
        for pieces in fetched:
            sums = ()
            for at in range(arc_length):
                sums = part_step(info[at], tiles[at], pieces, sums)
                if at + 1 < arc_length:
                    pieces = [next_shard(piece) for piece in pieces]
            terms.append(share_terms(*sums))
    terms = [[layers[part], terms[part][0], *terms[part][1]] for part in range(PARTS)]
    return finish(own, norm, terms)


def solution(mesh):
    in_specs = (
        P(("groups", "blk"), None),
        P(("groups", "blk")),
        P(("groups", "blk"), "rep", None, None, None, None),
        P(("groups", "blk"), "rep", None, None),
        P(("groups", "blk"), "rep", None, None),
        P(("groups", "blk"), "rep", None),
    )
    out_specs = P(("groups", "blk", "rep"), None)
    return jax.shard_map(
        per_device, mesh=mesh, in_specs=in_specs, out_specs=out_specs, check_vma=False
    )
```

```python
import functools

import jax
import jax.numpy as jnp
from jax import lax
from jax.experimental import pallas as pl
from jax.experimental.pallas import tpu as pltpu
from jax.sharding import PartitionSpec as P

LAYERS = 2
PARTS = 2
VMEM_LIMIT = 16 * 1024 * 1024
VMEM = pl.BlockSpec(memory_space=pltpu.VMEM)
ANY = pl.BlockSpec(memory_space=pl.ANY)


def pair_teams(team_index, column, team_count):
    columns = team_count // 2
    return 2 * lax.rem(team_index // 2 + column, columns) + lax.rem(team_index, 2)


def source_team(team, team_count):
    return 2 * (team % 2) + team // 2 if team_count == 4 else team


def lower_lanes(shape):
    return lax.broadcasted_iota(jnp.int32, shape, 1) < shape[1] // 2


def swap_lanes(value):
    return pltpu.roll(value, value.shape[1] // 2, 1)


def lane_join(lower, upper):
    return jnp.where(lower_lanes(lower.shape), lower, upper)


def norm_columns(degrees):
    return jnp.transpose(lax.rsqrt(degrees.astype(jnp.float32)))


def prepare_kernel(degrees_ref, embeddings_ref, tiles_ref, held_tiles_ref, own_ref, norm_ref, panel_ref, sems):
    share_rows, width = own_ref.shape
    half = share_rows // 2
    columns = norm_ref.shape[0] // half
    block_count, tile_size = degrees_ref.shape
    team_index = lax.axis_index("rep")
    start = pl.multiple_of(team_index * share_rows, share_rows)
    tiles_copy = pltpu.make_async_copy(tiles_ref, held_tiles_ref, sems.at[0])
    own_copy = pltpu.make_async_copy(embeddings_ref.at[pl.ds(start, share_rows), :], own_ref, sems.at[1])
    tiles_copy.start()
    own_copy.start()
    norms = norm_columns(degrees_ref[...])
    for block in range(block_count):
        panel_ref[block * tile_size : (block + 1) * tile_size, :] = jnp.broadcast_to(
            norms[:, block : block + 1], (tile_size, width)
        )
    for column in range(columns):
        row = pair_teams(team_index, column, 2 * columns) * share_rows
        top = panel_ref[pl.ds(pl.multiple_of(row, half), half), :]
        bottom = panel_ref[pl.ds(pl.multiple_of(row + half, half), half), :]
        norm_ref[pl.ds(column * half, half), :] = lane_join(top, bottom)
    own_copy.wait()
    tiles_copy.wait()


def prepare(degrees, embeddings, tile_values):
    panel_rows, width = embeddings.shape
    share_rows = panel_rows // lax.axis_size("rep")
    return pl.pallas_call(
        prepare_kernel,
        out_shape=[
            jax.ShapeDtypeStruct(tile_values.shape, tile_values.dtype),
            jax.ShapeDtypeStruct((share_rows, width), jnp.float32),
            jax.ShapeDtypeStruct((panel_rows // 4, width), jnp.float32),
        ],
        in_specs=[VMEM, ANY, ANY],
        out_specs=[VMEM] * 3,
        scratch_shapes=[pltpu.VMEM((panel_rows, width), jnp.float32), pltpu.SemaphoreType.DMA((2,))],
        compiler_params=pltpu.CompilerParams(vmem_limit_bytes=VMEM_LIMIT),
        cost_estimate=pl.CostEstimate(
            flops=panel_rows * width, bytes_accessed=4 * panel_rows * width, transcendentals=0
        ),
    )(degrees, embeddings, tile_values)


def multiply_slots(table_ref, tiles_ref, split_ref, sums_ref, fold):
    slot_total, tile_size, _ = tiles_ref.shape
    width = sums_ref.shape[1]
    block_count = sums_ref.shape[0] // tile_size - 1
    for j in range(slot_total):
        source = pl.multiple_of(table_ref[1 + slot_total + j] * tile_size, tile_size)
        product = jnp.dot(
            tiles_ref[j],
            split_ref[pl.ds(source, tile_size), :],
            preferred_element_type=jnp.float32,
        )
        row = jnp.where(j < table_ref[0], table_ref[1 + j], block_count)
        at = pl.ds(pl.multiple_of(row * tile_size, tile_size), tile_size)
        sums_ref[at, :] += product[:, :width] + product[:, width:] if fold else product


def write_shares(sums_ref, outs, partials, join):
    team_count = lax.axis_size("rep")
    team_index = lax.axis_index("rep")
    half = outs[0].shape[0] // (team_count // 2)
    for parity in range(2):
        for column in range(team_count // 2):
            team = pair_teams(team_index, column, team_count)
            team = team if parity == 0 else team ^ 1
            top = sums_ref[pl.ds(pl.multiple_of(team * 2 * half, half), half), :]
            bottom = sums_ref[pl.ds(pl.multiple_of(team * 2 * half + half, half), half), :]
            to = pl.ds(column * half, half)
            for part, value in enumerate(join(top, bottom)):
                at = 2 * part + parity
                outs[at][to, :] = value + partials[at][to, :] if partials else value


def panel_kernel(info_ref, tiles_ref, degrees_ref, panel_ref, *refs, partial_count):
    partials, refs = refs[:partial_count], refs[partial_count:]
    *outs, table_ref, split_ref, sums_ref, sem = refs
    panel_rows, width = panel_ref.shape
    block_count, tile_size = degrees_ref.shape
    table_copy = pltpu.make_async_copy(info_ref, table_ref, sem)
    table_copy.start()
    norms = norm_columns(degrees_ref[...])
    for block in range(block_count):
        at = pl.ds(block * tile_size, tile_size)
        value = panel_ref[at, :] * norms[:, block : block + 1]
        high = value.astype(jnp.bfloat16)
        split_ref[at, :width] = high
        split_ref[at, width:] = (value - high.astype(jnp.float32)).astype(jnp.bfloat16)
    sums_ref[...] = jnp.zeros_like(sums_ref)
    table_copy.wait()
    multiply_slots(table_ref, tiles_ref, split_ref, sums_ref, True)
    write_shares(
        sums_ref,
        outs,
        partials,
        lambda top, bottom: (lane_join(top, swap_lanes(bottom)), lane_join(swap_lanes(top), bottom)),
    )


def part_kernel(info_ref, tiles_ref, panel_ref, *refs, team_count, partial_count):
    partials, refs = refs[:partial_count], refs[partial_count:]
    *outs, table_ref, split_ref, sums_ref, sem = refs
    half = panel_ref.shape[0] // team_count
    columns = team_count // 2
    source = source_team(lax.axis_index("rep"), team_count)
    table_copy = pltpu.make_async_copy(info_ref, table_ref, sem)
    table_copy.start()
    for at in range(team_count):
        owner = pair_teams(source if at < columns else source ^ 1, at % columns, team_count)
        value = panel_ref[at * half : (at + 1) * half, :]
        high = value.astype(jnp.bfloat16).astype(jnp.float32)
        low = value - high
        top = lane_join(high, swap_lanes(low)).astype(jnp.bfloat16)
        bottom = lane_join(swap_lanes(high), low).astype(jnp.bfloat16)
        split_ref[pl.ds(pl.multiple_of(owner * 2 * half, half), half), :] = top
        split_ref[pl.ds(pl.multiple_of(owner * 2 * half + half, half), half), :] = bottom
    sums_ref[...] = jnp.zeros_like(sums_ref)
    table_copy.wait()
    multiply_slots(table_ref, tiles_ref, split_ref, sums_ref, False)
    write_shares(
        sums_ref,
        outs,
        partials,
        lambda top, bottom: (lane_join(top + swap_lanes(top), bottom + swap_lanes(bottom)),),
    )


def arc_call(kernel, info, tiles, operands, partials, parts, split_width):
    team_count = lax.axis_size("rep")
    slot_total, tile_size, _ = tiles.shape
    width = operands[-1].shape[1]
    panel_rows = sum(operand.shape[0] for operand in operands if operand.dtype == jnp.float32) * (3 - parts)
    parity = jax.ShapeDtypeStruct((panel_rows // 4, width), jnp.float32)
    return pl.pallas_call(
        kernel,
        out_shape=[parity] * (2 * parts),
        in_specs=[ANY] + [VMEM] * (1 + len(operands) + len(partials)),
        out_specs=[VMEM] * (2 * parts),
        scratch_shapes=[
            pltpu.SMEM(info.shape, info.dtype),
            pltpu.VMEM((panel_rows, split_width), jnp.bfloat16),
            pltpu.VMEM((panel_rows + tile_size, width), jnp.float32),
            pltpu.SemaphoreType.DMA,
        ],
        compiler_params=pltpu.CompilerParams(vmem_limit_bytes=VMEM_LIMIT),
        cost_estimate=pl.CostEstimate(
            flops=2 * slot_total * tile_size * tile_size * split_width,
            bytes_accessed=8 * panel_rows * width,
            transcendentals=0,
        ),
    )(info, tiles, *operands, *partials)


def panel_step(info, tiles, degrees, panel, partials):
    kernel = functools.partial(panel_kernel, partial_count=len(partials))
    return arc_call(kernel, info, tiles, [degrees, panel], partials, PARTS, 2 * panel.shape[1])


def part_step(info, tiles, panel, partials):
    kernel = functools.partial(part_kernel, team_count=lax.axis_size("rep"), partial_count=len(partials))
    return arc_call(kernel, info, tiles, [panel], partials, 1, panel.shape[1])


def layer_kernel(norm_ref, shares_ref, *refs):
    others, (current_ref, source_ref) = refs[:-2], refs[-2:]
    half = current_ref.shape[0]
    columns = shares_ref.shape[0] // half
    for column in range(columns):
        at = pl.ds(column * half, half)
        total = shares_ref[at, :]
        for distance, other_ref in enumerate(others, 1):
            total = total + other_ref[pl.ds((column - distance) % columns * half, half), :]
        current = total * norm_ref[at, :]
        if column == 0:
            current_ref[...] = current
        source_ref[at, :] = current * norm_ref[at, :]


def layer_shares(norm, shares, others):
    columns = len(others) + 1
    return pl.pallas_call(
        layer_kernel,
        out_shape=[
            jax.ShapeDtypeStruct((shares.shape[0] // columns, shares.shape[1]), jnp.float32),
            jax.ShapeDtypeStruct(shares.shape, jnp.float32),
        ],
        in_specs=[VMEM] * (2 + len(others)),
        out_specs=[VMEM] * 2,
        compiler_params=pltpu.CompilerParams(vmem_limit_bytes=VMEM_LIMIT),
    )(norm, shares, *others)


def finish_kernel(own_ref, norm_ref, *refs, layer_count):
    out_ref = refs[-1]
    half = out_ref.shape[0] // 2
    terms = len(refs[:-1]) // PARTS
    parts = []
    for part in range(PARTS):
        current_ref, shares_ref, *others = refs[part * terms : (part + 1) * terms]
        total = shares_ref[:half, :]
        for other_ref in others:
            total = total + other_ref[...]
        parts.append(current_ref[...] + total * norm_ref[:half, :])
    top = lane_join(parts[0], swap_lanes(parts[1]))
    bottom = lane_join(swap_lanes(parts[0]), parts[1])
    out_ref[:half, :] = (own_ref[:half, :] + top) / layer_count
    out_ref[half:, :] = (own_ref[half:, :] + bottom) / layer_count


def finish(own, norm, parts):
    operands = [operand for part in parts for operand in part]
    return pl.pallas_call(
        functools.partial(finish_kernel, layer_count=LAYERS + 1.0),
        out_shape=jax.ShapeDtypeStruct(own.shape, jnp.float32),
        in_specs=[VMEM] * (2 + len(operands)),
        out_specs=VMEM,
        compiler_params=pltpu.CompilerParams(vmem_limit_bytes=VMEM_LIMIT),
    )(own, norm, *operands)


def fetch(value, source_team, arc_length):
    cycle, team_count = lax.axis_size("blk"), lax.axis_size("rep")
    pairs = []
    for shard in range(cycle):
        for team in range(team_count):
            to_shard = (shard + team * arc_length) % cycle
            pairs.append((shard * team_count + source_team(team), to_shard * team_count + team))
    return lax.ppermute(value, ("blk", "rep"), pairs)


def next_shard(value):
    cycle = lax.axis_size("blk")
    return lax.ppermute(value, "blk", [(i, (i + 1) % cycle) for i in range(cycle)])


def from_mate(value):
    team_count = lax.axis_size("rep")
    return lax.ppermute(value, "rep", [(team, team ^ 1) for team in range(team_count)])


def from_column(value, distance):
    team_count = lax.axis_size("rep")
    pairs = [((team + 2 * distance) % team_count, team) for team in range(team_count)]
    return lax.ppermute(value, "rep", pairs)


def share_terms(keep, give):
    columns = lax.axis_size("rep") // 2
    sums = keep + from_mate(give)
    half = sums.shape[0] // columns
    others = [
        from_column(lax.slice_in_dim(sums, at * half, (at + 1) * half), columns - at) for at in range(1, columns)
    ]
    return sums, *others


def per_device(embeddings, degrees, tile_values, tile_rows, tile_columns, slot_counts):
    arc_length, _, tile_size, _ = tile_values.shape[2:]
    panel_rows = embeddings.shape[0]
    team_count = lax.axis_size("rep")
    columns = team_count // 2

    def sources(team):
        return source_team(team, team_count)

    degrees = degrees.reshape(panel_rows // tile_size, tile_size)

    panel = fetch(embeddings, sources, arc_length)
    source_degrees = fetch(degrees, sources, arc_length)
    tiles, own, norm = prepare(degrees, embeddings, tile_values[0, 0])
    info = jnp.concatenate([slot_counts[0, 0][:, None], tile_rows[0, 0], tile_columns[0, 0]], axis=1)

    sums = ()
    for at in range(arc_length):
        sums = panel_step(info[at], tiles[at], source_degrees, panel, sums)
        if at + 1 < arc_length:
            panel, source_degrees = next_shard(panel), next_shard(source_degrees)
    parts = [sums[2 * part : 2 * part + 2] for part in range(PARTS)]
    layers = [0.0] * PARTS
    for _ in range(LAYERS - 1):
        panels = []
        for part, (keep, give) in enumerate(parts):
            shares = keep + from_mate(give)
            others = [from_column(shares, distance) for distance in range(1, columns)]
            current, source = layer_shares(norm, shares, others)
            layers[part] = layers[part] + current
            panels.append(fetch(jnp.concatenate([source, from_mate(source)]), sources, arc_length))
        for part, panel in enumerate(panels):
            sums = ()
            for at in range(arc_length):
                sums = part_step(info[at], tiles[at], panel, sums)
                if at + 1 < arc_length:
                    panel = next_shard(panel)
            parts[part] = sums
    terms = [[layers[part], *share_terms(*parts[part])] for part in range(PARTS)]
    return finish(own, norm, terms)


def solution(mesh):
    in_specs = (
        P(("groups", "blk"), None),
        P(("groups", "blk")),
        P(("groups", "blk"), "rep", None, None, None, None),
        P(("groups", "blk"), "rep", None, None),
        P(("groups", "blk"), "rep", None, None),
        P(("groups", "blk"), "rep", None),
    )
    out_specs = P(("groups", "blk", "rep"), None)
    return jax.shard_map(
        per_device, mesh=mesh, in_specs=in_specs, out_specs=out_specs, check_vma=False
    )
```

```python
import functools

import jax
import jax.numpy as jnp
from jax import lax
from jax.experimental import pallas as pl
from jax.experimental.pallas import tpu as pltpu
from jax.sharding import PartitionSpec as P

LAYERS = 2
VMEM_LIMIT = 16 * 1024 * 1024
VMEM = pl.BlockSpec(memory_space=pltpu.VMEM)
ANY = pl.BlockSpec(memory_space=pl.ANY)


def pair_teams(team_index, column, team_count):
    columns = team_count // 2
    return 2 * lax.rem(team_index // 2 + column, columns) + lax.rem(team_index, 2)


def source_team(team, turn, team_count):
    if team_count == 4:
        return (2 * (team % 2) + team // 2) ^ turn
    return (team + turn) % team_count


def norm_columns(degrees):
    return jnp.transpose(lax.rsqrt(degrees.astype(jnp.float32)))


def prepare_kernel(degrees_ref, embeddings_ref, tiles_ref, held_tiles_ref, own_ref, norm_ref, panel_ref, sems):
    share_rows, width = own_ref.shape
    block_count, tile_size = degrees_ref.shape
    team_index = lax.axis_index("rep")
    at = pl.ds(pl.multiple_of(team_index * share_rows, share_rows), share_rows)
    tiles_copy = pltpu.make_async_copy(tiles_ref, held_tiles_ref, sems.at[0])
    own_copy = pltpu.make_async_copy(embeddings_ref.at[at, :], own_ref, sems.at[1])
    tiles_copy.start()
    own_copy.start()
    norms = norm_columns(degrees_ref[...])
    for block in range(block_count):
        panel_ref[block * tile_size : (block + 1) * tile_size, :] = jnp.broadcast_to(
            norms[:, block : block + 1], (tile_size, width)
        )
    norm_ref[...] = panel_ref[at, :]
    own_copy.wait()
    tiles_copy.wait()


def prepare(degrees, embeddings, tile_values):
    panel_rows, width = embeddings.shape
    share = jax.ShapeDtypeStruct((panel_rows // lax.axis_size("rep"), width), jnp.float32)
    return pl.pallas_call(
        prepare_kernel,
        out_shape=[jax.ShapeDtypeStruct(tile_values.shape, tile_values.dtype), share, share],
        in_specs=[VMEM, ANY, ANY],
        out_specs=[VMEM] * 3,
        scratch_shapes=[pltpu.VMEM((panel_rows, width), jnp.float32), pltpu.SemaphoreType.DMA((2,))],
        compiler_params=pltpu.CompilerParams(vmem_limit_bytes=VMEM_LIMIT),
        cost_estimate=pl.CostEstimate(
            flops=panel_rows * width, bytes_accessed=4 * panel_rows * width, transcendentals=0
        ),
    )(degrees, embeddings, tile_values)


def arc_kernel(info_ref, tiles_ref, *refs, team_count, piece_count, scaled, partial_count):
    columns = team_count // 2
    pieces, refs = refs[:piece_count], refs[piece_count:]
    partials, refs = refs[:partial_count], refs[partial_count:]
    outs, (table_ref, split_ref, sums_ref, sem) = refs[:team_count], refs[team_count:]
    team_index = lax.axis_index("rep")
    slot_total, tile_size, _ = tiles_ref.shape
    panel_rows, width = split_ref.shape[0], split_ref.shape[1] // 2
    share_rows = panel_rows // team_count
    block_count = panel_rows // tile_size
    table_copy = pltpu.make_async_copy(info_ref, table_ref, sem)
    table_copy.start()

    def split(value, at):
        high = value.astype(jnp.bfloat16)
        split_ref[at, :width] = high
        split_ref[at, width:] = (value - high.astype(jnp.float32)).astype(jnp.bfloat16)

    def split_scaled(degrees_ref, panel_ref):
        norms = norm_columns(degrees_ref[...])
        for block in range(block_count):
            at = pl.ds(block * tile_size, tile_size)
            split(panel_ref[at, :] * norms[:, block : block + 1], at)

    if scaled:

        @pl.when(team_index == 0)
        def _():
            split_scaled(*pieces[:2])

        @pl.when(team_index > 0)
        def _():
            split_scaled(*pieces[2:])
    else:
        for k in range(piece_count):
            owner = source_team(team_index, k, team_count)
            split(pieces[k][...], pl.ds(pl.multiple_of(owner * share_rows, share_rows), share_rows))
    sums_ref[...] = jnp.zeros_like(sums_ref)
    table_copy.wait()
    live_count = table_ref[0]
    for j in range(slot_total):
        source = pl.multiple_of(table_ref[1 + slot_total + j] * tile_size, tile_size)
        product = jnp.dot(
            tiles_ref[j],
            split_ref[pl.ds(source, tile_size), :],
            preferred_element_type=jnp.float32,
        )
        row = jnp.where(j < live_count, table_ref[1 + j], block_count)
        at = pl.ds(pl.multiple_of(row * tile_size, tile_size), tile_size)
        sums_ref[at, :] += product[:, :width] + product[:, width:]

    for parity in range(2):
        for column in range(columns):
            team = pair_teams(team_index, column, team_count)
            team = team if parity == 0 else team ^ 1
            value = sums_ref[pl.ds(pl.multiple_of(team * share_rows, share_rows), share_rows), :]
            at = parity * columns + column
            outs[at][...] = value + partials[at][...] if partials else value


def arc_step(info, tiles, pieces, partials, scaled):
    team_count = lax.axis_size("rep")
    panel_rows = pieces[1].shape[0] if scaled else sum(piece.shape[0] for piece in pieces)
    width = pieces[1].shape[1]
    slot_total, tile_size, _ = tiles.shape
    share = jax.ShapeDtypeStruct((panel_rows // team_count, width), jnp.float32)
    operands = [info, tiles, *pieces, *partials]
    return pl.pallas_call(
        functools.partial(
            arc_kernel,
            team_count=team_count,
            piece_count=len(pieces),
            scaled=scaled,
            partial_count=len(partials),
        ),
        out_shape=[share] * team_count,
        in_specs=[ANY] + [VMEM] * (len(operands) - 1),
        out_specs=[VMEM] * team_count,
        scratch_shapes=[
            pltpu.SMEM(info.shape, info.dtype),
            pltpu.VMEM((panel_rows, 2 * width), jnp.bfloat16),
            pltpu.VMEM((panel_rows + tile_size, width), jnp.float32),
            pltpu.SemaphoreType.DMA,
        ],
        compiler_params=pltpu.CompilerParams(vmem_limit_bytes=VMEM_LIMIT),
        cost_estimate=pl.CostEstimate(
            flops=4 * slot_total * tile_size * tile_size * width, bytes_accessed=8 * panel_rows * width, transcendentals=0
        ),
    )(*operands)


def fetch(value, source_team, teams, arc_length):
    cycle, team_count = lax.axis_size("blk"), lax.axis_size("rep")
    pairs = []
    for shard in range(cycle):
        for team in teams:
            to_shard = (shard + team * arc_length) % cycle
            pairs.append((shard * team_count + source_team(team), to_shard * team_count + team))
    return lax.ppermute(value, ("blk", "rep"), pairs)


def next_shard(value):
    cycle = lax.axis_size("blk")
    return lax.ppermute(value, "blk", [(i, (i + 1) % cycle) for i in range(cycle)])


def from_mate(value):
    team_count = lax.axis_size("rep")
    return lax.ppermute(value, "rep", [(team, team ^ 1) for team in range(team_count)])


def from_column(value, distance):
    team_count = lax.axis_size("rep")
    pairs = [((team + 2 * distance) % team_count, team) for team in range(team_count)]
    return lax.ppermute(value, "rep", pairs)


def team_sum(sums):
    columns = len(sums) // 2
    total = None
    for distance in [*range(1, columns), 0]:
        at = (columns - distance) % columns
        share = sums[at] + from_mate(sums[columns + at])
        share = from_column(share, distance) if distance else share
        total = share if total is None else total + share
    return total


def per_device(embeddings, degrees, tile_values, tile_rows, tile_columns, slot_counts):
    arc_length, _, tile_size, _ = tile_values.shape[2:]
    panel_rows = embeddings.shape[0]
    team_count = lax.axis_size("rep")
    spread = (0, 1, 2, 0) if team_count == 4 else tuple(range(team_count))
    degrees = degrees.reshape(panel_rows // tile_size, tile_size)

    pieces = [degrees, embeddings]
    panel = fetch(embeddings, lambda team: spread[team], range(1, team_count), arc_length)
    pieces += [fetch(degrees, lambda team: spread[team], range(1, team_count), arc_length), panel]
    tiles, own, norm_scale = prepare(degrees, embeddings, tile_values[0, 0])
    info = jnp.concatenate([slot_counts[0, 0][:, None], tile_rows[0, 0], tile_columns[0, 0]], axis=1)

    combined = own
    for layer in range(LAYERS):
        sums = ()
        for arc_slot in range(arc_length):
            sums = arc_step(info[arc_slot], tiles[arc_slot], pieces, sums, layer == 0)
            if arc_slot + 1 < arc_length:
                pieces = [next_shard(piece) for piece in pieces]
        current = team_sum(sums) * norm_scale
        combined = combined + current
        if layer + 1 < LAYERS:
            source = current * norm_scale
            pieces = [
                fetch(source, lambda team, k=k: source_team(team, k, team_count), range(team_count), arc_length)
                for k in range(team_count)
            ]
    return combined / (LAYERS + 1.0)


def solution(mesh):
    in_specs = (
        P(("groups", "blk"), None),
        P(("groups", "blk")),
        P(("groups", "blk"), "rep", None, None, None, None),
        P(("groups", "blk"), "rep", None, None),
        P(("groups", "blk"), "rep", None, None),
        P(("groups", "blk"), "rep", None),
    )
    out_specs = P(("groups", "blk", "rep"), None)
    return jax.shard_map(
        per_device, mesh=mesh, in_specs=in_specs, out_specs=out_specs, check_vma=False
    )
```

```python
import functools

import jax
import jax.numpy as jnp
from jax import lax
from jax.experimental import pallas as pl
from jax.experimental.pallas import tpu as pltpu
from jax.sharding import PartitionSpec as P

LAYERS = 2
VMEM_LIMIT = 16 * 1024 * 1024
VMEM = pl.BlockSpec(memory_space=pltpu.VMEM)
ANY = pl.BlockSpec(memory_space=pl.ANY)


def pair_teams(team_index, column, team_count):
    columns = team_count // 2
    return 2 * lax.rem(team_index // 2 + column, columns) + lax.rem(team_index, 2)


def source_team(team, turn, team_count):
    if team_count == 4:
        return (2 * (team % 2) + team // 2) ^ turn
    return (team + turn) % team_count


def norm_columns(degrees):
    return jnp.transpose(lax.rsqrt(degrees.astype(jnp.float32)))


def prepare_kernel(degrees_ref, embeddings_ref, tiles_ref, held_tiles_ref, own_ref, norm_ref, panel_ref, sems):
    share_rows, width = own_ref.shape
    block_count, tile_size = degrees_ref.shape
    team_index = lax.axis_index("rep")
    at = pl.ds(pl.multiple_of(team_index * share_rows, share_rows), share_rows)
    tiles_copy = pltpu.make_async_copy(tiles_ref, held_tiles_ref, sems.at[0])
    own_copy = pltpu.make_async_copy(embeddings_ref.at[at, :], own_ref, sems.at[1])
    tiles_copy.start()
    own_copy.start()
    norms = norm_columns(degrees_ref[...])
    for block in range(block_count):
        panel_ref[block * tile_size : (block + 1) * tile_size, :] = jnp.broadcast_to(
            norms[:, block : block + 1], (tile_size, width)
        )
    norm_ref[...] = panel_ref[at, :]
    own_copy.wait()
    tiles_copy.wait()


def prepare(degrees, embeddings, tile_values):
    panel_rows, width = embeddings.shape
    share = jax.ShapeDtypeStruct((panel_rows // lax.axis_size("rep"), width), jnp.float32)
    return pl.pallas_call(
        prepare_kernel,
        out_shape=[jax.ShapeDtypeStruct(tile_values.shape, tile_values.dtype), share, share],
        in_specs=[VMEM, ANY, ANY],
        out_specs=[VMEM] * 3,
        scratch_shapes=[pltpu.VMEM((panel_rows, width), jnp.float32), pltpu.SemaphoreType.DMA((2,))],
        compiler_params=pltpu.CompilerParams(vmem_limit_bytes=VMEM_LIMIT),
        cost_estimate=pl.CostEstimate(
            flops=panel_rows * width, bytes_accessed=4 * panel_rows * width, transcendentals=0
        ),
    )(degrees, embeddings, tile_values)


def arc_kernel(info_ref, tiles_ref, *refs, team_count, piece_count, scaled, partial_count):
    columns = team_count // 2
    pieces, refs = refs[:piece_count], refs[piece_count:]
    partials, refs = refs[:partial_count], refs[partial_count:]
    outs, (table_ref, split_ref, sums_ref, sem) = refs[:team_count], refs[team_count:]
    team_index = lax.axis_index("rep")
    slot_total, tile_size, _ = tiles_ref.shape
    panel_rows, width = split_ref.shape[0], split_ref.shape[1] // 2
    share_rows = panel_rows // team_count
    block_count = panel_rows // tile_size
    table_copy = pltpu.make_async_copy(info_ref, table_ref, sem)
    table_copy.start()

    def split(value, at):
        high = value.astype(jnp.bfloat16)
        split_ref[at, :width] = high
        split_ref[at, width:] = (value - high.astype(jnp.float32)).astype(jnp.bfloat16)

    if scaled:
        degrees_ref, panel_ref = pieces
        norms = norm_columns(degrees_ref[...])
        for block in range(block_count):
            at = pl.ds(block * tile_size, tile_size)
            split(panel_ref[at, :] * norms[:, block : block + 1], at)
    else:
        for k in range(piece_count):
            owner = source_team(team_index, k, team_count)
            split(pieces[k][...], pl.ds(pl.multiple_of(owner * share_rows, share_rows), share_rows))
    sums_ref[...] = jnp.zeros_like(sums_ref)
    table_copy.wait()
    live_count = table_ref[0]
    for j in range(slot_total):
        source = pl.multiple_of(table_ref[1 + slot_total + j] * tile_size, tile_size)
        product = jnp.dot(
            tiles_ref[j],
            split_ref[pl.ds(source, tile_size), :],
            preferred_element_type=jnp.float32,
        )
        row = jnp.where(j < live_count, table_ref[1 + j], block_count)
        at = pl.ds(pl.multiple_of(row * tile_size, tile_size), tile_size)
        sums_ref[at, :] += product[:, :width] + product[:, width:]

    for parity in range(2):
        for column in range(columns):
            team = pair_teams(team_index, column, team_count)
            team = team if parity == 0 else team ^ 1
            value = sums_ref[pl.ds(pl.multiple_of(team * share_rows, share_rows), share_rows), :]
            at = parity * columns + column
            outs[at][...] = value + partials[at][...] if partials else value


def arc_step(info, tiles, pieces, partials, scaled):
    team_count = lax.axis_size("rep")
    panel_rows = pieces[1].shape[0] if scaled else sum(piece.shape[0] for piece in pieces)
    width = pieces[1].shape[1]
    slot_total, tile_size, _ = tiles.shape
    share = jax.ShapeDtypeStruct((panel_rows // team_count, width), jnp.float32)
    operands = [info, tiles, *pieces, *partials]
    return pl.pallas_call(
        functools.partial(
            arc_kernel,
            team_count=team_count,
            piece_count=len(pieces),
            scaled=scaled,
            partial_count=len(partials),
        ),
        out_shape=[share] * team_count,
        in_specs=[ANY] + [VMEM] * (len(operands) - 1),
        out_specs=[VMEM] * team_count,
        scratch_shapes=[
            pltpu.SMEM(info.shape, info.dtype),
            pltpu.VMEM((panel_rows, 2 * width), jnp.bfloat16),
            pltpu.VMEM((panel_rows + tile_size, width), jnp.float32),
            pltpu.SemaphoreType.DMA,
        ],
        compiler_params=pltpu.CompilerParams(vmem_limit_bytes=VMEM_LIMIT),
        cost_estimate=pl.CostEstimate(
            flops=4 * slot_total * tile_size * tile_size * width, bytes_accessed=8 * panel_rows * width, transcendentals=0
        ),
    )(*operands)


def fetch(value, source_team, arc_length):
    cycle, team_count = lax.axis_size("blk"), lax.axis_size("rep")
    pairs = []
    for shard in range(cycle):
        for team in range(team_count):
            to_shard = (shard + team * arc_length) % cycle
            pairs.append((shard * team_count + source_team(team), to_shard * team_count + team))
    return lax.ppermute(value, ("blk", "rep"), pairs)


def next_shard(value):
    cycle = lax.axis_size("blk")
    return lax.ppermute(value, "blk", [(i, (i + 1) % cycle) for i in range(cycle)])


def from_mate(value):
    team_count = lax.axis_size("rep")
    return lax.ppermute(value, "rep", [(team, team ^ 1) for team in range(team_count)])


def from_column(value, distance):
    team_count = lax.axis_size("rep")
    pairs = [((team + 2 * distance) % team_count, team) for team in range(team_count)]
    return lax.ppermute(value, "rep", pairs)


def team_sum(sums):
    columns = len(sums) // 2
    total = None
    for distance in [*range(1, columns), 0]:
        at = (columns - distance) % columns
        share = sums[at] + from_mate(sums[columns + at])
        share = from_column(share, distance) if distance else share
        total = share if total is None else total + share
    return total


def per_device(embeddings, degrees, tile_values, tile_rows, tile_columns, slot_counts):
    arc_length, _, tile_size, _ = tile_values.shape[2:]
    panel_rows = embeddings.shape[0]
    team_count = lax.axis_size("rep")
    spread = (3, 1, 2, 0) if team_count == 4 else tuple(range(team_count))
    degrees = degrees.reshape(panel_rows // tile_size, tile_size)

    panel = fetch(embeddings, lambda team: spread[team], arc_length)
    pieces = [fetch(degrees, lambda team: spread[team], arc_length), panel]
    tiles, own, norm_scale = prepare(degrees, embeddings, tile_values[0, 0])
    info = jnp.concatenate([slot_counts[0, 0][:, None], tile_rows[0, 0], tile_columns[0, 0]], axis=1)

    combined = own
    for layer in range(LAYERS):
        sums = ()
        for arc_slot in range(arc_length):
            sums = arc_step(info[arc_slot], tiles[arc_slot], pieces, sums, layer == 0)
            if arc_slot + 1 < arc_length:
                pieces = [next_shard(piece) for piece in pieces]
        current = team_sum(sums) * norm_scale
        combined = combined + current
        if layer + 1 < LAYERS:
            source = current * norm_scale
            pieces = [
                fetch(source, lambda team, k=k: source_team(team, k, team_count), arc_length)
                for k in range(team_count)
            ]
    return combined / (LAYERS + 1.0)


def solution(mesh):
    in_specs = (
        P(("groups", "blk"), None),
        P(("groups", "blk")),
        P(("groups", "blk"), "rep", None, None, None, None),
        P(("groups", "blk"), "rep", None, None),
        P(("groups", "blk"), "rep", None, None),
        P(("groups", "blk"), "rep", None),
    )
    out_specs = P(("groups", "blk", "rep"), None)
    return jax.shard_map(
        per_device, mesh=mesh, in_specs=in_specs, out_specs=out_specs, check_vma=False
    )
```

```python
import functools

import jax
import jax.numpy as jnp
from jax import lax
from jax.experimental import pallas as pl
from jax.experimental.pallas import tpu as pltpu
from jax.sharding import PartitionSpec as P

LAYERS = 2
VMEM_LIMIT = 16 * 1024 * 1024
VMEM = pl.BlockSpec(memory_space=pltpu.VMEM)
ANY = pl.BlockSpec(memory_space=pl.ANY)


def pair_teams(team_index, column, team_count):
    columns = team_count // 2
    return 2 * lax.rem(team_index // 2 + column, columns) + lax.rem(team_index, 2)


def source_team(team, turn, team_count):
    if team_count == 4:
        return (2 * ((team + 1) % 2) + team // 2) ^ (3 * turn)
    return (team + 2 * turn) % team_count


def norm_columns(degrees):
    return jnp.transpose(lax.rsqrt(degrees.astype(jnp.float32)))


def prepare_kernel(degrees_ref, embeddings_ref, tiles_ref, held_tiles_ref, own_ref, norm_ref, panel_ref, sems):
    share_rows, width = own_ref.shape
    block_count, tile_size = degrees_ref.shape
    team_index = lax.axis_index("rep")
    at = pl.ds(pl.multiple_of(team_index * share_rows, share_rows), share_rows)
    tiles_copy = pltpu.make_async_copy(tiles_ref, held_tiles_ref, sems.at[0])
    own_copy = pltpu.make_async_copy(embeddings_ref.at[at, :], own_ref, sems.at[1])
    tiles_copy.start()
    own_copy.start()
    norms = norm_columns(degrees_ref[...])
    for block in range(block_count):
        panel_ref[block * tile_size : (block + 1) * tile_size, :] = jnp.broadcast_to(
            norms[:, block : block + 1], (tile_size, width)
        )
    norm_ref[...] = panel_ref[at, :]
    own_copy.wait()
    tiles_copy.wait()


def prepare(degrees, embeddings, tile_values):
    panel_rows, width = embeddings.shape
    share = jax.ShapeDtypeStruct((panel_rows // lax.axis_size("rep"), width), jnp.float32)
    return pl.pallas_call(
        prepare_kernel,
        out_shape=[jax.ShapeDtypeStruct(tile_values.shape, tile_values.dtype), share, share],
        in_specs=[VMEM, ANY, ANY],
        out_specs=[VMEM] * 3,
        scratch_shapes=[pltpu.VMEM((panel_rows, width), jnp.float32), pltpu.SemaphoreType.DMA((2,))],
        compiler_params=pltpu.CompilerParams(vmem_limit_bytes=VMEM_LIMIT),
        cost_estimate=pl.CostEstimate(
            flops=panel_rows * width, bytes_accessed=4 * panel_rows * width, transcendentals=0
        ),
    )(degrees, embeddings, tile_values)


def arc_kernel(info_ref, tiles_ref, *refs, team_count, piece_count, scaled, partial_count):
    columns = team_count // 2
    pieces, refs = refs[:piece_count], refs[piece_count:]
    partials, refs = refs[:partial_count], refs[partial_count:]
    outs, (table_ref, split_ref, sums_ref, sem) = refs[:team_count], refs[team_count:]
    team_index = lax.axis_index("rep")
    slot_total, tile_size, _ = tiles_ref.shape
    panel_rows, width = split_ref.shape[0], split_ref.shape[1] // 2
    share_rows = panel_rows // team_count
    block_count = panel_rows // tile_size
    table_copy = pltpu.make_async_copy(info_ref, table_ref, sem)
    table_copy.start()

    def split(value, at):
        high = value.astype(jnp.bfloat16)
        split_ref[at, :width] = high
        split_ref[at, width:] = (value - high.astype(jnp.float32)).astype(jnp.bfloat16)

    if scaled:
        degrees_ref, panel_ref = pieces
        norms = norm_columns(degrees_ref[...])
        for block in range(block_count):
            at = pl.ds(block * tile_size, tile_size)
            split(panel_ref[at, :] * norms[:, block : block + 1], at)
    else:
        for k in range(piece_count):
            source = source_team(team_index, k, team_count)
            for at, owner in enumerate((source, source ^ 1)):
                value = pieces[k][at * share_rows : (at + 1) * share_rows, :]
                split(value, pl.ds(pl.multiple_of(owner * share_rows, share_rows), share_rows))
    sums_ref[...] = jnp.zeros_like(sums_ref)
    table_copy.wait()
    live_count = table_ref[0]
    for j in range(slot_total):
        source = pl.multiple_of(table_ref[1 + slot_total + j] * tile_size, tile_size)
        product = jnp.dot(
            tiles_ref[j],
            split_ref[pl.ds(source, tile_size), :],
            preferred_element_type=jnp.float32,
        )
        row = jnp.where(j < live_count, table_ref[1 + j], block_count)
        at = pl.ds(pl.multiple_of(row * tile_size, tile_size), tile_size)
        sums_ref[at, :] += product[:, :width] + product[:, width:]

    for parity in range(2):
        for column in range(columns):
            team = pair_teams(team_index, column, team_count)
            team = team if parity == 0 else team ^ 1
            value = sums_ref[pl.ds(pl.multiple_of(team * share_rows, share_rows), share_rows), :]
            at = parity * columns + column
            outs[at][...] = value + partials[at][...] if partials else value


def arc_step(info, tiles, pieces, partials, scaled):
    team_count = lax.axis_size("rep")
    panel_rows = pieces[1].shape[0] if scaled else sum(piece.shape[0] for piece in pieces)
    width = pieces[1].shape[1]
    slot_total, tile_size, _ = tiles.shape
    share = jax.ShapeDtypeStruct((panel_rows // team_count, width), jnp.float32)
    operands = [info, tiles, *pieces, *partials]
    return pl.pallas_call(
        functools.partial(
            arc_kernel,
            team_count=team_count,
            piece_count=len(pieces),
            scaled=scaled,
            partial_count=len(partials),
        ),
        out_shape=[share] * team_count,
        in_specs=[ANY] + [VMEM] * (len(operands) - 1),
        out_specs=[VMEM] * team_count,
        scratch_shapes=[
            pltpu.SMEM(info.shape, info.dtype),
            pltpu.VMEM((panel_rows, 2 * width), jnp.bfloat16),
            pltpu.VMEM((panel_rows + tile_size, width), jnp.float32),
            pltpu.SemaphoreType.DMA,
        ],
        compiler_params=pltpu.CompilerParams(vmem_limit_bytes=VMEM_LIMIT),
        cost_estimate=pl.CostEstimate(
            flops=4 * slot_total * tile_size * tile_size * width, bytes_accessed=8 * panel_rows * width, transcendentals=0
        ),
    )(*operands)


def fetch(value, source_team, arc_length):
    cycle, team_count = lax.axis_size("blk"), lax.axis_size("rep")
    pairs = []
    for shard in range(cycle):
        for team in range(team_count):
            to_shard = (shard + team * arc_length) % cycle
            pairs.append((shard * team_count + source_team(team), to_shard * team_count + team))
    return lax.ppermute(value, ("blk", "rep"), pairs)


def next_shard(value):
    cycle = lax.axis_size("blk")
    return lax.ppermute(value, "blk", [(i, (i + 1) % cycle) for i in range(cycle)])


def from_mate(value):
    team_count = lax.axis_size("rep")
    return lax.ppermute(value, "rep", [(team, team ^ 1) for team in range(team_count)])


def from_column(value, distance):
    team_count = lax.axis_size("rep")
    pairs = [((team + 2 * distance) % team_count, team) for team in range(team_count)]
    return lax.ppermute(value, "rep", pairs)


def team_sum(sums):
    columns = len(sums) // 2
    total = None
    for distance in [*range(1, columns), 0]:
        at = (columns - distance) % columns
        share = sums[at] + from_mate(sums[columns + at])
        share = from_column(share, distance) if distance else share
        total = share if total is None else total + share
    return total


def per_device(embeddings, degrees, tile_values, tile_rows, tile_columns, slot_counts):
    arc_length, _, tile_size, _ = tile_values.shape[2:]
    panel_rows = embeddings.shape[0]
    team_count = lax.axis_size("rep")
    spread = (3, 1, 2, 0) if team_count == 4 else tuple(range(team_count))
    degrees = degrees.reshape(panel_rows // tile_size, tile_size)

    panel = fetch(embeddings, lambda team: spread[team], arc_length)
    pieces = [fetch(degrees, lambda team: spread[team], arc_length), panel]
    tiles, own, norm_scale = prepare(degrees, embeddings, tile_values[0, 0])
    info = jnp.concatenate([slot_counts[0, 0][:, None], tile_rows[0, 0], tile_columns[0, 0]], axis=1)

    combined = own
    for layer in range(LAYERS):
        sums = ()
        for arc_slot in range(arc_length):
            sums = arc_step(info[arc_slot], tiles[arc_slot], pieces, sums, layer == 0)
            if arc_slot + 1 < arc_length:
                pieces = [next_shard(piece) for piece in pieces]
        current = team_sum(sums) * norm_scale
        combined = combined + current
        if layer + 1 < LAYERS:
            source = current * norm_scale
            source = jnp.concatenate([source, from_mate(source)])
            pieces = [
                fetch(source, lambda team, k=k: source_team(team, k, team_count), arc_length)
                for k in range(team_count // 2)
            ]
    return combined / (LAYERS + 1.0)


def solution(mesh):
    in_specs = (
        P(("groups", "blk"), None),
        P(("groups", "blk")),
        P(("groups", "blk"), "rep", None, None, None, None),
        P(("groups", "blk"), "rep", None, None),
        P(("groups", "blk"), "rep", None, None),
        P(("groups", "blk"), "rep", None),
    )
    out_specs = P(("groups", "blk", "rep"), None)
    return jax.shard_map(
        per_device, mesh=mesh, in_specs=in_specs, out_specs=out_specs, check_vma=False
    )
```

```python
import functools

import jax
import jax.numpy as jnp
from jax import lax
from jax.experimental import pallas as pl
from jax.experimental.pallas import tpu as pltpu
from jax.sharding import PartitionSpec as P

LAYERS = 2
VMEM_LIMIT = 16 * 1024 * 1024
VMEM = pl.BlockSpec(memory_space=pltpu.VMEM)
ANY = pl.BlockSpec(memory_space=pl.ANY)


def pair_teams(team_index, column, team_count):
    columns = team_count // 2
    return 2 * lax.rem(team_index // 2 + column, columns) + lax.rem(team_index, 2)


def source_team(team, turn, team_count):
    if team_count == 4:
        return (2 * (team % 2) + team // 2) ^ (3 - turn)
    return (team + turn) % team_count


def norm_columns(degrees):
    return jnp.transpose(lax.rsqrt(degrees.astype(jnp.float32)))


def prepare_kernel(degrees_ref, embeddings_ref, tiles_ref, held_tiles_ref, own_ref, norm_ref, panel_ref, sems):
    share_rows, width = own_ref.shape
    block_count, tile_size = degrees_ref.shape
    team_index = lax.axis_index("rep")
    at = pl.ds(pl.multiple_of(team_index * share_rows, share_rows), share_rows)
    tiles_copy = pltpu.make_async_copy(tiles_ref, held_tiles_ref, sems.at[0])
    own_copy = pltpu.make_async_copy(embeddings_ref.at[at, :], own_ref, sems.at[1])
    tiles_copy.start()
    own_copy.start()
    norms = norm_columns(degrees_ref[...])
    for block in range(block_count):
        panel_ref[block * tile_size : (block + 1) * tile_size, :] = jnp.broadcast_to(
            norms[:, block : block + 1], (tile_size, width)
        )
    norm_ref[...] = panel_ref[at, :]
    own_copy.wait()
    tiles_copy.wait()


def prepare(degrees, embeddings, tile_values):
    panel_rows, width = embeddings.shape
    share = jax.ShapeDtypeStruct((panel_rows // lax.axis_size("rep"), width), jnp.float32)
    return pl.pallas_call(
        prepare_kernel,
        out_shape=[jax.ShapeDtypeStruct(tile_values.shape, tile_values.dtype), share, share],
        in_specs=[VMEM, ANY, ANY],
        out_specs=[VMEM] * 3,
        scratch_shapes=[pltpu.VMEM((panel_rows, width), jnp.float32), pltpu.SemaphoreType.DMA((2,))],
        compiler_params=pltpu.CompilerParams(vmem_limit_bytes=VMEM_LIMIT),
        cost_estimate=pl.CostEstimate(
            flops=panel_rows * width, bytes_accessed=4 * panel_rows * width, transcendentals=0
        ),
    )(degrees, embeddings, tile_values)


def arc_kernel(info_ref, tiles_ref, *refs, team_count, piece_count, scaled, partial_count):
    columns = team_count // 2
    pieces, refs = refs[:piece_count], refs[piece_count:]
    partials, refs = refs[:partial_count], refs[partial_count:]
    outs, (table_ref, split_ref, sums_ref, sem) = refs[:team_count], refs[team_count:]
    team_index = lax.axis_index("rep")
    slot_total, tile_size, _ = tiles_ref.shape
    panel_rows, width = split_ref.shape[0], split_ref.shape[1] // 2
    share_rows = panel_rows // team_count
    block_count = panel_rows // tile_size
    table_copy = pltpu.make_async_copy(info_ref, table_ref, sem)
    table_copy.start()

    def split(value, at):
        high = value.astype(jnp.bfloat16)
        split_ref[at, :width] = high
        split_ref[at, width:] = (value - high.astype(jnp.float32)).astype(jnp.bfloat16)

    if scaled:
        degrees_ref, panel_ref = pieces
        norms = norm_columns(degrees_ref[...])
        for block in range(block_count):
            at = pl.ds(block * tile_size, tile_size)
            split(panel_ref[at, :] * norms[:, block : block + 1], at)
    else:
        for k in range(piece_count):
            owner = source_team(team_index, k, team_count)
            split(pieces[k][...], pl.ds(pl.multiple_of(owner * share_rows, share_rows), share_rows))
    sums_ref[...] = jnp.zeros_like(sums_ref)
    table_copy.wait()
    live_count = table_ref[0]
    for j in range(slot_total):
        source = pl.multiple_of(table_ref[1 + slot_total + j] * tile_size, tile_size)
        product = jnp.dot(
            tiles_ref[j],
            split_ref[pl.ds(source, tile_size), :],
            preferred_element_type=jnp.float32,
        )
        row = jnp.where(j < live_count, table_ref[1 + j], block_count)
        at = pl.ds(pl.multiple_of(row * tile_size, tile_size), tile_size)
        sums_ref[at, :] += product[:, :width] + product[:, width:]

    for parity in range(2):
        for column in range(columns):
            team = pair_teams(team_index, column, team_count)
            team = team if parity == 0 else team ^ 1
            value = sums_ref[pl.ds(pl.multiple_of(team * share_rows, share_rows), share_rows), :]
            at = parity * columns + column
            outs[at][...] = value + partials[at][...] if partials else value


def arc_step(info, tiles, pieces, partials, scaled):
    team_count = lax.axis_size("rep")
    panel_rows = pieces[1].shape[0] if scaled else sum(piece.shape[0] for piece in pieces)
    width = pieces[1].shape[1]
    slot_total, tile_size, _ = tiles.shape
    share = jax.ShapeDtypeStruct((panel_rows // team_count, width), jnp.float32)
    operands = [info, tiles, *pieces, *partials]
    return pl.pallas_call(
        functools.partial(
            arc_kernel,
            team_count=team_count,
            piece_count=len(pieces),
            scaled=scaled,
            partial_count=len(partials),
        ),
        out_shape=[share] * team_count,
        in_specs=[ANY] + [VMEM] * (len(operands) - 1),
        out_specs=[VMEM] * team_count,
        scratch_shapes=[
            pltpu.SMEM(info.shape, info.dtype),
            pltpu.VMEM((panel_rows, 2 * width), jnp.bfloat16),
            pltpu.VMEM((panel_rows + tile_size, width), jnp.float32),
            pltpu.SemaphoreType.DMA,
        ],
        compiler_params=pltpu.CompilerParams(vmem_limit_bytes=VMEM_LIMIT),
        cost_estimate=pl.CostEstimate(
            flops=4 * slot_total * tile_size * tile_size * width, bytes_accessed=8 * panel_rows * width, transcendentals=0
        ),
    )(*operands)


def fetch(value, source_team, arc_length):
    cycle, team_count = lax.axis_size("blk"), lax.axis_size("rep")
    pairs = []
    for shard in range(cycle):
        for team in range(team_count):
            to_shard = (shard + team * arc_length) % cycle
            pairs.append((shard * team_count + source_team(team), to_shard * team_count + team))
    return lax.ppermute(value, ("blk", "rep"), pairs)


def next_shard(value):
    cycle = lax.axis_size("blk")
    return lax.ppermute(value, "blk", [(i, (i + 1) % cycle) for i in range(cycle)])


def from_mate(value):
    team_count = lax.axis_size("rep")
    return lax.ppermute(value, "rep", [(team, team ^ 1) for team in range(team_count)])


def from_column(value, distance):
    team_count = lax.axis_size("rep")
    pairs = [((team + 2 * distance) % team_count, team) for team in range(team_count)]
    return lax.ppermute(value, "rep", pairs)


def team_sum(sums):
    columns = len(sums) // 2
    total = None
    for distance in [*range(1, columns), 0]:
        at = (columns - distance) % columns
        share = sums[at] + from_mate(sums[columns + at])
        share = from_column(share, distance) if distance else share
        total = share if total is None else total + share
    return total


def per_device(embeddings, degrees, tile_values, tile_rows, tile_columns, slot_counts):
    arc_length, _, tile_size, _ = tile_values.shape[2:]
    panel_rows = embeddings.shape[0]
    team_count = lax.axis_size("rep")
    spread = (3, 1, 2, 0) if team_count == 4 else tuple(range(team_count))
    degrees = degrees.reshape(panel_rows // tile_size, tile_size)

    panel = fetch(embeddings, lambda team: spread[team], arc_length)
    pieces = [fetch(degrees, lambda team: spread[team], arc_length), panel]
    tiles, own, norm_scale = prepare(degrees, embeddings, tile_values[0, 0])
    info = jnp.concatenate([slot_counts[0, 0][:, None], tile_rows[0, 0], tile_columns[0, 0]], axis=1)

    combined = own
    for layer in range(LAYERS):
        sums = ()
        for arc_slot in range(arc_length):
            sums = arc_step(info[arc_slot], tiles[arc_slot], pieces, sums, layer == 0)
            if arc_slot + 1 < arc_length:
                pieces = [next_shard(piece) for piece in pieces]
        current = team_sum(sums) * norm_scale
        combined = combined + current
        if layer + 1 < LAYERS:
            source = current * norm_scale
            pieces = [
                fetch(source, lambda team, k=k: source_team(team, k, team_count), arc_length)
                for k in range(team_count)
            ]
    return combined / (LAYERS + 1.0)


def solution(mesh):
    in_specs = (
        P(("groups", "blk"), None),
        P(("groups", "blk")),
        P(("groups", "blk"), "rep", None, None, None, None),
        P(("groups", "blk"), "rep", None, None),
        P(("groups", "blk"), "rep", None, None),
        P(("groups", "blk"), "rep", None),
    )
    out_specs = P(("groups", "blk", "rep"), None)
    return jax.shard_map(
        per_device, mesh=mesh, in_specs=in_specs, out_specs=out_specs, check_vma=False
    )
```

```python
import functools

import jax
import jax.numpy as jnp
from jax import lax
from jax.experimental import pallas as pl
from jax.experimental.pallas import tpu as pltpu
from jax.sharding import PartitionSpec as P

LAYERS = 2
VMEM_LIMIT = 16 * 1024 * 1024
VMEM = pl.BlockSpec(memory_space=pltpu.VMEM)
ANY = pl.BlockSpec(memory_space=pl.ANY)


def pair_teams(team_index, column, team_count):
    columns = team_count // 2
    return 2 * lax.rem(team_index // 2 + column, columns) + lax.rem(team_index, 2)


def source_team(team, turn, team_count):
    if team_count == 4:
        return (2 * (team % 2) + team // 2) ^ turn
    return (team + turn) % team_count


def norm_columns(degrees):
    return jnp.transpose(lax.rsqrt(degrees.astype(jnp.float32)))


def prepare_kernel(degrees_ref, embeddings_ref, tiles_ref, held_tiles_ref, own_ref, norm_ref, panel_ref, sems):
    share_rows, width = own_ref.shape
    block_count, tile_size = degrees_ref.shape
    team_index = lax.axis_index("rep")
    at = pl.ds(pl.multiple_of(team_index * share_rows, share_rows), share_rows)
    tiles_copy = pltpu.make_async_copy(tiles_ref, held_tiles_ref, sems.at[0])
    own_copy = pltpu.make_async_copy(embeddings_ref.at[at, :], own_ref, sems.at[1])
    tiles_copy.start()
    own_copy.start()
    norms = norm_columns(degrees_ref[...])
    for block in range(block_count):
        panel_ref[block * tile_size : (block + 1) * tile_size, :] = jnp.broadcast_to(
            norms[:, block : block + 1], (tile_size, width)
        )
    norm_ref[...] = panel_ref[at, :]
    own_copy.wait()
    tiles_copy.wait()


def prepare(degrees, embeddings, tile_values):
    panel_rows, width = embeddings.shape
    share = jax.ShapeDtypeStruct((panel_rows // lax.axis_size("rep"), width), jnp.float32)
    return pl.pallas_call(
        prepare_kernel,
        out_shape=[jax.ShapeDtypeStruct(tile_values.shape, tile_values.dtype), share, share],
        in_specs=[VMEM, ANY, ANY],
        out_specs=[VMEM] * 3,
        scratch_shapes=[pltpu.VMEM((panel_rows, width), jnp.float32), pltpu.SemaphoreType.DMA((2,))],
        compiler_params=pltpu.CompilerParams(vmem_limit_bytes=VMEM_LIMIT),
        cost_estimate=pl.CostEstimate(
            flops=panel_rows * width, bytes_accessed=4 * panel_rows * width, transcendentals=0
        ),
    )(degrees, embeddings, tile_values)


def arc_kernel(info_ref, tiles_ref, *refs, team_count, piece_count, scaled, partial_count):
    columns = team_count // 2
    pieces, refs = refs[:piece_count], refs[piece_count:]
    partials, refs = refs[:partial_count], refs[partial_count:]
    outs, (table_ref, split_ref, sums_ref, sem) = refs[:team_count], refs[team_count:]
    team_index = lax.axis_index("rep")
    slot_total, tile_size, _ = tiles_ref.shape
    panel_rows, width = split_ref.shape[0], split_ref.shape[1] // 2
    share_rows = panel_rows // team_count
    block_count = panel_rows // tile_size
    table_copy = pltpu.make_async_copy(info_ref, table_ref, sem)
    table_copy.start()

    def split(value, at):
        high = value.astype(jnp.bfloat16)
        split_ref[at, :width] = high
        split_ref[at, width:] = (value - high.astype(jnp.float32)).astype(jnp.bfloat16)

    if scaled:
        degrees_ref, panel_ref = pieces
        norms = norm_columns(degrees_ref[...])
        for block in range(block_count):
            at = pl.ds(block * tile_size, tile_size)
            split(panel_ref[at, :] * norms[:, block : block + 1], at)
    else:
        for k in range(piece_count):
            owner = source_team(team_index, k, team_count)
            split(pieces[k][...], pl.ds(pl.multiple_of(owner * share_rows, share_rows), share_rows))
    sums_ref[...] = jnp.zeros_like(sums_ref)
    table_copy.wait()
    live_count = table_ref[0]
    for j in range(slot_total):
        source = pl.multiple_of(table_ref[1 + slot_total + j] * tile_size, tile_size)
        product = jnp.dot(
            tiles_ref[j],
            split_ref[pl.ds(source, tile_size), :],
            preferred_element_type=jnp.float32,
        )
        row = jnp.where(j < live_count, table_ref[1 + j], block_count)
        at = pl.ds(pl.multiple_of(row * tile_size, tile_size), tile_size)
        sums_ref[at, :] += product[:, :width] + product[:, width:]

    for parity in range(2):
        for column in range(columns):
            team = pair_teams(team_index, column, team_count)
            team = team if parity == 0 else team ^ 1
            value = sums_ref[pl.ds(pl.multiple_of(team * share_rows, share_rows), share_rows), :]
            at = parity * columns + column
            outs[at][...] = value + partials[at][...] if partials else value


def arc_step(info, tiles, pieces, partials, scaled):
    team_count = lax.axis_size("rep")
    panel_rows = pieces[1].shape[0] if scaled else sum(piece.shape[0] for piece in pieces)
    width = pieces[1].shape[1]
    slot_total, tile_size, _ = tiles.shape
    share = jax.ShapeDtypeStruct((panel_rows // team_count, width), jnp.float32)
    operands = [info, tiles, *pieces, *partials]
    return pl.pallas_call(
        functools.partial(
            arc_kernel,
            team_count=team_count,
            piece_count=len(pieces),
            scaled=scaled,
            partial_count=len(partials),
        ),
        out_shape=[share] * team_count,
        in_specs=[ANY] + [VMEM] * (len(operands) - 1),
        out_specs=[VMEM] * team_count,
        scratch_shapes=[
            pltpu.SMEM(info.shape, info.dtype),
            pltpu.VMEM((panel_rows, 2 * width), jnp.bfloat16),
            pltpu.VMEM((panel_rows + tile_size, width), jnp.float32),
            pltpu.SemaphoreType.DMA,
        ],
        compiler_params=pltpu.CompilerParams(vmem_limit_bytes=VMEM_LIMIT),
        cost_estimate=pl.CostEstimate(
            flops=4 * slot_total * tile_size * tile_size * width, bytes_accessed=8 * panel_rows * width, transcendentals=0
        ),
    )(*operands)


def fetch(value, source_team, arc_length):
    cycle, team_count = lax.axis_size("blk"), lax.axis_size("rep")
    pairs = []
    for shard in range(cycle):
        for team in range(team_count):
            to_shard = (shard + team * arc_length) % cycle
            pairs.append((shard * team_count + source_team(team), to_shard * team_count + team))
    return lax.ppermute(value, ("blk", "rep"), pairs)


def next_shard(value):
    cycle = lax.axis_size("blk")
    return lax.ppermute(value, "blk", [(i, (i + 1) % cycle) for i in range(cycle)])


def from_mate(value):
    team_count = lax.axis_size("rep")
    return lax.ppermute(value, "rep", [(team, team ^ 1) for team in range(team_count)])


def from_column(value, distance):
    team_count = lax.axis_size("rep")
    pairs = [((team + 2 * distance) % team_count, team) for team in range(team_count)]
    return lax.ppermute(value, "rep", pairs)


def team_sum(sums):
    columns = len(sums) // 2
    total = None
    for distance in [*range(1, columns), 0]:
        at = (columns - distance) % columns
        share = sums[at] + from_mate(sums[columns + at])
        share = from_column(share, distance) if distance else share
        total = share if total is None else total + share
    return total


def per_device(embeddings, degrees, tile_values, tile_rows, tile_columns, slot_counts):
    arc_length, _, tile_size, _ = tile_values.shape[2:]
    panel_rows = embeddings.shape[0]
    team_count = lax.axis_size("rep")
    spread = (1, 3, 0, 2) if team_count == 4 else tuple(range(team_count))
    degrees = degrees.reshape(panel_rows // tile_size, tile_size)

    panel = fetch(embeddings, lambda team: spread[team], arc_length)
    pieces = [fetch(degrees, lambda team: spread[team], arc_length), panel]
    tiles, own, norm_scale = prepare(degrees, embeddings, tile_values[0, 0])
    info = jnp.concatenate([slot_counts[0, 0][:, None], tile_rows[0, 0], tile_columns[0, 0]], axis=1)

    combined = own
    for layer in range(LAYERS):
        sums = ()
        for arc_slot in range(arc_length):
            sums = arc_step(info[arc_slot], tiles[arc_slot], pieces, sums, layer == 0)
            if arc_slot + 1 < arc_length:
                pieces = [next_shard(piece) for piece in pieces]
        current = team_sum(sums) * norm_scale
        combined = combined + current
        if layer + 1 < LAYERS:
            source = current * norm_scale
            pieces = [
                fetch(source, lambda team, k=k: source_team(team, k, team_count), arc_length)
                for k in range(team_count)
            ]
    return combined / (LAYERS + 1.0)


def solution(mesh):
    in_specs = (
        P(("groups", "blk"), None),
        P(("groups", "blk")),
        P(("groups", "blk"), "rep", None, None, None, None),
        P(("groups", "blk"), "rep", None, None),
        P(("groups", "blk"), "rep", None, None),
        P(("groups", "blk"), "rep", None),
    )
    out_specs = P(("groups", "blk", "rep"), None)
    return jax.shard_map(
        per_device, mesh=mesh, in_specs=in_specs, out_specs=out_specs, check_vma=False
    )
```

```python
import functools

import jax
import jax.numpy as jnp
from jax import lax
from jax.experimental import pallas as pl
from jax.experimental.pallas import tpu as pltpu
from jax.sharding import PartitionSpec as P

LAYERS = 2
VMEM_LIMIT = 16 * 1024 * 1024
VMEM = pl.BlockSpec(memory_space=pltpu.VMEM)
ANY = pl.BlockSpec(memory_space=pl.ANY)


def pair_teams(team_index, column, team_count):
    columns = team_count // 2
    return 2 * lax.rem(team_index // 2 + column, columns) + lax.rem(team_index, 2)


def source_team(team, turn, team_count):
    if team_count == 4:
        return (2 * (team % 2) + team // 2) ^ (0, 2, 1, 3)[turn]
    return (team + turn) % team_count


def norm_columns(degrees):
    return jnp.transpose(lax.rsqrt(degrees.astype(jnp.float32)))


def prepare_kernel(degrees_ref, embeddings_ref, tiles_ref, held_tiles_ref, own_ref, norm_ref, panel_ref, sems):
    share_rows, width = own_ref.shape
    block_count, tile_size = degrees_ref.shape
    team_index = lax.axis_index("rep")
    at = pl.ds(pl.multiple_of(team_index * share_rows, share_rows), share_rows)
    tiles_copy = pltpu.make_async_copy(tiles_ref, held_tiles_ref, sems.at[0])
    own_copy = pltpu.make_async_copy(embeddings_ref.at[at, :], own_ref, sems.at[1])
    tiles_copy.start()
    own_copy.start()
    norms = norm_columns(degrees_ref[...])
    for block in range(block_count):
        panel_ref[block * tile_size : (block + 1) * tile_size, :] = jnp.broadcast_to(
            norms[:, block : block + 1], (tile_size, width)
        )
    norm_ref[...] = panel_ref[at, :]
    own_copy.wait()
    tiles_copy.wait()


def prepare(degrees, embeddings, tile_values):
    panel_rows, width = embeddings.shape
    share = jax.ShapeDtypeStruct((panel_rows // lax.axis_size("rep"), width), jnp.float32)
    return pl.pallas_call(
        prepare_kernel,
        out_shape=[jax.ShapeDtypeStruct(tile_values.shape, tile_values.dtype), share, share],
        in_specs=[VMEM, ANY, ANY],
        out_specs=[VMEM] * 3,
        scratch_shapes=[pltpu.VMEM((panel_rows, width), jnp.float32), pltpu.SemaphoreType.DMA((2,))],
        compiler_params=pltpu.CompilerParams(vmem_limit_bytes=VMEM_LIMIT),
        cost_estimate=pl.CostEstimate(
            flops=panel_rows * width, bytes_accessed=4 * panel_rows * width, transcendentals=0
        ),
    )(degrees, embeddings, tile_values)


def arc_kernel(info_ref, tiles_ref, *refs, team_count, piece_count, scaled, partial_count):
    columns = team_count // 2
    pieces, refs = refs[:piece_count], refs[piece_count:]
    partials, refs = refs[:partial_count], refs[partial_count:]
    outs, (table_ref, split_ref, sums_ref, sem) = refs[:team_count], refs[team_count:]
    team_index = lax.axis_index("rep")
    slot_total, tile_size, _ = tiles_ref.shape
    panel_rows, width = split_ref.shape[0], split_ref.shape[1] // 2
    share_rows = panel_rows // team_count
    block_count = panel_rows // tile_size
    table_copy = pltpu.make_async_copy(info_ref, table_ref, sem)
    table_copy.start()

    def split(value, at):
        high = value.astype(jnp.bfloat16)
        split_ref[at, :width] = high
        split_ref[at, width:] = (value - high.astype(jnp.float32)).astype(jnp.bfloat16)

    if scaled:
        degrees_ref, panel_ref = pieces
        norms = norm_columns(degrees_ref[...])
        for block in range(block_count):
            at = pl.ds(block * tile_size, tile_size)
            split(panel_ref[at, :] * norms[:, block : block + 1], at)
    else:
        for k in range(piece_count):
            owner = source_team(team_index, k, team_count)
            split(pieces[k][...], pl.ds(pl.multiple_of(owner * share_rows, share_rows), share_rows))
    sums_ref[...] = jnp.zeros_like(sums_ref)
    table_copy.wait()
    live_count = table_ref[0]
    for j in range(slot_total):
        source = pl.multiple_of(table_ref[1 + slot_total + j] * tile_size, tile_size)
        product = jnp.dot(
            tiles_ref[j],
            split_ref[pl.ds(source, tile_size), :],
            preferred_element_type=jnp.float32,
        )
        row = jnp.where(j < live_count, table_ref[1 + j], block_count)
        at = pl.ds(pl.multiple_of(row * tile_size, tile_size), tile_size)
        sums_ref[at, :] += product[:, :width] + product[:, width:]

    for parity in range(2):
        for column in range(columns):
            team = pair_teams(team_index, column, team_count)
            team = team if parity == 0 else team ^ 1
            value = sums_ref[pl.ds(pl.multiple_of(team * share_rows, share_rows), share_rows), :]
            at = parity * columns + column
            outs[at][...] = value + partials[at][...] if partials else value


def arc_step(info, tiles, pieces, partials, scaled):
    team_count = lax.axis_size("rep")
    panel_rows = pieces[1].shape[0] if scaled else sum(piece.shape[0] for piece in pieces)
    width = pieces[1].shape[1]
    slot_total, tile_size, _ = tiles.shape
    share = jax.ShapeDtypeStruct((panel_rows // team_count, width), jnp.float32)
    operands = [info, tiles, *pieces, *partials]
    return pl.pallas_call(
        functools.partial(
            arc_kernel,
            team_count=team_count,
            piece_count=len(pieces),
            scaled=scaled,
            partial_count=len(partials),
        ),
        out_shape=[share] * team_count,
        in_specs=[ANY] + [VMEM] * (len(operands) - 1),
        out_specs=[VMEM] * team_count,
        scratch_shapes=[
            pltpu.SMEM(info.shape, info.dtype),
            pltpu.VMEM((panel_rows, 2 * width), jnp.bfloat16),
            pltpu.VMEM((panel_rows + tile_size, width), jnp.float32),
            pltpu.SemaphoreType.DMA,
        ],
        compiler_params=pltpu.CompilerParams(vmem_limit_bytes=VMEM_LIMIT),
        cost_estimate=pl.CostEstimate(
            flops=4 * slot_total * tile_size * tile_size * width, bytes_accessed=8 * panel_rows * width, transcendentals=0
        ),
    )(*operands)


def fetch(value, source_team, arc_length):
    cycle, team_count = lax.axis_size("blk"), lax.axis_size("rep")
    pairs = []
    for shard in range(cycle):
        for team in range(team_count):
            to_shard = (shard + team * arc_length) % cycle
            pairs.append((shard * team_count + source_team(team), to_shard * team_count + team))
    return lax.ppermute(value, ("blk", "rep"), pairs)


def next_shard(value):
    cycle = lax.axis_size("blk")
    return lax.ppermute(value, "blk", [(i, (i + 1) % cycle) for i in range(cycle)])


def from_mate(value):
    team_count = lax.axis_size("rep")
    return lax.ppermute(value, "rep", [(team, team ^ 1) for team in range(team_count)])


def from_column(value, distance):
    team_count = lax.axis_size("rep")
    pairs = [((team + 2 * distance) % team_count, team) for team in range(team_count)]
    return lax.ppermute(value, "rep", pairs)


def team_sum(sums):
    columns = len(sums) // 2
    total = None
    for distance in [*range(1, columns), 0]:
        at = (columns - distance) % columns
        share = sums[at] + from_mate(sums[columns + at])
        share = from_column(share, distance) if distance else share
        total = share if total is None else total + share
    return total


def per_device(embeddings, degrees, tile_values, tile_rows, tile_columns, slot_counts):
    arc_length, _, tile_size, _ = tile_values.shape[2:]
    panel_rows = embeddings.shape[0]
    team_count = lax.axis_size("rep")
    spread = (3, 1, 2, 0) if team_count == 4 else tuple(range(team_count))
    degrees = degrees.reshape(panel_rows // tile_size, tile_size)

    panel = fetch(embeddings, lambda team: spread[team], arc_length)
    pieces = [fetch(degrees, lambda team: spread[team], arc_length), panel]
    tiles, own, norm_scale = prepare(degrees, embeddings, tile_values[0, 0])
    info = jnp.concatenate([slot_counts[0, 0][:, None], tile_rows[0, 0], tile_columns[0, 0]], axis=1)

    combined = own
    for layer in range(LAYERS):
        sums = ()
        for arc_slot in range(arc_length):
            sums = arc_step(info[arc_slot], tiles[arc_slot], pieces, sums, layer == 0)
            if arc_slot + 1 < arc_length:
                pieces = [next_shard(piece) for piece in pieces]
        current = team_sum(sums) * norm_scale
        combined = combined + current
        if layer + 1 < LAYERS:
            source = current * norm_scale
            pieces = [
                fetch(source, lambda team, k=k: source_team(team, k, team_count), arc_length)
                for k in range(team_count)
            ]
    return combined / (LAYERS + 1.0)


def solution(mesh):
    in_specs = (
        P(("groups", "blk"), None),
        P(("groups", "blk")),
        P(("groups", "blk"), "rep", None, None, None, None),
        P(("groups", "blk"), "rep", None, None),
        P(("groups", "blk"), "rep", None, None),
        P(("groups", "blk"), "rep", None),
    )
    out_specs = P(("groups", "blk", "rep"), None)
    return jax.shard_map(
        per_device, mesh=mesh, in_specs=in_specs, out_specs=out_specs, check_vma=False
    )
```

```python
import functools

import jax
import jax.numpy as jnp
from jax import lax
from jax.experimental import pallas as pl
from jax.experimental.pallas import tpu as pltpu
from jax.sharding import PartitionSpec as P

LAYERS = 2
VMEM_LIMIT = 16 * 1024 * 1024
VMEM = pl.BlockSpec(memory_space=pltpu.VMEM)
ANY = pl.BlockSpec(memory_space=pl.ANY)


def pair_teams(team_index, column, team_count):
    columns = team_count // 2
    return 2 * lax.rem(team_index // 2 + column, columns) + lax.rem(team_index, 2)


def source_team(team, turn, team_count):
    if team_count == 4:
        return (2 * (team % 2) + team // 2) ^ (0, 2, 1, 3)[turn]
    return (team + turn) % team_count


def norm_columns(degrees):
    return jnp.transpose(lax.rsqrt(degrees.astype(jnp.float32)))


def prepare_kernel(degrees_ref, embeddings_ref, tiles_ref, held_tiles_ref, own_ref, norm_ref, panel_ref, sems):
    share_rows, width = own_ref.shape
    block_count, tile_size = degrees_ref.shape
    team_index = lax.axis_index("rep")
    at = pl.ds(pl.multiple_of(team_index * share_rows, share_rows), share_rows)
    tiles_copy = pltpu.make_async_copy(tiles_ref, held_tiles_ref, sems.at[0])
    own_copy = pltpu.make_async_copy(embeddings_ref.at[at, :], own_ref, sems.at[1])
    tiles_copy.start()
    own_copy.start()
    norms = norm_columns(degrees_ref[...])
    for block in range(block_count):
        panel_ref[block * tile_size : (block + 1) * tile_size, :] = jnp.broadcast_to(
            norms[:, block : block + 1], (tile_size, width)
        )
    norm_ref[...] = panel_ref[at, :]
    own_copy.wait()
    tiles_copy.wait()


def prepare(degrees, embeddings, tile_values):
    panel_rows, width = embeddings.shape
    share = jax.ShapeDtypeStruct((panel_rows // lax.axis_size("rep"), width), jnp.float32)
    return pl.pallas_call(
        prepare_kernel,
        out_shape=[jax.ShapeDtypeStruct(tile_values.shape, tile_values.dtype), share, share],
        in_specs=[VMEM, ANY, ANY],
        out_specs=[VMEM] * 3,
        scratch_shapes=[pltpu.VMEM((panel_rows, width), jnp.float32), pltpu.SemaphoreType.DMA((2,))],
        compiler_params=pltpu.CompilerParams(vmem_limit_bytes=VMEM_LIMIT),
        cost_estimate=pl.CostEstimate(
            flops=panel_rows * width, bytes_accessed=4 * panel_rows * width, transcendentals=0
        ),
    )(degrees, embeddings, tile_values)


def arc_kernel(info_ref, tiles_ref, *refs, team_count, piece_count, scaled, partial_count):
    columns = team_count // 2
    pieces, refs = refs[:piece_count], refs[piece_count:]
    partials, refs = refs[:partial_count], refs[partial_count:]
    outs, (split_ref, sums_ref) = refs[:team_count], refs[team_count:]
    team_index = lax.axis_index("rep")
    slot_total, tile_size, _ = tiles_ref.shape
    panel_rows, width = split_ref.shape[0], split_ref.shape[1] // 2
    share_rows = panel_rows // team_count
    block_count = panel_rows // tile_size

    def split(value, at):
        high = value.astype(jnp.bfloat16)
        split_ref[at, :width] = high
        split_ref[at, width:] = (value - high.astype(jnp.float32)).astype(jnp.bfloat16)

    if scaled:
        degrees_ref, panel_ref = pieces
        norms = norm_columns(degrees_ref[...])
        for block in range(block_count):
            at = pl.ds(block * tile_size, tile_size)
            split(panel_ref[at, :] * norms[:, block : block + 1], at)
    else:
        for k in range(piece_count):
            owner = source_team(team_index, k, team_count)
            split(pieces[k][...], pl.ds(pl.multiple_of(owner * share_rows, share_rows), share_rows))
    sums_ref[...] = jnp.zeros_like(sums_ref)
    live_count = info_ref[0, 0]
    for j in range(slot_total):
        source = pl.multiple_of(info_ref[1 + slot_total + j, 0] * tile_size, tile_size)
        product = jnp.dot(
            tiles_ref[j],
            split_ref[pl.ds(source, tile_size), :],
            preferred_element_type=jnp.float32,
        )
        row = jnp.where(j < live_count, info_ref[1 + j, 0], block_count)
        at = pl.ds(pl.multiple_of(row * tile_size, tile_size), tile_size)
        sums_ref[at, :] += product[:, :width] + product[:, width:]

    for parity in range(2):
        for column in range(columns):
            team = pair_teams(team_index, column, team_count)
            team = team if parity == 0 else team ^ 1
            value = sums_ref[pl.ds(pl.multiple_of(team * share_rows, share_rows), share_rows), :]
            at = parity * columns + column
            outs[at][...] = value + partials[at][...] if partials else value


def arc_step(info, tiles, pieces, partials, scaled):
    team_count = lax.axis_size("rep")
    panel_rows = pieces[1].shape[0] if scaled else sum(piece.shape[0] for piece in pieces)
    width = pieces[1].shape[1]
    slot_total, tile_size, _ = tiles.shape
    share = jax.ShapeDtypeStruct((panel_rows // team_count, width), jnp.float32)
    operands = [info, tiles, *pieces, *partials]
    return pl.pallas_call(
        functools.partial(
            arc_kernel,
            team_count=team_count,
            piece_count=len(pieces),
            scaled=scaled,
            partial_count=len(partials),
        ),
        out_shape=[share] * team_count,
        in_specs=[VMEM] * len(operands),
        out_specs=[VMEM] * team_count,
        scratch_shapes=[
            pltpu.VMEM((panel_rows, 2 * width), jnp.bfloat16),
            pltpu.VMEM((panel_rows + tile_size, width), jnp.float32),
        ],
        compiler_params=pltpu.CompilerParams(vmem_limit_bytes=VMEM_LIMIT),
        cost_estimate=pl.CostEstimate(
            flops=4 * slot_total * tile_size * tile_size * width, bytes_accessed=8 * panel_rows * width, transcendentals=0
        ),
    )(*operands)


def fetch(value, source_team, arc_length):
    cycle, team_count = lax.axis_size("blk"), lax.axis_size("rep")
    pairs = []
    for shard in range(cycle):
        for team in range(team_count):
            to_shard = (shard + team * arc_length) % cycle
            pairs.append((shard * team_count + source_team(team), to_shard * team_count + team))
    return lax.ppermute(value, ("blk", "rep"), pairs)


def next_shard(value):
    cycle = lax.axis_size("blk")
    return lax.ppermute(value, "blk", [(i, (i + 1) % cycle) for i in range(cycle)])


def from_mate(value):
    team_count = lax.axis_size("rep")
    return lax.ppermute(value, "rep", [(team, team ^ 1) for team in range(team_count)])


def from_column(value, distance):
    team_count = lax.axis_size("rep")
    pairs = [((team + 2 * distance) % team_count, team) for team in range(team_count)]
    return lax.ppermute(value, "rep", pairs)


def team_sum(sums):
    columns = len(sums) // 2
    total = None
    for distance in [*range(1, columns), 0]:
        at = (columns - distance) % columns
        share = sums[at] + from_mate(sums[columns + at])
        share = from_column(share, distance) if distance else share
        total = share if total is None else total + share
    return total


def per_device(embeddings, degrees, tile_values, tile_rows, tile_columns, slot_counts):
    arc_length, _, tile_size, _ = tile_values.shape[2:]
    panel_rows = embeddings.shape[0]
    team_count = lax.axis_size("rep")
    spread = (3, 1, 2, 0) if team_count == 4 else tuple(range(team_count))
    degrees = degrees.reshape(panel_rows // tile_size, tile_size)

    panel = fetch(embeddings, lambda team: spread[team], arc_length)
    pieces = [fetch(degrees, lambda team: spread[team], arc_length), panel]
    tiles, own, norm_scale = prepare(degrees, embeddings, tile_values[0, 0])
    info = jnp.concatenate([slot_counts[0, 0][:, None], tile_rows[0, 0], tile_columns[0, 0]], axis=1)
    info = jnp.broadcast_to(info[:, :, None], (*info.shape, embeddings.shape[1]))

    combined = own
    for layer in range(LAYERS):
        sums = ()
        for arc_slot in range(arc_length):
            sums = arc_step(info[arc_slot], tiles[arc_slot], pieces, sums, layer == 0)
            if arc_slot + 1 < arc_length:
                pieces = [next_shard(piece) for piece in pieces]
        current = team_sum(sums) * norm_scale
        combined = combined + current
        if layer + 1 < LAYERS:
            source = current * norm_scale
            pieces = [
                fetch(source, lambda team, k=k: source_team(team, k, team_count), arc_length)
                for k in range(team_count)
            ]
    return combined / (LAYERS + 1.0)


def solution(mesh):
    in_specs = (
        P(("groups", "blk"), None),
        P(("groups", "blk")),
        P(("groups", "blk"), "rep", None, None, None, None),
        P(("groups", "blk"), "rep", None, None),
        P(("groups", "blk"), "rep", None, None),
        P(("groups", "blk"), "rep", None),
    )
    out_specs = P(("groups", "blk", "rep"), None)
    return jax.shard_map(
        per_device, mesh=mesh, in_specs=in_specs, out_specs=out_specs, check_vma=False
    )
```

```python
import functools

import jax
import jax.numpy as jnp
from jax import lax
from jax.experimental import pallas as pl
from jax.experimental.pallas import tpu as pltpu
from jax.sharding import PartitionSpec as P

LAYERS = 2
VMEM_LIMIT = 16 * 1024 * 1024
VMEM = pl.BlockSpec(memory_space=pltpu.VMEM)
ANY = pl.BlockSpec(memory_space=pl.ANY)


def pair_teams(team_index, column, team_count):
    columns = team_count // 2
    return 2 * lax.rem(team_index // 2 + column, columns) + lax.rem(team_index, 2)


def source_team(team, turn, team_count):
    if team_count == 4:
        return (3 * (team % 2)) ^ (team // 2) ^ turn
    return (team + turn) % team_count


def norm_columns(degrees):
    return jnp.transpose(lax.rsqrt(degrees.astype(jnp.float32)))


def prepare_kernel(
    degrees_ref, embeddings_ref, tiles_ref, after_ref, held_tiles_ref, own_ref, norm_ref, panel_ref, sems
):
    del after_ref
    share_rows, width = own_ref.shape
    block_count, tile_size = degrees_ref.shape
    team_index = lax.axis_index("rep")
    at = pl.ds(pl.multiple_of(team_index * share_rows, share_rows), share_rows)
    tiles_copy = pltpu.make_async_copy(tiles_ref, held_tiles_ref, sems.at[0])
    own_copy = pltpu.make_async_copy(embeddings_ref.at[at, :], own_ref, sems.at[1])
    tiles_copy.start()
    own_copy.start()
    norms = norm_columns(degrees_ref[...])
    for block in range(block_count):
        panel_ref[block * tile_size : (block + 1) * tile_size, :] = jnp.broadcast_to(
            norms[:, block : block + 1], (tile_size, width)
        )
    norm_ref[...] = panel_ref[at, :]
    own_copy.wait()
    tiles_copy.wait()


def prepare(degrees, embeddings, tile_values, after):
    panel_rows, width = embeddings.shape
    share = jax.ShapeDtypeStruct((panel_rows // lax.axis_size("rep"), width), jnp.float32)
    return pl.pallas_call(
        prepare_kernel,
        out_shape=[jax.ShapeDtypeStruct(tile_values.shape, tile_values.dtype), share, share],
        in_specs=[VMEM, ANY, ANY, ANY],
        out_specs=[VMEM] * 3,
        scratch_shapes=[pltpu.VMEM((panel_rows, width), jnp.float32), pltpu.SemaphoreType.DMA((2,))],
        compiler_params=pltpu.CompilerParams(vmem_limit_bytes=VMEM_LIMIT),
        cost_estimate=pl.CostEstimate(
            flops=panel_rows * width, bytes_accessed=4 * panel_rows * width, transcendentals=0
        ),
    )(degrees, embeddings, tile_values, after)


def arc_kernel(info_ref, tiles_ref, *refs, team_count, piece_count, scaled, partial_count):
    columns = team_count // 2
    pieces, refs = refs[:piece_count], refs[piece_count:]
    partials, refs = refs[:partial_count], refs[partial_count:]
    outs, (split_ref, sums_ref) = refs[:team_count], refs[team_count:]
    team_index = lax.axis_index("rep")
    slot_total, tile_size, _ = tiles_ref.shape
    panel_rows, width = split_ref.shape[0], split_ref.shape[1] // 2
    share_rows = panel_rows // team_count
    block_count = panel_rows // tile_size

    def split(value, at):
        high = value.astype(jnp.bfloat16)
        split_ref[at, :width] = high
        split_ref[at, width:] = (value - high.astype(jnp.float32)).astype(jnp.bfloat16)

    if scaled:
        degrees_ref, panel_ref = pieces
        norms = norm_columns(degrees_ref[...])
        for block in range(block_count):
            at = pl.ds(block * tile_size, tile_size)
            split(panel_ref[at, :] * norms[:, block : block + 1], at)
    else:
        for k in range(piece_count):
            owner = source_team(team_index, k, team_count)
            split(pieces[k][...], pl.ds(pl.multiple_of(owner * share_rows, share_rows), share_rows))
    sums_ref[...] = jnp.zeros_like(sums_ref)
    live_count = info_ref[0, 0]
    for j in range(slot_total):
        source = pl.multiple_of(info_ref[1 + slot_total + j, 0] * tile_size, tile_size)
        product = jnp.dot(
            tiles_ref[j],
            split_ref[pl.ds(source, tile_size), :],
            preferred_element_type=jnp.float32,
        )
        row = jnp.where(j < live_count, info_ref[1 + j, 0], block_count)
        at = pl.ds(pl.multiple_of(row * tile_size, tile_size), tile_size)
        sums_ref[at, :] += product[:, :width] + product[:, width:]

    for parity in range(2):
        for column in range(columns):
            team = pair_teams(team_index, column, team_count)
            team = team if parity == 0 else team ^ 1
            value = sums_ref[pl.ds(pl.multiple_of(team * share_rows, share_rows), share_rows), :]
            at = parity * columns + column
            outs[at][...] = value + partials[at][...] if partials else value


def arc_step(info, tiles, pieces, partials, scaled):
    team_count = lax.axis_size("rep")
    panel_rows = pieces[1].shape[0] if scaled else sum(piece.shape[0] for piece in pieces)
    width = pieces[1].shape[1]
    slot_total, tile_size, _ = tiles.shape
    share = jax.ShapeDtypeStruct((panel_rows // team_count, width), jnp.float32)
    operands = [info, tiles, *pieces, *partials]
    return pl.pallas_call(
        functools.partial(
            arc_kernel,
            team_count=team_count,
            piece_count=len(pieces),
            scaled=scaled,
            partial_count=len(partials),
        ),
        out_shape=[share] * team_count,
        in_specs=[VMEM] * len(operands),
        out_specs=[VMEM] * team_count,
        scratch_shapes=[
            pltpu.VMEM((panel_rows, 2 * width), jnp.bfloat16),
            pltpu.VMEM((panel_rows + tile_size, width), jnp.float32),
        ],
        compiler_params=pltpu.CompilerParams(vmem_limit_bytes=VMEM_LIMIT),
        cost_estimate=pl.CostEstimate(
            flops=4 * slot_total * tile_size * tile_size * width, bytes_accessed=8 * panel_rows * width, transcendentals=0
        ),
    )(*operands)


def fetch(value, source_team, arc_length):
    cycle, team_count = lax.axis_size("blk"), lax.axis_size("rep")
    pairs = []
    for shard in range(cycle):
        for team in range(team_count):
            to_shard = (shard + team * arc_length) % cycle
            pairs.append((shard * team_count + source_team(team), to_shard * team_count + team))
    return lax.ppermute(value, ("blk", "rep"), pairs)


def next_shard(value):
    cycle = lax.axis_size("blk")
    return lax.ppermute(value, "blk", [(i, (i + 1) % cycle) for i in range(cycle)])


def from_mate(value):
    team_count = lax.axis_size("rep")
    return lax.ppermute(value, "rep", [(team, team ^ 1) for team in range(team_count)])


def from_column(value, distance):
    team_count = lax.axis_size("rep")
    pairs = [((team + 2 * distance) % team_count, team) for team in range(team_count)]
    return lax.ppermute(value, "rep", pairs)


def team_sum(sums):
    columns = len(sums) // 2
    total = None
    for distance in [*range(1, columns), 0]:
        at = (columns - distance) % columns
        share = sums[at] + from_mate(sums[columns + at])
        share = from_column(share, distance) if distance else share
        total = share if total is None else total + share
    return total


def per_device(embeddings, degrees, tile_values, tile_rows, tile_columns, slot_counts):
    arc_length, _, tile_size, _ = tile_values.shape[2:]
    panel_rows = embeddings.shape[0]
    team_count = lax.axis_size("rep")
    spread = (3, 1, 2, 0) if team_count == 4 else tuple(range(team_count))
    degrees = degrees.reshape(panel_rows // tile_size, tile_size)

    panel = fetch(embeddings, lambda team: spread[team], arc_length)
    pieces = [fetch(degrees, lambda team: spread[team], arc_length), panel]
    info = jnp.concatenate([slot_counts[0, 0][:, None], tile_rows[0, 0], tile_columns[0, 0]], axis=1)
    info = jnp.broadcast_to(info[:, :, None], (*info.shape, embeddings.shape[1]))
    tiles, own, norm_scale = prepare(degrees, embeddings, tile_values[0, 0], info)

    combined = own
    for layer in range(LAYERS):
        sums = ()
        for arc_slot in range(arc_length):
            sums = arc_step(info[arc_slot], tiles[arc_slot], pieces, sums, layer == 0)
            if arc_slot + 1 < arc_length:
                pieces = [next_shard(piece) for piece in pieces]
        current = team_sum(sums) * norm_scale
        combined = combined + current
        if layer + 1 < LAYERS:
            source = current * norm_scale
            pieces = [
                fetch(source, lambda team, k=k: source_team(team, k, team_count), arc_length)
                for k in range(team_count)
            ]
    return combined / (LAYERS + 1.0)


def solution(mesh):
    in_specs = (
        P(("groups", "blk"), None),
        P(("groups", "blk")),
        P(("groups", "blk"), "rep", None, None, None, None),
        P(("groups", "blk"), "rep", None, None),
        P(("groups", "blk"), "rep", None, None),
        P(("groups", "blk"), "rep", None),
    )
    out_specs = P(("groups", "blk", "rep"), None)
    return jax.shard_map(
        per_device, mesh=mesh, in_specs=in_specs, out_specs=out_specs, check_vma=False
    )
```

```python
import functools

import jax
import jax.numpy as jnp
from jax import lax
from jax.experimental import pallas as pl
from jax.experimental.pallas import tpu as pltpu
from jax.sharding import PartitionSpec as P

LAYERS = 2
VMEM_LIMIT = 16 * 1024 * 1024
VMEM = pl.BlockSpec(memory_space=pltpu.VMEM)
ANY = pl.BlockSpec(memory_space=pl.ANY)


def pair_teams(team_index, column, team_count):
    columns = team_count // 2
    return 2 * lax.rem(team_index // 2 + column, columns) + lax.rem(team_index, 2)


def source_team(team, turn, team_count):
    if team_count == 4:
        return (3 * (team % 2)) ^ (team // 2) ^ (2, 1, 0, 3)[turn]
    return (team + turn) % team_count


def norm_columns(degrees):
    return jnp.transpose(lax.rsqrt(degrees.astype(jnp.float32)))


def prepare_kernel(
    degrees_ref, embeddings_ref, tiles_ref, after_ref, held_tiles_ref, own_ref, norm_ref, panel_ref, sems
):
    del after_ref
    share_rows, width = own_ref.shape
    block_count, tile_size = degrees_ref.shape
    team_index = lax.axis_index("rep")
    at = pl.ds(pl.multiple_of(team_index * share_rows, share_rows), share_rows)
    tiles_copy = pltpu.make_async_copy(tiles_ref, held_tiles_ref, sems.at[0])
    own_copy = pltpu.make_async_copy(embeddings_ref.at[at, :], own_ref, sems.at[1])
    tiles_copy.start()
    own_copy.start()
    norms = norm_columns(degrees_ref[...])
    for block in range(block_count):
        panel_ref[block * tile_size : (block + 1) * tile_size, :] = jnp.broadcast_to(
            norms[:, block : block + 1], (tile_size, width)
        )
    norm_ref[...] = panel_ref[at, :]
    own_copy.wait()
    tiles_copy.wait()


def prepare(degrees, embeddings, tile_values, after):
    panel_rows, width = embeddings.shape
    share = jax.ShapeDtypeStruct((panel_rows // lax.axis_size("rep"), width), jnp.float32)
    return pl.pallas_call(
        prepare_kernel,
        out_shape=[jax.ShapeDtypeStruct(tile_values.shape, tile_values.dtype), share, share],
        in_specs=[VMEM, ANY, ANY, ANY],
        out_specs=[VMEM] * 3,
        scratch_shapes=[pltpu.VMEM((panel_rows, width), jnp.float32), pltpu.SemaphoreType.DMA((2,))],
        compiler_params=pltpu.CompilerParams(vmem_limit_bytes=VMEM_LIMIT),
        cost_estimate=pl.CostEstimate(
            flops=panel_rows * width, bytes_accessed=4 * panel_rows * width, transcendentals=0
        ),
    )(degrees, embeddings, tile_values, after)


def arc_kernel(info_ref, tiles_ref, *refs, team_count, piece_count, scaled, partial_count):
    columns = team_count // 2
    pieces, refs = refs[:piece_count], refs[piece_count:]
    partials, refs = refs[:partial_count], refs[partial_count:]
    outs, (split_ref, sums_ref) = refs[:team_count], refs[team_count:]
    team_index = lax.axis_index("rep")
    slot_total, tile_size, _ = tiles_ref.shape
    panel_rows, width = split_ref.shape[0], split_ref.shape[1] // 2
    share_rows = panel_rows // team_count
    block_count = panel_rows // tile_size

    def split(value, at):
        high = value.astype(jnp.bfloat16)
        split_ref[at, :width] = high
        split_ref[at, width:] = (value - high.astype(jnp.float32)).astype(jnp.bfloat16)

    if scaled:
        degrees_ref, panel_ref = pieces
        norms = norm_columns(degrees_ref[...])
        for block in range(block_count):
            at = pl.ds(block * tile_size, tile_size)
            split(panel_ref[at, :] * norms[:, block : block + 1], at)
    else:
        for k in range(piece_count):
            owner = source_team(team_index, k, team_count)
            split(pieces[k][...], pl.ds(pl.multiple_of(owner * share_rows, share_rows), share_rows))
    sums_ref[...] = jnp.zeros_like(sums_ref)
    live_count = info_ref[0, 0]
    for j in range(slot_total):
        source = pl.multiple_of(info_ref[1 + slot_total + j, 0] * tile_size, tile_size)
        product = jnp.dot(
            tiles_ref[j],
            split_ref[pl.ds(source, tile_size), :],
            preferred_element_type=jnp.float32,
        )
        row = jnp.where(j < live_count, info_ref[1 + j, 0], block_count)
        at = pl.ds(pl.multiple_of(row * tile_size, tile_size), tile_size)
        sums_ref[at, :] += product[:, :width] + product[:, width:]

    for parity in range(2):
        for column in range(columns):
            team = pair_teams(team_index, column, team_count)
            team = team if parity == 0 else team ^ 1
            value = sums_ref[pl.ds(pl.multiple_of(team * share_rows, share_rows), share_rows), :]
            at = parity * columns + column
            outs[at][...] = value + partials[at][...] if partials else value


def arc_step(info, tiles, pieces, partials, scaled):
    team_count = lax.axis_size("rep")
    panel_rows = pieces[1].shape[0] if scaled else sum(piece.shape[0] for piece in pieces)
    width = pieces[1].shape[1]
    slot_total, tile_size, _ = tiles.shape
    share = jax.ShapeDtypeStruct((panel_rows // team_count, width), jnp.float32)
    operands = [info, tiles, *pieces, *partials]
    return pl.pallas_call(
        functools.partial(
            arc_kernel,
            team_count=team_count,
            piece_count=len(pieces),
            scaled=scaled,
            partial_count=len(partials),
        ),
        out_shape=[share] * team_count,
        in_specs=[VMEM] * len(operands),
        out_specs=[VMEM] * team_count,
        scratch_shapes=[
            pltpu.VMEM((panel_rows, 2 * width), jnp.bfloat16),
            pltpu.VMEM((panel_rows + tile_size, width), jnp.float32),
        ],
        compiler_params=pltpu.CompilerParams(vmem_limit_bytes=VMEM_LIMIT),
        cost_estimate=pl.CostEstimate(
            flops=4 * slot_total * tile_size * tile_size * width, bytes_accessed=8 * panel_rows * width, transcendentals=0
        ),
    )(*operands)


def fetch(value, source_team, arc_length):
    cycle, team_count = lax.axis_size("blk"), lax.axis_size("rep")
    pairs = []
    for shard in range(cycle):
        for team in range(team_count):
            to_shard = (shard + team * arc_length) % cycle
            pairs.append((shard * team_count + source_team(team), to_shard * team_count + team))
    return lax.ppermute(value, ("blk", "rep"), pairs)


def next_shard(value):
    cycle = lax.axis_size("blk")
    return lax.ppermute(value, "blk", [(i, (i + 1) % cycle) for i in range(cycle)])


def from_mate(value):
    team_count = lax.axis_size("rep")
    return lax.ppermute(value, "rep", [(team, team ^ 1) for team in range(team_count)])


def from_column(value, distance):
    team_count = lax.axis_size("rep")
    pairs = [((team + 2 * distance) % team_count, team) for team in range(team_count)]
    return lax.ppermute(value, "rep", pairs)


def team_sum(sums):
    columns = len(sums) // 2
    total = None
    for distance in [*range(1, columns), 0]:
        at = (columns - distance) % columns
        share = sums[at] + from_mate(sums[columns + at])
        share = from_column(share, distance) if distance else share
        total = share if total is None else total + share
    return total


def per_device(embeddings, degrees, tile_values, tile_rows, tile_columns, slot_counts):
    arc_length, _, tile_size, _ = tile_values.shape[2:]
    panel_rows = embeddings.shape[0]
    team_count = lax.axis_size("rep")
    spread = (3, 1, 2, 0) if team_count == 4 else tuple(range(team_count))
    degrees = degrees.reshape(panel_rows // tile_size, tile_size)

    panel = fetch(embeddings, lambda team: spread[team], arc_length)
    pieces = [fetch(degrees, lambda team: spread[team], arc_length), panel]
    info = jnp.concatenate([slot_counts[0, 0][:, None], tile_rows[0, 0], tile_columns[0, 0]], axis=1)
    info = jnp.broadcast_to(info[:, :, None], (*info.shape, embeddings.shape[1]))
    tiles, own, norm_scale = prepare(degrees, embeddings, tile_values[0, 0], info)

    combined = own
    for layer in range(LAYERS):
        sums = ()
        for arc_slot in range(arc_length):
            sums = arc_step(info[arc_slot], tiles[arc_slot], pieces, sums, layer == 0)
            if arc_slot + 1 < arc_length:
                pieces = [next_shard(piece) for piece in pieces]
        current = team_sum(sums) * norm_scale
        combined = combined + current
        if layer + 1 < LAYERS:
            source = current * norm_scale
            pieces = [
                fetch(source, lambda team, k=k: source_team(team, k, team_count), arc_length)
                for k in range(team_count)
            ]
    return combined / (LAYERS + 1.0)


def solution(mesh):
    in_specs = (
        P(("groups", "blk"), None),
        P(("groups", "blk")),
        P(("groups", "blk"), "rep", None, None, None, None),
        P(("groups", "blk"), "rep", None, None),
        P(("groups", "blk"), "rep", None, None),
        P(("groups", "blk"), "rep", None),
    )
    out_specs = P(("groups", "blk", "rep"), None)
    return jax.shard_map(
        per_device, mesh=mesh, in_specs=in_specs, out_specs=out_specs, check_vma=False
    )
```

```python
import functools

import jax
import jax.numpy as jnp
from jax import lax
from jax.experimental import pallas as pl
from jax.experimental.pallas import tpu as pltpu
from jax.sharding import PartitionSpec as P

LAYERS = 2
VMEM_LIMIT = 16 * 1024 * 1024
VMEM = pl.BlockSpec(memory_space=pltpu.VMEM)
ANY = pl.BlockSpec(memory_space=pl.ANY)


def pair_teams(team_index, column, team_count):
    columns = team_count // 2
    return 2 * lax.rem(team_index // 2 + column, columns) + lax.rem(team_index, 2)


def source_team(team, turn, team_count):
    if team_count == 4:
        return (2 * (team % 2) + team // 2) ^ (2, 0, 1, 3)[turn]
    return (team + turn) % team_count


def norm_columns(degrees):
    return jnp.transpose(lax.rsqrt(degrees.astype(jnp.float32)))


def prepare_kernel(
    degrees_ref, embeddings_ref, tiles_ref, after_ref, held_tiles_ref, own_ref, norm_ref, panel_ref, sems
):
    del after_ref
    share_rows, width = own_ref.shape
    block_count, tile_size = degrees_ref.shape
    team_index = lax.axis_index("rep")
    at = pl.ds(pl.multiple_of(team_index * share_rows, share_rows), share_rows)
    tiles_copy = pltpu.make_async_copy(tiles_ref, held_tiles_ref, sems.at[0])
    own_copy = pltpu.make_async_copy(embeddings_ref.at[at, :], own_ref, sems.at[1])
    tiles_copy.start()
    own_copy.start()
    norms = norm_columns(degrees_ref[...])
    for block in range(block_count):
        panel_ref[block * tile_size : (block + 1) * tile_size, :] = jnp.broadcast_to(
            norms[:, block : block + 1], (tile_size, width)
        )
    norm_ref[...] = panel_ref[at, :]
    own_copy.wait()
    tiles_copy.wait()


def prepare(degrees, embeddings, tile_values, after):
    panel_rows, width = embeddings.shape
    share = jax.ShapeDtypeStruct((panel_rows // lax.axis_size("rep"), width), jnp.float32)
    return pl.pallas_call(
        prepare_kernel,
        out_shape=[jax.ShapeDtypeStruct(tile_values.shape, tile_values.dtype), share, share],
        in_specs=[VMEM, ANY, ANY, ANY],
        out_specs=[VMEM] * 3,
        scratch_shapes=[pltpu.VMEM((panel_rows, width), jnp.float32), pltpu.SemaphoreType.DMA((2,))],
        compiler_params=pltpu.CompilerParams(vmem_limit_bytes=VMEM_LIMIT),
        cost_estimate=pl.CostEstimate(
            flops=panel_rows * width, bytes_accessed=4 * panel_rows * width, transcendentals=0
        ),
    )(degrees, embeddings, tile_values, after)


def arc_kernel(info_ref, tiles_ref, *refs, team_count, piece_count, scaled, partial_count):
    columns = team_count // 2
    pieces, refs = refs[:piece_count], refs[piece_count:]
    partials, refs = refs[:partial_count], refs[partial_count:]
    outs, (split_ref, sums_ref) = refs[:team_count], refs[team_count:]
    team_index = lax.axis_index("rep")
    slot_total, tile_size, _ = tiles_ref.shape
    panel_rows, width = split_ref.shape[0], split_ref.shape[1] // 2
    share_rows = panel_rows // team_count
    block_count = panel_rows // tile_size

    def split(value, at):
        high = value.astype(jnp.bfloat16)
        split_ref[at, :width] = high
        split_ref[at, width:] = (value - high.astype(jnp.float32)).astype(jnp.bfloat16)

    if scaled:
        degrees_ref, panel_ref = pieces
        norms = norm_columns(degrees_ref[...])
        for block in range(block_count):
            at = pl.ds(block * tile_size, tile_size)
            split(panel_ref[at, :] * norms[:, block : block + 1], at)
    else:
        for k in range(piece_count):
            owner = source_team(team_index, k, team_count)
            split(pieces[k][...], pl.ds(pl.multiple_of(owner * share_rows, share_rows), share_rows))
    sums_ref[...] = jnp.zeros_like(sums_ref)
    live_count = info_ref[0, 0]
    for j in range(slot_total):
        source = pl.multiple_of(info_ref[1 + slot_total + j, 0] * tile_size, tile_size)
        product = jnp.dot(
            tiles_ref[j],
            split_ref[pl.ds(source, tile_size), :],
            preferred_element_type=jnp.float32,
        )
        row = jnp.where(j < live_count, info_ref[1 + j, 0], block_count)
        at = pl.ds(pl.multiple_of(row * tile_size, tile_size), tile_size)
        sums_ref[at, :] += product[:, :width] + product[:, width:]

    for parity in range(2):
        for column in range(columns):
            team = pair_teams(team_index, column, team_count)
            team = team if parity == 0 else team ^ 1
            value = sums_ref[pl.ds(pl.multiple_of(team * share_rows, share_rows), share_rows), :]
            at = parity * columns + column
            outs[at][...] = value + partials[at][...] if partials else value


def arc_step(info, tiles, pieces, partials, scaled):
    team_count = lax.axis_size("rep")
    panel_rows = pieces[1].shape[0] if scaled else sum(piece.shape[0] for piece in pieces)
    width = pieces[1].shape[1]
    slot_total, tile_size, _ = tiles.shape
    share = jax.ShapeDtypeStruct((panel_rows // team_count, width), jnp.float32)
    operands = [info, tiles, *pieces, *partials]
    return pl.pallas_call(
        functools.partial(
            arc_kernel,
            team_count=team_count,
            piece_count=len(pieces),
            scaled=scaled,
            partial_count=len(partials),
        ),
        out_shape=[share] * team_count,
        in_specs=[VMEM] * len(operands),
        out_specs=[VMEM] * team_count,
        scratch_shapes=[
            pltpu.VMEM((panel_rows, 2 * width), jnp.bfloat16),
            pltpu.VMEM((panel_rows + tile_size, width), jnp.float32),
        ],
        compiler_params=pltpu.CompilerParams(vmem_limit_bytes=VMEM_LIMIT),
        cost_estimate=pl.CostEstimate(
            flops=4 * slot_total * tile_size * tile_size * width, bytes_accessed=8 * panel_rows * width, transcendentals=0
        ),
    )(*operands)


def hold_kernel(value_ref, after_ref, out_ref):
    del value_ref, after_ref, out_ref


def hold(value, after):
    return pl.pallas_call(
        hold_kernel,
        out_shape=jax.ShapeDtypeStruct(value.shape, value.dtype),
        in_specs=[ANY, ANY],
        out_specs=ANY,
        input_output_aliases={0: 0},
        compiler_params=pltpu.CompilerParams(vmem_limit_bytes=VMEM_LIMIT),
    )(value, after)


def fetch(value, source_team, arc_length):
    cycle, team_count = lax.axis_size("blk"), lax.axis_size("rep")
    pairs = []
    for shard in range(cycle):
        for team in range(team_count):
            to_shard = (shard + team * arc_length) % cycle
            pairs.append((shard * team_count + source_team(team), to_shard * team_count + team))
    return lax.ppermute(value, ("blk", "rep"), pairs)


def next_shard(value):
    cycle = lax.axis_size("blk")
    return lax.ppermute(value, "blk", [(i, (i + 1) % cycle) for i in range(cycle)])


def from_mate(value):
    team_count = lax.axis_size("rep")
    return lax.ppermute(value, "rep", [(team, team ^ 1) for team in range(team_count)])


def from_column(value, distance):
    team_count = lax.axis_size("rep")
    pairs = [((team + 2 * distance) % team_count, team) for team in range(team_count)]
    return lax.ppermute(value, "rep", pairs)


def team_sum(sums):
    columns = len(sums) // 2
    own, give = sums[0], sums[columns]
    others = []
    for distance in range(1, columns):
        at = columns - distance
        share = sums[at] + from_mate(sums[columns + at])
        give = hold(give, share)
        others.append(from_column(share, distance))
    total = own + from_mate(give)
    for other in others:
        total = total + other
    return total


def per_device(embeddings, degrees, tile_values, tile_rows, tile_columns, slot_counts):
    arc_length, _, tile_size, _ = tile_values.shape[2:]
    panel_rows = embeddings.shape[0]
    team_count = lax.axis_size("rep")
    spread = (3, 1, 2, 0) if team_count == 4 else tuple(range(team_count))
    degrees = degrees.reshape(panel_rows // tile_size, tile_size)

    panel = fetch(embeddings, lambda team: spread[team], arc_length)
    pieces = [fetch(degrees, lambda team: spread[team], arc_length), panel]
    info = jnp.concatenate([slot_counts[0, 0][:, None], tile_rows[0, 0], tile_columns[0, 0]], axis=1)
    info = jnp.broadcast_to(info[:, :, None], (*info.shape, embeddings.shape[1]))
    info = [info[at] for at in range(arc_length)]
    tiles, own, norm_scale = prepare(degrees, embeddings, tile_values[0, 0], info[0])

    combined = own
    for layer in range(LAYERS):
        sums = ()
        for arc_slot in range(arc_length):
            sums = arc_step(info[arc_slot], tiles[arc_slot], pieces, sums, layer == 0)
            if arc_slot + 1 < arc_length:
                pieces = [next_shard(piece) for piece in pieces]
        current = team_sum(sums) * norm_scale
        combined = combined + current
        if layer + 1 < LAYERS:
            source = current * norm_scale
            pieces = [
                fetch(source, lambda team, k=k: source_team(team, k, team_count), arc_length)
                for k in range(team_count)
            ]
    return combined / (LAYERS + 1.0)


def solution(mesh):
    in_specs = (
        P(("groups", "blk"), None),
        P(("groups", "blk")),
        P(("groups", "blk"), "rep", None, None, None, None),
        P(("groups", "blk"), "rep", None, None),
        P(("groups", "blk"), "rep", None, None),
        P(("groups", "blk"), "rep", None),
    )
    out_specs = P(("groups", "blk", "rep"), None)
    return jax.shard_map(
        per_device, mesh=mesh, in_specs=in_specs, out_specs=out_specs, check_vma=False
    )
```

```python
import functools

import jax
import jax.numpy as jnp
from jax import lax
from jax.experimental import pallas as pl
from jax.experimental.pallas import tpu as pltpu
from jax.sharding import PartitionSpec as P

LAYERS = 2
PARTS = 2
VMEM_LIMIT = 16 * 1024 * 1024
VMEM = pl.BlockSpec(memory_space=pltpu.VMEM)
ANY = pl.BlockSpec(memory_space=pl.ANY)


def pair_teams(team_index, column, team_count):
    columns = team_count // 2
    return 2 * lax.rem(team_index // 2 + column, columns) + lax.rem(team_index, 2)


def source_team(team, turn, team_count):
    if team_count == 4:
        return (2 * ((team + 1) % 2) + team // 2) ^ (3 * turn)
    return (team + 2 * turn) % team_count


def lower_lanes(shape):
    return lax.broadcasted_iota(jnp.int32, shape, 1) < shape[1] // 2


def swap_lanes(value):
    return pltpu.roll(value, value.shape[1] // 2, 1)


def lane_join(lower, upper):
    return jnp.where(lower_lanes(lower.shape), lower, upper)


def norm_columns(degrees):
    return jnp.transpose(lax.rsqrt(degrees.astype(jnp.float32)))


def prepare_kernel(
    degrees_ref, embeddings_ref, tiles_ref, after_ref, held_tiles_ref, own_ref, norm_ref, panel_ref, sems
):
    del after_ref
    share_rows, width = own_ref.shape
    half = share_rows // 2
    block_count, tile_size = degrees_ref.shape
    start = pl.multiple_of(lax.axis_index("rep") * share_rows, share_rows)
    tiles_copy = pltpu.make_async_copy(tiles_ref, held_tiles_ref, sems.at[0])
    own_copy = pltpu.make_async_copy(embeddings_ref.at[pl.ds(start, share_rows), :], own_ref, sems.at[1])
    tiles_copy.start()
    own_copy.start()
    norms = norm_columns(degrees_ref[...])
    for block in range(block_count):
        panel_ref[block * tile_size : (block + 1) * tile_size, :] = jnp.broadcast_to(
            norms[:, block : block + 1], (tile_size, width)
        )
    top = panel_ref[pl.ds(start, half), :]
    bottom = panel_ref[pl.ds(pl.multiple_of(start + half, half), half), :]
    norm_ref[...] = lane_join(top, bottom)
    own_copy.wait()
    tiles_copy.wait()


def prepare(degrees, embeddings, tile_values, after):
    panel_rows, width = embeddings.shape
    share_rows = panel_rows // lax.axis_size("rep")
    return pl.pallas_call(
        prepare_kernel,
        out_shape=[
            jax.ShapeDtypeStruct(tile_values.shape, tile_values.dtype),
            jax.ShapeDtypeStruct((share_rows, width), jnp.float32),
            jax.ShapeDtypeStruct((share_rows // 2, width), jnp.float32),
        ],
        in_specs=[VMEM, ANY, ANY, ANY],
        out_specs=[VMEM] * 3,
        scratch_shapes=[pltpu.VMEM((panel_rows, width), jnp.float32), pltpu.SemaphoreType.DMA((2,))],
        compiler_params=pltpu.CompilerParams(vmem_limit_bytes=VMEM_LIMIT),
        cost_estimate=pl.CostEstimate(
            flops=panel_rows * width, bytes_accessed=4 * panel_rows * width, transcendentals=0
        ),
    )(degrees, embeddings, tile_values, after)


def multiply_slots(info_ref, tiles_ref, split_ref, sums_ref, fold):
    slot_total, tile_size, _ = tiles_ref.shape
    width = sums_ref.shape[1]
    block_count = sums_ref.shape[0] // tile_size - 1
    live_count = info_ref[0, 0]
    for j in range(slot_total):
        source = pl.multiple_of(info_ref[1 + slot_total + j, 0] * tile_size, tile_size)
        product = jnp.dot(
            tiles_ref[j],
            split_ref[pl.ds(source, tile_size), :],
            preferred_element_type=jnp.float32,
        )
        row = jnp.where(j < live_count, info_ref[1 + j, 0], block_count)
        at = pl.ds(pl.multiple_of(row * tile_size, tile_size), tile_size)
        sums_ref[at, :] += product[:, :width] + product[:, width:] if fold else product


def write_shares(sums_ref, outs, partials, join):
    team_count = lax.axis_size("rep")
    team_index = lax.axis_index("rep")
    half = outs[0].shape[0] // (team_count // 2)
    for parity in range(2):
        for column in range(team_count // 2):
            team = pair_teams(team_index, column, team_count)
            team = team if parity == 0 else team ^ 1
            top = sums_ref[pl.ds(pl.multiple_of(team * 2 * half, half), half), :]
            bottom = sums_ref[pl.ds(pl.multiple_of(team * 2 * half + half, half), half), :]
            to = pl.ds(column * half, half)
            for part, value in enumerate(join(top, bottom)):
                at = 2 * part + parity
                outs[at][to, :] = value + partials[at][to, :] if partials else value


def panel_kernel(info_ref, tiles_ref, degrees_ref, panel_ref, *refs, partial_count):
    partials, refs = refs[:partial_count], refs[partial_count:]
    *outs, split_ref, sums_ref = refs
    panel_rows, width = panel_ref.shape
    block_count, tile_size = degrees_ref.shape
    norms = norm_columns(degrees_ref[...])
    for block in range(block_count):
        at = pl.ds(block * tile_size, tile_size)
        value = panel_ref[at, :] * norms[:, block : block + 1]
        high = value.astype(jnp.bfloat16)
        split_ref[at, :width] = high
        split_ref[at, width:] = (value - high.astype(jnp.float32)).astype(jnp.bfloat16)
    sums_ref[...] = jnp.zeros_like(sums_ref)
    multiply_slots(info_ref, tiles_ref, split_ref, sums_ref, True)
    write_shares(
        sums_ref,
        outs,
        partials,
        lambda top, bottom: (lane_join(top, swap_lanes(bottom)), lane_join(swap_lanes(top), bottom)),
    )


def part_kernel(info_ref, tiles_ref, *refs, team_count, partial_count):
    columns = team_count // 2
    pieces, refs = refs[:columns], refs[columns:]
    partials, refs = refs[:partial_count], refs[partial_count:]
    *outs, split_ref, sums_ref = refs
    half = pieces[0].shape[0] // 2
    team_index = lax.axis_index("rep")
    for k in range(columns):
        source = source_team(team_index, k, team_count)
        for at, owner in enumerate((source, source ^ 1)):
            value = pieces[k][at * half : (at + 1) * half, :]
            high = value.astype(jnp.bfloat16).astype(jnp.float32)
            low = value - high
            top = lane_join(high, swap_lanes(low)).astype(jnp.bfloat16)
            bottom = lane_join(swap_lanes(high), low).astype(jnp.bfloat16)
            split_ref[pl.ds(pl.multiple_of(owner * 2 * half, half), half), :] = top
            split_ref[pl.ds(pl.multiple_of(owner * 2 * half + half, half), half), :] = bottom
    sums_ref[...] = jnp.zeros_like(sums_ref)
    multiply_slots(info_ref, tiles_ref, split_ref, sums_ref, False)
    write_shares(
        sums_ref,
        outs,
        partials,
        lambda top, bottom: (lane_join(top + swap_lanes(top), bottom + swap_lanes(bottom)),),
    )


def arc_call(kernel, info, tiles, operands, partials, parts, split_width):
    team_count = lax.axis_size("rep")
    slot_total, tile_size, _ = tiles.shape
    width = operands[-1].shape[1]
    panel_rows = sum(operand.shape[0] for operand in operands if operand.dtype == jnp.float32) * (3 - parts)
    parity = jax.ShapeDtypeStruct((panel_rows // 4, width), jnp.float32)
    return pl.pallas_call(
        kernel,
        out_shape=[parity] * (2 * parts),
        in_specs=[VMEM] * (2 + len(operands) + len(partials)),
        out_specs=[VMEM] * (2 * parts),
        scratch_shapes=[
            pltpu.VMEM((panel_rows, split_width), jnp.bfloat16),
            pltpu.VMEM((panel_rows + tile_size, width), jnp.float32),
        ],
        compiler_params=pltpu.CompilerParams(vmem_limit_bytes=VMEM_LIMIT),
        cost_estimate=pl.CostEstimate(
            flops=2 * slot_total * tile_size * tile_size * split_width,
            bytes_accessed=8 * panel_rows * width,
            transcendentals=0,
        ),
    )(info, tiles, *operands, *partials)


def panel_step(info, tiles, degrees, panel, partials):
    kernel = functools.partial(panel_kernel, partial_count=len(partials))
    return arc_call(kernel, info, tiles, [degrees, panel], partials, PARTS, 2 * panel.shape[1])


def part_step(info, tiles, pieces, partials):
    kernel = functools.partial(part_kernel, team_count=lax.axis_size("rep"), partial_count=len(partials))
    return arc_call(kernel, info, tiles, pieces, partials, 1, pieces[0].shape[1])


def layer_kernel(norm_ref, shares_ref, *refs):
    others, (current_ref, source_ref) = refs[:-2], refs[-2:]
    total = shares_ref[: norm_ref.shape[0], :]
    for other_ref in others:
        total = total + other_ref[...]
    current = total * norm_ref[...]
    current_ref[...] = current
    source_ref[...] = current * norm_ref[...]


def layer_share(norm, shares, others):
    share = jax.ShapeDtypeStruct(norm.shape, jnp.float32)
    return pl.pallas_call(
        layer_kernel,
        out_shape=[share] * 2,
        in_specs=[VMEM] * (2 + len(others)),
        out_specs=[VMEM] * 2,
        compiler_params=pltpu.CompilerParams(vmem_limit_bytes=VMEM_LIMIT),
    )(norm, shares, *others)


def finish_kernel(own_ref, norm_ref, *refs, layer_count):
    out_ref = refs[-1]
    half = out_ref.shape[0] // 2
    terms = len(refs[:-1]) // PARTS
    parts = []
    for part in range(PARTS):
        current_ref, shares_ref, *others = refs[part * terms : (part + 1) * terms]
        total = shares_ref[:half, :]
        for other_ref in others:
            total = total + other_ref[...]
        parts.append(current_ref[...] + total * norm_ref[...])
    top = lane_join(parts[0], swap_lanes(parts[1]))
    bottom = lane_join(swap_lanes(parts[0]), parts[1])
    out_ref[:half, :] = (own_ref[:half, :] + top) / layer_count
    out_ref[half:, :] = (own_ref[half:, :] + bottom) / layer_count


def finish(own, norm, parts):
    operands = [operand for part in parts for operand in part]
    return pl.pallas_call(
        functools.partial(finish_kernel, layer_count=LAYERS + 1.0),
        out_shape=jax.ShapeDtypeStruct(own.shape, jnp.float32),
        in_specs=[VMEM] * (2 + len(operands)),
        out_specs=VMEM,
        compiler_params=pltpu.CompilerParams(vmem_limit_bytes=VMEM_LIMIT),
    )(own, norm, *operands)


def fetch(value, source_team, arc_length):
    cycle, team_count = lax.axis_size("blk"), lax.axis_size("rep")
    pairs = []
    for shard in range(cycle):
        for team in range(team_count):
            to_shard = (shard + team * arc_length) % cycle
            pairs.append((shard * team_count + source_team(team), to_shard * team_count + team))
    return lax.ppermute(value, ("blk", "rep"), pairs)


def next_shard(value):
    cycle = lax.axis_size("blk")
    return lax.ppermute(value, "blk", [(i, (i + 1) % cycle) for i in range(cycle)])


def from_mate(value):
    team_count = lax.axis_size("rep")
    return lax.ppermute(value, "rep", [(team, team ^ 1) for team in range(team_count)])


def from_column(value, distance):
    team_count = lax.axis_size("rep")
    pairs = [((team + 2 * distance) % team_count, team) for team in range(team_count)]
    return lax.ppermute(value, "rep", pairs)


def share_terms(keep, give):
    columns = lax.axis_size("rep") // 2
    sums = keep + from_mate(give)
    half = sums.shape[0] // columns
    others = [
        from_column(lax.slice_in_dim(sums, at * half, (at + 1) * half), columns - at) for at in range(1, columns)
    ]
    return sums, others


def per_device(embeddings, degrees, tile_values, tile_rows, tile_columns, slot_counts):
    arc_length, _, tile_size, _ = tile_values.shape[2:]
    panel_rows = embeddings.shape[0]
    team_count = lax.axis_size("rep")
    columns = team_count // 2
    half = panel_rows // team_count // 2
    spread = (3, 1, 2, 0) if team_count == 4 else tuple(range(team_count))
    degrees = degrees.reshape(panel_rows // tile_size, tile_size)

    panel = fetch(embeddings, lambda team: spread[team], arc_length)
    source_degrees = fetch(degrees, lambda team: spread[team], arc_length)
    info = jnp.concatenate([slot_counts[0, 0][:, None], tile_rows[0, 0], tile_columns[0, 0]], axis=1)
    info = jnp.broadcast_to(info[:, :, None], (*info.shape, embeddings.shape[1]))
    info = [info[at] for at in range(arc_length)]
    tiles, own, norm = prepare(degrees, embeddings, tile_values[0, 0], info[0])

    sums = ()
    for at in range(arc_length):
        sums = panel_step(info[at], tiles[at], source_degrees, panel, sums)
        if at + 1 < arc_length:
            panel, source_degrees = next_shard(panel), next_shard(source_degrees)
    parts = [sums[2 * part : 2 * part + 2] for part in range(PARTS)]
    layers = [0.0] * PARTS
    for _ in range(LAYERS - 1):
        terms = [share_terms(*part) for part in parts]
        fetched = []
        for part in range(PARTS):
            current, source = layer_share(norm, *terms[part])
            layers[part] = layers[part] + current
            source = jnp.concatenate([source, from_mate(source)])
            fetched.append(
                [
                    fetch(source, lambda team, k=k: source_team(team, k, team_count), arc_length)
                    for k in range(columns)
                ]
            )
        terms = []
        for pieces in fetched:
            sums = ()
            for at in range(arc_length):
                sums = part_step(info[at], tiles[at], pieces, sums)
                if at + 1 < arc_length:
                    pieces = [next_shard(piece) for piece in pieces]
            terms.append(share_terms(*sums))
    terms = [[layers[part], terms[part][0], *terms[part][1]] for part in range(PARTS)]
    return finish(own, norm, terms)


def solution(mesh):
    in_specs = (
        P(("groups", "blk"), None),
        P(("groups", "blk")),
        P(("groups", "blk"), "rep", None, None, None, None),
        P(("groups", "blk"), "rep", None, None),
        P(("groups", "blk"), "rep", None, None),
        P(("groups", "blk"), "rep", None),
    )
    out_specs = P(("groups", "blk", "rep"), None)
    return jax.shard_map(
        per_device, mesh=mesh, in_specs=in_specs, out_specs=out_specs, check_vma=False
    )
```

```python
import functools

import jax
import jax.numpy as jnp
from jax import lax
from jax.experimental import pallas as pl
from jax.experimental.pallas import tpu as pltpu
from jax.sharding import PartitionSpec as P

LAYERS = 2
VMEM_LIMIT = 16 * 1024 * 1024
VMEM = pl.BlockSpec(memory_space=pltpu.VMEM)
ANY = pl.BlockSpec(memory_space=pl.ANY)


def pair_teams(team_index, column, team_count):
    columns = team_count // 2
    return 2 * lax.rem(team_index // 2 + column, columns) + lax.rem(team_index, 2)


def source_team(team, turn, team_count):
    if team_count == 4:
        return (2 * (team % 2) + team // 2) ^ (0, 2, 3, 1)[turn]
    return (team + turn) % team_count


def norm_columns(degrees):
    return jnp.transpose(lax.rsqrt(degrees.astype(jnp.float32)))


def prepare_kernel(degrees_ref, embeddings_ref, tiles_ref, held_tiles_ref, own_ref, norm_ref, panel_ref, sems):
    share_rows, width = own_ref.shape
    block_count, tile_size = degrees_ref.shape
    team_index = lax.axis_index("rep")
    at = pl.ds(pl.multiple_of(team_index * share_rows, share_rows), share_rows)
    tiles_copy = pltpu.make_async_copy(tiles_ref, held_tiles_ref, sems.at[0])
    own_copy = pltpu.make_async_copy(embeddings_ref.at[at, :], own_ref, sems.at[1])
    tiles_copy.start()
    own_copy.start()
    norms = norm_columns(degrees_ref[...])
    for block in range(block_count):
        panel_ref[block * tile_size : (block + 1) * tile_size, :] = jnp.broadcast_to(
            norms[:, block : block + 1], (tile_size, width)
        )
    norm_ref[...] = panel_ref[at, :]
    own_copy.wait()
    tiles_copy.wait()


def prepare(degrees, embeddings, tile_values):
    panel_rows, width = embeddings.shape
    share = jax.ShapeDtypeStruct((panel_rows // lax.axis_size("rep"), width), jnp.float32)
    return pl.pallas_call(
        prepare_kernel,
        out_shape=[jax.ShapeDtypeStruct(tile_values.shape, tile_values.dtype), share, share],
        in_specs=[VMEM, ANY, ANY],
        out_specs=[VMEM] * 3,
        scratch_shapes=[pltpu.VMEM((panel_rows, width), jnp.float32), pltpu.SemaphoreType.DMA((2,))],
        compiler_params=pltpu.CompilerParams(vmem_limit_bytes=VMEM_LIMIT),
        cost_estimate=pl.CostEstimate(
            flops=panel_rows * width, bytes_accessed=4 * panel_rows * width, transcendentals=0
        ),
    )(degrees, embeddings, tile_values)


def arc_kernel(info_ref, tiles_ref, *refs, team_count, piece_count, scaled, partial_count):
    columns = team_count // 2
    pieces, refs = refs[:piece_count], refs[piece_count:]
    partials, refs = refs[:partial_count], refs[partial_count:]
    outs, (split_ref, sums_ref) = refs[:team_count], refs[team_count:]
    team_index = lax.axis_index("rep")
    slot_total, tile_size, _ = tiles_ref.shape
    panel_rows, width = split_ref.shape[0], split_ref.shape[1] // 2
    share_rows = panel_rows // team_count
    block_count = panel_rows // tile_size

    def split(value, at):
        high = value.astype(jnp.bfloat16)
        split_ref[at, :width] = high
        split_ref[at, width:] = (value - high.astype(jnp.float32)).astype(jnp.bfloat16)

    if scaled:
        degrees_ref, panel_ref = pieces
        norms = norm_columns(degrees_ref[...])
        for block in range(block_count):
            at = pl.ds(block * tile_size, tile_size)
            split(panel_ref[at, :] * norms[:, block : block + 1], at)
    else:
        for k in range(piece_count):
            owner = source_team(team_index, k, team_count)
            split(pieces[k][...], pl.ds(pl.multiple_of(owner * share_rows, share_rows), share_rows))
    sums_ref[...] = jnp.zeros_like(sums_ref)
    live_count = info_ref[0, 0]
    for j in range(slot_total):
        source = pl.multiple_of(info_ref[1 + slot_total + j, 0] * tile_size, tile_size)
        product = jnp.dot(
            tiles_ref[j],
            split_ref[pl.ds(source, tile_size), :],
            preferred_element_type=jnp.float32,
        )
        row = jnp.where(j < live_count, info_ref[1 + j, 0], block_count)
        at = pl.ds(pl.multiple_of(row * tile_size, tile_size), tile_size)
        sums_ref[at, :] += product[:, :width] + product[:, width:]

    for parity in range(2):
        for column in range(columns):
            team = pair_teams(team_index, column, team_count)
            team = team if parity == 0 else team ^ 1
            value = sums_ref[pl.ds(pl.multiple_of(team * share_rows, share_rows), share_rows), :]
            at = parity * columns + column
            outs[at][...] = value + partials[at][...] if partials else value


def arc_step(info, tiles, pieces, partials, scaled):
    team_count = lax.axis_size("rep")
    panel_rows = pieces[1].shape[0] if scaled else sum(piece.shape[0] for piece in pieces)
    width = pieces[1].shape[1]
    slot_total, tile_size, _ = tiles.shape
    share = jax.ShapeDtypeStruct((panel_rows // team_count, width), jnp.float32)
    operands = [info, tiles, *pieces, *partials]
    return pl.pallas_call(
        functools.partial(
            arc_kernel,
            team_count=team_count,
            piece_count=len(pieces),
            scaled=scaled,
            partial_count=len(partials),
        ),
        out_shape=[share] * team_count,
        in_specs=[VMEM] * len(operands),
        out_specs=[VMEM] * team_count,
        scratch_shapes=[
            pltpu.VMEM((panel_rows, 2 * width), jnp.bfloat16),
            pltpu.VMEM((panel_rows + tile_size, width), jnp.float32),
        ],
        compiler_params=pltpu.CompilerParams(vmem_limit_bytes=VMEM_LIMIT),
        cost_estimate=pl.CostEstimate(
            flops=4 * slot_total * tile_size * tile_size * width, bytes_accessed=8 * panel_rows * width, transcendentals=0
        ),
    )(*operands)


def fetch(value, source_team, arc_length):
    cycle, team_count = lax.axis_size("blk"), lax.axis_size("rep")
    pairs = []
    for shard in range(cycle):
        for team in range(team_count):
            to_shard = (shard + team * arc_length) % cycle
            pairs.append((shard * team_count + source_team(team), to_shard * team_count + team))
    return lax.ppermute(value, ("blk", "rep"), pairs)


def next_shard(value):
    cycle = lax.axis_size("blk")
    return lax.ppermute(value, "blk", [(i, (i + 1) % cycle) for i in range(cycle)])


def from_mate(value):
    team_count = lax.axis_size("rep")
    return lax.ppermute(value, "rep", [(team, team ^ 1) for team in range(team_count)])


def from_column(value, distance):
    team_count = lax.axis_size("rep")
    pairs = [((team + 2 * distance) % team_count, team) for team in range(team_count)]
    return lax.ppermute(value, "rep", pairs)


def team_sum(sums):
    columns = len(sums) // 2
    total = None
    for distance in [*range(1, columns), 0]:
        at = (columns - distance) % columns
        share = sums[at] + from_mate(sums[columns + at])
        share = from_column(share, distance) if distance else share
        total = share if total is None else total + share
    return total


def per_device(embeddings, degrees, tile_values, tile_rows, tile_columns, slot_counts):
    arc_length, _, tile_size, _ = tile_values.shape[2:]
    panel_rows = embeddings.shape[0]
    team_count = lax.axis_size("rep")
    spread = (3, 1, 2, 0) if team_count == 4 else tuple(range(team_count))
    degrees = degrees.reshape(panel_rows // tile_size, tile_size)

    panel = fetch(embeddings, lambda team: spread[team], arc_length)
    pieces = [fetch(degrees, lambda team: spread[team], arc_length), panel]
    tiles, own, norm_scale = prepare(degrees, embeddings, tile_values[0, 0])
    info = jnp.concatenate([slot_counts[0, 0][:, None], tile_rows[0, 0], tile_columns[0, 0]], axis=1)
    info = jnp.broadcast_to(info[:, :, None], (*info.shape, embeddings.shape[1]))

    combined = own
    for layer in range(LAYERS):
        sums = ()
        for arc_slot in range(arc_length):
            sums = arc_step(info[arc_slot], tiles[arc_slot], pieces, sums, layer == 0)
            if arc_slot + 1 < arc_length:
                pieces = [next_shard(piece) for piece in pieces]
        current = team_sum(sums) * norm_scale
        combined = combined + current
        if layer + 1 < LAYERS:
            source = current * norm_scale
            pieces = [
                fetch(source, lambda team, k=k: source_team(team, k, team_count), arc_length)
                for k in range(team_count)
            ]
    return combined / (LAYERS + 1.0)


def solution(mesh):
    in_specs = (
        P(("groups", "blk"), None),
        P(("groups", "blk")),
        P(("groups", "blk"), "rep", None, None, None, None),
        P(("groups", "blk"), "rep", None, None),
        P(("groups", "blk"), "rep", None, None),
        P(("groups", "blk"), "rep", None),
    )
    out_specs = P(("groups", "blk", "rep"), None)
    return jax.shard_map(
        per_device, mesh=mesh, in_specs=in_specs, out_specs=out_specs, check_vma=False
    )
```

```python
import functools

import jax
import jax.numpy as jnp
from jax import lax
from jax.experimental import pallas as pl
from jax.experimental.pallas import tpu as pltpu
from jax.sharding import PartitionSpec as P

LAYERS = 2
VMEM_LIMIT = 16 * 1024 * 1024
VMEM = pl.BlockSpec(memory_space=pltpu.VMEM)
ANY = pl.BlockSpec(memory_space=pl.ANY)


def pair_teams(team_index, column, team_count):
    columns = team_count // 2
    return 2 * lax.rem(team_index // 2 + column, columns) + lax.rem(team_index, 2)


def source_team(shard, team, turn, team_count):
    if team_count == 4:
        row, late_row = (0, 2, 1, 3)[turn], (2, 0, 1, 3)[turn]
        swap = (shard == 2) * (row ^ late_row)
        return (2 * (team % 2) + team // 2) ^ row ^ swap
    return (team + turn) % team_count


def norm_columns(degrees):
    return jnp.transpose(lax.rsqrt(degrees.astype(jnp.float32)))


def prepare_kernel(degrees_ref, embeddings_ref, tiles_ref, held_tiles_ref, own_ref, norm_ref, panel_ref, sems):
    share_rows, width = own_ref.shape
    block_count, tile_size = degrees_ref.shape
    team_index = lax.axis_index("rep")
    at = pl.ds(pl.multiple_of(team_index * share_rows, share_rows), share_rows)
    tiles_copy = pltpu.make_async_copy(tiles_ref, held_tiles_ref, sems.at[0])
    own_copy = pltpu.make_async_copy(embeddings_ref.at[at, :], own_ref, sems.at[1])
    tiles_copy.start()
    own_copy.start()
    norms = norm_columns(degrees_ref[...])
    for block in range(block_count):
        panel_ref[block * tile_size : (block + 1) * tile_size, :] = jnp.broadcast_to(
            norms[:, block : block + 1], (tile_size, width)
        )
    norm_ref[...] = panel_ref[at, :]
    own_copy.wait()
    tiles_copy.wait()


def prepare(degrees, embeddings, tile_values):
    panel_rows, width = embeddings.shape
    share = jax.ShapeDtypeStruct((panel_rows // lax.axis_size("rep"), width), jnp.float32)
    return pl.pallas_call(
        prepare_kernel,
        out_shape=[jax.ShapeDtypeStruct(tile_values.shape, tile_values.dtype), share, share],
        in_specs=[VMEM, ANY, ANY],
        out_specs=[VMEM] * 3,
        scratch_shapes=[pltpu.VMEM((panel_rows, width), jnp.float32), pltpu.SemaphoreType.DMA((2,))],
        compiler_params=pltpu.CompilerParams(vmem_limit_bytes=VMEM_LIMIT),
        cost_estimate=pl.CostEstimate(
            flops=panel_rows * width, bytes_accessed=4 * panel_rows * width, transcendentals=0
        ),
    )(degrees, embeddings, tile_values)


def arc_kernel(info_ref, tiles_ref, *refs, team_count, arc_length, arc_slot, piece_count, scaled, partial_count):
    columns = team_count // 2
    pieces, refs = refs[:piece_count], refs[piece_count:]
    partials, refs = refs[:partial_count], refs[partial_count:]
    outs, (split_ref, sums_ref) = refs[:team_count], refs[team_count:]
    team_index = lax.axis_index("rep")
    slot_total, tile_size, _ = tiles_ref.shape
    panel_rows, width = split_ref.shape[0], split_ref.shape[1] // 2
    share_rows = panel_rows // team_count
    block_count = panel_rows // tile_size

    def split(value, at):
        high = value.astype(jnp.bfloat16)
        split_ref[at, :width] = high
        split_ref[at, width:] = (value - high.astype(jnp.float32)).astype(jnp.bfloat16)

    if scaled:
        degrees_ref, panel_ref = pieces
        norms = norm_columns(degrees_ref[...])
        for block in range(block_count):
            at = pl.ds(block * tile_size, tile_size)
            split(panel_ref[at, :] * norms[:, block : block + 1], at)
    else:
        cycle = lax.axis_size("blk")
        shard = lax.rem(lax.axis_index("blk") + cycle - lax.rem(team_index * arc_length + arc_slot, cycle), cycle)
        for k in range(piece_count):
            owner = source_team(shard, team_index, k, team_count)
            split(pieces[k][...], pl.ds(pl.multiple_of(owner * share_rows, share_rows), share_rows))
    sums_ref[...] = jnp.zeros_like(sums_ref)
    live_count = info_ref[0, 0]
    for j in range(slot_total):
        source = pl.multiple_of(info_ref[1 + slot_total + j, 0] * tile_size, tile_size)
        product = jnp.dot(
            tiles_ref[j],
            split_ref[pl.ds(source, tile_size), :],
            preferred_element_type=jnp.float32,
        )
        row = jnp.where(j < live_count, info_ref[1 + j, 0], block_count)
        at = pl.ds(pl.multiple_of(row * tile_size, tile_size), tile_size)
        sums_ref[at, :] += product[:, :width] + product[:, width:]

    for parity in range(2):
        for column in range(columns):
            team = pair_teams(team_index, column, team_count)
            team = team if parity == 0 else team ^ 1
            value = sums_ref[pl.ds(pl.multiple_of(team * share_rows, share_rows), share_rows), :]
            at = parity * columns + column
            outs[at][...] = value + partials[at][...] if partials else value


def arc_step(info, tiles, pieces, partials, scaled, arc_length, arc_slot):
    team_count = lax.axis_size("rep")
    panel_rows = pieces[1].shape[0] if scaled else sum(piece.shape[0] for piece in pieces)
    width = pieces[1].shape[1]
    slot_total, tile_size, _ = tiles.shape
    share = jax.ShapeDtypeStruct((panel_rows // team_count, width), jnp.float32)
    operands = [info, tiles, *pieces, *partials]
    return pl.pallas_call(
        functools.partial(
            arc_kernel,
            team_count=team_count,
            arc_length=arc_length,
            arc_slot=arc_slot,
            piece_count=len(pieces),
            scaled=scaled,
            partial_count=len(partials),
        ),
        out_shape=[share] * team_count,
        in_specs=[VMEM] * len(operands),
        out_specs=[VMEM] * team_count,
        scratch_shapes=[
            pltpu.VMEM((panel_rows, 2 * width), jnp.bfloat16),
            pltpu.VMEM((panel_rows + tile_size, width), jnp.float32),
        ],
        compiler_params=pltpu.CompilerParams(vmem_limit_bytes=VMEM_LIMIT),
        cost_estimate=pl.CostEstimate(
            flops=4 * slot_total * tile_size * tile_size * width, bytes_accessed=8 * panel_rows * width, transcendentals=0
        ),
    )(*operands)


def fetch(value, source, arc_length):
    cycle, team_count = lax.axis_size("blk"), lax.axis_size("rep")
    pairs = []
    for shard in range(cycle):
        for team in range(team_count):
            to_shard = (shard + team * arc_length) % cycle
            pairs.append((shard * team_count + source(shard, team), to_shard * team_count + team))
    return lax.ppermute(value, ("blk", "rep"), pairs)


def next_shard(value):
    cycle = lax.axis_size("blk")
    return lax.ppermute(value, "blk", [(i, (i + 1) % cycle) for i in range(cycle)])


def from_mate(value):
    team_count = lax.axis_size("rep")
    return lax.ppermute(value, "rep", [(team, team ^ 1) for team in range(team_count)])


def from_column(value, distance):
    team_count = lax.axis_size("rep")
    pairs = [((team + 2 * distance) % team_count, team) for team in range(team_count)]
    return lax.ppermute(value, "rep", pairs)


def team_sum(sums):
    columns = len(sums) // 2
    total = None
    for distance in [*range(1, columns), 0]:
        at = (columns - distance) % columns
        share = sums[at] + from_mate(sums[columns + at])
        share = from_column(share, distance) if distance else share
        total = share if total is None else total + share
    return total


def per_device(embeddings, degrees, tile_values, tile_rows, tile_columns, slot_counts):
    arc_length, _, tile_size, _ = tile_values.shape[2:]
    panel_rows = embeddings.shape[0]
    team_count = lax.axis_size("rep")
    spread = (3, 1, 2, 0) if team_count == 4 else tuple(range(team_count))
    degrees = degrees.reshape(panel_rows // tile_size, tile_size)

    panel = fetch(embeddings, lambda shard, team: spread[team], arc_length)
    pieces = [fetch(degrees, lambda shard, team: spread[team], arc_length), panel]
    tiles, own, norm_scale = prepare(degrees, embeddings, tile_values[0, 0])
    info = jnp.concatenate([slot_counts[0, 0][:, None], tile_rows[0, 0], tile_columns[0, 0]], axis=1)
    info = jnp.broadcast_to(info[:, :, None], (*info.shape, embeddings.shape[1]))

    combined = own
    for layer in range(LAYERS):
        sums = ()
        for arc_slot in range(arc_length):
            sums = arc_step(info[arc_slot], tiles[arc_slot], pieces, sums, layer == 0, arc_length, arc_slot)
            if arc_slot + 1 < arc_length:
                pieces = [next_shard(piece) for piece in pieces]
        current = team_sum(sums) * norm_scale
        combined = combined + current
        if layer + 1 < LAYERS:
            source = current * norm_scale
            pieces = [
                fetch(source, lambda shard, team, k=k: source_team(shard, team, k, team_count), arc_length)
                for k in range(team_count)
            ]
    return combined / (LAYERS + 1.0)


def solution(mesh):
    in_specs = (
        P(("groups", "blk"), None),
        P(("groups", "blk")),
        P(("groups", "blk"), "rep", None, None, None, None),
        P(("groups", "blk"), "rep", None, None),
        P(("groups", "blk"), "rep", None, None),
        P(("groups", "blk"), "rep", None),
    )
    out_specs = P(("groups", "blk", "rep"), None)
    return jax.shard_map(
        per_device, mesh=mesh, in_specs=in_specs, out_specs=out_specs, check_vma=False
    )
```

```python
import functools

import jax
import jax.numpy as jnp
from jax import lax
from jax.experimental import pallas as pl
from jax.experimental.pallas import tpu as pltpu
from jax.sharding import PartitionSpec as P

LAYERS = 2
VMEM_LIMIT = 16 * 1024 * 1024
VMEM = pl.BlockSpec(memory_space=pltpu.VMEM)
ANY = pl.BlockSpec(memory_space=pl.ANY)


def pair_teams(team_index, column, team_count):
    columns = team_count // 2
    return 2 * lax.rem(team_index // 2 + column, columns) + lax.rem(team_index, 2)


def source_team(team, turn, team_count):
    if team_count == 4:
        return (2 * (team % 2) + team // 2) ^ (0, 2, 1, 3)[turn]
    return (team + turn) % team_count


def norm_columns(degrees):
    return jnp.transpose(lax.rsqrt(degrees.astype(jnp.float32)))


def prepare_kernel(
    degrees_ref, embeddings_ref, tiles_ref, after_ref, held_tiles_ref, own_ref, norm_ref, panel_ref, sems
):
    del after_ref
    share_rows, width = own_ref.shape
    block_count, tile_size = degrees_ref.shape
    team_index = lax.axis_index("rep")
    at = pl.ds(pl.multiple_of(team_index * share_rows, share_rows), share_rows)
    tiles_copy = pltpu.make_async_copy(tiles_ref, held_tiles_ref, sems.at[0])
    own_copy = pltpu.make_async_copy(embeddings_ref.at[at, :], own_ref, sems.at[1])
    tiles_copy.start()
    own_copy.start()
    norms = norm_columns(degrees_ref[...])
    for block in range(block_count):
        panel_ref[block * tile_size : (block + 1) * tile_size, :] = jnp.broadcast_to(
            norms[:, block : block + 1], (tile_size, width)
        )
    norm_ref[...] = panel_ref[at, :]
    own_copy.wait()
    tiles_copy.wait()


def prepare(degrees, embeddings, tile_values, after):
    panel_rows, width = embeddings.shape
    share = jax.ShapeDtypeStruct((panel_rows // lax.axis_size("rep"), width), jnp.float32)
    return pl.pallas_call(
        prepare_kernel,
        out_shape=[jax.ShapeDtypeStruct(tile_values.shape, tile_values.dtype), share, share],
        in_specs=[VMEM, ANY, ANY, ANY],
        out_specs=[VMEM] * 3,
        scratch_shapes=[pltpu.VMEM((panel_rows, width), jnp.float32), pltpu.SemaphoreType.DMA((2,))],
        compiler_params=pltpu.CompilerParams(vmem_limit_bytes=VMEM_LIMIT),
        cost_estimate=pl.CostEstimate(
            flops=panel_rows * width, bytes_accessed=4 * panel_rows * width, transcendentals=0
        ),
    )(degrees, embeddings, tile_values, after)


def arc_kernel(info_ref, tiles_ref, *refs, team_count, piece_count, scaled, partial_count):
    columns = team_count // 2
    pieces, refs = refs[:piece_count], refs[piece_count:]
    partials, refs = refs[:partial_count], refs[partial_count:]
    outs, (split_ref, sums_ref) = refs[:team_count], refs[team_count:]
    team_index = lax.axis_index("rep")
    slot_total, tile_size, _ = tiles_ref.shape
    panel_rows, width = split_ref.shape[0], split_ref.shape[1] // 2
    share_rows = panel_rows // team_count
    block_count = panel_rows // tile_size

    def split(value, at):
        high = value.astype(jnp.bfloat16)
        split_ref[at, :width] = high
        split_ref[at, width:] = (value - high.astype(jnp.float32)).astype(jnp.bfloat16)

    if scaled:
        degrees_ref, panel_ref = pieces
        norms = norm_columns(degrees_ref[...])
        for block in range(block_count):
            at = pl.ds(block * tile_size, tile_size)
            split(panel_ref[at, :] * norms[:, block : block + 1], at)
    else:
        for k in range(piece_count):
            owner = source_team(team_index, k, team_count)
            split(pieces[k][...], pl.ds(pl.multiple_of(owner * share_rows, share_rows), share_rows))
    sums_ref[...] = jnp.zeros_like(sums_ref)
    live_count = info_ref[0, 0]
    for j in range(slot_total):
        source = pl.multiple_of(info_ref[1 + slot_total + j, 0] * tile_size, tile_size)
        product = jnp.dot(
            tiles_ref[j],
            split_ref[pl.ds(source, tile_size), :],
            preferred_element_type=jnp.float32,
        )
        row = jnp.where(j < live_count, info_ref[1 + j, 0], block_count)
        at = pl.ds(pl.multiple_of(row * tile_size, tile_size), tile_size)
        sums_ref[at, :] += product[:, :width] + product[:, width:]

    for parity in range(2):
        for column in range(columns):
            team = pair_teams(team_index, column, team_count)
            team = team if parity == 0 else team ^ 1
            value = sums_ref[pl.ds(pl.multiple_of(team * share_rows, share_rows), share_rows), :]
            at = parity * columns + column
            outs[at][...] = value + partials[at][...] if partials else value


def arc_step(info, tiles, pieces, partials, scaled):
    team_count = lax.axis_size("rep")
    panel_rows = pieces[1].shape[0] if scaled else sum(piece.shape[0] for piece in pieces)
    width = pieces[1].shape[1]
    slot_total, tile_size, _ = tiles.shape
    share = jax.ShapeDtypeStruct((panel_rows // team_count, width), jnp.float32)
    operands = [info, tiles, *pieces, *partials]
    return pl.pallas_call(
        functools.partial(
            arc_kernel,
            team_count=team_count,
            piece_count=len(pieces),
            scaled=scaled,
            partial_count=len(partials),
        ),
        out_shape=[share] * team_count,
        in_specs=[VMEM] * len(operands),
        out_specs=[VMEM] * team_count,
        scratch_shapes=[
            pltpu.VMEM((panel_rows, 2 * width), jnp.bfloat16),
            pltpu.VMEM((panel_rows + tile_size, width), jnp.float32),
        ],
        compiler_params=pltpu.CompilerParams(vmem_limit_bytes=VMEM_LIMIT),
        cost_estimate=pl.CostEstimate(
            flops=4 * slot_total * tile_size * tile_size * width, bytes_accessed=8 * panel_rows * width, transcendentals=0
        ),
    )(*operands)


def fetch(value, source_team, arc_length):
    cycle, team_count = lax.axis_size("blk"), lax.axis_size("rep")
    pairs = []
    for shard in range(cycle):
        for team in range(team_count):
            to_shard = (shard + team * arc_length) % cycle
            pairs.append((shard * team_count + source_team(team), to_shard * team_count + team))
    return lax.ppermute(value, ("blk", "rep"), pairs)


def next_shard(value):
    cycle = lax.axis_size("blk")
    return lax.ppermute(value, "blk", [(i, (i + 1) % cycle) for i in range(cycle)])


def from_mate(value):
    team_count = lax.axis_size("rep")
    return lax.ppermute(value, "rep", [(team, team ^ 1) for team in range(team_count)])


def from_column(value, distance):
    team_count = lax.axis_size("rep")
    pairs = [((team + 2 * distance) % team_count, team) for team in range(team_count)]
    return lax.ppermute(value, "rep", pairs)


def team_terms(sums):
    columns = len(sums) // 2
    others = []
    for distance in range(1, columns):
        at = columns - distance
        others.append(from_column(sums[at] + from_mate(sums[columns + at]), distance))
    return [sums[0], from_mate(sums[columns]), *others]


def finish_kernel(base_ref, norm_ref, *refs, layer_count):
    *terms, out_hbm, held_ref, sems = refs
    pieces = sems.shape[0]
    rows = held_ref.shape[0] // pieces
    copies = []
    for piece in range(pieces):
        at = pl.ds(piece * rows, rows)
        total = terms[0][at, :]
        for term_ref in terms[1:]:
            total = total + term_ref[at, :]
        held_ref[at, :] = (base_ref[at, :] + total * norm_ref[at, :]) / layer_count
        copies.append(pltpu.make_async_copy(held_ref.at[at, :], out_hbm.at[at, :], sems.at[piece]))
        copies[-1].start()
    for copy in copies:
        copy.wait()


def finish(base, norm_scale, terms):
    return pl.pallas_call(
        functools.partial(finish_kernel, layer_count=LAYERS + 1.0),
        out_shape=jax.ShapeDtypeStruct(base.shape, jnp.float32),
        in_specs=[VMEM] * (2 + len(terms)),
        out_specs=ANY,
        scratch_shapes=[pltpu.VMEM(base.shape, jnp.float32), pltpu.SemaphoreType.DMA((2,))],
        compiler_params=pltpu.CompilerParams(vmem_limit_bytes=VMEM_LIMIT),
    )(base, norm_scale, *terms)


def per_device(embeddings, degrees, tile_values, tile_rows, tile_columns, slot_counts):
    arc_length, _, tile_size, _ = tile_values.shape[2:]
    panel_rows = embeddings.shape[0]
    team_count = lax.axis_size("rep")
    spread = (3, 1, 2, 0) if team_count == 4 else tuple(range(team_count))
    degrees = degrees.reshape(panel_rows // tile_size, tile_size)

    panel = fetch(embeddings, lambda team: spread[team], arc_length)
    pieces = [fetch(degrees, lambda team: spread[team], arc_length), panel]
    info = jnp.concatenate([slot_counts[0, 0][:, None], tile_rows[0, 0], tile_columns[0, 0]], axis=1)
    info = jnp.broadcast_to(info[:, :, None], (*info.shape, embeddings.shape[1]))
    info = [info[at] for at in range(arc_length)]
    tiles, own, norm_scale = prepare(degrees, embeddings, tile_values[0, 0], info[0])

    combined = own
    for layer in range(LAYERS):
        sums = ()
        for arc_slot in range(arc_length):
            sums = arc_step(info[arc_slot], tiles[arc_slot], pieces, sums, layer == 0)
            if arc_slot + 1 < arc_length:
                pieces = [next_shard(piece) for piece in pieces]
        terms = team_terms(sums)
        if layer + 1 == LAYERS:
            return finish(combined, norm_scale, terms)
        current = functools.reduce(jnp.add, terms) * norm_scale
        combined = combined + current
        source = current * norm_scale
        pieces = [
            fetch(source, lambda team, k=k: source_team(team, k, team_count), arc_length)
            for k in range(team_count)
        ]


def solution(mesh):
    in_specs = (
        P(("groups", "blk"), None),
        P(("groups", "blk")),
        P(("groups", "blk"), "rep", None, None, None, None),
        P(("groups", "blk"), "rep", None, None),
        P(("groups", "blk"), "rep", None, None),
        P(("groups", "blk"), "rep", None),
    )
    out_specs = P(("groups", "blk", "rep"), None)
    return jax.shard_map(
        per_device, mesh=mesh, in_specs=in_specs, out_specs=out_specs, check_vma=False
    )
```

```python
import functools

import jax
import jax.numpy as jnp
from jax import lax
from jax.experimental import pallas as pl
from jax.experimental.pallas import tpu as pltpu
from jax.sharding import PartitionSpec as P

LAYERS = 2
VMEM_LIMIT = 16 * 1024 * 1024
VMEM = pl.BlockSpec(memory_space=pltpu.VMEM)
ANY = pl.BlockSpec(memory_space=pl.ANY)


def pair_teams(team_index, column, team_count):
    columns = team_count // 2
    return 2 * lax.rem(team_index // 2 + column, columns) + lax.rem(team_index, 2)


def source_team(team, turn, team_count):
    if team_count == 4:
        return (2 * (team % 2) + team // 2) ^ (0, 1, 3, 2)[turn]
    return (team + turn) % team_count


def norm_columns(degrees):
    return jnp.transpose(lax.rsqrt(degrees.astype(jnp.float32)))


def prepare_kernel(
    degrees_ref, embeddings_ref, tiles_ref, after_ref, held_tiles_ref, own_ref, norm_ref, panel_ref, sems
):
    del after_ref
    share_rows, width = own_ref.shape
    block_count, tile_size = degrees_ref.shape
    team_index = lax.axis_index("rep")
    at = pl.ds(pl.multiple_of(team_index * share_rows, share_rows), share_rows)
    tiles_copy = pltpu.make_async_copy(tiles_ref, held_tiles_ref, sems.at[0])
    own_copy = pltpu.make_async_copy(embeddings_ref.at[at, :], own_ref, sems.at[1])
    tiles_copy.start()
    own_copy.start()
    norms = norm_columns(degrees_ref[...])
    for block in range(block_count):
        panel_ref[block * tile_size : (block + 1) * tile_size, :] = jnp.broadcast_to(
            norms[:, block : block + 1], (tile_size, width)
        )
    norm_ref[...] = panel_ref[at, :]
    own_copy.wait()
    tiles_copy.wait()


def prepare(degrees, embeddings, tile_values, after):
    panel_rows, width = embeddings.shape
    share = jax.ShapeDtypeStruct((panel_rows // lax.axis_size("rep"), width), jnp.float32)
    return pl.pallas_call(
        prepare_kernel,
        out_shape=[jax.ShapeDtypeStruct(tile_values.shape, tile_values.dtype), share, share],
        in_specs=[VMEM, ANY, ANY, ANY],
        out_specs=[VMEM] * 3,
        scratch_shapes=[pltpu.VMEM((panel_rows, width), jnp.float32), pltpu.SemaphoreType.DMA((2,))],
        compiler_params=pltpu.CompilerParams(vmem_limit_bytes=VMEM_LIMIT),
        cost_estimate=pl.CostEstimate(
            flops=panel_rows * width, bytes_accessed=4 * panel_rows * width, transcendentals=0
        ),
    )(degrees, embeddings, tile_values, after)


def arc_kernel(info_ref, tiles_ref, *refs, team_count, piece_count, scaled, partial_count):
    columns = team_count // 2
    pieces, refs = refs[:piece_count], refs[piece_count:]
    partials, refs = refs[:partial_count], refs[partial_count:]
    outs, (split_ref, sums_ref) = refs[:team_count], refs[team_count:]
    team_index = lax.axis_index("rep")
    slot_total, tile_size, _ = tiles_ref.shape
    panel_rows, width = split_ref.shape[0], split_ref.shape[1] // 2
    share_rows = panel_rows // team_count
    block_count = panel_rows // tile_size

    def split(value, at):
        high = value.astype(jnp.bfloat16)
        split_ref[at, :width] = high
        split_ref[at, width:] = (value - high.astype(jnp.float32)).astype(jnp.bfloat16)

    if scaled:
        degrees_ref, panel_ref = pieces
        norms = norm_columns(degrees_ref[...])
        for block in range(block_count):
            at = pl.ds(block * tile_size, tile_size)
            split(panel_ref[at, :] * norms[:, block : block + 1], at)
    else:
        for k in range(piece_count):
            owner = source_team(team_index, k, team_count)
            split(pieces[k][...], pl.ds(pl.multiple_of(owner * share_rows, share_rows), share_rows))
    sums_ref[...] = jnp.zeros_like(sums_ref)
    live_count = info_ref[0, 0]
    for j in range(slot_total):
        source = pl.multiple_of(info_ref[1 + slot_total + j, 0] * tile_size, tile_size)
        product = jnp.dot(
            tiles_ref[j],
            split_ref[pl.ds(source, tile_size), :],
            preferred_element_type=jnp.float32,
        )
        row = jnp.where(j < live_count, info_ref[1 + j, 0], block_count)
        at = pl.ds(pl.multiple_of(row * tile_size, tile_size), tile_size)
        sums_ref[at, :] += product[:, :width] + product[:, width:]

    for parity in range(2):
        for column in range(columns):
            team = pair_teams(team_index, column, team_count)
            team = team if parity == 0 else team ^ 1
            value = sums_ref[pl.ds(pl.multiple_of(team * share_rows, share_rows), share_rows), :]
            at = parity * columns + column
            outs[at][...] = value + partials[at][...] if partials else value


def arc_step(info, tiles, pieces, partials, scaled):
    team_count = lax.axis_size("rep")
    panel_rows = pieces[1].shape[0] if scaled else sum(piece.shape[0] for piece in pieces)
    width = pieces[1].shape[1]
    slot_total, tile_size, _ = tiles.shape
    share = jax.ShapeDtypeStruct((panel_rows // team_count, width), jnp.float32)
    operands = [info, tiles, *pieces, *partials]
    return pl.pallas_call(
        functools.partial(
            arc_kernel,
            team_count=team_count,
            piece_count=len(pieces),
            scaled=scaled,
            partial_count=len(partials),
        ),
        out_shape=[share] * team_count,
        in_specs=[VMEM] * len(operands),
        out_specs=[VMEM] * team_count,
        scratch_shapes=[
            pltpu.VMEM((panel_rows, 2 * width), jnp.bfloat16),
            pltpu.VMEM((panel_rows + tile_size, width), jnp.float32),
        ],
        compiler_params=pltpu.CompilerParams(vmem_limit_bytes=VMEM_LIMIT),
        cost_estimate=pl.CostEstimate(
            flops=4 * slot_total * tile_size * tile_size * width, bytes_accessed=8 * panel_rows * width, transcendentals=0
        ),
    )(*operands)


def fetch(value, source_team, arc_length):
    cycle, team_count = lax.axis_size("blk"), lax.axis_size("rep")
    pairs = []
    for shard in range(cycle):
        for team in range(team_count):
            to_shard = (shard + team * arc_length) % cycle
            pairs.append((shard * team_count + source_team(team), to_shard * team_count + team))
    return lax.ppermute(value, ("blk", "rep"), pairs)


def next_shard(value):
    cycle = lax.axis_size("blk")
    return lax.ppermute(value, "blk", [(i, (i + 1) % cycle) for i in range(cycle)])


def from_mate(value):
    team_count = lax.axis_size("rep")
    return lax.ppermute(value, "rep", [(team, team ^ 1) for team in range(team_count)])


def from_column(value, distance):
    team_count = lax.axis_size("rep")
    pairs = [((team + 2 * distance) % team_count, team) for team in range(team_count)]
    return lax.ppermute(value, "rep", pairs)


def team_terms(sums):
    columns = len(sums) // 2
    others = []
    for distance in range(1, columns):
        at = columns - distance
        others.append(from_column(sums[at] + from_mate(sums[columns + at]), distance))
    return [sums[0], from_mate(sums[columns]), *others]


def finish_kernel(base_ref, norm_ref, *refs, layer_count):
    *terms, out_hbm, held_ref, sems = refs
    pieces = sems.shape[0]
    rows = held_ref.shape[0] // pieces
    copies = []
    for piece in range(pieces):
        at = pl.ds(piece * rows, rows)
        total = terms[0][at, :]
        for term_ref in terms[1:]:
            total = total + term_ref[at, :]
        held_ref[at, :] = (base_ref[at, :] + total * norm_ref[at, :]) / layer_count
        copies.append(pltpu.make_async_copy(held_ref.at[at, :], out_hbm.at[at, :], sems.at[piece]))
        copies[-1].start()
    for copy in copies:
        copy.wait()


def finish(base, norm_scale, terms):
    return pl.pallas_call(
        functools.partial(finish_kernel, layer_count=LAYERS + 1.0),
        out_shape=jax.ShapeDtypeStruct(base.shape, jnp.float32),
        in_specs=[VMEM] * (2 + len(terms)),
        out_specs=ANY,
        scratch_shapes=[pltpu.VMEM(base.shape, jnp.float32), pltpu.SemaphoreType.DMA((2,))],
        compiler_params=pltpu.CompilerParams(vmem_limit_bytes=VMEM_LIMIT),
    )(base, norm_scale, *terms)


def per_device(embeddings, degrees, tile_values, tile_rows, tile_columns, slot_counts):
    arc_length, _, tile_size, _ = tile_values.shape[2:]
    panel_rows = embeddings.shape[0]
    team_count = lax.axis_size("rep")
    spread = (3, 1, 2, 0) if team_count == 4 else tuple(range(team_count))
    degrees = degrees.reshape(panel_rows // tile_size, tile_size)

    panel = fetch(embeddings, lambda team: spread[team], arc_length)
    pieces = [fetch(degrees, lambda team: spread[team], arc_length), panel]
    info = jnp.concatenate([slot_counts[0, 0][:, None], tile_rows[0, 0], tile_columns[0, 0]], axis=1)
    info = jnp.broadcast_to(info[:, :, None], (*info.shape, embeddings.shape[1]))
    info = [info[at] for at in range(arc_length)]
    tiles, own, norm_scale = prepare(degrees, embeddings, tile_values[0, 0], info[0])

    combined = own
    for layer in range(LAYERS):
        sums = ()
        for arc_slot in range(arc_length):
            sums = arc_step(info[arc_slot], tiles[arc_slot], pieces, sums, layer == 0)
            if arc_slot + 1 < arc_length:
                pieces = [next_shard(piece) for piece in pieces]
        terms = team_terms(sums)
        if layer + 1 == LAYERS:
            return finish(combined, norm_scale, terms)
        current = functools.reduce(jnp.add, terms) * norm_scale
        combined = combined + current
        source = current * norm_scale
        pieces = [
            fetch(source, lambda team, k=k: source_team(team, k, team_count), arc_length)
            for k in range(team_count)
        ]


def solution(mesh):
    in_specs = (
        P(("groups", "blk"), None),
        P(("groups", "blk")),
        P(("groups", "blk"), "rep", None, None, None, None),
        P(("groups", "blk"), "rep", None, None),
        P(("groups", "blk"), "rep", None, None),
        P(("groups", "blk"), "rep", None),
    )
    out_specs = P(("groups", "blk", "rep"), None)
    return jax.shard_map(
        per_device, mesh=mesh, in_specs=in_specs, out_specs=out_specs, check_vma=False
    )
```

```python
import functools

import jax
import jax.numpy as jnp
from jax import lax
from jax.experimental import pallas as pl
from jax.experimental.pallas import tpu as pltpu
from jax.sharding import PartitionSpec as P

LAYERS = 2
VMEM_LIMIT = 16 * 1024 * 1024
VMEM = pl.BlockSpec(memory_space=pltpu.VMEM)
ANY = pl.BlockSpec(memory_space=pl.ANY)


def pair_teams(team_index, column, team_count):
    columns = team_count // 2
    return 2 * lax.rem(team_index // 2 + column, columns) + lax.rem(team_index, 2)


def source_team(shard, team, turn, cycle, team_count):
    if team_count == 4:
        lower, upper = (0, 1, 3, 2)[turn], (3, 1, 0, 2)[turn]
        return (2 * (team % 2) + team // 2) ^ lower ^ ((shard >= cycle // 2) * (lower ^ upper))
    return (team + turn) % team_count


def norm_columns(degrees):
    return jnp.transpose(lax.rsqrt(degrees.astype(jnp.float32)))


def prepare_kernel(
    degrees_ref, embeddings_ref, tiles_ref, after_ref, held_tiles_ref, own_ref, norm_ref, panel_ref, sems
):
    del after_ref
    share_rows, width = own_ref.shape
    block_count, tile_size = degrees_ref.shape
    team_index = lax.axis_index("rep")
    at = pl.ds(pl.multiple_of(team_index * share_rows, share_rows), share_rows)
    tiles_copy = pltpu.make_async_copy(tiles_ref, held_tiles_ref, sems.at[0])
    own_copy = pltpu.make_async_copy(embeddings_ref.at[at, :], own_ref, sems.at[1])
    tiles_copy.start()
    own_copy.start()
    norms = norm_columns(degrees_ref[...])
    for block in range(block_count):
        panel_ref[block * tile_size : (block + 1) * tile_size, :] = jnp.broadcast_to(
            norms[:, block : block + 1], (tile_size, width)
        )
    norm_ref[...] = panel_ref[at, :]
    own_copy.wait()
    tiles_copy.wait()


def prepare(degrees, embeddings, tile_values, after):
    panel_rows, width = embeddings.shape
    share = jax.ShapeDtypeStruct((panel_rows // lax.axis_size("rep"), width), jnp.float32)
    return pl.pallas_call(
        prepare_kernel,
        out_shape=[jax.ShapeDtypeStruct(tile_values.shape, tile_values.dtype), share, share],
        in_specs=[VMEM, ANY, ANY, ANY],
        out_specs=[VMEM] * 3,
        scratch_shapes=[pltpu.VMEM((panel_rows, width), jnp.float32), pltpu.SemaphoreType.DMA((2,))],
        compiler_params=pltpu.CompilerParams(vmem_limit_bytes=VMEM_LIMIT),
        cost_estimate=pl.CostEstimate(
            flops=panel_rows * width, bytes_accessed=4 * panel_rows * width, transcendentals=0
        ),
    )(degrees, embeddings, tile_values, after)


def arc_kernel(info_ref, tiles_ref, *refs, team_count, arc_length, arc_slot, piece_count, scaled, partial_count):
    columns = team_count // 2
    pieces, refs = refs[:piece_count], refs[piece_count:]
    partials, refs = refs[:partial_count], refs[partial_count:]
    outs, (split_ref, sums_ref) = refs[:team_count], refs[team_count:]
    team_index = lax.axis_index("rep")
    slot_total, tile_size, _ = tiles_ref.shape
    panel_rows, width = split_ref.shape[0], split_ref.shape[1] // 2
    share_rows = panel_rows // team_count
    block_count = panel_rows // tile_size

    def split(value, at):
        high = value.astype(jnp.bfloat16)
        split_ref[at, :width] = high
        split_ref[at, width:] = (value - high.astype(jnp.float32)).astype(jnp.bfloat16)

    if scaled:
        degrees_ref, panel_ref = pieces
        norms = norm_columns(degrees_ref[...])
        for block in range(block_count):
            at = pl.ds(block * tile_size, tile_size)
            split(panel_ref[at, :] * norms[:, block : block + 1], at)
    else:
        cycle = lax.axis_size("blk")
        shard = lax.rem(lax.axis_index("blk") + cycle - lax.rem(team_index * arc_length + arc_slot, cycle), cycle)
        for k in range(piece_count):
            owner = source_team(shard, team_index, k, cycle, team_count)
            split(pieces[k][...], pl.ds(pl.multiple_of(owner * share_rows, share_rows), share_rows))
    sums_ref[...] = jnp.zeros_like(sums_ref)
    live_count = info_ref[0, 0]
    for j in range(slot_total):
        source = pl.multiple_of(info_ref[1 + slot_total + j, 0] * tile_size, tile_size)
        product = jnp.dot(
            tiles_ref[j],
            split_ref[pl.ds(source, tile_size), :],
            preferred_element_type=jnp.float32,
        )
        row = jnp.where(j < live_count, info_ref[1 + j, 0], block_count)
        at = pl.ds(pl.multiple_of(row * tile_size, tile_size), tile_size)
        sums_ref[at, :] += product[:, :width] + product[:, width:]

    for parity in range(2):
        for column in range(columns):
            team = pair_teams(team_index, column, team_count)
            team = team if parity == 0 else team ^ 1
            value = sums_ref[pl.ds(pl.multiple_of(team * share_rows, share_rows), share_rows), :]
            at = parity * columns + column
            outs[at][...] = value + partials[at][...] if partials else value


def arc_step(info, tiles, pieces, partials, scaled, arc_length, arc_slot):
    team_count = lax.axis_size("rep")
    panel_rows = pieces[1].shape[0] if scaled else sum(piece.shape[0] for piece in pieces)
    width = pieces[1].shape[1]
    slot_total, tile_size, _ = tiles.shape
    share = jax.ShapeDtypeStruct((panel_rows // team_count, width), jnp.float32)
    operands = [info, tiles, *pieces, *partials]
    return pl.pallas_call(
        functools.partial(
            arc_kernel,
            team_count=team_count,
            arc_length=arc_length,
            arc_slot=arc_slot,
            piece_count=len(pieces),
            scaled=scaled,
            partial_count=len(partials),
        ),
        out_shape=[share] * team_count,
        in_specs=[VMEM] * len(operands),
        out_specs=[VMEM] * team_count,
        scratch_shapes=[
            pltpu.VMEM((panel_rows, 2 * width), jnp.bfloat16),
            pltpu.VMEM((panel_rows + tile_size, width), jnp.float32),
        ],
        compiler_params=pltpu.CompilerParams(vmem_limit_bytes=VMEM_LIMIT),
        cost_estimate=pl.CostEstimate(
            flops=4 * slot_total * tile_size * tile_size * width, bytes_accessed=8 * panel_rows * width, transcendentals=0
        ),
    )(*operands)


def fetch(value, source, arc_length):
    cycle, team_count = lax.axis_size("blk"), lax.axis_size("rep")
    pairs = []
    for shard in range(cycle):
        for team in range(team_count):
            to_shard = (shard + team * arc_length) % cycle
            pairs.append((shard * team_count + source(shard, team), to_shard * team_count + team))
    return lax.ppermute(value, ("blk", "rep"), pairs)


def next_shard(value):
    cycle = lax.axis_size("blk")
    return lax.ppermute(value, "blk", [(i, (i + 1) % cycle) for i in range(cycle)])


def from_mate(value):
    team_count = lax.axis_size("rep")
    return lax.ppermute(value, "rep", [(team, team ^ 1) for team in range(team_count)])


def from_column(value, distance):
    team_count = lax.axis_size("rep")
    pairs = [((team + 2 * distance) % team_count, team) for team in range(team_count)]
    return lax.ppermute(value, "rep", pairs)


def team_terms(sums):
    columns = len(sums) // 2
    others = []
    for distance in range(1, columns):
        at = columns - distance
        others.append(from_column(sums[at] + from_mate(sums[columns + at]), distance))
    return [sums[0], from_mate(sums[columns]), *others]


def finish_kernel(base_ref, norm_ref, *refs, layer_count):
    *terms, out_hbm, held_ref, sems = refs
    pieces = sems.shape[0]
    rows = held_ref.shape[0] // pieces
    copies = []
    for piece in range(pieces):
        at = pl.ds(piece * rows, rows)
        total = terms[0][at, :]
        for term_ref in terms[1:]:
            total = total + term_ref[at, :]
        held_ref[at, :] = (base_ref[at, :] + total * norm_ref[at, :]) / layer_count
        copies.append(pltpu.make_async_copy(held_ref.at[at, :], out_hbm.at[at, :], sems.at[piece]))
        copies[-1].start()
    for copy in copies:
        copy.wait()


def finish(base, norm_scale, terms):
    return pl.pallas_call(
        functools.partial(finish_kernel, layer_count=LAYERS + 1.0),
        out_shape=jax.ShapeDtypeStruct(base.shape, jnp.float32),
        in_specs=[VMEM] * (2 + len(terms)),
        out_specs=ANY,
        scratch_shapes=[pltpu.VMEM(base.shape, jnp.float32), pltpu.SemaphoreType.DMA((2,))],
        compiler_params=pltpu.CompilerParams(vmem_limit_bytes=VMEM_LIMIT),
    )(base, norm_scale, *terms)


def per_device(embeddings, degrees, tile_values, tile_rows, tile_columns, slot_counts):
    arc_length, _, tile_size, _ = tile_values.shape[2:]
    panel_rows = embeddings.shape[0]
    cycle, team_count = lax.axis_size("blk"), lax.axis_size("rep")
    spread = (3, 1, 2, 0) if team_count == 4 else tuple(range(team_count))
    degrees = degrees.reshape(panel_rows // tile_size, tile_size)

    panel = fetch(embeddings, lambda shard, team: spread[team], arc_length)
    pieces = [fetch(degrees, lambda shard, team: spread[team], arc_length), panel]
    info = jnp.concatenate([slot_counts[0, 0][:, None], tile_rows[0, 0], tile_columns[0, 0]], axis=1)
    info = jnp.broadcast_to(info[:, :, None], (*info.shape, embeddings.shape[1]))
    info = [info[at] for at in range(arc_length)]
    tiles, own, norm_scale = prepare(degrees, embeddings, tile_values[0, 0], info[0])

    combined = own
    for layer in range(LAYERS):
        sums = ()
        for arc_slot in range(arc_length):
            sums = arc_step(info[arc_slot], tiles[arc_slot], pieces, sums, layer == 0, arc_length, arc_slot)
            if arc_slot + 1 < arc_length:
                pieces = [next_shard(piece) for piece in pieces]
        terms = team_terms(sums)
        if layer + 1 == LAYERS:
            return finish(combined, norm_scale, terms)
        current = functools.reduce(jnp.add, terms) * norm_scale
        combined = combined + current
        source = current * norm_scale
        pieces = [
            fetch(source, lambda shard, team, k=k: source_team(shard, team, k, cycle, team_count), arc_length)
            for k in range(team_count)
        ]


def solution(mesh):
    in_specs = (
        P(("groups", "blk"), None),
        P(("groups", "blk")),
        P(("groups", "blk"), "rep", None, None, None, None),
        P(("groups", "blk"), "rep", None, None),
        P(("groups", "blk"), "rep", None, None),
        P(("groups", "blk"), "rep", None),
    )
    out_specs = P(("groups", "blk", "rep"), None)
    return jax.shard_map(
        per_device, mesh=mesh, in_specs=in_specs, out_specs=out_specs, check_vma=False
    )
```

```python
import functools

import jax
import jax.numpy as jnp
from jax import lax
from jax.experimental import pallas as pl
from jax.experimental.pallas import tpu as pltpu
from jax.sharding import PartitionSpec as P

LAYERS = 2
VMEM_LIMIT = 16 * 1024 * 1024
VMEM = pl.BlockSpec(memory_space=pltpu.VMEM)
ANY = pl.BlockSpec(memory_space=pl.ANY)


def pair_teams(team_index, column, team_count):
    columns = team_count // 2
    return 2 * lax.rem(team_index // 2 + column, columns) + lax.rem(team_index, 2)


def source_team(team, turn, team_count):
    if team_count == 4:
        return (2 * (team % 2) + team // 2) ^ (0, 2, 1, 3)[turn]
    return (team + turn) % team_count


def norm_columns(degrees):
    return jnp.transpose(lax.rsqrt(degrees.astype(jnp.float32)))


def prepare_kernel(
    degrees_ref, embeddings_ref, tiles_ref, after_ref, held_tiles_ref, own_ref, norm_ref, panel_ref, sems
):
    del after_ref
    share_rows, width = own_ref.shape
    block_count, tile_size = degrees_ref.shape
    team_index = lax.axis_index("rep")
    at = pl.ds(pl.multiple_of(team_index * share_rows, share_rows), share_rows)
    tiles_copy = pltpu.make_async_copy(tiles_ref, held_tiles_ref, sems.at[0])
    own_copy = pltpu.make_async_copy(embeddings_ref.at[at, :], own_ref, sems.at[1])
    tiles_copy.start()
    own_copy.start()
    norms = norm_columns(degrees_ref[...])
    for block in range(block_count):
        panel_ref[block * tile_size : (block + 1) * tile_size, :] = jnp.broadcast_to(
            norms[:, block : block + 1], (tile_size, width)
        )
    norm_ref[...] = panel_ref[at, :]
    own_copy.wait()
    tiles_copy.wait()


def prepare(degrees, embeddings, tile_values, after):
    panel_rows, width = embeddings.shape
    share = jax.ShapeDtypeStruct((panel_rows // lax.axis_size("rep"), width), jnp.float32)
    return pl.pallas_call(
        prepare_kernel,
        out_shape=[jax.ShapeDtypeStruct(tile_values.shape, tile_values.dtype), share, share],
        in_specs=[VMEM, ANY, ANY, ANY],
        out_specs=[VMEM] * 3,
        scratch_shapes=[pltpu.VMEM((panel_rows, width), jnp.float32), pltpu.SemaphoreType.DMA((2,))],
        compiler_params=pltpu.CompilerParams(vmem_limit_bytes=VMEM_LIMIT),
        cost_estimate=pl.CostEstimate(
            flops=panel_rows * width, bytes_accessed=4 * panel_rows * width, transcendentals=0
        ),
    )(degrees, embeddings, tile_values, after)


def arc_kernel(info_ref, tiles_ref, *refs, team_count, piece_count, scaled, partial_count):
    columns = team_count // 2
    pieces, refs = refs[:piece_count], refs[piece_count:]
    partials, refs = refs[:partial_count], refs[partial_count:]
    outs, (split_ref, sums_ref) = refs[:team_count], refs[team_count:]
    team_index = lax.axis_index("rep")
    slot_total, tile_size, _ = tiles_ref.shape
    panel_rows, width = split_ref.shape[0], split_ref.shape[1] // 2
    share_rows = panel_rows // team_count
    block_count = panel_rows // tile_size

    def split(value, at):
        high = value.astype(jnp.bfloat16)
        split_ref[at, :width] = high
        split_ref[at, width:] = (value - high.astype(jnp.float32)).astype(jnp.bfloat16)

    if scaled:
        degrees_ref, panel_ref = pieces
        norms = norm_columns(degrees_ref[...])
        for block in range(block_count):
            at = pl.ds(block * tile_size, tile_size)
            split(panel_ref[at, :] * norms[:, block : block + 1], at)
    else:
        for k in range(piece_count):
            owner = source_team(team_index, k, team_count)
            split(pieces[k][...], pl.ds(pl.multiple_of(owner * share_rows, share_rows), share_rows))
    sums_ref[...] = jnp.zeros_like(sums_ref)
    live_count = info_ref[0, 0]
    for j in range(slot_total):
        source = pl.multiple_of(info_ref[1 + slot_total + j, 0] * tile_size, tile_size)
        product = jnp.dot(
            tiles_ref[j],
            split_ref[pl.ds(source, tile_size), :],
            preferred_element_type=jnp.float32,
        )
        row = jnp.where(j < live_count, info_ref[1 + j, 0], block_count)
        at = pl.ds(pl.multiple_of(row * tile_size, tile_size), tile_size)
        sums_ref[at, :] += product[:, :width] + product[:, width:]

    for parity in range(2):
        for column in range(columns):
            team = pair_teams(team_index, column, team_count)
            team = team if parity == 0 else team ^ 1
            value = sums_ref[pl.ds(pl.multiple_of(team * share_rows, share_rows), share_rows), :]
            at = parity * columns + column
            outs[at][...] = value + partials[at][...] if partials else value


def arc_step(info, tiles, pieces, partials, scaled):
    team_count = lax.axis_size("rep")
    panel_rows = pieces[1].shape[0] if scaled else sum(piece.shape[0] for piece in pieces)
    width = pieces[1].shape[1]
    slot_total, tile_size, _ = tiles.shape
    share = jax.ShapeDtypeStruct((panel_rows // team_count, width), jnp.float32)
    operands = [info, tiles, *pieces, *partials]
    return pl.pallas_call(
        functools.partial(
            arc_kernel,
            team_count=team_count,
            piece_count=len(pieces),
            scaled=scaled,
            partial_count=len(partials),
        ),
        out_shape=[share] * team_count,
        in_specs=[VMEM] * len(operands),
        out_specs=[VMEM] * team_count,
        scratch_shapes=[
            pltpu.VMEM((panel_rows, 2 * width), jnp.bfloat16),
            pltpu.VMEM((panel_rows + tile_size, width), jnp.float32),
        ],
        compiler_params=pltpu.CompilerParams(vmem_limit_bytes=VMEM_LIMIT),
        cost_estimate=pl.CostEstimate(
            flops=4 * slot_total * tile_size * tile_size * width, bytes_accessed=8 * panel_rows * width, transcendentals=0
        ),
    )(*operands)


def fetch(value, source_team, arc_length):
    cycle, team_count = lax.axis_size("blk"), lax.axis_size("rep")
    pairs = []
    for shard in range(cycle):
        for team in range(team_count):
            to_shard = (shard + team * arc_length) % cycle
            pairs.append((shard * team_count + source_team(team), to_shard * team_count + team))
    return lax.ppermute(value, ("blk", "rep"), pairs)


def next_shard(value):
    cycle = lax.axis_size("blk")
    return lax.ppermute(value, "blk", [(i, (i + 1) % cycle) for i in range(cycle)])


def from_mate(value):
    team_count = lax.axis_size("rep")
    return lax.ppermute(value, "rep", [(team, team ^ 1) for team in range(team_count)])


def from_column(value, distance):
    team_count = lax.axis_size("rep")
    pairs = [((team + 2 * distance) % team_count, team) for team in range(team_count)]
    return lax.ppermute(value, "rep", pairs)


def team_terms(sums):
    columns = len(sums) // 2
    others = []
    for distance in range(1, columns):
        at = columns - distance
        others.append(from_column(sums[at] + from_mate(sums[columns + at]), distance))
    return [sums[0], from_mate(sums[columns]), *others]


def finish_kernel(base_ref, norm_ref, *refs, layer_count):
    *terms, out_hbm, held_ref, sems = refs
    pieces = sems.shape[0]
    rows = held_ref.shape[0] // pieces
    copies = []
    for piece in range(pieces):
        at = pl.ds(piece * rows, rows)
        total = terms[0][at, :]
        for term_ref in terms[1:]:
            total = total + term_ref[at, :]
        held_ref[at, :] = (base_ref[at, :] + total * norm_ref[at, :]) / layer_count
        copies.append(pltpu.make_async_copy(held_ref.at[at, :], out_hbm.at[at, :], sems.at[piece]))
        copies[-1].start()
    for copy in copies:
        copy.wait()


def finish(base, norm_scale, terms):
    return pl.pallas_call(
        functools.partial(finish_kernel, layer_count=LAYERS + 1.0),
        out_shape=jax.ShapeDtypeStruct(base.shape, jnp.float32),
        in_specs=[VMEM] * (2 + len(terms)),
        out_specs=ANY,
        scratch_shapes=[pltpu.VMEM(base.shape, jnp.float32), pltpu.SemaphoreType.DMA((2,))],
        compiler_params=pltpu.CompilerParams(vmem_limit_bytes=VMEM_LIMIT),
    )(base, norm_scale, *terms)


def per_device(embeddings, degrees, tile_values, tile_rows, tile_columns, slot_counts):
    arc_length, _, tile_size, _ = tile_values.shape[2:]
    panel_rows = embeddings.shape[0]
    team_count = lax.axis_size("rep")
    spread = (3, 1, 2, 0) if team_count == 4 else tuple(range(team_count))
    degrees = degrees.reshape(panel_rows // tile_size, tile_size)

    panel = fetch(embeddings, lambda team: spread[team], arc_length)
    beside = (1, 3, 0, 2) if team_count == 4 else tuple((team + 1) % team_count for team in range(team_count))
    pieces = [fetch(degrees, lambda team: beside[team], arc_length), panel]
    info = jnp.concatenate([slot_counts[0, 0][:, None], tile_rows[0, 0], tile_columns[0, 0]], axis=1)
    info = jnp.broadcast_to(info[:, :, None], (*info.shape, embeddings.shape[1]))
    info = [info[at] for at in range(arc_length)]
    tiles, own, norm_scale = prepare(degrees, embeddings, tile_values[0, 0], info[0])

    combined = own
    for layer in range(LAYERS):
        sums = ()
        for arc_slot in range(arc_length):
            sums = arc_step(info[arc_slot], tiles[arc_slot], pieces, sums, layer == 0)
            if arc_slot + 1 < arc_length:
                pieces = [next_shard(piece) for piece in pieces]
        terms = team_terms(sums)
        if layer + 1 == LAYERS:
            return finish(combined, norm_scale, terms)
        current = functools.reduce(jnp.add, terms) * norm_scale
        combined = combined + current
        source = current * norm_scale
        pieces = [
            fetch(source, lambda team, k=k: source_team(team, k, team_count), arc_length)
            for k in range(team_count)
        ]


def solution(mesh):
    in_specs = (
        P(("groups", "blk"), None),
        P(("groups", "blk")),
        P(("groups", "blk"), "rep", None, None, None, None),
        P(("groups", "blk"), "rep", None, None),
        P(("groups", "blk"), "rep", None, None),
        P(("groups", "blk"), "rep", None),
    )
    out_specs = P(("groups", "blk", "rep"), None)
    return jax.shard_map(
        per_device, mesh=mesh, in_specs=in_specs, out_specs=out_specs, check_vma=False
    )
```

```python
import functools

import jax
import jax.numpy as jnp
from jax import lax
from jax.experimental import pallas as pl
from jax.experimental.pallas import tpu as pltpu
from jax.sharding import PartitionSpec as P

LAYERS = 2
VMEM_LIMIT = 16 * 1024 * 1024
VMEM = pl.BlockSpec(memory_space=pltpu.VMEM)
ANY = pl.BlockSpec(memory_space=pl.ANY)


def pair_teams(team_index, column, team_count):
    columns = team_count // 2
    return 2 * lax.rem(team_index // 2 + column, columns) + lax.rem(team_index, 2)


def source_team(team, turn, team_count):
    if team_count == 4:
        return (2 * (team % 2) + team // 2) ^ (0, 3, 2, 1)[turn]
    return (team + turn) % team_count


def norm_columns(degrees):
    return jnp.transpose(lax.rsqrt(degrees.astype(jnp.float32)))


def prepare_kernel(
    degrees_ref, embeddings_ref, tiles_ref, after_ref, held_tiles_ref, own_ref, norm_ref, panel_ref, sems
):
    del after_ref
    share_rows, width = own_ref.shape
    block_count, tile_size = degrees_ref.shape
    team_index = lax.axis_index("rep")
    at = pl.ds(pl.multiple_of(team_index * share_rows, share_rows), share_rows)
    tiles_copy = pltpu.make_async_copy(tiles_ref, held_tiles_ref, sems.at[0])
    own_copy = pltpu.make_async_copy(embeddings_ref.at[at, :], own_ref, sems.at[1])
    tiles_copy.start()
    own_copy.start()
    norms = norm_columns(degrees_ref[...])
    for block in range(block_count):
        panel_ref[block * tile_size : (block + 1) * tile_size, :] = jnp.broadcast_to(
            norms[:, block : block + 1], (tile_size, width)
        )
    norm_ref[...] = panel_ref[at, :]
    own_copy.wait()
    tiles_copy.wait()


def prepare(degrees, embeddings, tile_values, after):
    panel_rows, width = embeddings.shape
    share = jax.ShapeDtypeStruct((panel_rows // lax.axis_size("rep"), width), jnp.float32)
    return pl.pallas_call(
        prepare_kernel,
        out_shape=[jax.ShapeDtypeStruct(tile_values.shape, tile_values.dtype), share, share],
        in_specs=[VMEM, ANY, ANY, ANY],
        out_specs=[VMEM] * 3,
        scratch_shapes=[pltpu.VMEM((panel_rows, width), jnp.float32), pltpu.SemaphoreType.DMA((2,))],
        compiler_params=pltpu.CompilerParams(vmem_limit_bytes=VMEM_LIMIT),
        cost_estimate=pl.CostEstimate(
            flops=panel_rows * width, bytes_accessed=4 * panel_rows * width, transcendentals=0
        ),
    )(degrees, embeddings, tile_values, after)


def arc_kernel(info_ref, tiles_ref, *refs, team_count, piece_count, scaled, partial_count):
    columns = team_count // 2
    pieces, refs = refs[:piece_count], refs[piece_count:]
    partials, refs = refs[:partial_count], refs[partial_count:]
    outs, (split_ref, sums_ref) = refs[:team_count], refs[team_count:]
    team_index = lax.axis_index("rep")
    slot_total, tile_size, _ = tiles_ref.shape
    panel_rows, width = split_ref.shape[0], split_ref.shape[1] // 2
    share_rows = panel_rows // team_count
    block_count = panel_rows // tile_size

    def split(value, at):
        high = value.astype(jnp.bfloat16)
        split_ref[at, :width] = high
        split_ref[at, width:] = (value - high.astype(jnp.float32)).astype(jnp.bfloat16)

    if scaled:
        degrees_ref, panel_ref = pieces
        norms = norm_columns(degrees_ref[...])
        for block in range(block_count):
            at = pl.ds(block * tile_size, tile_size)
            split(panel_ref[at, :] * norms[:, block : block + 1], at)
    else:
        for k in range(piece_count):
            owner = source_team(team_index, k, team_count)
            split(pieces[k][...], pl.ds(pl.multiple_of(owner * share_rows, share_rows), share_rows))
    sums_ref[...] = jnp.zeros_like(sums_ref)
    live_count = info_ref[0, 0]
    for j in range(slot_total):
        source = pl.multiple_of(info_ref[1 + slot_total + j, 0] * tile_size, tile_size)
        product = jnp.dot(
            tiles_ref[j],
            split_ref[pl.ds(source, tile_size), :],
            preferred_element_type=jnp.float32,
        )
        row = jnp.where(j < live_count, info_ref[1 + j, 0], block_count)
        at = pl.ds(pl.multiple_of(row * tile_size, tile_size), tile_size)
        sums_ref[at, :] += product[:, :width] + product[:, width:]

    for parity in range(2):
        for column in range(columns):
            team = pair_teams(team_index, column, team_count)
            team = team if parity == 0 else team ^ 1
            value = sums_ref[pl.ds(pl.multiple_of(team * share_rows, share_rows), share_rows), :]
            at = parity * columns + column
            outs[at][...] = value + partials[at][...] if partials else value


def arc_step(info, tiles, pieces, partials, scaled):
    team_count = lax.axis_size("rep")
    panel_rows = pieces[1].shape[0] if scaled else sum(piece.shape[0] for piece in pieces)
    width = pieces[1].shape[1]
    slot_total, tile_size, _ = tiles.shape
    share = jax.ShapeDtypeStruct((panel_rows // team_count, width), jnp.float32)
    operands = [info, tiles, *pieces, *partials]
    return pl.pallas_call(
        functools.partial(
            arc_kernel,
            team_count=team_count,
            piece_count=len(pieces),
            scaled=scaled,
            partial_count=len(partials),
        ),
        out_shape=[share] * team_count,
        in_specs=[VMEM] * len(operands),
        out_specs=[VMEM] * team_count,
        scratch_shapes=[
            pltpu.VMEM((panel_rows, 2 * width), jnp.bfloat16),
            pltpu.VMEM((panel_rows + tile_size, width), jnp.float32),
        ],
        compiler_params=pltpu.CompilerParams(vmem_limit_bytes=VMEM_LIMIT),
        cost_estimate=pl.CostEstimate(
            flops=4 * slot_total * tile_size * tile_size * width, bytes_accessed=8 * panel_rows * width, transcendentals=0
        ),
    )(*operands)


def fetch(value, source_team, arc_length):
    cycle, team_count = lax.axis_size("blk"), lax.axis_size("rep")
    pairs = []
    for shard in range(cycle):
        for team in range(team_count):
            to_shard = (shard + team * arc_length) % cycle
            pairs.append((shard * team_count + source_team(team), to_shard * team_count + team))
    return lax.ppermute(value, ("blk", "rep"), pairs)


def next_shard(value):
    cycle = lax.axis_size("blk")
    return lax.ppermute(value, "blk", [(i, (i + 1) % cycle) for i in range(cycle)])


def from_mate(value):
    team_count = lax.axis_size("rep")
    return lax.ppermute(value, "rep", [(team, team ^ 1) for team in range(team_count)])


def from_column(value, distance):
    team_count = lax.axis_size("rep")
    pairs = [((team + 2 * distance) % team_count, team) for team in range(team_count)]
    return lax.ppermute(value, "rep", pairs)


def team_terms(sums):
    columns = len(sums) // 2
    others = []
    for distance in range(1, columns):
        at = columns - distance
        others.append(from_column(sums[at] + from_mate(sums[columns + at]), distance))
    return [sums[0], from_mate(sums[columns]), *others]


def finish_kernel(base_ref, norm_ref, *refs, layer_count):
    *terms, out_hbm, held_ref, sems = refs
    pieces = sems.shape[0]
    rows = held_ref.shape[0] // pieces
    copies = []
    for piece in range(pieces):
        at = pl.ds(piece * rows, rows)
        total = terms[0][at, :]
        for term_ref in terms[1:]:
            total = total + term_ref[at, :]
        held_ref[at, :] = (base_ref[at, :] + total * norm_ref[at, :]) / layer_count
        copies.append(pltpu.make_async_copy(held_ref.at[at, :], out_hbm.at[at, :], sems.at[piece]))
        copies[-1].start()
    for copy in copies:
        copy.wait()


def finish(base, norm_scale, terms):
    return pl.pallas_call(
        functools.partial(finish_kernel, layer_count=LAYERS + 1.0),
        out_shape=jax.ShapeDtypeStruct(base.shape, jnp.float32),
        in_specs=[VMEM] * (2 + len(terms)),
        out_specs=ANY,
        scratch_shapes=[pltpu.VMEM(base.shape, jnp.float32), pltpu.SemaphoreType.DMA((2,))],
        compiler_params=pltpu.CompilerParams(vmem_limit_bytes=VMEM_LIMIT),
    )(base, norm_scale, *terms)


def per_device(embeddings, degrees, tile_values, tile_rows, tile_columns, slot_counts):
    arc_length, _, tile_size, _ = tile_values.shape[2:]
    panel_rows = embeddings.shape[0]
    team_count = lax.axis_size("rep")
    spread = (3, 1, 2, 0) if team_count == 4 else tuple(range(team_count))
    degrees = degrees.reshape(panel_rows // tile_size, tile_size)

    panel = fetch(embeddings, lambda team: spread[team], arc_length)
    pieces = [fetch(degrees, lambda team: spread[team], arc_length), panel]
    info = jnp.concatenate([slot_counts[0, 0][:, None], tile_rows[0, 0], tile_columns[0, 0]], axis=1)
    info = jnp.broadcast_to(info[:, :, None], (*info.shape, embeddings.shape[1]))
    info = [info[at] for at in range(arc_length)]
    tiles, own, norm_scale = prepare(degrees, embeddings, tile_values[0, 0], info[0])

    combined = own
    for layer in range(LAYERS):
        sums = ()
        for arc_slot in range(arc_length):
            sums = arc_step(info[arc_slot], tiles[arc_slot], pieces, sums, layer == 0)
            if arc_slot + 1 < arc_length:
                pieces = [next_shard(piece) for piece in pieces]
        terms = team_terms(sums)
        if layer + 1 == LAYERS:
            return finish(combined, norm_scale, terms)
        current = functools.reduce(jnp.add, terms) * norm_scale
        combined = combined + current
        source = current * norm_scale
        pieces = [
            fetch(source, lambda team, k=k: source_team(team, k, team_count), arc_length)
            for k in range(team_count)
        ]


def solution(mesh):
    in_specs = (
        P(("groups", "blk"), None),
        P(("groups", "blk")),
        P(("groups", "blk"), "rep", None, None, None, None),
        P(("groups", "blk"), "rep", None, None),
        P(("groups", "blk"), "rep", None, None),
        P(("groups", "blk"), "rep", None),
    )
    out_specs = P(("groups", "blk", "rep"), None)
    return jax.shard_map(
        per_device, mesh=mesh, in_specs=in_specs, out_specs=out_specs, check_vma=False
    )
```

```python
import functools

import jax
import jax.numpy as jnp
from jax import lax
from jax.experimental import pallas as pl
from jax.experimental.pallas import tpu as pltpu
from jax.sharding import PartitionSpec as P

LAYERS = 2
VMEM_LIMIT = 16 * 1024 * 1024
VMEM = pl.BlockSpec(memory_space=pltpu.VMEM)
ANY = pl.BlockSpec(memory_space=pl.ANY)


def pair_teams(team_index, column, team_count):
    columns = team_count // 2
    return 2 * lax.rem(team_index // 2 + column, columns) + lax.rem(team_index, 2)


def source_team(team, turn, team_count):
    if team_count == 4:
        return (2 * (team % 2) + team // 2) ^ (3, 0, 2, 1)[turn]
    return (team + turn) % team_count


def norm_columns(degrees):
    return jnp.transpose(lax.rsqrt(degrees.astype(jnp.float32)))


def prepare_kernel(
    degrees_ref, embeddings_ref, tiles_ref, after_ref, held_tiles_ref, own_ref, norm_ref, panel_ref, sems
):
    del after_ref
    share_rows, width = own_ref.shape
    block_count, tile_size = degrees_ref.shape
    team_index = lax.axis_index("rep")
    at = pl.ds(pl.multiple_of(team_index * share_rows, share_rows), share_rows)
    tiles_copy = pltpu.make_async_copy(tiles_ref, held_tiles_ref, sems.at[0])
    own_copy = pltpu.make_async_copy(embeddings_ref.at[at, :], own_ref, sems.at[1])
    tiles_copy.start()
    own_copy.start()
    norms = norm_columns(degrees_ref[...])
    for block in range(block_count):
        panel_ref[block * tile_size : (block + 1) * tile_size, :] = jnp.broadcast_to(
            norms[:, block : block + 1], (tile_size, width)
        )
    norm_ref[...] = panel_ref[at, :]
    own_copy.wait()
    tiles_copy.wait()


def prepare(degrees, embeddings, tile_values, after):
    panel_rows, width = embeddings.shape
    share = jax.ShapeDtypeStruct((panel_rows // lax.axis_size("rep"), width), jnp.float32)
    return pl.pallas_call(
        prepare_kernel,
        out_shape=[jax.ShapeDtypeStruct(tile_values.shape, tile_values.dtype), share, share],
        in_specs=[VMEM, ANY, ANY, ANY],
        out_specs=[VMEM] * 3,
        scratch_shapes=[pltpu.VMEM((panel_rows, width), jnp.float32), pltpu.SemaphoreType.DMA((2,))],
        compiler_params=pltpu.CompilerParams(vmem_limit_bytes=VMEM_LIMIT),
        cost_estimate=pl.CostEstimate(
            flops=panel_rows * width, bytes_accessed=4 * panel_rows * width, transcendentals=0
        ),
    )(degrees, embeddings, tile_values, after)


def arc_kernel(info_ref, tiles_ref, *refs, team_count, piece_count, scaled, partial_count):
    columns = team_count // 2
    pieces, refs = refs[:piece_count], refs[piece_count:]
    partials, refs = refs[:partial_count], refs[partial_count:]
    outs, (split_ref, sums_ref) = refs[:team_count], refs[team_count:]
    team_index = lax.axis_index("rep")
    slot_total, tile_size, _ = tiles_ref.shape
    panel_rows, width = split_ref.shape[0], split_ref.shape[1] // 2
    share_rows = panel_rows // team_count
    block_count = panel_rows // tile_size

    def split(value, at):
        high = value.astype(jnp.bfloat16)
        split_ref[at, :width] = high
        split_ref[at, width:] = (value - high.astype(jnp.float32)).astype(jnp.bfloat16)

    if scaled:
        degrees_ref, panel_ref = pieces
        norms = norm_columns(degrees_ref[...])
        for block in range(block_count):
            at = pl.ds(block * tile_size, tile_size)
            split(panel_ref[at, :] * norms[:, block : block + 1], at)
    else:
        for k in range(piece_count):
            owner = source_team(team_index, k, team_count)
            split(pieces[k][...], pl.ds(pl.multiple_of(owner * share_rows, share_rows), share_rows))
    sums_ref[...] = jnp.zeros_like(sums_ref)
    live_count = info_ref[0, 0]
    for j in range(slot_total):
        source = pl.multiple_of(info_ref[1 + slot_total + j, 0] * tile_size, tile_size)
        product = jnp.dot(
            tiles_ref[j],
            split_ref[pl.ds(source, tile_size), :],
            preferred_element_type=jnp.float32,
        )
        row = jnp.where(j < live_count, info_ref[1 + j, 0], block_count)
        at = pl.ds(pl.multiple_of(row * tile_size, tile_size), tile_size)
        sums_ref[at, :] += product[:, :width] + product[:, width:]

    for parity in range(2):
        for column in range(columns):
            team = pair_teams(team_index, column, team_count)
            team = team if parity == 0 else team ^ 1
            value = sums_ref[pl.ds(pl.multiple_of(team * share_rows, share_rows), share_rows), :]
            at = parity * columns + column
            outs[at][...] = value + partials[at][...] if partials else value


def arc_step(info, tiles, pieces, partials, scaled):
    team_count = lax.axis_size("rep")
    panel_rows = pieces[1].shape[0] if scaled else sum(piece.shape[0] for piece in pieces)
    width = pieces[1].shape[1]
    slot_total, tile_size, _ = tiles.shape
    share = jax.ShapeDtypeStruct((panel_rows // team_count, width), jnp.float32)
    operands = [info, tiles, *pieces, *partials]
    return pl.pallas_call(
        functools.partial(
            arc_kernel,
            team_count=team_count,
            piece_count=len(pieces),
            scaled=scaled,
            partial_count=len(partials),
        ),
        out_shape=[share] * team_count,
        in_specs=[VMEM] * len(operands),
        out_specs=[VMEM] * team_count,
        scratch_shapes=[
            pltpu.VMEM((panel_rows, 2 * width), jnp.bfloat16),
            pltpu.VMEM((panel_rows + tile_size, width), jnp.float32),
        ],
        compiler_params=pltpu.CompilerParams(vmem_limit_bytes=VMEM_LIMIT),
        cost_estimate=pl.CostEstimate(
            flops=4 * slot_total * tile_size * tile_size * width, bytes_accessed=8 * panel_rows * width, transcendentals=0
        ),
    )(*operands)


def fetch(value, source_team, arc_length):
    cycle, team_count = lax.axis_size("blk"), lax.axis_size("rep")
    pairs = []
    for shard in range(cycle):
        for team in range(team_count):
            to_shard = (shard + team * arc_length) % cycle
            pairs.append((shard * team_count + source_team(team), to_shard * team_count + team))
    return lax.ppermute(value, ("blk", "rep"), pairs)


def next_shard(value):
    cycle = lax.axis_size("blk")
    return lax.ppermute(value, "blk", [(i, (i + 1) % cycle) for i in range(cycle)])


def from_mate(value):
    team_count = lax.axis_size("rep")
    return lax.ppermute(value, "rep", [(team, team ^ 1) for team in range(team_count)])


def from_column(value, distance):
    team_count = lax.axis_size("rep")
    pairs = [((team + 2 * distance) % team_count, team) for team in range(team_count)]
    return lax.ppermute(value, "rep", pairs)


def team_terms(sums):
    columns = len(sums) // 2
    others = []
    for distance in range(1, columns):
        at = columns - distance
        others.append(from_column(sums[at] + from_mate(sums[columns + at]), distance))
    return [sums[0], from_mate(sums[columns]), *others]


def finish_kernel(base_ref, norm_ref, *refs, layer_count):
    *terms, out_hbm, held_ref, sems = refs
    pieces = sems.shape[0]
    rows = held_ref.shape[0] // pieces
    copies = []
    for piece in range(pieces):
        at = pl.ds(piece * rows, rows)
        total = terms[0][at, :]
        for term_ref in terms[1:]:
            total = total + term_ref[at, :]
        held_ref[at, :] = (base_ref[at, :] + total * norm_ref[at, :]) / layer_count
        copies.append(pltpu.make_async_copy(held_ref.at[at, :], out_hbm.at[at, :], sems.at[piece]))
        copies[-1].start()
    for copy in copies:
        copy.wait()


def finish(base, norm_scale, terms):
    return pl.pallas_call(
        functools.partial(finish_kernel, layer_count=LAYERS + 1.0),
        out_shape=jax.ShapeDtypeStruct(base.shape, jnp.float32),
        in_specs=[VMEM] * (2 + len(terms)),
        out_specs=ANY,
        scratch_shapes=[pltpu.VMEM(base.shape, jnp.float32), pltpu.SemaphoreType.DMA((2,))],
        compiler_params=pltpu.CompilerParams(vmem_limit_bytes=VMEM_LIMIT),
    )(base, norm_scale, *terms)


def per_device(embeddings, degrees, tile_values, tile_rows, tile_columns, slot_counts):
    arc_length, _, tile_size, _ = tile_values.shape[2:]
    panel_rows = embeddings.shape[0]
    team_count = lax.axis_size("rep")
    spread = (3, 1, 2, 0) if team_count == 4 else tuple(range(team_count))
    degrees = degrees.reshape(panel_rows // tile_size, tile_size)

    panel = fetch(embeddings, lambda team: spread[team], arc_length)
    pieces = [fetch(degrees, lambda team: spread[team], arc_length), panel]
    info = jnp.concatenate([slot_counts[0, 0][:, None], tile_rows[0, 0], tile_columns[0, 0]], axis=1)
    info = jnp.broadcast_to(info[:, :, None], (*info.shape, embeddings.shape[1]))
    info = [info[at] for at in range(arc_length)]
    tiles, own, norm_scale = prepare(degrees, embeddings, tile_values[0, 0], info[0])

    combined = own
    for layer in range(LAYERS):
        sums = ()
        for arc_slot in range(arc_length):
            sums = arc_step(info[arc_slot], tiles[arc_slot], pieces, sums, layer == 0)
            if arc_slot + 1 < arc_length:
                pieces = [next_shard(piece) for piece in pieces]
        terms = team_terms(sums)
        if layer + 1 == LAYERS:
            return finish(combined, norm_scale, terms)
        current = functools.reduce(jnp.add, terms) * norm_scale
        combined = combined + current
        source = current * norm_scale
        pieces = [
            fetch(source, lambda team, k=k: source_team(team, k, team_count), arc_length)
            for k in range(team_count)
        ]


def solution(mesh):
    in_specs = (
        P(("groups", "blk"), None),
        P(("groups", "blk")),
        P(("groups", "blk"), "rep", None, None, None, None),
        P(("groups", "blk"), "rep", None, None),
        P(("groups", "blk"), "rep", None, None),
        P(("groups", "blk"), "rep", None),
    )
    out_specs = P(("groups", "blk", "rep"), None)
    return jax.shard_map(
        per_device, mesh=mesh, in_specs=in_specs, out_specs=out_specs, check_vma=False
    )
```

```python
import functools

import jax
import jax.numpy as jnp
from jax import lax
from jax.experimental import pallas as pl
from jax.experimental.pallas import tpu as pltpu
from jax.sharding import PartitionSpec as P

LAYERS = 2
VMEM_LIMIT = 16 * 1024 * 1024
VMEM = pl.BlockSpec(memory_space=pltpu.VMEM)
ANY = pl.BlockSpec(memory_space=pl.ANY)


def pair_teams(team_index, column, team_count):
    columns = team_count // 2
    return 2 * lax.rem(team_index // 2 + column, columns) + lax.rem(team_index, 2)


def source_team(team, turn, team_count):
    if team_count == 4:
        return (2 * (team % 2) + team // 2) ^ (0, 2, 1, 3)[turn]
    return (team + turn) % team_count


def norm_columns(degrees):
    return jnp.transpose(lax.rsqrt(degrees.astype(jnp.float32)))


def prepare_kernel(
    degrees_ref, embeddings_ref, tiles_ref, after_ref, held_tiles_ref, own_ref, norm_ref, panel_ref, sems
):
    del after_ref
    share_rows, width = own_ref.shape
    block_count, tile_size = degrees_ref.shape
    team_index = lax.axis_index("rep")
    at = pl.ds(pl.multiple_of(team_index * share_rows, share_rows), share_rows)
    tiles_copy = pltpu.make_async_copy(tiles_ref, held_tiles_ref, sems.at[0])
    own_copy = pltpu.make_async_copy(embeddings_ref.at[at, :], own_ref, sems.at[1])
    tiles_copy.start()
    own_copy.start()
    norms = norm_columns(degrees_ref[...])
    for block in range(block_count):
        panel_ref[block * tile_size : (block + 1) * tile_size, :] = jnp.broadcast_to(
            norms[:, block : block + 1], (tile_size, width)
        )
    norm_ref[...] = panel_ref[at, :]
    own_copy.wait()
    tiles_copy.wait()


def prepare(degrees, embeddings, tile_values, after):
    panel_rows, width = embeddings.shape
    share = jax.ShapeDtypeStruct((panel_rows // lax.axis_size("rep"), width), jnp.float32)
    return pl.pallas_call(
        prepare_kernel,
        out_shape=[jax.ShapeDtypeStruct(tile_values.shape, tile_values.dtype), share, share],
        in_specs=[VMEM, ANY, ANY, ANY],
        out_specs=[VMEM] * 3,
        scratch_shapes=[pltpu.VMEM((panel_rows, width), jnp.float32), pltpu.SemaphoreType.DMA((2,))],
        compiler_params=pltpu.CompilerParams(vmem_limit_bytes=VMEM_LIMIT),
        cost_estimate=pl.CostEstimate(
            flops=panel_rows * width, bytes_accessed=4 * panel_rows * width, transcendentals=0
        ),
    )(degrees, embeddings, tile_values, after)


def arc_kernel(info_ref, tiles_ref, *refs, team_count, piece_count, scaled, partial_count):
    columns = team_count // 2
    pieces, refs = refs[:piece_count], refs[piece_count:]
    partials, refs = refs[:partial_count], refs[partial_count:]
    outs, (split_ref, sums_ref) = refs[:team_count], refs[team_count:]
    team_index = lax.axis_index("rep")
    slot_total, tile_size, _ = tiles_ref.shape
    panel_rows, width = split_ref.shape[0], split_ref.shape[1] // 2
    share_rows = panel_rows // team_count
    block_count = panel_rows // tile_size

    def split(value, at):
        high = value.astype(jnp.bfloat16)
        split_ref[at, :width] = high
        split_ref[at, width:] = (value - high.astype(jnp.float32)).astype(jnp.bfloat16)

    if scaled:
        degrees_ref, panel_ref = pieces
        norms = norm_columns(degrees_ref[...])
        for block in range(block_count):
            at = pl.ds(block * tile_size, tile_size)
            split(panel_ref[at, :] * norms[:, block : block + 1], at)
    else:
        for k in range(piece_count):
            owner = source_team(team_index, k, team_count)
            split(pieces[k][...], pl.ds(pl.multiple_of(owner * share_rows, share_rows), share_rows))
    sums_ref[...] = jnp.zeros_like(sums_ref)
    live_count = info_ref[0, 0]
    for j in range(slot_total):
        source = pl.multiple_of(info_ref[1 + slot_total + j, 0] * tile_size, tile_size)
        product = jnp.dot(
            tiles_ref[j],
            split_ref[pl.ds(source, tile_size), :],
            preferred_element_type=jnp.float32,
        )
        row = jnp.where(j < live_count, info_ref[1 + j, 0], block_count)
        at = pl.ds(pl.multiple_of(row * tile_size, tile_size), tile_size)
        sums_ref[at, :] += product[:, :width] + product[:, width:]

    for parity in range(2):
        for column in range(columns):
            team = pair_teams(team_index, column, team_count)
            team = team if parity == 0 else team ^ 1
            value = sums_ref[pl.ds(pl.multiple_of(team * share_rows, share_rows), share_rows), :]
            at = parity * columns + column
            outs[at][...] = value + partials[at][...] if partials else value


def arc_step(info, tiles, pieces, partials, scaled):
    team_count = lax.axis_size("rep")
    panel_rows = pieces[1].shape[0] if scaled else sum(piece.shape[0] for piece in pieces)
    width = pieces[1].shape[1]
    slot_total, tile_size, _ = tiles.shape
    share = jax.ShapeDtypeStruct((panel_rows // team_count, width), jnp.float32)
    operands = [info, tiles, *pieces, *partials]
    return pl.pallas_call(
        functools.partial(
            arc_kernel,
            team_count=team_count,
            piece_count=len(pieces),
            scaled=scaled,
            partial_count=len(partials),
        ),
        out_shape=[share] * team_count,
        in_specs=[VMEM] * len(operands),
        out_specs=[VMEM] * team_count,
        scratch_shapes=[
            pltpu.VMEM((panel_rows, 2 * width), jnp.bfloat16),
            pltpu.VMEM((panel_rows + tile_size, width), jnp.float32),
        ],
        compiler_params=pltpu.CompilerParams(vmem_limit_bytes=VMEM_LIMIT),
        cost_estimate=pl.CostEstimate(
            flops=4 * slot_total * tile_size * tile_size * width, bytes_accessed=8 * panel_rows * width, transcendentals=0
        ),
    )(*operands)


def fetch(value, source, arc_length):
    cycle, team_count = lax.axis_size("blk"), lax.axis_size("rep")
    pairs = []
    for shard in range(cycle):
        for team in range(team_count):
            to_shard = (shard + team * arc_length) % cycle
            pairs.append((shard * team_count + source(shard, team), to_shard * team_count + team))
    return lax.ppermute(value, ("blk", "rep"), pairs)


def next_shard(value):
    cycle = lax.axis_size("blk")
    return lax.ppermute(value, "blk", [(i, (i + 1) % cycle) for i in range(cycle)])


def from_mate(value):
    team_count = lax.axis_size("rep")
    return lax.ppermute(value, "rep", [(team, team ^ 1) for team in range(team_count)])


def from_column(value, distance):
    team_count = lax.axis_size("rep")
    pairs = [((team + 2 * distance) % team_count, team) for team in range(team_count)]
    return lax.ppermute(value, "rep", pairs)


def team_terms(sums):
    columns = len(sums) // 2
    others = []
    for distance in range(1, columns):
        at = columns - distance
        others.append(from_column(sums[at] + from_mate(sums[columns + at]), distance))
    return [sums[0], from_mate(sums[columns]), *others]


def finish_kernel(base_ref, norm_ref, *refs, layer_count):
    *terms, out_hbm, held_ref, sems = refs
    pieces = sems.shape[0]
    rows = held_ref.shape[0] // pieces
    copies = []
    for piece in range(pieces):
        at = pl.ds(piece * rows, rows)
        total = terms[0][at, :]
        for term_ref in terms[1:]:
            total = total + term_ref[at, :]
        held_ref[at, :] = (base_ref[at, :] + total * norm_ref[at, :]) / layer_count
        copies.append(pltpu.make_async_copy(held_ref.at[at, :], out_hbm.at[at, :], sems.at[piece]))
        copies[-1].start()
    for copy in copies:
        copy.wait()


def finish(base, norm_scale, terms):
    return pl.pallas_call(
        functools.partial(finish_kernel, layer_count=LAYERS + 1.0),
        out_shape=jax.ShapeDtypeStruct(base.shape, jnp.float32),
        in_specs=[VMEM] * (2 + len(terms)),
        out_specs=ANY,
        scratch_shapes=[pltpu.VMEM(base.shape, jnp.float32), pltpu.SemaphoreType.DMA((2,))],
        compiler_params=pltpu.CompilerParams(vmem_limit_bytes=VMEM_LIMIT),
    )(base, norm_scale, *terms)


def per_device(embeddings, degrees, tile_values, tile_rows, tile_columns, slot_counts):
    arc_length, _, tile_size, _ = tile_values.shape[2:]
    panel_rows = embeddings.shape[0]
    cycle, team_count = lax.axis_size("blk"), lax.axis_size("rep")
    spread = [tuple(range(team_count))] * cycle
    if (cycle, team_count) == (4, 4):
        spread = [(2, 1, 0, 3), (0, 1, 2, 3), (3, 0, 2, 1), (0, 1, 2, 3)]
    degrees = degrees.reshape(panel_rows // tile_size, tile_size)

    panel = fetch(embeddings, lambda shard, team: spread[shard][team], arc_length)
    pieces = [fetch(degrees, lambda shard, team: spread[shard][team], arc_length), panel]
    info = jnp.concatenate([slot_counts[0, 0][:, None], tile_rows[0, 0], tile_columns[0, 0]], axis=1)
    info = jnp.broadcast_to(info[:, :, None], (*info.shape, embeddings.shape[1]))
    info = [info[at] for at in range(arc_length)]
    tiles, own, norm_scale = prepare(degrees, embeddings, tile_values[0, 0], info[0])

    combined = own
    for layer in range(LAYERS):
        sums = ()
        for arc_slot in range(arc_length):
            sums = arc_step(info[arc_slot], tiles[arc_slot], pieces, sums, layer == 0)
            if arc_slot + 1 < arc_length:
                pieces = [next_shard(piece) for piece in pieces]
        terms = team_terms(sums)
        if layer + 1 == LAYERS:
            return finish(combined, norm_scale, terms)
        current = functools.reduce(jnp.add, terms) * norm_scale
        combined = combined + current
        source = current * norm_scale
        pieces = [
            fetch(source, lambda shard, team, k=k: source_team(team, k, team_count), arc_length)
            for k in range(team_count)
        ]


def solution(mesh):
    in_specs = (
        P(("groups", "blk"), None),
        P(("groups", "blk")),
        P(("groups", "blk"), "rep", None, None, None, None),
        P(("groups", "blk"), "rep", None, None),
        P(("groups", "blk"), "rep", None, None),
        P(("groups", "blk"), "rep", None),
    )
    out_specs = P(("groups", "blk", "rep"), None)
    return jax.shard_map(
        per_device, mesh=mesh, in_specs=in_specs, out_specs=out_specs, check_vma=False
    )
```

```python
import functools

import jax
import jax.numpy as jnp
from jax import lax
from jax.experimental import pallas as pl
from jax.experimental.pallas import tpu as pltpu
from jax.sharding import PartitionSpec as P

LAYERS = 2
VMEM_LIMIT = 16 * 1024 * 1024
VMEM = pl.BlockSpec(memory_space=pltpu.VMEM)
ANY = pl.BlockSpec(memory_space=pl.ANY)


def pair_teams(team_index, column, team_count):
    columns = team_count // 2
    return 2 * lax.rem(team_index // 2 + column, columns) + lax.rem(team_index, 2)


def source_team(shard, team, turn, team_count):
    if team_count == 4:
        row, first_row = (0, 2, 1, 3)[turn], (1, 2, 0, 3)[turn]
        return (2 * (team % 2) + team // 2) ^ row ^ ((shard == 0) * (row ^ first_row))
    return (team + turn) % team_count


def norm_columns(degrees):
    return jnp.transpose(lax.rsqrt(degrees.astype(jnp.float32)))


def prepare_kernel(
    degrees_ref, embeddings_ref, tiles_ref, after_ref, held_tiles_ref, own_ref, norm_ref, panel_ref, sems
):
    del after_ref
    share_rows, width = own_ref.shape
    block_count, tile_size = degrees_ref.shape
    team_index = lax.axis_index("rep")
    at = pl.ds(pl.multiple_of(team_index * share_rows, share_rows), share_rows)
    tiles_copy = pltpu.make_async_copy(tiles_ref, held_tiles_ref, sems.at[0])
    own_copy = pltpu.make_async_copy(embeddings_ref.at[at, :], own_ref, sems.at[1])
    tiles_copy.start()
    own_copy.start()
    norms = norm_columns(degrees_ref[...])
    for block in range(block_count):
        panel_ref[block * tile_size : (block + 1) * tile_size, :] = jnp.broadcast_to(
            norms[:, block : block + 1], (tile_size, width)
        )
    norm_ref[...] = panel_ref[at, :]
    own_copy.wait()
    tiles_copy.wait()


def prepare(degrees, embeddings, tile_values, after):
    panel_rows, width = embeddings.shape
    share = jax.ShapeDtypeStruct((panel_rows // lax.axis_size("rep"), width), jnp.float32)
    return pl.pallas_call(
        prepare_kernel,
        out_shape=[jax.ShapeDtypeStruct(tile_values.shape, tile_values.dtype), share, share],
        in_specs=[VMEM, ANY, ANY, ANY],
        out_specs=[VMEM] * 3,
        scratch_shapes=[pltpu.VMEM((panel_rows, width), jnp.float32), pltpu.SemaphoreType.DMA((2,))],
        compiler_params=pltpu.CompilerParams(vmem_limit_bytes=VMEM_LIMIT),
        cost_estimate=pl.CostEstimate(
            flops=panel_rows * width, bytes_accessed=4 * panel_rows * width, transcendentals=0
        ),
    )(degrees, embeddings, tile_values, after)


def arc_kernel(info_ref, tiles_ref, *refs, team_count, arc_length, arc_slot, piece_count, scaled, partial_count):
    columns = team_count // 2
    pieces, refs = refs[:piece_count], refs[piece_count:]
    partials, refs = refs[:partial_count], refs[partial_count:]
    outs, (split_ref, sums_ref) = refs[:team_count], refs[team_count:]
    team_index = lax.axis_index("rep")
    slot_total, tile_size, _ = tiles_ref.shape
    panel_rows, width = split_ref.shape[0], split_ref.shape[1] // 2
    share_rows = panel_rows // team_count
    block_count = panel_rows // tile_size

    def split(value, at):
        high = value.astype(jnp.bfloat16)
        split_ref[at, :width] = high
        split_ref[at, width:] = (value - high.astype(jnp.float32)).astype(jnp.bfloat16)

    if scaled:
        degrees_ref, panel_ref = pieces
        norms = norm_columns(degrees_ref[...])
        for block in range(block_count):
            at = pl.ds(block * tile_size, tile_size)
            split(panel_ref[at, :] * norms[:, block : block + 1], at)
    else:
        cycle = lax.axis_size("blk")
        shard = lax.rem(lax.axis_index("blk") + cycle - lax.rem(team_index * arc_length + arc_slot, cycle), cycle)
        for k in range(piece_count):
            owner = source_team(shard, team_index, k, team_count)
            split(pieces[k][...], pl.ds(pl.multiple_of(owner * share_rows, share_rows), share_rows))
    sums_ref[...] = jnp.zeros_like(sums_ref)
    live_count = info_ref[0, 0]
    for j in range(slot_total):
        source = pl.multiple_of(info_ref[1 + slot_total + j, 0] * tile_size, tile_size)
        product = jnp.dot(
            tiles_ref[j],
            split_ref[pl.ds(source, tile_size), :],
            preferred_element_type=jnp.float32,
        )
        row = jnp.where(j < live_count, info_ref[1 + j, 0], block_count)
        at = pl.ds(pl.multiple_of(row * tile_size, tile_size), tile_size)
        sums_ref[at, :] += product[:, :width] + product[:, width:]

    for parity in range(2):
        for column in range(columns):
            team = pair_teams(team_index, column, team_count)
            team = team if parity == 0 else team ^ 1
            value = sums_ref[pl.ds(pl.multiple_of(team * share_rows, share_rows), share_rows), :]
            at = parity * columns + column
            outs[at][...] = value + partials[at][...] if partials else value


def arc_step(info, tiles, pieces, partials, scaled, arc_length, arc_slot):
    team_count = lax.axis_size("rep")
    panel_rows = pieces[1].shape[0] if scaled else sum(piece.shape[0] for piece in pieces)
    width = pieces[1].shape[1]
    slot_total, tile_size, _ = tiles.shape
    share = jax.ShapeDtypeStruct((panel_rows // team_count, width), jnp.float32)
    operands = [info, tiles, *pieces, *partials]
    return pl.pallas_call(
        functools.partial(
            arc_kernel,
            team_count=team_count,
            arc_length=arc_length,
            arc_slot=arc_slot,
            piece_count=len(pieces),
            scaled=scaled,
            partial_count=len(partials),
        ),
        out_shape=[share] * team_count,
        in_specs=[VMEM] * len(operands),
        out_specs=[VMEM] * team_count,
        scratch_shapes=[
            pltpu.VMEM((panel_rows, 2 * width), jnp.bfloat16),
            pltpu.VMEM((panel_rows + tile_size, width), jnp.float32),
        ],
        compiler_params=pltpu.CompilerParams(vmem_limit_bytes=VMEM_LIMIT),
        cost_estimate=pl.CostEstimate(
            flops=4 * slot_total * tile_size * tile_size * width, bytes_accessed=8 * panel_rows * width, transcendentals=0
        ),
    )(*operands)


def fetch(value, source, arc_length):
    cycle, team_count = lax.axis_size("blk"), lax.axis_size("rep")
    pairs = []
    for shard in range(cycle):
        for team in range(team_count):
            to_shard = (shard + team * arc_length) % cycle
            pairs.append((shard * team_count + source(shard, team), to_shard * team_count + team))
    return lax.ppermute(value, ("blk", "rep"), pairs)


def next_shard(value):
    cycle = lax.axis_size("blk")
    return lax.ppermute(value, "blk", [(i, (i + 1) % cycle) for i in range(cycle)])


def from_mate(value):
    team_count = lax.axis_size("rep")
    return lax.ppermute(value, "rep", [(team, team ^ 1) for team in range(team_count)])


def from_column(value, distance):
    team_count = lax.axis_size("rep")
    pairs = [((team + 2 * distance) % team_count, team) for team in range(team_count)]
    return lax.ppermute(value, "rep", pairs)


def team_terms(sums):
    columns = len(sums) // 2
    others = []
    for distance in range(1, columns):
        at = columns - distance
        others.append(from_column(sums[at] + from_mate(sums[columns + at]), distance))
    return [sums[0], from_mate(sums[columns]), *others]


def finish_kernel(base_ref, norm_ref, *refs, layer_count):
    *terms, out_hbm, held_ref, sems = refs
    pieces = sems.shape[0]
    rows = held_ref.shape[0] // pieces
    copies = []
    for piece in range(pieces):
        at = pl.ds(piece * rows, rows)
        total = terms[0][at, :]
        for term_ref in terms[1:]:
            total = total + term_ref[at, :]
        held_ref[at, :] = (base_ref[at, :] + total * norm_ref[at, :]) / layer_count
        copies.append(pltpu.make_async_copy(held_ref.at[at, :], out_hbm.at[at, :], sems.at[piece]))
        copies[-1].start()
    for copy in copies:
        copy.wait()


def finish(base, norm_scale, terms):
    return pl.pallas_call(
        functools.partial(finish_kernel, layer_count=LAYERS + 1.0),
        out_shape=jax.ShapeDtypeStruct(base.shape, jnp.float32),
        in_specs=[VMEM] * (2 + len(terms)),
        out_specs=ANY,
        scratch_shapes=[pltpu.VMEM(base.shape, jnp.float32), pltpu.SemaphoreType.DMA((2,))],
        compiler_params=pltpu.CompilerParams(vmem_limit_bytes=VMEM_LIMIT),
    )(base, norm_scale, *terms)


def per_device(embeddings, degrees, tile_values, tile_rows, tile_columns, slot_counts):
    arc_length, _, tile_size, _ = tile_values.shape[2:]
    panel_rows = embeddings.shape[0]
    team_count = lax.axis_size("rep")
    spread = (3, 1, 2, 0) if team_count == 4 else tuple(range(team_count))
    degrees = degrees.reshape(panel_rows // tile_size, tile_size)

    panel = fetch(embeddings, lambda shard, team: spread[team], arc_length)
    pieces = [fetch(degrees, lambda shard, team: spread[team], arc_length), panel]
    info = jnp.concatenate([slot_counts[0, 0][:, None], tile_rows[0, 0], tile_columns[0, 0]], axis=1)
    info = jnp.broadcast_to(info[:, :, None], (*info.shape, embeddings.shape[1]))
    info = [info[at] for at in range(arc_length)]
    tiles, own, norm_scale = prepare(degrees, embeddings, tile_values[0, 0], info[0])

    combined = own
    for layer in range(LAYERS):
        sums = ()
        for arc_slot in range(arc_length):
            sums = arc_step(info[arc_slot], tiles[arc_slot], pieces, sums, layer == 0, arc_length, arc_slot)
            if arc_slot + 1 < arc_length:
                pieces = [next_shard(piece) for piece in pieces]
        terms = team_terms(sums)
        if layer + 1 == LAYERS:
            return finish(combined, norm_scale, terms)
        current = functools.reduce(jnp.add, terms) * norm_scale
        combined = combined + current
        source = current * norm_scale
        pieces = [
            fetch(source, lambda shard, team, k=k: source_team(shard, team, k, team_count), arc_length)
            for k in range(team_count)
        ]


def solution(mesh):
    in_specs = (
        P(("groups", "blk"), None),
        P(("groups", "blk")),
        P(("groups", "blk"), "rep", None, None, None, None),
        P(("groups", "blk"), "rep", None, None),
        P(("groups", "blk"), "rep", None, None),
        P(("groups", "blk"), "rep", None),
    )
    out_specs = P(("groups", "blk", "rep"), None)
    return jax.shard_map(
        per_device, mesh=mesh, in_specs=in_specs, out_specs=out_specs, check_vma=False
    )
```

```python
import functools

import jax
import jax.numpy as jnp
from jax import lax
from jax.experimental import pallas as pl
from jax.experimental.pallas import tpu as pltpu
from jax.sharding import PartitionSpec as P

LAYERS = 2
VMEM_LIMIT = 16 * 1024 * 1024
VMEM = pl.BlockSpec(memory_space=pltpu.VMEM)
ANY = pl.BlockSpec(memory_space=pl.ANY)


def pair_teams(team_index, column, team_count):
    columns = team_count // 2
    return 2 * lax.rem(team_index // 2 + column, columns) + lax.rem(team_index, 2)


def source_team(team, turn, team_count):
    if team_count == 4:
        return (3 * (team % 2)) ^ (team // 2) ^ (3, 0, 1, 2)[turn]
    return (team + turn) % team_count


def norm_columns(degrees):
    return jnp.transpose(lax.rsqrt(degrees.astype(jnp.float32)))


def prepare_kernel(
    degrees_ref, embeddings_ref, tiles_ref, after_ref, held_tiles_ref, own_ref, norm_ref, panel_ref, sems
):
    del after_ref
    share_rows, width = own_ref.shape
    block_count, tile_size = degrees_ref.shape
    team_index = lax.axis_index("rep")
    at = pl.ds(pl.multiple_of(team_index * share_rows, share_rows), share_rows)
    tiles_copy = pltpu.make_async_copy(tiles_ref, held_tiles_ref, sems.at[0])
    own_copy = pltpu.make_async_copy(embeddings_ref.at[at, :], own_ref, sems.at[1])
    tiles_copy.start()
    own_copy.start()
    norms = norm_columns(degrees_ref[...])
    for block in range(block_count):
        panel_ref[block * tile_size : (block + 1) * tile_size, :] = jnp.broadcast_to(
            norms[:, block : block + 1], (tile_size, width)
        )
    norm_ref[...] = panel_ref[at, :]
    own_copy.wait()
    tiles_copy.wait()


def prepare(degrees, embeddings, tile_values, after):
    panel_rows, width = embeddings.shape
    share = jax.ShapeDtypeStruct((panel_rows // lax.axis_size("rep"), width), jnp.float32)
    return pl.pallas_call(
        prepare_kernel,
        out_shape=[jax.ShapeDtypeStruct(tile_values.shape, tile_values.dtype), share, share],
        in_specs=[VMEM, ANY, ANY, ANY],
        out_specs=[VMEM] * 3,
        scratch_shapes=[pltpu.VMEM((panel_rows, width), jnp.float32), pltpu.SemaphoreType.DMA((2,))],
        compiler_params=pltpu.CompilerParams(vmem_limit_bytes=VMEM_LIMIT),
        cost_estimate=pl.CostEstimate(
            flops=panel_rows * width, bytes_accessed=4 * panel_rows * width, transcendentals=0
        ),
    )(degrees, embeddings, tile_values, after)


def arc_kernel(info_ref, tiles_ref, *refs, team_count, piece_count, scaled, partial_count):
    columns = team_count // 2
    pieces, refs = refs[:piece_count], refs[piece_count:]
    partials, refs = refs[:partial_count], refs[partial_count:]
    outs, (split_ref, sums_ref) = refs[:team_count], refs[team_count:]
    team_index = lax.axis_index("rep")
    slot_total, tile_size, _ = tiles_ref.shape
    panel_rows, width = split_ref.shape[0], split_ref.shape[1] // 2
    share_rows = panel_rows // team_count
    block_count = panel_rows // tile_size

    def split(value, at):
        high = value.astype(jnp.bfloat16)
        split_ref[at, :width] = high
        split_ref[at, width:] = (value - high.astype(jnp.float32)).astype(jnp.bfloat16)

    if scaled:
        degrees_ref, panel_ref = pieces
        norms = norm_columns(degrees_ref[...])
        for block in range(block_count):
            at = pl.ds(block * tile_size, tile_size)
            split(panel_ref[at, :] * norms[:, block : block + 1], at)
    else:
        for k in range(piece_count):
            owner = source_team(team_index, k, team_count)
            split(pieces[k][...], pl.ds(pl.multiple_of(owner * share_rows, share_rows), share_rows))
    sums_ref[...] = jnp.zeros_like(sums_ref)
    live_count = info_ref[0, 0]
    for j in range(slot_total):
        source = pl.multiple_of(info_ref[1 + slot_total + j, 0] * tile_size, tile_size)
        product = jnp.dot(
            tiles_ref[j],
            split_ref[pl.ds(source, tile_size), :],
            preferred_element_type=jnp.float32,
        )
        row = jnp.where(j < live_count, info_ref[1 + j, 0], block_count)
        at = pl.ds(pl.multiple_of(row * tile_size, tile_size), tile_size)
        sums_ref[at, :] += product[:, :width] + product[:, width:]

    for parity in range(2):
        for column in range(columns):
            team = pair_teams(team_index, column, team_count)
            team = team if parity == 0 else team ^ 1
            value = sums_ref[pl.ds(pl.multiple_of(team * share_rows, share_rows), share_rows), :]
            at = parity * columns + column
            outs[at][...] = value + partials[at][...] if partials else value


def arc_step(info, tiles, pieces, partials, scaled):
    team_count = lax.axis_size("rep")
    panel_rows = pieces[1].shape[0] if scaled else sum(piece.shape[0] for piece in pieces)
    width = pieces[1].shape[1]
    slot_total, tile_size, _ = tiles.shape
    share = jax.ShapeDtypeStruct((panel_rows // team_count, width), jnp.float32)
    operands = [info, tiles, *pieces, *partials]
    return pl.pallas_call(
        functools.partial(
            arc_kernel,
            team_count=team_count,
            piece_count=len(pieces),
            scaled=scaled,
            partial_count=len(partials),
        ),
        out_shape=[share] * team_count,
        in_specs=[VMEM] * len(operands),
        out_specs=[VMEM] * team_count,
        scratch_shapes=[
            pltpu.VMEM((panel_rows, 2 * width), jnp.bfloat16),
            pltpu.VMEM((panel_rows + tile_size, width), jnp.float32),
        ],
        compiler_params=pltpu.CompilerParams(vmem_limit_bytes=VMEM_LIMIT),
        cost_estimate=pl.CostEstimate(
            flops=4 * slot_total * tile_size * tile_size * width, bytes_accessed=8 * panel_rows * width, transcendentals=0
        ),
    )(*operands)


def fetch(value, source_team, arc_length):
    cycle, team_count = lax.axis_size("blk"), lax.axis_size("rep")
    pairs = []
    for shard in range(cycle):
        for team in range(team_count):
            to_shard = (shard + team * arc_length) % cycle
            pairs.append((shard * team_count + source_team(team), to_shard * team_count + team))
    return lax.ppermute(value, ("blk", "rep"), pairs)


def next_shard(value):
    cycle = lax.axis_size("blk")
    return lax.ppermute(value, "blk", [(i, (i + 1) % cycle) for i in range(cycle)])


def from_mate(value):
    team_count = lax.axis_size("rep")
    return lax.ppermute(value, "rep", [(team, team ^ 1) for team in range(team_count)])


def from_column(value, distance):
    team_count = lax.axis_size("rep")
    pairs = [((team + 2 * distance) % team_count, team) for team in range(team_count)]
    return lax.ppermute(value, "rep", pairs)


def team_terms(sums):
    columns = len(sums) // 2
    others = []
    for distance in range(1, columns):
        at = columns - distance
        others.append(from_column(sums[at] + from_mate(sums[columns + at]), distance))
    return [sums[0], from_mate(sums[columns]), *others]


def finish_kernel(base_ref, norm_ref, *refs, layer_count):
    *terms, out_hbm, held_ref, sems = refs
    pieces = sems.shape[0]
    rows = held_ref.shape[0] // pieces
    copies = []
    for piece in range(pieces):
        at = pl.ds(piece * rows, rows)
        total = terms[0][at, :]
        for term_ref in terms[1:]:
            total = total + term_ref[at, :]
        held_ref[at, :] = (base_ref[at, :] + total * norm_ref[at, :]) / layer_count
        copies.append(pltpu.make_async_copy(held_ref.at[at, :], out_hbm.at[at, :], sems.at[piece]))
        copies[-1].start()
    for copy in copies:
        copy.wait()


def finish(base, norm_scale, terms):
    return pl.pallas_call(
        functools.partial(finish_kernel, layer_count=LAYERS + 1.0),
        out_shape=jax.ShapeDtypeStruct(base.shape, jnp.float32),
        in_specs=[VMEM] * (2 + len(terms)),
        out_specs=ANY,
        scratch_shapes=[pltpu.VMEM(base.shape, jnp.float32), pltpu.SemaphoreType.DMA((2,))],
        compiler_params=pltpu.CompilerParams(vmem_limit_bytes=VMEM_LIMIT),
    )(base, norm_scale, *terms)


def per_device(embeddings, degrees, tile_values, tile_rows, tile_columns, slot_counts):
    arc_length, _, tile_size, _ = tile_values.shape[2:]
    panel_rows = embeddings.shape[0]
    team_count = lax.axis_size("rep")
    spread = (3, 1, 2, 0) if team_count == 4 else tuple(range(team_count))
    degrees = degrees.reshape(panel_rows // tile_size, tile_size)

    panel = fetch(embeddings, lambda team: spread[team], arc_length)
    pieces = [fetch(degrees, lambda team: spread[team], arc_length), panel]
    info = jnp.concatenate([slot_counts[0, 0][:, None], tile_rows[0, 0], tile_columns[0, 0]], axis=1)
    info = jnp.broadcast_to(info[:, :, None], (*info.shape, embeddings.shape[1]))
    info = [info[at] for at in range(arc_length)]
    tiles, own, norm_scale = prepare(degrees, embeddings, tile_values[0, 0], info[0])

    combined = own
    for layer in range(LAYERS):
        sums = ()
        for arc_slot in range(arc_length):
            sums = arc_step(info[arc_slot], tiles[arc_slot], pieces, sums, layer == 0)
            if arc_slot + 1 < arc_length:
                pieces = [next_shard(piece) for piece in pieces]
        terms = team_terms(sums)
        if layer + 1 == LAYERS:
            return finish(combined, norm_scale, terms)
        current = functools.reduce(jnp.add, terms) * norm_scale
        combined = combined + current
        source = current * norm_scale
        pieces = [
            fetch(source, lambda team, k=k: source_team(team, k, team_count), arc_length)
            for k in range(team_count)
        ]


def solution(mesh):
    in_specs = (
        P(("groups", "blk"), None),
        P(("groups", "blk")),
        P(("groups", "blk"), "rep", None, None, None, None),
        P(("groups", "blk"), "rep", None, None),
        P(("groups", "blk"), "rep", None, None),
        P(("groups", "blk"), "rep", None),
    )
    out_specs = P(("groups", "blk", "rep"), None)
    return jax.shard_map(
        per_device, mesh=mesh, in_specs=in_specs, out_specs=out_specs, check_vma=False
    )
```

```python
import functools

import jax
import jax.numpy as jnp
from jax import lax
from jax.experimental import pallas as pl
from jax.experimental.pallas import tpu as pltpu
from jax.sharding import PartitionSpec as P

LAYERS = 2
VMEM_LIMIT = 16 * 1024 * 1024
VMEM = pl.BlockSpec(memory_space=pltpu.VMEM)
ANY = pl.BlockSpec(memory_space=pl.ANY)


def pair_teams(team_index, column, team_count):
    columns = team_count // 2
    return 2 * lax.rem(team_index // 2 + column, columns) + lax.rem(team_index, 2)


def source_team(team, turn, team_count):
    if team_count == 4:
        return (2 * (team % 2) + team // 2) ^ (0, 2, 1, 3)[turn]
    return (team + turn) % team_count


def norm_columns(degrees):
    return jnp.transpose(lax.rsqrt(degrees.astype(jnp.float32)))


def prepare_kernel(
    degrees_ref, embeddings_ref, tiles_ref, after_ref, held_tiles_ref, own_ref, norm_ref, panel_ref, sems
):
    del after_ref
    share_rows, width = own_ref.shape
    block_count, tile_size = degrees_ref.shape
    team_index = lax.axis_index("rep")
    at = pl.ds(pl.multiple_of(team_index * share_rows, share_rows), share_rows)
    tiles_copy = pltpu.make_async_copy(tiles_ref, held_tiles_ref, sems.at[0])
    own_copy = pltpu.make_async_copy(embeddings_ref.at[at, :], own_ref, sems.at[1])
    tiles_copy.start()
    own_copy.start()
    norms = norm_columns(degrees_ref[...])
    for block in range(block_count):
        panel_ref[block * tile_size : (block + 1) * tile_size, :] = jnp.broadcast_to(
            norms[:, block : block + 1], (tile_size, width)
        )
    norm_ref[...] = panel_ref[at, :]
    own_copy.wait()
    tiles_copy.wait()


def prepare(degrees, embeddings, tile_values, after):
    panel_rows, width = embeddings.shape
    share = jax.ShapeDtypeStruct((panel_rows // lax.axis_size("rep"), width), jnp.float32)
    return pl.pallas_call(
        prepare_kernel,
        out_shape=[jax.ShapeDtypeStruct(tile_values.shape, tile_values.dtype), share, share],
        in_specs=[VMEM, ANY, ANY, ANY],
        out_specs=[VMEM] * 3,
        scratch_shapes=[pltpu.VMEM((panel_rows, width), jnp.float32), pltpu.SemaphoreType.DMA((2,))],
        compiler_params=pltpu.CompilerParams(vmem_limit_bytes=VMEM_LIMIT),
        cost_estimate=pl.CostEstimate(
            flops=panel_rows * width, bytes_accessed=4 * panel_rows * width, transcendentals=0
        ),
    )(degrees, embeddings, tile_values, after)


def arc_kernel(info_ref, tiles_ref, *refs, team_count, piece_count, scaled, partial_count):
    columns = team_count // 2
    pieces, refs = refs[:piece_count], refs[piece_count:]
    partials, refs = refs[:partial_count], refs[partial_count:]
    outs, (split_ref, sums_ref) = refs[:team_count], refs[team_count:]
    team_index = lax.axis_index("rep")
    slot_total, tile_size, _ = tiles_ref.shape
    panel_rows, width = split_ref.shape[0], split_ref.shape[1] // 2
    share_rows = panel_rows // team_count
    block_count = panel_rows // tile_size

    def split(value, at):
        high = value.astype(jnp.bfloat16)
        split_ref[at, :width] = high
        split_ref[at, width:] = (value - high.astype(jnp.float32)).astype(jnp.bfloat16)

    if scaled:
        degrees_ref, panel_ref = pieces
        norms = norm_columns(degrees_ref[...])
        for block in range(block_count):
            at = pl.ds(block * tile_size, tile_size)
            split(panel_ref[at, :] * norms[:, block : block + 1], at)
    else:
        for k in range(piece_count):
            owner = source_team(team_index, k, team_count)
            split(pieces[k][...], pl.ds(pl.multiple_of(owner * share_rows, share_rows), share_rows))
    sums_ref[...] = jnp.zeros_like(sums_ref)
    live_count = info_ref[0, 0]
    for j in range(slot_total):
        source = pl.multiple_of(info_ref[1 + slot_total + j, 0] * tile_size, tile_size)
        product = jnp.dot(
            tiles_ref[j],
            split_ref[pl.ds(source, tile_size), :],
            preferred_element_type=jnp.float32,
        )
        row = jnp.where(j < live_count, info_ref[1 + j, 0], block_count)
        at = pl.ds(pl.multiple_of(row * tile_size, tile_size), tile_size)
        sums_ref[at, :] += product[:, :width] + product[:, width:]

    for parity in range(2):
        for column in range(columns):
            team = pair_teams(team_index, column, team_count)
            team = team if parity == 0 else team ^ 1
            value = sums_ref[pl.ds(pl.multiple_of(team * share_rows, share_rows), share_rows), :]
            at = parity * columns + column
            outs[at][...] = value + partials[at][...] if partials else value


def arc_step(info, tiles, pieces, partials, scaled):
    team_count = lax.axis_size("rep")
    panel_rows = pieces[1].shape[0] if scaled else sum(piece.shape[0] for piece in pieces)
    width = pieces[1].shape[1]
    slot_total, tile_size, _ = tiles.shape
    share = jax.ShapeDtypeStruct((panel_rows // team_count, width), jnp.float32)
    operands = [info, tiles, *pieces, *partials]
    return pl.pallas_call(
        functools.partial(
            arc_kernel,
            team_count=team_count,
            piece_count=len(pieces),
            scaled=scaled,
            partial_count=len(partials),
        ),
        out_shape=[share] * team_count,
        in_specs=[VMEM] * len(operands),
        out_specs=[VMEM] * team_count,
        scratch_shapes=[
            pltpu.VMEM((panel_rows, 2 * width), jnp.bfloat16),
            pltpu.VMEM((panel_rows + tile_size, width), jnp.float32),
        ],
        compiler_params=pltpu.CompilerParams(vmem_limit_bytes=VMEM_LIMIT),
        cost_estimate=pl.CostEstimate(
            flops=4 * slot_total * tile_size * tile_size * width, bytes_accessed=8 * panel_rows * width, transcendentals=0
        ),
    )(*operands)


def fetch(value, source_team, arc_length):
    cycle, team_count = lax.axis_size("blk"), lax.axis_size("rep")
    pairs = []
    for shard in range(cycle):
        for team in range(team_count):
            to_shard = (shard + team * arc_length) % cycle
            pairs.append((shard * team_count + source_team(team), to_shard * team_count + team))
    return lax.ppermute(value, ("blk", "rep"), pairs)


def next_shard(value):
    cycle = lax.axis_size("blk")
    return lax.ppermute(value, "blk", [(i, (i + 1) % cycle) for i in range(cycle)])


def from_mate(value):
    team_count = lax.axis_size("rep")
    return lax.ppermute(value, "rep", [(team, team ^ 1) for team in range(team_count)])


def from_column(value, distance):
    team_count = lax.axis_size("rep")
    pairs = [((team + 2 * distance) % team_count, team) for team in range(team_count)]
    return lax.ppermute(value, "rep", pairs)


def team_terms(sums):
    columns = len(sums) // 2
    others = []
    for distance in range(1, columns):
        at = columns - distance
        others.append(from_column(sums[at] + from_mate(sums[columns + at]), distance))
    return [sums[0], from_mate(sums[columns]), *others]


def finish_kernel(base_ref, norm_ref, *refs, layer_count):
    *terms, out_hbm, held_ref, sems = refs
    pieces = sems.shape[0]
    rows = held_ref.shape[0] // pieces
    copies = []
    for piece in range(pieces):
        at = pl.ds(piece * rows, rows)
        total = terms[0][at, :]
        for term_ref in terms[1:]:
            total = total + term_ref[at, :]
        held_ref[at, :] = (base_ref[at, :] + total * norm_ref[at, :]) / layer_count
        copies.append(pltpu.make_async_copy(held_ref.at[at, :], out_hbm.at[at, :], sems.at[piece]))
        copies[-1].start()
    for copy in copies:
        copy.wait()


def finish(base, norm_scale, terms):
    return pl.pallas_call(
        functools.partial(finish_kernel, layer_count=LAYERS + 1.0),
        out_shape=jax.ShapeDtypeStruct(base.shape, jnp.float32),
        in_specs=[VMEM] * (2 + len(terms)),
        out_specs=ANY,
        scratch_shapes=[pltpu.VMEM(base.shape, jnp.float32), pltpu.SemaphoreType.DMA((2,))],
        compiler_params=pltpu.CompilerParams(vmem_limit_bytes=VMEM_LIMIT),
    )(base, norm_scale, *terms)


def per_device(embeddings, degrees, tile_values, tile_rows, tile_columns, slot_counts):
    arc_length, _, tile_size, _ = tile_values.shape[2:]
    panel_rows = embeddings.shape[0]
    team_count = lax.axis_size("rep")
    spread = (3, 0, 2, 1) if team_count == 4 else tuple(range(team_count))
    degrees = degrees.reshape(panel_rows // tile_size, tile_size)

    panel = fetch(embeddings, lambda team: spread[team], arc_length)
    pieces = [fetch(degrees, lambda team: spread[team], arc_length), panel]
    info = jnp.concatenate([slot_counts[0, 0][:, None], tile_rows[0, 0], tile_columns[0, 0]], axis=1)
    info = jnp.broadcast_to(info[:, :, None], (*info.shape, embeddings.shape[1]))
    info = [info[at] for at in range(arc_length)]
    tiles, own, norm_scale = prepare(degrees, embeddings, tile_values[0, 0], info[0])

    combined = own
    for layer in range(LAYERS):
        sums = ()
        for arc_slot in range(arc_length):
            sums = arc_step(info[arc_slot], tiles[arc_slot], pieces, sums, layer == 0)
            if arc_slot + 1 < arc_length:
                pieces = [next_shard(piece) for piece in pieces]
        terms = team_terms(sums)
        if layer + 1 == LAYERS:
            return finish(combined, norm_scale, terms)
        current = functools.reduce(jnp.add, terms) * norm_scale
        combined = combined + current
        source = current * norm_scale
        pieces = [
            fetch(source, lambda team, k=k: source_team(team, k, team_count), arc_length)
            for k in range(team_count)
        ]


def solution(mesh):
    in_specs = (
        P(("groups", "blk"), None),
        P(("groups", "blk")),
        P(("groups", "blk"), "rep", None, None, None, None),
        P(("groups", "blk"), "rep", None, None),
        P(("groups", "blk"), "rep", None, None),
        P(("groups", "blk"), "rep", None),
    )
    out_specs = P(("groups", "blk", "rep"), None)
    return jax.shard_map(
        per_device, mesh=mesh, in_specs=in_specs, out_specs=out_specs, check_vma=False
    )
```

```python
import functools

import jax
import jax.numpy as jnp
from jax import lax
from jax.experimental import pallas as pl
from jax.experimental.pallas import tpu as pltpu
from jax.sharding import PartitionSpec as P

LAYERS = 2
VMEM_LIMIT = 16 * 1024 * 1024
VMEM = pl.BlockSpec(memory_space=pltpu.VMEM)
ANY = pl.BlockSpec(memory_space=pl.ANY)


def pair_teams(team_index, column, team_count):
    columns = team_count // 2
    return 2 * lax.rem(team_index // 2 + column, columns) + lax.rem(team_index, 2)


def source_team(team, turn, team_count):
    if team_count == 4:
        return (2 * (team % 2) + team // 2) ^ (0, 2, 1, 3)[turn]
    return (team + turn) % team_count


def norm_columns(degrees):
    return jnp.transpose(lax.rsqrt(degrees.astype(jnp.float32)))


def prepare_kernel(
    degrees_ref, embeddings_ref, tiles_ref, after_ref, held_tiles_ref, own_ref, norm_ref, panel_ref, sems
):
    del after_ref
    share_rows, width = own_ref.shape
    block_count, tile_size = degrees_ref.shape
    team_index = lax.axis_index("rep")
    at = pl.ds(pl.multiple_of(team_index * share_rows, share_rows), share_rows)
    tiles_copy = pltpu.make_async_copy(tiles_ref, held_tiles_ref, sems.at[0])
    own_copy = pltpu.make_async_copy(embeddings_ref.at[at, :], own_ref, sems.at[1])
    tiles_copy.start()
    own_copy.start()
    norms = norm_columns(degrees_ref[...])
    for block in range(block_count):
        panel_ref[block * tile_size : (block + 1) * tile_size, :] = jnp.broadcast_to(
            norms[:, block : block + 1], (tile_size, width)
        )
    norm_ref[...] = panel_ref[at, :]
    own_copy.wait()
    tiles_copy.wait()


def prepare(degrees, embeddings, tile_values, after):
    panel_rows, width = embeddings.shape
    share = jax.ShapeDtypeStruct((panel_rows // lax.axis_size("rep"), width), jnp.float32)
    return pl.pallas_call(
        prepare_kernel,
        out_shape=[jax.ShapeDtypeStruct(tile_values.shape, tile_values.dtype), share, share],
        in_specs=[VMEM, ANY, ANY, ANY],
        out_specs=[VMEM] * 3,
        scratch_shapes=[pltpu.VMEM((panel_rows, width), jnp.float32), pltpu.SemaphoreType.DMA((2,))],
        compiler_params=pltpu.CompilerParams(vmem_limit_bytes=VMEM_LIMIT),
        cost_estimate=pl.CostEstimate(
            flops=panel_rows * width, bytes_accessed=4 * panel_rows * width, transcendentals=0
        ),
    )(degrees, embeddings, tile_values, after)


def arc_kernel(info_ref, tiles_ref, *refs, team_count, piece_count, scaled, partial_count):
    columns = team_count // 2
    pieces, refs = refs[:piece_count], refs[piece_count:]
    partials, refs = refs[:partial_count], refs[partial_count:]
    outs, (split_ref, sums_ref) = refs[:team_count], refs[team_count:]
    team_index = lax.axis_index("rep")
    slot_total, tile_size, _ = tiles_ref.shape
    panel_rows, width = split_ref.shape[0], split_ref.shape[1] // 2
    share_rows = panel_rows // team_count
    block_count = panel_rows // tile_size

    def split(value, at):
        high = value.astype(jnp.bfloat16)
        split_ref[at, :width] = high
        split_ref[at, width:] = (value - high.astype(jnp.float32)).astype(jnp.bfloat16)

    if scaled:
        degrees_ref, panel_ref = pieces
        norms = norm_columns(degrees_ref[...])
        for block in range(block_count):
            at = pl.ds(block * tile_size, tile_size)
            split(panel_ref[at, :] * norms[:, block : block + 1], at)
    else:
        for k in range(piece_count):
            owner = source_team(team_index, k, team_count)
            split(pieces[k][...], pl.ds(pl.multiple_of(owner * share_rows, share_rows), share_rows))
    sums_ref[...] = jnp.zeros_like(sums_ref)
    live_count = info_ref[0, 0]
    for j in range(slot_total):
        source = pl.multiple_of(info_ref[1 + slot_total + j, 0] * tile_size, tile_size)
        product = jnp.dot(
            tiles_ref[j],
            split_ref[pl.ds(source, tile_size), :],
            preferred_element_type=jnp.float32,
        )
        row = jnp.where(j < live_count, info_ref[1 + j, 0], block_count)
        at = pl.ds(pl.multiple_of(row * tile_size, tile_size), tile_size)
        sums_ref[at, :] += product[:, :width] + product[:, width:]

    for parity in range(2):
        for column in range(columns):
            team = pair_teams(team_index, column, team_count)
            team = team if parity == 0 else team ^ 1
            value = sums_ref[pl.ds(pl.multiple_of(team * share_rows, share_rows), share_rows), :]
            at = parity * columns + column
            outs[at][...] = value + partials[at][...] if partials else value


def arc_step(info, tiles, pieces, partials, scaled):
    team_count = lax.axis_size("rep")
    panel_rows = pieces[1].shape[0] if scaled else sum(piece.shape[0] for piece in pieces)
    width = pieces[1].shape[1]
    slot_total, tile_size, _ = tiles.shape
    share = jax.ShapeDtypeStruct((panel_rows // team_count, width), jnp.float32)
    operands = [info, tiles, *pieces, *partials]
    return pl.pallas_call(
        functools.partial(
            arc_kernel,
            team_count=team_count,
            piece_count=len(pieces),
            scaled=scaled,
            partial_count=len(partials),
        ),
        out_shape=[share] * team_count,
        in_specs=[VMEM] * len(operands),
        out_specs=[VMEM] * team_count,
        scratch_shapes=[
            pltpu.VMEM((panel_rows, 2 * width), jnp.bfloat16),
            pltpu.VMEM((panel_rows + tile_size, width), jnp.float32),
        ],
        compiler_params=pltpu.CompilerParams(vmem_limit_bytes=VMEM_LIMIT),
        cost_estimate=pl.CostEstimate(
            flops=4 * slot_total * tile_size * tile_size * width, bytes_accessed=8 * panel_rows * width, transcendentals=0
        ),
    )(*operands)


def fetch(value, source, arc_length):
    cycle, team_count = lax.axis_size("blk"), lax.axis_size("rep")
    pairs = []
    for shard in range(cycle):
        for team in range(team_count):
            to_shard = (shard + team * arc_length) % cycle
            pairs.append((shard * team_count + source(shard, team), to_shard * team_count + team))
    return lax.ppermute(value, ("blk", "rep"), pairs)


def next_shard(value):
    cycle = lax.axis_size("blk")
    return lax.ppermute(value, "blk", [(i, (i + 1) % cycle) for i in range(cycle)])


def from_mate(value):
    team_count = lax.axis_size("rep")
    return lax.ppermute(value, "rep", [(team, team ^ 1) for team in range(team_count)])


def from_column(value, distance):
    team_count = lax.axis_size("rep")
    pairs = [((team + 2 * distance) % team_count, team) for team in range(team_count)]
    return lax.ppermute(value, "rep", pairs)


def team_terms(sums):
    columns = len(sums) // 2
    others = []
    for distance in range(1, columns):
        at = columns - distance
        others.append(from_column(sums[at] + from_mate(sums[columns + at]), distance))
    return [sums[0], from_mate(sums[columns]), *others]


def finish_kernel(base_ref, norm_ref, *refs, layer_count):
    *terms, out_hbm, held_ref, sems = refs
    pieces = sems.shape[0]
    rows = held_ref.shape[0] // pieces
    copies = []
    for piece in range(pieces):
        at = pl.ds(piece * rows, rows)
        total = terms[0][at, :]
        for term_ref in terms[1:]:
            total = total + term_ref[at, :]
        held_ref[at, :] = (base_ref[at, :] + total * norm_ref[at, :]) / layer_count
        copies.append(pltpu.make_async_copy(held_ref.at[at, :], out_hbm.at[at, :], sems.at[piece]))
        copies[-1].start()
    for copy in copies:
        copy.wait()


def finish(base, norm_scale, terms):
    return pl.pallas_call(
        functools.partial(finish_kernel, layer_count=LAYERS + 1.0),
        out_shape=jax.ShapeDtypeStruct(base.shape, jnp.float32),
        in_specs=[VMEM] * (2 + len(terms)),
        out_specs=ANY,
        scratch_shapes=[pltpu.VMEM(base.shape, jnp.float32), pltpu.SemaphoreType.DMA((2,))],
        compiler_params=pltpu.CompilerParams(vmem_limit_bytes=VMEM_LIMIT),
    )(base, norm_scale, *terms)


def per_device(embeddings, degrees, tile_values, tile_rows, tile_columns, slot_counts):
    arc_length, _, tile_size, _ = tile_values.shape[2:]
    panel_rows = embeddings.shape[0]
    cycle, team_count = lax.axis_size("blk"), lax.axis_size("rep")
    spread = [tuple(range(team_count))] * cycle
    if team_count == 4:
        spread = [(3, 0, 2, 1)] * (cycle - 1) + [(3, 1, 2, 0)]
    degrees = degrees.reshape(panel_rows // tile_size, tile_size)

    panel = fetch(embeddings, lambda shard, team: spread[shard][team], arc_length)
    pieces = [fetch(degrees, lambda shard, team: spread[shard][team], arc_length), panel]
    info = jnp.concatenate([slot_counts[0, 0][:, None], tile_rows[0, 0], tile_columns[0, 0]], axis=1)
    info = jnp.broadcast_to(info[:, :, None], (*info.shape, embeddings.shape[1]))
    info = [info[at] for at in range(arc_length)]
    tiles, own, norm_scale = prepare(degrees, embeddings, tile_values[0, 0], info[0])

    combined = own
    for layer in range(LAYERS):
        sums = ()
        for arc_slot in range(arc_length):
            sums = arc_step(info[arc_slot], tiles[arc_slot], pieces, sums, layer == 0)
            if arc_slot + 1 < arc_length:
                pieces = [next_shard(piece) for piece in pieces]
        terms = team_terms(sums)
        if layer + 1 == LAYERS:
            return finish(combined, norm_scale, terms)
        current = functools.reduce(jnp.add, terms) * norm_scale
        combined = combined + current
        source = current * norm_scale
        pieces = [
            fetch(source, lambda shard, team, k=k: source_team(team, k, team_count), arc_length)
            for k in range(team_count)
        ]


def solution(mesh):
    in_specs = (
        P(("groups", "blk"), None),
        P(("groups", "blk")),
        P(("groups", "blk"), "rep", None, None, None, None),
        P(("groups", "blk"), "rep", None, None),
        P(("groups", "blk"), "rep", None, None),
        P(("groups", "blk"), "rep", None),
    )
    out_specs = P(("groups", "blk", "rep"), None)
    return jax.shard_map(
        per_device, mesh=mesh, in_specs=in_specs, out_specs=out_specs, check_vma=False
    )
```

```python
import functools

import jax
import jax.numpy as jnp
from jax import lax
from jax.experimental import pallas as pl
from jax.experimental.pallas import tpu as pltpu
from jax.sharding import PartitionSpec as P

LAYERS = 2
VMEM_LIMIT = 16 * 1024 * 1024
VMEM = pl.BlockSpec(memory_space=pltpu.VMEM)
ANY = pl.BlockSpec(memory_space=pl.ANY)


def pair_teams(team_index, column, team_count):
    columns = team_count // 2
    return 2 * lax.rem(team_index // 2 + column, columns) + lax.rem(team_index, 2)


def source_team(team, turn, team_count):
    if team_count == 4:
        return (2 * (team % 2) + team // 2) ^ (0, 2, 1, 3)[turn]
    return (team + turn) % team_count


def norm_columns(degrees):
    return jnp.transpose(lax.rsqrt(degrees.astype(jnp.float32)))


def prepare_kernel(
    degrees_ref, embeddings_ref, tiles_ref, after_ref, held_tiles_ref, own_ref, norm_ref, panel_ref, sems
):
    del after_ref
    share_rows, width = own_ref.shape
    block_count, tile_size = degrees_ref.shape
    team_index = lax.axis_index("rep")
    at = pl.ds(pl.multiple_of(team_index * share_rows, share_rows), share_rows)
    tiles_copy = pltpu.make_async_copy(tiles_ref, held_tiles_ref, sems.at[0])
    own_copy = pltpu.make_async_copy(embeddings_ref.at[at, :], own_ref, sems.at[1])
    tiles_copy.start()
    own_copy.start()
    norms = norm_columns(degrees_ref[...])
    for block in range(block_count):
        panel_ref[block * tile_size : (block + 1) * tile_size, :] = jnp.broadcast_to(
            norms[:, block : block + 1], (tile_size, width)
        )
    norm_ref[...] = panel_ref[at, :]
    own_copy.wait()
    tiles_copy.wait()


def prepare(degrees, embeddings, tile_values, after):
    panel_rows, width = embeddings.shape
    share = jax.ShapeDtypeStruct((panel_rows // lax.axis_size("rep"), width), jnp.float32)
    return pl.pallas_call(
        prepare_kernel,
        out_shape=[jax.ShapeDtypeStruct(tile_values.shape, tile_values.dtype), share, share],
        in_specs=[VMEM, ANY, ANY, ANY],
        out_specs=[VMEM] * 3,
        scratch_shapes=[pltpu.VMEM((panel_rows, width), jnp.float32), pltpu.SemaphoreType.DMA((2,))],
        compiler_params=pltpu.CompilerParams(vmem_limit_bytes=VMEM_LIMIT),
        cost_estimate=pl.CostEstimate(
            flops=panel_rows * width, bytes_accessed=4 * panel_rows * width, transcendentals=0
        ),
    )(degrees, embeddings, tile_values, after)


def arc_kernel(info_ref, tiles_ref, *refs, team_count, piece_count, scaled, partial_count):
    columns = team_count // 2
    pieces, refs = refs[:piece_count], refs[piece_count:]
    partials, refs = refs[:partial_count], refs[partial_count:]
    outs, (split_ref, sums_ref) = refs[:team_count], refs[team_count:]
    team_index = lax.axis_index("rep")
    slot_total, tile_size, _ = tiles_ref.shape
    panel_rows, width = split_ref.shape[0], split_ref.shape[1] // 2
    share_rows = panel_rows // team_count
    block_count = panel_rows // tile_size

    def split(value, at):
        high = value.astype(jnp.bfloat16)
        split_ref[at, :width] = high
        split_ref[at, width:] = (value - high.astype(jnp.float32)).astype(jnp.bfloat16)

    if scaled:
        degrees_ref, panel_ref = pieces
        norms = norm_columns(degrees_ref[...])
        for block in range(block_count):
            at = pl.ds(block * tile_size, tile_size)
            split(panel_ref[at, :] * norms[:, block : block + 1], at)
    else:
        for k in range(piece_count):
            owner = source_team(team_index, k, team_count)
            split(pieces[k][...], pl.ds(pl.multiple_of(owner * share_rows, share_rows), share_rows))
    sums_ref[...] = jnp.zeros_like(sums_ref)
    live_count = info_ref[0, 0]
    for j in range(slot_total):
        source = pl.multiple_of(info_ref[1 + slot_total + j, 0] * tile_size, tile_size)
        product = jnp.dot(
            tiles_ref[j],
            split_ref[pl.ds(source, tile_size), :],
            preferred_element_type=jnp.float32,
        )
        row = jnp.where(j < live_count, info_ref[1 + j, 0], block_count)
        at = pl.ds(pl.multiple_of(row * tile_size, tile_size), tile_size)
        sums_ref[at, :] += product[:, :width] + product[:, width:]

    for parity in range(2):
        for column in range(columns):
            team = pair_teams(team_index, column, team_count)
            team = team if parity == 0 else team ^ 1
            value = sums_ref[pl.ds(pl.multiple_of(team * share_rows, share_rows), share_rows), :]
            at = parity * columns + column
            outs[at][...] = value + partials[at][...] if partials else value


def arc_step(info, tiles, pieces, partials, scaled):
    team_count = lax.axis_size("rep")
    panel_rows = pieces[1].shape[0] if scaled else sum(piece.shape[0] for piece in pieces)
    width = pieces[1].shape[1]
    slot_total, tile_size, _ = tiles.shape
    share = jax.ShapeDtypeStruct((panel_rows // team_count, width), jnp.float32)
    operands = [info, tiles, *pieces, *partials]
    return pl.pallas_call(
        functools.partial(
            arc_kernel,
            team_count=team_count,
            piece_count=len(pieces),
            scaled=scaled,
            partial_count=len(partials),
        ),
        out_shape=[share] * team_count,
        in_specs=[VMEM] * len(operands),
        out_specs=[VMEM] * team_count,
        scratch_shapes=[
            pltpu.VMEM((panel_rows, 2 * width), jnp.bfloat16),
            pltpu.VMEM((panel_rows + tile_size, width), jnp.float32),
        ],
        compiler_params=pltpu.CompilerParams(vmem_limit_bytes=VMEM_LIMIT),
        cost_estimate=pl.CostEstimate(
            flops=4 * slot_total * tile_size * tile_size * width, bytes_accessed=8 * panel_rows * width, transcendentals=0
        ),
    )(*operands)


def fetch(value, source, arc_length):
    cycle, team_count = lax.axis_size("blk"), lax.axis_size("rep")
    pairs = []
    for shard in range(cycle):
        for team in range(team_count):
            to_shard = (shard + team * arc_length) % cycle
            pairs.append((shard * team_count + source(shard, team), to_shard * team_count + team))
    return lax.ppermute(value, ("blk", "rep"), pairs)


def next_shard(value):
    cycle = lax.axis_size("blk")
    return lax.ppermute(value, "blk", [(i, (i + 1) % cycle) for i in range(cycle)])


def from_mate(value):
    team_count = lax.axis_size("rep")
    return lax.ppermute(value, "rep", [(team, team ^ 1) for team in range(team_count)])


def from_column(value, distance):
    team_count = lax.axis_size("rep")
    pairs = [((team + 2 * distance) % team_count, team) for team in range(team_count)]
    return lax.ppermute(value, "rep", pairs)


def team_terms(sums):
    columns = len(sums) // 2
    others = []
    for distance in range(1, columns):
        at = columns - distance
        others.append(from_column(sums[at] + from_mate(sums[columns + at]), distance))
    return [sums[0], from_mate(sums[columns]), *others]


def finish_kernel(base_ref, norm_ref, *refs, layer_count):
    *terms, out_hbm, held_ref, sems = refs
    pieces = sems.shape[0]
    rows = held_ref.shape[0] // pieces
    copies = []
    for piece in range(pieces):
        at = pl.ds(piece * rows, rows)
        total = terms[0][at, :]
        for term_ref in terms[1:]:
            total = total + term_ref[at, :]
        held_ref[at, :] = (base_ref[at, :] + total * norm_ref[at, :]) / layer_count
        copies.append(pltpu.make_async_copy(held_ref.at[at, :], out_hbm.at[at, :], sems.at[piece]))
        copies[-1].start()
    for copy in copies:
        copy.wait()


def finish(base, norm_scale, terms):
    return pl.pallas_call(
        functools.partial(finish_kernel, layer_count=LAYERS + 1.0),
        out_shape=jax.ShapeDtypeStruct(base.shape, jnp.float32),
        in_specs=[VMEM] * (2 + len(terms)),
        out_specs=ANY,
        scratch_shapes=[pltpu.VMEM(base.shape, jnp.float32), pltpu.SemaphoreType.DMA((2,))],
        compiler_params=pltpu.CompilerParams(vmem_limit_bytes=VMEM_LIMIT),
    )(base, norm_scale, *terms)


def per_device(embeddings, degrees, tile_values, tile_rows, tile_columns, slot_counts):
    arc_length, _, tile_size, _ = tile_values.shape[2:]
    panel_rows = embeddings.shape[0]
    cycle, team_count = lax.axis_size("blk"), lax.axis_size("rep")
    spread = [tuple(range(team_count))] * cycle
    if team_count == 4:
        spread = [(1, 2, 0, 3)] + [(3, 0, 2, 1)] * (cycle - 2) + [(1, 3, 0, 2)]
    degrees = degrees.reshape(panel_rows // tile_size, tile_size)

    panel = fetch(embeddings, lambda shard, team: spread[shard][team], arc_length)
    pieces = [fetch(degrees, lambda shard, team: spread[shard][team], arc_length), panel]
    info = jnp.concatenate([slot_counts[0, 0][:, None], tile_rows[0, 0], tile_columns[0, 0]], axis=1)
    info = jnp.broadcast_to(info[:, :, None], (*info.shape, embeddings.shape[1]))
    info = [info[at] for at in range(arc_length)]
    tiles, own, norm_scale = prepare(degrees, embeddings, tile_values[0, 0], info[0])

    combined = own
    for layer in range(LAYERS):
        sums = ()
        for arc_slot in range(arc_length):
            sums = arc_step(info[arc_slot], tiles[arc_slot], pieces, sums, layer == 0)
            if arc_slot + 1 < arc_length:
                pieces = [next_shard(piece) for piece in pieces]
        terms = team_terms(sums)
        if layer + 1 == LAYERS:
            return finish(combined, norm_scale, terms)
        current = functools.reduce(jnp.add, terms) * norm_scale
        combined = combined + current
        source = current * norm_scale
        pieces = [
            fetch(source, lambda shard, team, k=k: source_team(team, k, team_count), arc_length)
            for k in range(team_count)
        ]


def solution(mesh):
    in_specs = (
        P(("groups", "blk"), None),
        P(("groups", "blk")),
        P(("groups", "blk"), "rep", None, None, None, None),
        P(("groups", "blk"), "rep", None, None),
        P(("groups", "blk"), "rep", None, None),
        P(("groups", "blk"), "rep", None),
    )
    out_specs = P(("groups", "blk", "rep"), None)
    return jax.shard_map(
        per_device, mesh=mesh, in_specs=in_specs, out_specs=out_specs, check_vma=False
    )
```

```python
import functools

import jax
import jax.numpy as jnp
from jax import lax
from jax.experimental import pallas as pl
from jax.experimental.pallas import tpu as pltpu
from jax.sharding import PartitionSpec as P

LAYERS = 2
VMEM_LIMIT = 16 * 1024 * 1024
VMEM = pl.BlockSpec(memory_space=pltpu.VMEM)
ANY = pl.BlockSpec(memory_space=pl.ANY)


def pair_teams(team_index, column, team_count):
    columns = team_count // 2
    return 2 * lax.rem(team_index // 2 + column, columns) + lax.rem(team_index, 2)


def source_team(team, turn, team_count):
    if team_count == 4:
        return (2 * (team % 2) + team // 2) ^ (1, 0, 2, 3)[turn]
    return (team + turn) % team_count


def norm_columns(degrees):
    return jnp.transpose(lax.rsqrt(degrees.astype(jnp.float32)))


def prepare_kernel(
    degrees_ref, embeddings_ref, tiles_ref, after_ref, held_tiles_ref, own_ref, norm_ref, panel_ref, sems
):
    del after_ref
    share_rows, width = own_ref.shape
    block_count, tile_size = degrees_ref.shape
    team_index = lax.axis_index("rep")
    at = pl.ds(pl.multiple_of(team_index * share_rows, share_rows), share_rows)
    tiles_copy = pltpu.make_async_copy(tiles_ref, held_tiles_ref, sems.at[0])
    own_copy = pltpu.make_async_copy(embeddings_ref.at[at, :], own_ref, sems.at[1])
    tiles_copy.start()
    own_copy.start()
    norms = norm_columns(degrees_ref[...])
    for block in range(block_count):
        panel_ref[block * tile_size : (block + 1) * tile_size, :] = jnp.broadcast_to(
            norms[:, block : block + 1], (tile_size, width)
        )
    norm_ref[...] = panel_ref[at, :]
    own_copy.wait()
    tiles_copy.wait()


def prepare(degrees, embeddings, tile_values, after):
    panel_rows, width = embeddings.shape
    share = jax.ShapeDtypeStruct((panel_rows // lax.axis_size("rep"), width), jnp.float32)
    return pl.pallas_call(
        prepare_kernel,
        out_shape=[jax.ShapeDtypeStruct(tile_values.shape, tile_values.dtype), share, share],
        in_specs=[VMEM, ANY, ANY, ANY],
        out_specs=[VMEM] * 3,
        scratch_shapes=[pltpu.VMEM((panel_rows, width), jnp.float32), pltpu.SemaphoreType.DMA((2,))],
        compiler_params=pltpu.CompilerParams(vmem_limit_bytes=VMEM_LIMIT),
        cost_estimate=pl.CostEstimate(
            flops=panel_rows * width, bytes_accessed=4 * panel_rows * width, transcendentals=0
        ),
    )(degrees, embeddings, tile_values, after)


def arc_kernel(info_ref, tiles_ref, *refs, team_count, piece_count, scaled, partial_count):
    columns = team_count // 2
    pieces, refs = refs[:piece_count], refs[piece_count:]
    partials, refs = refs[:partial_count], refs[partial_count:]
    outs, (split_ref, sums_ref) = refs[:team_count], refs[team_count:]
    team_index = lax.axis_index("rep")
    slot_total, tile_size, _ = tiles_ref.shape
    panel_rows, width = split_ref.shape[0], split_ref.shape[1] // 2
    share_rows = panel_rows // team_count
    block_count = panel_rows // tile_size

    def split(value, at):
        high = value.astype(jnp.bfloat16)
        split_ref[at, :width] = high
        split_ref[at, width:] = (value - high.astype(jnp.float32)).astype(jnp.bfloat16)

    if scaled:
        degrees_ref, panel_ref = pieces
        norms = norm_columns(degrees_ref[...])
        for block in range(block_count):
            at = pl.ds(block * tile_size, tile_size)
            split(panel_ref[at, :] * norms[:, block : block + 1], at)
    else:
        for k in range(piece_count):
            owner = source_team(team_index, k, team_count)
            split(pieces[k][...], pl.ds(pl.multiple_of(owner * share_rows, share_rows), share_rows))
    sums_ref[...] = jnp.zeros_like(sums_ref)
    live_count = info_ref[0, 0]
    for j in range(slot_total):
        source = pl.multiple_of(info_ref[1 + slot_total + j, 0] * tile_size, tile_size)
        product = jnp.dot(
            tiles_ref[j],
            split_ref[pl.ds(source, tile_size), :],
            preferred_element_type=jnp.float32,
        )
        row = jnp.where(j < live_count, info_ref[1 + j, 0], block_count)
        at = pl.ds(pl.multiple_of(row * tile_size, tile_size), tile_size)
        sums_ref[at, :] += product[:, :width] + product[:, width:]

    for parity in range(2):
        for column in range(columns):
            team = pair_teams(team_index, column, team_count)
            team = team if parity == 0 else team ^ 1
            value = sums_ref[pl.ds(pl.multiple_of(team * share_rows, share_rows), share_rows), :]
            at = parity * columns + column
            outs[at][...] = value + partials[at][...] if partials else value


def arc_step(info, tiles, pieces, partials, scaled):
    team_count = lax.axis_size("rep")
    panel_rows = pieces[1].shape[0] if scaled else sum(piece.shape[0] for piece in pieces)
    width = pieces[1].shape[1]
    slot_total, tile_size, _ = tiles.shape
    share = jax.ShapeDtypeStruct((panel_rows // team_count, width), jnp.float32)
    operands = [info, tiles, *pieces, *partials]
    return pl.pallas_call(
        functools.partial(
            arc_kernel,
            team_count=team_count,
            piece_count=len(pieces),
            scaled=scaled,
            partial_count=len(partials),
        ),
        out_shape=[share] * team_count,
        in_specs=[VMEM] * len(operands),
        out_specs=[VMEM] * team_count,
        scratch_shapes=[
            pltpu.VMEM((panel_rows, 2 * width), jnp.bfloat16),
            pltpu.VMEM((panel_rows + tile_size, width), jnp.float32),
        ],
        compiler_params=pltpu.CompilerParams(vmem_limit_bytes=VMEM_LIMIT),
        cost_estimate=pl.CostEstimate(
            flops=4 * slot_total * tile_size * tile_size * width, bytes_accessed=8 * panel_rows * width, transcendentals=0
        ),
    )(*operands)


def fetch(value, source_team, arc_length):
    cycle, team_count = lax.axis_size("blk"), lax.axis_size("rep")
    pairs = []
    for shard in range(cycle):
        for team in range(team_count):
            to_shard = (shard + team * arc_length) % cycle
            pairs.append((shard * team_count + source_team(team), to_shard * team_count + team))
    return lax.ppermute(value, ("blk", "rep"), pairs)


def next_shard(value):
    cycle = lax.axis_size("blk")
    return lax.ppermute(value, "blk", [(i, (i + 1) % cycle) for i in range(cycle)])


def from_mate(value):
    team_count = lax.axis_size("rep")
    return lax.ppermute(value, "rep", [(team, team ^ 1) for team in range(team_count)])


def from_column(value, distance):
    team_count = lax.axis_size("rep")
    pairs = [((team + 2 * distance) % team_count, team) for team in range(team_count)]
    return lax.ppermute(value, "rep", pairs)


def team_terms(sums):
    columns = len(sums) // 2
    others = []
    for distance in range(1, columns):
        at = columns - distance
        others.append(from_column(sums[at] + from_mate(sums[columns + at]), distance))
    return [sums[0], from_mate(sums[columns]), *others]


def finish_kernel(base_ref, norm_ref, *refs, layer_count):
    *terms, out_hbm, held_ref, sems = refs
    pieces = sems.shape[0]
    rows = held_ref.shape[0] // pieces
    copies = []
    for piece in range(pieces):
        at = pl.ds(piece * rows, rows)
        total = terms[0][at, :]
        for term_ref in terms[1:]:
            total = total + term_ref[at, :]
        held_ref[at, :] = (base_ref[at, :] + total * norm_ref[at, :]) / layer_count
        copies.append(pltpu.make_async_copy(held_ref.at[at, :], out_hbm.at[at, :], sems.at[piece]))
        copies[-1].start()
    for copy in copies:
        copy.wait()


def finish(base, norm_scale, terms):
    return pl.pallas_call(
        functools.partial(finish_kernel, layer_count=LAYERS + 1.0),
        out_shape=jax.ShapeDtypeStruct(base.shape, jnp.float32),
        in_specs=[VMEM] * (2 + len(terms)),
        out_specs=ANY,
        scratch_shapes=[pltpu.VMEM(base.shape, jnp.float32), pltpu.SemaphoreType.DMA((2,))],
        compiler_params=pltpu.CompilerParams(vmem_limit_bytes=VMEM_LIMIT),
    )(base, norm_scale, *terms)


def per_device(embeddings, degrees, tile_values, tile_rows, tile_columns, slot_counts):
    arc_length, _, tile_size, _ = tile_values.shape[2:]
    panel_rows = embeddings.shape[0]
    team_count = lax.axis_size("rep")
    spread = (3, 0, 2, 1) if team_count == 4 else tuple(range(team_count))
    degrees = degrees.reshape(panel_rows // tile_size, tile_size)

    panel = fetch(embeddings, lambda team: spread[team], arc_length)
    pieces = [fetch(degrees, lambda team: spread[team], arc_length), panel]
    info = jnp.concatenate([slot_counts[0, 0][:, None], tile_rows[0, 0], tile_columns[0, 0]], axis=1)
    info = jnp.broadcast_to(info[:, :, None], (*info.shape, embeddings.shape[1]))
    info = [info[at] for at in range(arc_length)]
    tiles, own, norm_scale = prepare(degrees, embeddings, tile_values[0, 0], info[0])

    combined = own
    for layer in range(LAYERS):
        sums = ()
        for arc_slot in range(arc_length):
            sums = arc_step(info[arc_slot], tiles[arc_slot], pieces, sums, layer == 0)
            if arc_slot + 1 < arc_length:
                pieces = [next_shard(piece) for piece in pieces]
        terms = team_terms(sums)
        if layer + 1 == LAYERS:
            return finish(combined, norm_scale, terms)
        current = functools.reduce(jnp.add, terms) * norm_scale
        combined = combined + current
        source = current * norm_scale
        pieces = [
            fetch(source, lambda team, k=k: source_team(team, k, team_count), arc_length)
            for k in range(team_count)
        ]


def solution(mesh):
    in_specs = (
        P(("groups", "blk"), None),
        P(("groups", "blk")),
        P(("groups", "blk"), "rep", None, None, None, None),
        P(("groups", "blk"), "rep", None, None),
        P(("groups", "blk"), "rep", None, None),
        P(("groups", "blk"), "rep", None),
    )
    out_specs = P(("groups", "blk", "rep"), None)
    return jax.shard_map(
        per_device, mesh=mesh, in_specs=in_specs, out_specs=out_specs, check_vma=False
    )
```

```python
import functools

import jax
import jax.numpy as jnp
from jax import lax
from jax.experimental import pallas as pl
from jax.experimental.pallas import tpu as pltpu
from jax.sharding import PartitionSpec as P

LAYERS = 2
VMEM_LIMIT = 16 * 1024 * 1024
VMEM = pl.BlockSpec(memory_space=pltpu.VMEM)
ANY = pl.BlockSpec(memory_space=pl.ANY)


def pair_teams(team_index, column, team_count):
    columns = team_count // 2
    return 2 * lax.rem(team_index // 2 + column, columns) + lax.rem(team_index, 2)


def source_team(team, turn, team_count):
    if team_count == 4:
        return (3 * (team % 2)) ^ (team // 2) ^ (0, 2, 1, 3)[turn]
    return (team + turn) % team_count


def norm_columns(degrees):
    return jnp.transpose(lax.rsqrt(degrees.astype(jnp.float32)))


def prepare_kernel(
    degrees_ref, embeddings_ref, tiles_ref, after_ref, held_tiles_ref, own_ref, norm_ref, panel_ref, sems
):
    del after_ref
    share_rows, width = own_ref.shape
    block_count, tile_size = degrees_ref.shape
    team_index = lax.axis_index("rep")
    at = pl.ds(pl.multiple_of(team_index * share_rows, share_rows), share_rows)
    tiles_copy = pltpu.make_async_copy(tiles_ref, held_tiles_ref, sems.at[0])
    own_copy = pltpu.make_async_copy(embeddings_ref.at[at, :], own_ref, sems.at[1])
    tiles_copy.start()
    own_copy.start()
    norms = norm_columns(degrees_ref[...])
    for block in range(block_count):
        panel_ref[block * tile_size : (block + 1) * tile_size, :] = jnp.broadcast_to(
            norms[:, block : block + 1], (tile_size, width)
        )
    norm_ref[...] = panel_ref[at, :]
    own_copy.wait()
    tiles_copy.wait()


def prepare(degrees, embeddings, tile_values, after):
    panel_rows, width = embeddings.shape
    share = jax.ShapeDtypeStruct((panel_rows // lax.axis_size("rep"), width), jnp.float32)
    return pl.pallas_call(
        prepare_kernel,
        out_shape=[jax.ShapeDtypeStruct(tile_values.shape, tile_values.dtype), share, share],
        in_specs=[VMEM, ANY, ANY, ANY],
        out_specs=[VMEM] * 3,
        scratch_shapes=[pltpu.VMEM((panel_rows, width), jnp.float32), pltpu.SemaphoreType.DMA((2,))],
        compiler_params=pltpu.CompilerParams(vmem_limit_bytes=VMEM_LIMIT),
        cost_estimate=pl.CostEstimate(
            flops=panel_rows * width, bytes_accessed=4 * panel_rows * width, transcendentals=0
        ),
    )(degrees, embeddings, tile_values, after)


def arc_kernel(info_ref, tiles_ref, *refs, team_count, piece_count, scaled, partial_count):
    columns = team_count // 2
    pieces, refs = refs[:piece_count], refs[piece_count:]
    partials, refs = refs[:partial_count], refs[partial_count:]
    outs, (split_ref, sums_ref) = refs[:team_count], refs[team_count:]
    team_index = lax.axis_index("rep")
    slot_total, tile_size, _ = tiles_ref.shape
    panel_rows, width = split_ref.shape[0], split_ref.shape[1] // 2
    share_rows = panel_rows // team_count
    block_count = panel_rows // tile_size

    def split(value, at):
        high = value.astype(jnp.bfloat16)
        split_ref[at, :width] = high
        split_ref[at, width:] = (value - high.astype(jnp.float32)).astype(jnp.bfloat16)

    if scaled:
        degrees_ref, panel_ref = pieces
        norms = norm_columns(degrees_ref[...])
        for block in range(block_count):
            at = pl.ds(block * tile_size, tile_size)
            split(panel_ref[at, :] * norms[:, block : block + 1], at)
    else:
        for k in range(piece_count):
            owner = source_team(team_index, k, team_count)
            split(pieces[k][...], pl.ds(pl.multiple_of(owner * share_rows, share_rows), share_rows))
    sums_ref[...] = jnp.zeros_like(sums_ref)
    live_count = info_ref[0, 0]
    for j in range(slot_total):
        source = pl.multiple_of(info_ref[1 + slot_total + j, 0] * tile_size, tile_size)
        product = jnp.dot(
            tiles_ref[j],
            split_ref[pl.ds(source, tile_size), :],
            preferred_element_type=jnp.float32,
        )
        row = jnp.where(j < live_count, info_ref[1 + j, 0], block_count)
        at = pl.ds(pl.multiple_of(row * tile_size, tile_size), tile_size)
        sums_ref[at, :] += product[:, :width] + product[:, width:]

    for parity in range(2):
        for column in range(columns):
            team = pair_teams(team_index, column, team_count)
            team = team if parity == 0 else team ^ 1
            value = sums_ref[pl.ds(pl.multiple_of(team * share_rows, share_rows), share_rows), :]
            at = parity * columns + column
            outs[at][...] = value + partials[at][...] if partials else value


def arc_step(info, tiles, pieces, partials, scaled):
    team_count = lax.axis_size("rep")
    panel_rows = pieces[1].shape[0] if scaled else sum(piece.shape[0] for piece in pieces)
    width = pieces[1].shape[1]
    slot_total, tile_size, _ = tiles.shape
    share = jax.ShapeDtypeStruct((panel_rows // team_count, width), jnp.float32)
    operands = [info, tiles, *pieces, *partials]
    return pl.pallas_call(
        functools.partial(
            arc_kernel,
            team_count=team_count,
            piece_count=len(pieces),
            scaled=scaled,
            partial_count=len(partials),
        ),
        out_shape=[share] * team_count,
        in_specs=[VMEM] * len(operands),
        out_specs=[VMEM] * team_count,
        scratch_shapes=[
            pltpu.VMEM((panel_rows, 2 * width), jnp.bfloat16),
            pltpu.VMEM((panel_rows + tile_size, width), jnp.float32),
        ],
        compiler_params=pltpu.CompilerParams(vmem_limit_bytes=VMEM_LIMIT),
        cost_estimate=pl.CostEstimate(
            flops=4 * slot_total * tile_size * tile_size * width, bytes_accessed=8 * panel_rows * width, transcendentals=0
        ),
    )(*operands)


def fetch(value, source_team, arc_length):
    cycle, team_count = lax.axis_size("blk"), lax.axis_size("rep")
    pairs = []
    for shard in range(cycle):
        for team in range(team_count):
            to_shard = (shard + team * arc_length) % cycle
            pairs.append((shard * team_count + source_team(team), to_shard * team_count + team))
    return lax.ppermute(value, ("blk", "rep"), pairs)


def next_shard(value):
    cycle = lax.axis_size("blk")
    return lax.ppermute(value, "blk", [(i, (i + 1) % cycle) for i in range(cycle)])


def from_mate(value):
    team_count = lax.axis_size("rep")
    return lax.ppermute(value, "rep", [(team, team ^ 1) for team in range(team_count)])


def from_column(value, distance):
    team_count = lax.axis_size("rep")
    pairs = [((team + 2 * distance) % team_count, team) for team in range(team_count)]
    return lax.ppermute(value, "rep", pairs)


def team_terms(sums):
    columns = len(sums) // 2
    others = []
    for distance in range(1, columns):
        at = columns - distance
        others.append(from_column(sums[at] + from_mate(sums[columns + at]), distance))
    return [sums[0], from_mate(sums[columns]), *others]


def finish_kernel(base_ref, norm_ref, *refs, layer_count):
    *terms, out_hbm, held_ref, sems = refs
    pieces = sems.shape[0]
    rows = held_ref.shape[0] // pieces
    copies = []
    for piece in range(pieces):
        at = pl.ds(piece * rows, rows)
        total = terms[0][at, :]
        for term_ref in terms[1:]:
            total = total + term_ref[at, :]
        held_ref[at, :] = (base_ref[at, :] + total * norm_ref[at, :]) / layer_count
        copies.append(pltpu.make_async_copy(held_ref.at[at, :], out_hbm.at[at, :], sems.at[piece]))
        copies[-1].start()
    for copy in copies:
        copy.wait()


def finish(base, norm_scale, terms):
    return pl.pallas_call(
        functools.partial(finish_kernel, layer_count=LAYERS + 1.0),
        out_shape=jax.ShapeDtypeStruct(base.shape, jnp.float32),
        in_specs=[VMEM] * (2 + len(terms)),
        out_specs=ANY,
        scratch_shapes=[pltpu.VMEM(base.shape, jnp.float32), pltpu.SemaphoreType.DMA((2,))],
        compiler_params=pltpu.CompilerParams(vmem_limit_bytes=VMEM_LIMIT),
    )(base, norm_scale, *terms)


def per_device(embeddings, degrees, tile_values, tile_rows, tile_columns, slot_counts):
    arc_length, _, tile_size, _ = tile_values.shape[2:]
    panel_rows = embeddings.shape[0]
    team_count = lax.axis_size("rep")
    spread = (3, 0, 2, 1) if team_count == 4 else tuple(range(team_count))
    degrees = degrees.reshape(panel_rows // tile_size, tile_size)

    panel = fetch(embeddings, lambda team: spread[team], arc_length)
    pieces = [fetch(degrees, lambda team: spread[team], arc_length), panel]
    info = jnp.concatenate([slot_counts[0, 0][:, None], tile_rows[0, 0], tile_columns[0, 0]], axis=1)
    info = jnp.broadcast_to(info[:, :, None], (*info.shape, embeddings.shape[1]))
    info = [info[at] for at in range(arc_length)]
    tiles, own, norm_scale = prepare(degrees, embeddings, tile_values[0, 0], info[0])

    combined = own
    for layer in range(LAYERS):
        sums = ()
        for arc_slot in range(arc_length):
            sums = arc_step(info[arc_slot], tiles[arc_slot], pieces, sums, layer == 0)
            if arc_slot + 1 < arc_length:
                pieces = [next_shard(piece) for piece in pieces]
        terms = team_terms(sums)
        if layer + 1 == LAYERS:
            return finish(combined, norm_scale, terms)
        current = functools.reduce(jnp.add, terms) * norm_scale
        combined = combined + current
        source = current * norm_scale
        pieces = [
            fetch(source, lambda team, k=k: source_team(team, k, team_count), arc_length)
            for k in range(team_count)
        ]


def solution(mesh):
    in_specs = (
        P(("groups", "blk"), None),
        P(("groups", "blk")),
        P(("groups", "blk"), "rep", None, None, None, None),
        P(("groups", "blk"), "rep", None, None),
        P(("groups", "blk"), "rep", None, None),
        P(("groups", "blk"), "rep", None),
    )
    out_specs = P(("groups", "blk", "rep"), None)
    return jax.shard_map(
        per_device, mesh=mesh, in_specs=in_specs, out_specs=out_specs, check_vma=False
    )
```

```python
import functools

import jax
import jax.numpy as jnp
from jax import lax
from jax.experimental import pallas as pl
from jax.experimental.pallas import tpu as pltpu
from jax.sharding import PartitionSpec as P

LAYERS = 2
VMEM_LIMIT = 16 * 1024 * 1024
VMEM = pl.BlockSpec(memory_space=pltpu.VMEM)
ANY = pl.BlockSpec(memory_space=pl.ANY)


def pair_teams(team_index, column, team_count):
    columns = team_count // 2
    return 2 * lax.rem(team_index // 2 + column, columns) + lax.rem(team_index, 2)


def source_team(team, turn, team_count):
    if team_count == 4:
        return (2 * (team % 2) + team // 2) ^ (0, 2, 1, 3)[turn]
    return (team + turn) % team_count


def norm_columns(degrees):
    return jnp.transpose(lax.rsqrt(degrees.astype(jnp.float32)))


def prepare_kernel(
    degrees_ref, embeddings_ref, tiles_ref, after_ref, held_tiles_ref, own_ref, norm_ref, panel_ref, sems
):
    del after_ref
    share_rows, width = own_ref.shape
    block_count, tile_size = degrees_ref.shape
    team_index = lax.axis_index("rep")
    at = pl.ds(pl.multiple_of(team_index * share_rows, share_rows), share_rows)
    tiles_copy = pltpu.make_async_copy(tiles_ref, held_tiles_ref, sems.at[0])
    own_copy = pltpu.make_async_copy(embeddings_ref.at[at, :], own_ref, sems.at[1])
    tiles_copy.start()
    own_copy.start()
    norms = norm_columns(degrees_ref[...])
    for block in range(block_count):
        panel_ref[block * tile_size : (block + 1) * tile_size, :] = jnp.broadcast_to(
            norms[:, block : block + 1], (tile_size, width)
        )
    norm_ref[...] = panel_ref[at, :]
    own_copy.wait()
    tiles_copy.wait()


def prepare(degrees, embeddings, tile_values, after):
    panel_rows, width = embeddings.shape
    share = jax.ShapeDtypeStruct((panel_rows // lax.axis_size("rep"), width), jnp.float32)
    return pl.pallas_call(
        prepare_kernel,
        out_shape=[jax.ShapeDtypeStruct(tile_values.shape, tile_values.dtype), share, share],
        in_specs=[VMEM, ANY, ANY, ANY],
        out_specs=[VMEM] * 3,
        scratch_shapes=[pltpu.VMEM((panel_rows, width), jnp.float32), pltpu.SemaphoreType.DMA((2,))],
        compiler_params=pltpu.CompilerParams(vmem_limit_bytes=VMEM_LIMIT),
        cost_estimate=pl.CostEstimate(
            flops=panel_rows * width, bytes_accessed=4 * panel_rows * width, transcendentals=0
        ),
    )(degrees, embeddings, tile_values, after)


def arc_kernel(info_ref, tiles_ref, *refs, team_count, piece_count, scaled, partial_count):
    columns = team_count // 2
    pieces, refs = refs[:piece_count], refs[piece_count:]
    partials, refs = refs[:partial_count], refs[partial_count:]
    outs, (split_ref, sums_ref) = refs[:team_count], refs[team_count:]
    team_index = lax.axis_index("rep")
    slot_total, tile_size, _ = tiles_ref.shape
    panel_rows, width = split_ref.shape[0], split_ref.shape[1] // 2
    share_rows = panel_rows // team_count
    block_count = panel_rows // tile_size

    def split(value, at):
        high = value.astype(jnp.bfloat16)
        split_ref[at, :width] = high
        split_ref[at, width:] = (value - high.astype(jnp.float32)).astype(jnp.bfloat16)

    if scaled:
        degrees_ref, panel_ref = pieces
        norms = norm_columns(degrees_ref[...])
        for block in range(block_count):
            at = pl.ds(block * tile_size, tile_size)
            split(panel_ref[at, :] * norms[:, block : block + 1], at)
    else:
        for k in range(piece_count):
            owner = source_team(team_index, k, team_count)
            split(pieces[k][...], pl.ds(pl.multiple_of(owner * share_rows, share_rows), share_rows))
    sums_ref[...] = jnp.zeros_like(sums_ref)
    live_count = info_ref[0, 0]
    for j in range(slot_total):
        source = pl.multiple_of(info_ref[1 + slot_total + j, 0] * tile_size, tile_size)
        product = jnp.dot(
            tiles_ref[j],
            split_ref[pl.ds(source, tile_size), :],
            preferred_element_type=jnp.float32,
        )
        row = jnp.where(j < live_count, info_ref[1 + j, 0], block_count)
        at = pl.ds(pl.multiple_of(row * tile_size, tile_size), tile_size)
        sums_ref[at, :] += product[:, :width] + product[:, width:]

    for parity in range(2):
        for column in range(columns):
            team = pair_teams(team_index, column, team_count)
            team = team if parity == 0 else team ^ 1
            value = sums_ref[pl.ds(pl.multiple_of(team * share_rows, share_rows), share_rows), :]
            at = parity * columns + column
            outs[at][...] = value + partials[at][...] if partials else value


def arc_step(info, tiles, pieces, partials, scaled):
    team_count = lax.axis_size("rep")
    panel_rows = pieces[1].shape[0] if scaled else sum(piece.shape[0] for piece in pieces)
    width = pieces[1].shape[1]
    slot_total, tile_size, _ = tiles.shape
    share = jax.ShapeDtypeStruct((panel_rows // team_count, width), jnp.float32)
    operands = [info, tiles, *pieces, *partials]
    return pl.pallas_call(
        functools.partial(
            arc_kernel,
            team_count=team_count,
            piece_count=len(pieces),
            scaled=scaled,
            partial_count=len(partials),
        ),
        out_shape=[share] * team_count,
        in_specs=[VMEM] * len(operands),
        out_specs=[VMEM] * team_count,
        scratch_shapes=[
            pltpu.VMEM((panel_rows, 2 * width), jnp.bfloat16),
            pltpu.VMEM((panel_rows + tile_size, width), jnp.float32),
        ],
        compiler_params=pltpu.CompilerParams(vmem_limit_bytes=VMEM_LIMIT),
        cost_estimate=pl.CostEstimate(
            flops=4 * slot_total * tile_size * tile_size * width, bytes_accessed=8 * panel_rows * width, transcendentals=0
        ),
    )(*operands)


def fetch(value, source_team, arc_length):
    cycle, team_count = lax.axis_size("blk"), lax.axis_size("rep")
    pairs = []
    for shard in range(cycle):
        for team in range(team_count):
            to_shard = (shard + team * arc_length) % cycle
            pairs.append((shard * team_count + source_team(team), to_shard * team_count + team))
    return lax.ppermute(value, ("blk", "rep"), pairs)


def next_shard(value):
    cycle = lax.axis_size("blk")
    return lax.ppermute(value, "blk", [(i, (i + 1) % cycle) for i in range(cycle)])


def from_mate(value):
    team_count = lax.axis_size("rep")
    return lax.ppermute(value, "rep", [(team, team ^ 1) for team in range(team_count)])


def from_column(value, distance):
    team_count = lax.axis_size("rep")
    pairs = [((team + 2 * distance) % team_count, team) for team in range(team_count)]
    return lax.ppermute(value, "rep", pairs)


def team_terms(sums):
    columns = len(sums) // 2
    others = []
    for distance in range(1, columns):
        at = columns - distance
        others.append(from_column(sums[at] + from_mate(sums[columns + at]), distance))
    return [sums[0], from_mate(sums[columns]), *others]


def finish_kernel(base_ref, norm_ref, *refs, layer_count):
    *terms, out_hbm, held_ref, sems = refs
    pieces = sems.shape[0]
    rows = held_ref.shape[0] // pieces
    copies = []
    for piece in range(pieces):
        at = pl.ds(piece * rows, rows)
        total = terms[0][at, :]
        for term_ref in terms[1:]:
            total = total + term_ref[at, :]
        held_ref[at, :] = (base_ref[at, :] + total * norm_ref[at, :]) / layer_count
        copies.append(pltpu.make_async_copy(held_ref.at[at, :], out_hbm.at[at, :], sems.at[piece]))
        copies[-1].start()
    for copy in copies:
        copy.wait()


def finish(base, norm_scale, terms):
    return pl.pallas_call(
        functools.partial(finish_kernel, layer_count=LAYERS + 1.0),
        out_shape=jax.ShapeDtypeStruct(base.shape, jnp.float32),
        in_specs=[VMEM] * (2 + len(terms)),
        out_specs=ANY,
        scratch_shapes=[pltpu.VMEM(base.shape, jnp.float32), pltpu.SemaphoreType.DMA((2,))],
        compiler_params=pltpu.CompilerParams(vmem_limit_bytes=VMEM_LIMIT),
    )(base, norm_scale, *terms)


def per_device(embeddings, degrees, tile_values, tile_rows, tile_columns, slot_counts):
    arc_length, _, tile_size, _ = tile_values.shape[2:]
    panel_rows = embeddings.shape[0]
    team_count = lax.axis_size("rep")
    spread = (2, 0, 3, 1) if team_count == 4 else tuple(range(team_count))
    degrees = degrees.reshape(panel_rows // tile_size, tile_size)

    panel = fetch(embeddings, lambda team: spread[team], arc_length)
    pieces = [fetch(degrees, lambda team: spread[team], arc_length), panel]
    info = jnp.concatenate([slot_counts[0, 0][:, None], tile_rows[0, 0], tile_columns[0, 0]], axis=1)
    info = jnp.broadcast_to(info[:, :, None], (*info.shape, embeddings.shape[1]))
    info = [info[at] for at in range(arc_length)]
    tiles, own, norm_scale = prepare(degrees, embeddings, tile_values[0, 0], info[0])

    combined = own
    for layer in range(LAYERS):
        sums = ()
        for arc_slot in range(arc_length):
            sums = arc_step(info[arc_slot], tiles[arc_slot], pieces, sums, layer == 0)
            if arc_slot + 1 < arc_length:
                pieces = [next_shard(piece) for piece in pieces]
        terms = team_terms(sums)
        if layer + 1 == LAYERS:
            return finish(combined, norm_scale, terms)
        current = functools.reduce(jnp.add, terms) * norm_scale
        combined = combined + current
        source = current * norm_scale
        pieces = [
            fetch(source, lambda team, k=k: source_team(team, k, team_count), arc_length)
            for k in range(team_count)
        ]


def solution(mesh):
    in_specs = (
        P(("groups", "blk"), None),
        P(("groups", "blk")),
        P(("groups", "blk"), "rep", None, None, None, None),
        P(("groups", "blk"), "rep", None, None),
        P(("groups", "blk"), "rep", None, None),
        P(("groups", "blk"), "rep", None),
    )
    out_specs = P(("groups", "blk", "rep"), None)
    return jax.shard_map(
        per_device, mesh=mesh, in_specs=in_specs, out_specs=out_specs, check_vma=False
    )
```

```python
import functools

import jax
import jax.numpy as jnp
from jax import lax
from jax.experimental import pallas as pl
from jax.experimental.pallas import tpu as pltpu
from jax.sharding import PartitionSpec as P

LAYERS = 2
VMEM_LIMIT = 16 * 1024 * 1024
VMEM = pl.BlockSpec(memory_space=pltpu.VMEM)
ANY = pl.BlockSpec(memory_space=pl.ANY)


def pair_teams(team_index, column, team_count):
    columns = team_count // 2
    return 2 * lax.rem(team_index // 2 + column, columns) + lax.rem(team_index, 2)


def source_team(team, turn, team_count):
    if team_count == 4:
        return (2 * (team % 2) + team // 2) ^ (0, 2, 1, 3)[turn]
    return (team + turn) % team_count


def norm_columns(degrees):
    return jnp.transpose(lax.rsqrt(degrees.astype(jnp.float32)))


def prepare_kernel(
    degrees_ref, embeddings_ref, tiles_ref, after_ref, held_tiles_ref, own_ref, norm_ref, panel_ref, sems
):
    del after_ref
    share_rows, width = own_ref.shape
    block_count, tile_size = degrees_ref.shape
    team_index = lax.axis_index("rep")
    at = pl.ds(pl.multiple_of(team_index * share_rows, share_rows), share_rows)
    tiles_copy = pltpu.make_async_copy(tiles_ref, held_tiles_ref, sems.at[0])
    own_copy = pltpu.make_async_copy(embeddings_ref.at[at, :], own_ref, sems.at[1])
    tiles_copy.start()
    own_copy.start()
    norms = norm_columns(degrees_ref[...])
    for block in range(block_count):
        panel_ref[block * tile_size : (block + 1) * tile_size, :] = jnp.broadcast_to(
            norms[:, block : block + 1], (tile_size, width)
        )
    norm_ref[...] = panel_ref[at, :]
    own_copy.wait()
    tiles_copy.wait()


def prepare(degrees, embeddings, tile_values, after):
    panel_rows, width = embeddings.shape
    share = jax.ShapeDtypeStruct((panel_rows // lax.axis_size("rep"), width), jnp.float32)
    return pl.pallas_call(
        prepare_kernel,
        out_shape=[jax.ShapeDtypeStruct(tile_values.shape, tile_values.dtype), share, share],
        in_specs=[VMEM, ANY, ANY, ANY],
        out_specs=[VMEM] * 3,
        scratch_shapes=[pltpu.VMEM((panel_rows, width), jnp.float32), pltpu.SemaphoreType.DMA((2,))],
        compiler_params=pltpu.CompilerParams(vmem_limit_bytes=VMEM_LIMIT),
        cost_estimate=pl.CostEstimate(
            flops=panel_rows * width, bytes_accessed=4 * panel_rows * width, transcendentals=0
        ),
    )(degrees, embeddings, tile_values, after)


def arc_kernel(info_ref, tiles_ref, *refs, team_count, piece_count, scaled, partial_count):
    columns = team_count // 2
    pieces, refs = refs[:piece_count], refs[piece_count:]
    partials, refs = refs[:partial_count], refs[partial_count:]
    outs, (split_ref, sums_ref) = refs[:team_count], refs[team_count:]
    team_index = lax.axis_index("rep")
    slot_total, tile_size, _ = tiles_ref.shape
    panel_rows, width = split_ref.shape[0], split_ref.shape[1] // 2
    share_rows = panel_rows // team_count
    block_count = panel_rows // tile_size

    def split(value, at):
        high = value.astype(jnp.bfloat16)
        split_ref[at, :width] = high
        split_ref[at, width:] = (value - high.astype(jnp.float32)).astype(jnp.bfloat16)

    if scaled:
        degrees_ref, panel_ref = pieces
        norms = norm_columns(degrees_ref[...])
        for block in range(block_count):
            at = pl.ds(block * tile_size, tile_size)
            split(panel_ref[at, :] * norms[:, block : block + 1], at)
    else:
        for k in range(piece_count):
            owner = source_team(team_index, k, team_count)
            split(pieces[k][...], pl.ds(pl.multiple_of(owner * share_rows, share_rows), share_rows))
    sums_ref[...] = jnp.zeros_like(sums_ref)
    live_count = info_ref[0, 0]
    for j in range(slot_total):
        source = pl.multiple_of(info_ref[1 + slot_total + j, 0] * tile_size, tile_size)
        product = jnp.dot(
            tiles_ref[j],
            split_ref[pl.ds(source, tile_size), :],
            preferred_element_type=jnp.float32,
        )
        row = jnp.where(j < live_count, info_ref[1 + j, 0], block_count)
        at = pl.ds(pl.multiple_of(row * tile_size, tile_size), tile_size)
        sums_ref[at, :] += product[:, :width] + product[:, width:]

    for parity in range(2):
        for column in range(columns):
            team = pair_teams(team_index, column, team_count)
            team = team if parity == 0 else team ^ 1
            value = sums_ref[pl.ds(pl.multiple_of(team * share_rows, share_rows), share_rows), :]
            at = parity * columns + column
            outs[at][...] = value + partials[at][...] if partials else value


def arc_step(info, tiles, pieces, partials, scaled):
    team_count = lax.axis_size("rep")
    panel_rows = pieces[1].shape[0] if scaled else sum(piece.shape[0] for piece in pieces)
    width = pieces[1].shape[1]
    slot_total, tile_size, _ = tiles.shape
    share = jax.ShapeDtypeStruct((panel_rows // team_count, width), jnp.float32)
    operands = [info, tiles, *pieces, *partials]
    return pl.pallas_call(
        functools.partial(
            arc_kernel,
            team_count=team_count,
            piece_count=len(pieces),
            scaled=scaled,
            partial_count=len(partials),
        ),
        out_shape=[share] * team_count,
        in_specs=[VMEM] * len(operands),
        out_specs=[VMEM] * team_count,
        scratch_shapes=[
            pltpu.VMEM((panel_rows, 2 * width), jnp.bfloat16),
            pltpu.VMEM((panel_rows + tile_size, width), jnp.float32),
        ],
        compiler_params=pltpu.CompilerParams(vmem_limit_bytes=VMEM_LIMIT),
        cost_estimate=pl.CostEstimate(
            flops=4 * slot_total * tile_size * tile_size * width, bytes_accessed=8 * panel_rows * width, transcendentals=0
        ),
    )(*operands)


def fetch(value, source_team, arc_length):
    cycle, team_count = lax.axis_size("blk"), lax.axis_size("rep")
    pairs = []
    for shard in range(cycle):
        for team in range(team_count):
            to_shard = (shard + team * arc_length) % cycle
            pairs.append((shard * team_count + source_team(team), to_shard * team_count + team))
    return lax.ppermute(value, ("blk", "rep"), pairs)


def next_shard(value):
    cycle = lax.axis_size("blk")
    return lax.ppermute(value, "blk", [(i, (i + 1) % cycle) for i in range(cycle)])


def from_mate(value):
    team_count = lax.axis_size("rep")
    return lax.ppermute(value, "rep", [(team, team ^ 1) for team in range(team_count)])


def from_column(value, distance):
    team_count = lax.axis_size("rep")
    pairs = [((team + 2 * distance) % team_count, team) for team in range(team_count)]
    return lax.ppermute(value, "rep", pairs)


def team_terms(sums):
    columns = len(sums) // 2
    others = []
    for distance in range(1, columns):
        at = columns - distance
        others.append(from_column(sums[at] + from_mate(sums[columns + at]), distance))
    return [sums[0], from_mate(sums[columns]), *others]


def finish_kernel(base_ref, norm_ref, *refs, layer_count):
    *terms, out_hbm, held_ref, sems = refs
    pieces = sems.shape[0]
    rows = held_ref.shape[0] // pieces
    copies = []
    for piece in range(pieces):
        at = pl.ds(piece * rows, rows)
        total = terms[0][at, :]
        for term_ref in terms[1:]:
            total = total + term_ref[at, :]
        held_ref[at, :] = (base_ref[at, :] + total * norm_ref[at, :]) / layer_count
        copies.append(pltpu.make_async_copy(held_ref.at[at, :], out_hbm.at[at, :], sems.at[piece]))
        copies[-1].start()
    for copy in copies:
        copy.wait()


def finish(base, norm_scale, terms):
    return pl.pallas_call(
        functools.partial(finish_kernel, layer_count=LAYERS + 1.0),
        out_shape=jax.ShapeDtypeStruct(base.shape, jnp.float32),
        in_specs=[VMEM] * (2 + len(terms)),
        out_specs=ANY,
        scratch_shapes=[pltpu.VMEM(base.shape, jnp.float32), pltpu.SemaphoreType.DMA((2,))],
        compiler_params=pltpu.CompilerParams(vmem_limit_bytes=VMEM_LIMIT),
    )(base, norm_scale, *terms)


def per_device(embeddings, degrees, tile_values, tile_rows, tile_columns, slot_counts):
    arc_length, _, tile_size, _ = tile_values.shape[2:]
    panel_rows = embeddings.shape[0]
    team_count = lax.axis_size("rep")
    spread = (2, 0, 3, 1) if team_count == 4 else tuple(range(team_count))
    degrees = degrees.reshape(panel_rows // tile_size, tile_size)

    panel = fetch(embeddings, lambda team: spread[team], arc_length)
    beside = (3, 1, 2, 0) if team_count == 4 else spread
    pieces = [fetch(degrees, lambda team: beside[team], arc_length), panel]
    info = jnp.concatenate([slot_counts[0, 0][:, None], tile_rows[0, 0], tile_columns[0, 0]], axis=1)
    info = jnp.broadcast_to(info[:, :, None], (*info.shape, embeddings.shape[1]))
    info = [info[at] for at in range(arc_length)]
    tiles, own, norm_scale = prepare(degrees, embeddings, tile_values[0, 0], info[0])

    combined = own
    for layer in range(LAYERS):
        sums = ()
        for arc_slot in range(arc_length):
            sums = arc_step(info[arc_slot], tiles[arc_slot], pieces, sums, layer == 0)
            if arc_slot + 1 < arc_length:
                pieces = [next_shard(piece) for piece in pieces]
        terms = team_terms(sums)
        if layer + 1 == LAYERS:
            return finish(combined, norm_scale, terms)
        current = functools.reduce(jnp.add, terms) * norm_scale
        combined = combined + current
        source = current * norm_scale
        pieces = [
            fetch(source, lambda team, k=k: source_team(team, k, team_count), arc_length)
            for k in range(team_count)
        ]


def solution(mesh):
    in_specs = (
        P(("groups", "blk"), None),
        P(("groups", "blk")),
        P(("groups", "blk"), "rep", None, None, None, None),
        P(("groups", "blk"), "rep", None, None),
        P(("groups", "blk"), "rep", None, None),
        P(("groups", "blk"), "rep", None),
    )
    out_specs = P(("groups", "blk", "rep"), None)
    return jax.shard_map(
        per_device, mesh=mesh, in_specs=in_specs, out_specs=out_specs, check_vma=False
    )
```
